32 devices in a mesh: dp: 4 (over z), sp: 8 (over y, x, core).
Axes of the slice: x: 2, y: 2, z: 4, core: 2. Of those that a mesh axis runs over, the one named last changes fastest.
Arguments:
- tokens: bfloat16 [4, 4096, 2048], P('dp', 'sp'), may hold values from -6 to 6
- segment_ids: int32 [4, 4096], P('dp', 'sp'), may hold values from 0 to 1, as said below
- selected: int32 [4, 4096], P('dp', 'sp'), may hold values from 0 to 1, as said below
- cotangent: bfloat16 [4, 4096, 2048], P('dp', 'sp'), may hold values from -6 to 6
- w_qkv: bfloat16 [2048, 2560], P('sp'), may hold values from -0.125 to 0.125
- w_out: bfloat16 [2048, 2048], P('sp'), may hold values from -1.5 to 1.5
- w_gate_up: bfloat16 [2048, 11264], P('sp'), may hold values from -0.125 to 0.125
- w_down: bfloat16 [5632, 2048], P('sp'), may hold values from -0.078125 to 0.078125
- g_attn: bfloat16 [2048], P('sp'), may hold values from 0.5 to 1.5
- g_mlp: bfloat16 [2048], P('sp'), may hold values from 0.5 to 1.5
Outputs:
- output: bfloat16 [4, 4096, 2048], P('dp', 'sp')
- grad_tokens: bfloat16 [4, 4096, 2048], P('dp', 'sp')
- grad_w_qkv: float32 [2048, 2560], P('sp')
- grad_w_out: float32 [2048, 2048], P('sp')
- grad_w_gate_up: float32 [2048, 11264], P('sp')
- grad_w_down: float32 [5632, 2048], P('sp')
- grad_g_attn: float32 [2048], P('sp')
- grad_g_mlp: float32 [2048], P('sp')
The draws below stay inside these ranges and needn't reach their ends.
Inputs may be any that keep to these rules, and one draw needn't show every extreme that they name: `segment_ids`: 0 on a stream's first document and 1 on its second, never falling along a stream; one stream of all, drawn from the seed, is a single document, and in the others the second document begins at a place from 1024 to 3072. `selected`: 1 where a token's output gradient counts, else 0.
All inputs are finite; a program needn't handle non-finite values.
Results may differ from the reference program's by a relative error of at most 0.02.
Values may be sent and summed in bfloat16 or wider, within the bound.
No kernel may reach another device: no remote copies, remote signals or barrier semaphores. Data moves between devices by JAX's collectives and lax.ppermute only.
A program may use at most 640 MiB of HBM per device.

```python
import jax
import jax.numpy as jnp
from jax import lax

D = 2048
H = 32
KV = 4
HD = 64
FF = 5632
LEN = 4096
STREAMS = 4


def stream_bounds(key):
    bounds_drawn = jax.random.randint(key, (STREAMS,), LEN // 4, 3 * LEN // 4 + 1)
    single = jax.random.randint(jax.random.fold_in(key, 1), (), 0, STREAMS)
    whole_doc = jnp.arange(STREAMS, dtype=jnp.int32) == single
    return jnp.where(whole_doc, LEN, bounds_drawn)


def draw_segment_ids(key, part):
    bounds = stream_bounds(key)
    return (jnp.arange(LEN, dtype=jnp.int32)[None, :] >= bounds[:, None]).astype(jnp.int32)


def draw_selected(key, part):
    bounds = stream_bounds(key)
    key = jax.random.fold_in(key, 9)
    levels = jax.random.randint(key, (STREAMS, 2), 5, 10)
    dice_rolls = jax.random.randint(jax.random.fold_in(key, 2), (STREAMS, LEN), 0, 10)
    second = jnp.arange(LEN, dtype=jnp.int32)[None, :] >= bounds[:, None]
    keep_limit = jnp.where(second, levels[:, 1:2], levels[:, 0:1])
    return (dice_rolls < keep_limit).astype(jnp.int32)


def block_scale(key, extent, shards, least, top_value):
    def one(dim, parts):
        heights = jax.random.uniform(jax.random.fold_in(jax.random.fold_in(key, 6), dim), (parts,), jnp.float32, least / len(shards), top_value / len(shards))
        return jnp.repeat(jnp.exp(heights), extent[dim] // parts).reshape((-1,) + (1,) * (len(extent) - dim - 1))

    level = one(*shards[0])
    for cut in shards[1:]:
        level = level * one(*cut)
    return level


def scatter_about(own_key, dims, width, reach, cuts=(), kind=jnp.bfloat16):
    array = width * jax.random.normal(own_key, dims, jnp.float32)
    if cuts:
        array = array * block_scale(own_key, dims, cuts, -0.22, 0.18)
    return jnp.clip(array, -reach, reach).astype(kind)


def setup_inputs(seed: int = 0) -> dict:
    keys = jax.random.split(jax.random.key(seed), 11)
    return {
        "tokens": scatter_about(keys[0], (STREAMS, LEN, D), 1.0, 6.0, ((0, 4), (1, 8))),
        "segment_ids": draw_segment_ids(jax.random.fold_in(keys[10], 71), 0),
        "selected": draw_selected(jax.random.fold_in(keys[10], 71), 0),
        "cotangent": scatter_about(keys[3], (STREAMS, LEN, D), 1.0, 6.0, ((0, 4), (1, 8))),
        "w_qkv": scatter_about(keys[4], (D, D + 2 * KV * HD), D ** -0.5, 0.125, ((0, 8),)),
        "w_out": scatter_about(keys[5], (D, D), (D // 128) ** -0.5, 1.5, ((0, 8),)),
        "w_gate_up": scatter_about(keys[6], (D, 2 * FF), D ** -0.5, 0.125, ((0, 8),)),
        "w_down": scatter_about(keys[7], (FF, D), FF ** -0.5, 0.078125, ((0, 8),)),
        "g_attn": jnp.clip(1.0 + 0.1 * jax.random.normal(keys[8], (D,), jnp.float32), 0.5, 1.5).astype(jnp.bfloat16),
        "g_mlp": jnp.clip(1.0 + 0.1 * jax.random.normal(keys[9], (D,), jnp.float32), 0.5, 1.5).astype(jnp.bfloat16),
    }


EPSILON = 1e-05
ROPE_BASE = 10000.0
MASKED = -1e+30
PRECISE = lax.Precision.HIGHEST

@jax.custom_vjp
def low(v):
    return lax.optimization_barrier(v.astype(jnp.bfloat16)).astype(jnp.float32)

@jax.custom_vjp
def low_back(v):
    return v

def low_keep(v):
    return (low(v), None)

def low_pass(kept, grad):
    return (grad,)

def back_keep(v):
    return (v, None)

def back_low(kept, grad):
    return (low(grad),)
low.defvjp(low_keep, low_pass)
low_back.defvjp(back_keep, back_low)

def rope_table(seg_stream):
    length = seg_stream.shape[0]
    first_count = jnp.sum((seg_stream == 0).astype(jnp.int32))
    position = jnp.arange(length, dtype=jnp.int32) - seg_stream * first_count
    frequency = ROPE_BASE ** (-(jnp.arange(HD // 2, dtype=jnp.float32) * 2.0 / HD))
    angles = position.astype(jnp.float32)[:, None] * frequency[None, :]
    return (jnp.cos(angles), jnp.sin(angles))

def rotate(values, cosine, sine_tab):
    half_dim = values.shape[-1] // 2
    first_half = values[..., :half_dim]
    second = values[..., half_dim:]
    cos_wide = cosine[:, None, :]
    sin_wide = sine_tab[:, None, :]
    return jnp.concatenate([first_half * cos_wide - second * sin_wide, second * cos_wide + first_half * sin_wide], axis=-1)

def rms_norm(values, gain_vec):
    return values * lax.rsqrt(lax.optimization_barrier(jnp.mean(values * values, axis=-1, keepdims=True)) + EPSILON) * gain_vec

def attend(queries, key_heads, value_heads, seg_stream):
    length = queries.shape[0]
    block_rows = min(512, length)
    position = jnp.arange(length, dtype=jnp.int32)

    def one_block(block_start):
        query_rows = lax.dynamic_slice_in_dim(queries, block_start, block_rows, 0)
        row_seg = lax.dynamic_slice_in_dim(seg_stream, block_start, block_rows, 0)
        row_pos = block_start + jnp.arange(block_rows, dtype=jnp.int32)
        scores = jnp.einsum('qhd,khd->hqk', query_rows, key_heads, precision=PRECISE) * HD ** (-0.5)
        scores = low_back(scores)
        allowed = (row_seg[:, None] == seg_stream[None, :]) & (row_pos[:, None] >= position[None, :])
        scores = jnp.where(allowed[None], scores, MASKED)
        row_max = lax.optimization_barrier(jnp.max(scores, axis=-1, keepdims=True))
        shifted = jnp.exp(scores - row_max)
        softmax_w = low(shifted / lax.optimization_barrier(jnp.sum(shifted, axis=-1, keepdims=True)))
        return jnp.einsum('hqk,khd->qhd', softmax_w, value_heads, precision=PRECISE)
    block_starts = jnp.arange(length // block_rows, dtype=jnp.int32) * block_rows
    blocks_out = lax.map(jax.checkpoint(one_block), block_starts)
    return blocks_out.reshape(length, H, HD)

def layer_forward(stream_in, w_qkv, w_out, w_gate_up, w_down, g_attn, g_mlp, seg_stream):
    length = stream_in.shape[0]
    cosine, sine_tab = rope_table(seg_stream)
    group_size = H // KV
    normed = low(rms_norm(stream_in, g_attn))
    projected = jnp.dot(normed, w_qkv, precision=PRECISE)
    queries = low_back(projected[:, :D]).reshape(length, H, HD)
    queries = low(low_back(rotate(queries, cosine, sine_tab)))
    key_heads = low_back(projected[:, D:D + KV * HD]).reshape(length, KV, HD)
    key_heads = low(low_back(jnp.repeat(rotate(key_heads, cosine, sine_tab), group_size, axis=1)))
    value_heads = low_back(projected[:, D + KV * HD:]).reshape(length, KV, HD)
    value_heads = low(low_back(jnp.repeat(value_heads, group_size, axis=1)))
    attended = attend(queries, key_heads, value_heads, seg_stream).reshape(length, D)
    attended = low(low_back(attended))
    branch = low_back(jnp.dot(attended, w_out, precision=PRECISE))
    residual = stream_in + branch
    inner_in = low(rms_norm(residual, g_mlp))
    gate_up = low_back(jnp.dot(inner_in, w_gate_up, precision=PRECISE))
    hidden = low(jax.nn.silu(gate_up[:, :FF]) * gate_up[:, FF:])
    return residual + jnp.dot(hidden, w_down, precision=PRECISE)

def reference(tokens, segment_ids, selected, cotangent, w_qkv, w_out, w_gate_up, w_down, g_attn, g_mlp):
    params = tuple((weight.astype(jnp.float32) for weight in (w_qkv, w_out, w_gate_up, w_down, g_attn, g_mlp)))

    def scan_step(grad_total, scan_item):
        stream_in, seg_stream, keep_mask, cot_stream = scan_item

        def forward(input_f, *weights_f):
            return layer_forward(input_f, *weights_f, seg_stream)
        layer_out, pullback = jax.vjp(forward, stream_in.astype(jnp.float32), *params)
        upstream = cot_stream.astype(jnp.float32) * keep_mask.astype(jnp.float32)[:, None]
        gradients = pullback(upstream)
        grad_total = tuple((left + right for left, right in zip(grad_total, gradients[1:])))
        return (grad_total, (layer_out.astype(jnp.bfloat16), gradients[0].astype(jnp.bfloat16)))
    zero_grads = tuple((jnp.zeros(weight.shape, jnp.float32) for weight in params))
    grad_total, (outputs, input_grads) = lax.scan(scan_step, zero_grads, (tokens, segment_ids, selected, cotangent))
    return (outputs, input_grads, grad_total[0], grad_total[1], grad_total[2], grad_total[3], grad_total[4], grad_total[5])
```

```python
import functools
import math

import jax
import jax.numpy as jnp
from jax import lax
from jax.experimental import pallas as pl
from jax.experimental.pallas import tpu as pltpu
from jax.sharding import PartitionSpec as P

D = 2048
H = 32
KV = 4
HD = 64
FF = 5632


EPSILON = 1e-05
ROPE_BASE = 10000.0
MASKED = -1e30


def rope_tables(positions, head_size):
    half_dim = head_size // 2
    frequency = ROPE_BASE ** (-(jnp.arange(half_dim, dtype=jnp.float32) * 2.0 / head_size))
    angles = positions.astype(jnp.float32)[:, None] * frequency[None, :]
    return (jnp.cos(angles), jnp.sin(angles))


def rotate(values, cosine, sine_tab, inverse_turn):
    half_dim = values.shape[-1] // 2
    first_half = values[..., :half_dim]
    second = values[..., half_dim:]
    cos_wide = cosine[:, None, :]
    sin_wide = sine_tab[:, None, :]
    if inverse_turn:
        sin_wide = -sin_wide
    return jnp.concatenate(
        [first_half * cos_wide - second * sin_wide, second * cos_wide + first_half * sin_wide],
        axis=-1,
    )


def rms_norm(values, gain_vec):
    inverse = lax.rsqrt(jnp.mean(values * values, axis=-1, keepdims=True) + EPSILON)
    return (values * inverse * gain_vec, inverse)


def norm_back(values, inverse, gain_vec, upstream):
    scaled = upstream * gain_vec
    inner_mean = jnp.mean(scaled * values, axis=-1, keepdims=True)
    through = inverse * scaled - values * inverse**3 * inner_mean
    gain_grad = jnp.sum(upstream * values * inverse, axis=0)
    return (through, gain_grad)


def attention_inputs(flat_in, qkv_full, gain_vec, cosine, sine_tab):
    row_count = flat_in.shape[0]
    group_size = H // KV
    normed, inverse = rms_norm(flat_in, gain_vec)
    normed = normed.astype(jnp.bfloat16)
    projected = jnp.dot(normed, qkv_full, preferred_element_type=jnp.float32)
    queries = rotate(projected[:, :D].reshape(row_count, H, HD), cosine, sine_tab, False)
    key_heads = rotate(
        projected[:, D : D + KV * HD].reshape(row_count, KV, HD), cosine, sine_tab, False
    )
    value_heads = projected[:, D + KV * HD :].reshape(row_count, KV, HD)
    key_wide = jnp.broadcast_to(key_heads[:, :, None], (row_count, KV, group_size, HD)).reshape(
        row_count, D
    )
    value_wide = jnp.broadcast_to(value_heads[:, :, None], (row_count, KV, group_size, HD)).reshape(
        row_count, D
    )
    stacked = jnp.stack([queries.reshape(row_count, D), key_wide, value_wide]).astype(jnp.bfloat16)
    return (normed, inverse, stacked)


def block_mask(seg_full, position, row_begin, finish):
    row_seg = seg_full[:, row_begin:finish]
    col_seg = seg_full[:, :finish]
    same_doc = row_seg[:, :, None] == col_seg[:, None, :]
    causal = position[row_begin:finish, None] >= position[None, :finish]
    return same_doc & causal[None]


def attention_forward(queries, key_heads, value_heads, seg_full, score_scale):
    length = queries.shape[1]
    block_rows = min(512, length)
    position = jnp.arange(length, dtype=jnp.int32)
    outputs = []
    lse_parts = []
    for block_num in range(length // block_rows):
        row_begin = block_num * block_rows
        finish = row_begin + block_rows
        scores = (
            jnp.einsum(
                "sqhd,skhd->shqk",
                queries[:, row_begin:finish],
                key_heads[:, :finish],
                preferred_element_type=jnp.float32,
            )
            * score_scale
        )
        allowed = block_mask(seg_full, position, row_begin, finish)
        scores = jnp.where(allowed[:, None], scores, MASKED)
        row_max = jnp.max(scores, axis=-1, keepdims=True)
        shifted = jnp.exp(scores - row_max)
        row_total = jnp.sum(shifted, axis=-1, keepdims=True)
        softmax_w = (shifted / row_total).astype(jnp.bfloat16)
        outputs.append(
            jnp.einsum(
                "shqk,skhd->sqhd",
                softmax_w,
                value_heads[:, :finish],
                preferred_element_type=jnp.float32,
            )
        )
        lse_parts.append(row_max + jnp.log(row_total))
    return (jnp.concatenate(outputs, axis=1), jnp.concatenate(lse_parts, axis=2))


def attention_backward(queries, key_heads, value_heads, seg_full, log_sums, grad_out, score_scale):
    length = queries.shape[1]
    block_rows = min(512, length)
    position = jnp.arange(length, dtype=jnp.int32)
    grad_query = []
    grad_key = jnp.zeros(key_heads.shape, jnp.float32)
    grad_value = jnp.zeros(value_heads.shape, jnp.float32)
    for block_num in range(length // block_rows):
        row_begin = block_num * block_rows
        finish = row_begin + block_rows
        query_rows = queries[:, row_begin:finish]
        grad_rows = grad_out[:, row_begin:finish]
        key_part = key_heads[:, :finish]
        value_part = value_heads[:, :finish]
        scores = (
            jnp.einsum("sqhd,skhd->shqk", query_rows, key_part, preferred_element_type=jnp.float32)
            * score_scale
        )
        allowed = block_mask(seg_full, position, row_begin, finish)
        softmax_f = jnp.where(
            allowed[:, None], jnp.exp(scores - log_sums[:, :, row_begin:finish]), 0.0
        )
        grad_probs = jnp.einsum(
            "sqhd,skhd->shqk", grad_rows, value_part, preferred_element_type=jnp.float32
        )
        row_delta = jnp.sum(softmax_f * grad_probs, axis=-1, keepdims=True)
        grad_scores = (softmax_f * (grad_probs - row_delta)).astype(jnp.bfloat16)
        grad_query.append(
            jnp.einsum("shqk,skhd->sqhd", grad_scores, key_part, preferred_element_type=jnp.float32)
            * score_scale
        )
        grad_key = grad_key.at[:, :finish].add(
            jnp.einsum(
                "shqk,sqhd->skhd", grad_scores, query_rows, preferred_element_type=jnp.float32
            )
            * score_scale
        )
        grad_value = grad_value.at[:, :finish].add(
            jnp.einsum(
                "shqk,sqhd->skhd",
                softmax_f.astype(jnp.bfloat16),
                grad_rows,
                preferred_element_type=jnp.float32,
            )
        )
    return (jnp.concatenate(grad_query, axis=1), grad_key, grad_value)


def general_body(tokens, segment_ids, selected, cotangent, w_qkv, w_out, w_gate_up, w_down, g_attn, g_mlp):
    streams, local_len, model_dim = tokens.shape
    sp_count = lax.axis_size("sp")
    sp_index = lax.axis_index("sp")
    row_count = streams * local_len
    group_size = H // KV
    kv_width = KV * HD
    score_scale = HD ** (-0.5)
    contract = (((0,), (0,)), ((), ()))
    seg_full = lax.all_gather(segment_ids, "sp", axis=1, tiled=True)
    first_count = jnp.sum((seg_full == 0).astype(jnp.int32), axis=1, keepdims=True)
    local_pos = (
        sp_index * local_len
        + jnp.arange(local_len, dtype=jnp.int32)[None, :]
        - segment_ids * first_count
    )
    cosine, sine_tab = rope_tables(local_pos.reshape(row_count), HD)
    shards = (w_qkv, w_out, w_gate_up, w_down, g_attn, g_mlp)
    gathered = (
        lax.all_gather(shards[0], "sp", axis=0, tiled=True),
        lax.all_gather(shards[1], "sp", axis=0, tiled=True),
        lax.all_gather(shards[2], "sp", axis=0, tiled=True),
        lax.all_gather(shards[3], "sp", axis=0, tiled=True),
        lax.all_gather(shards[4], "sp", axis=0, tiled=True),
        lax.all_gather(shards[5], "sp", axis=0, tiled=True),
    )
    qkv_full, out_full, gate_up_full, down_full, attn_gain, mlp_gain = gathered
    attn_gain = attn_gain.astype(jnp.float32)
    mlp_gain = mlp_gain.astype(jnp.float32)
    flat_in = tokens.reshape(row_count, model_dim).astype(jnp.float32)
    normed, inverse_one, stacked = attention_inputs(flat_in, qkv_full, attn_gain, cosine, sine_tab)
    head_view = lax.all_to_all(
        stacked.reshape(3, streams, local_len, model_dim),
        "sp",
        split_axis=3,
        concat_axis=2,
        tiled=True,
    )
    length = head_view.shape[2]
    heads_here = head_view.shape[3] // HD
    head_shape = (streams, length, heads_here, HD)
    queries = head_view[0].reshape(head_shape)
    key_heads = head_view[1].reshape(head_shape)
    value_heads = head_view[2].reshape(head_shape)
    attn_heads, log_sums = attention_forward(queries, key_heads, value_heads, seg_full, score_scale)
    attn_send = attn_heads.astype(jnp.bfloat16).reshape(streams, length, heads_here * HD)
    attn_tok = lax.all_to_all(attn_send, "sp", split_axis=1, concat_axis=2, tiled=True).reshape(
        row_count, model_dim
    )
    branch = jnp.dot(attn_tok, out_full, preferred_element_type=jnp.float32)
    residual = flat_in + branch
    inner_f, inverse_two = rms_norm(residual, mlp_gain)
    inner_in = inner_f.astype(jnp.bfloat16)
    gate_up = jnp.dot(inner_in, gate_up_full, preferred_element_type=jnp.float32)
    gate_part = gate_up[:, :FF]
    up_part = gate_up[:, FF:]
    sigmoid_g = jax.nn.sigmoid(gate_part)
    silu_gate = gate_part * sigmoid_g
    hidden = (silu_gate * up_part).astype(jnp.bfloat16)
    result = residual + jnp.dot(hidden, down_full, preferred_element_type=jnp.float32)
    output = result.astype(jnp.bfloat16).reshape(streams, local_len, model_dim)
    qkv_back, out_back, gate_up_back, down_back, attn_gain_b, mlp_gain_b = gathered
    attn_gain_b = attn_gain_b.astype(jnp.float32)
    mlp_gain_b = mlp_gain_b.astype(jnp.float32)
    grad_y = (cotangent * selected[:, :, None].astype(jnp.bfloat16)).reshape(row_count, model_dim)
    grad_hidden = jnp.dot(grad_y, down_back.T, preferred_element_type=jnp.float32)
    silu_slope = sigmoid_g * (1.0 + gate_part * (1.0 - sigmoid_g))
    grad_both = jnp.concatenate(
        [grad_hidden * up_part * silu_slope, grad_hidden * silu_gate], axis=1
    ).astype(jnp.bfloat16)
    grad_inner = jnp.dot(grad_both, gate_up_back.T, preferred_element_type=jnp.float32)
    grad_resid, gain_two = norm_back(residual, inverse_two, mlp_gain_b, grad_inner)
    grad_resid = grad_resid + grad_y.astype(jnp.float32)
    grad_branch = grad_resid.astype(jnp.bfloat16)
    grad_attn = jnp.dot(grad_branch, out_back.T, preferred_element_type=jnp.float32).astype(
        jnp.bfloat16
    )
    grad_view = lax.all_to_all(
        grad_attn.reshape(streams, local_len, model_dim),
        "sp",
        split_axis=2,
        concat_axis=1,
        tiled=True,
    )
    grad_view = grad_view.reshape(head_shape)
    grad_q, grad_k, grad_v = attention_backward(
        queries, key_heads, value_heads, seg_full, log_sums, grad_view, score_scale
    )
    back_send = (
        jnp.stack([grad_q, grad_k, grad_v])
        .astype(jnp.bfloat16)
        .reshape(3, streams, length, heads_here * HD)
    )
    returned = lax.all_to_all(back_send, "sp", split_axis=2, concat_axis=3, tiled=True)
    returned = returned.astype(jnp.float32).reshape(3, row_count, H, HD)
    grad_pq = rotate(returned[0], cosine, sine_tab, True).reshape(row_count, model_dim)
    key_summed = jnp.sum(returned[1].reshape(row_count, KV, group_size, HD), axis=2)
    grad_pk = rotate(key_summed, cosine, sine_tab, True).reshape(row_count, kv_width)
    grad_pv = jnp.sum(returned[2].reshape(row_count, KV, group_size, HD), axis=2).reshape(
        row_count, kv_width
    )
    grad_mixed = jnp.concatenate(
        [grad_pq.astype(jnp.bfloat16), grad_pk.astype(jnp.bfloat16), grad_pv.astype(jnp.bfloat16)],
        axis=1,
    )
    grad_normed = jnp.dot(grad_mixed, qkv_back.T, preferred_element_type=jnp.float32)
    grad_in, gain_one = norm_back(flat_in, inverse_one, attn_gain_b, grad_normed)
    grad_in = grad_in + grad_resid
    grad_tokens = grad_in.astype(jnp.bfloat16).reshape(streams, local_len, model_dim)
    gain_totals = lax.psum((gain_one, gain_two), ("dp", "sp"))
    gain_share = model_dim // sp_count
    grad_g_attn = lax.dynamic_slice_in_dim(gain_totals[0], sp_index * gain_share, gain_share, 0)
    grad_g_mlp = lax.dynamic_slice_in_dim(gain_totals[1], sp_index * gain_share, gain_share, 0)
    row_sums = lax.psum_scatter(
        jnp.concatenate(
            [
                lax.dot_general(normed, grad_mixed, contract, preferred_element_type=jnp.float32),
                lax.dot_general(
                    attn_tok, grad_branch, contract, preferred_element_type=jnp.float32
                ),
                lax.dot_general(inner_in, grad_both, contract, preferred_element_type=jnp.float32),
            ],
            axis=1,
        ).astype(jnp.bfloat16),
        "sp",
        scatter_dimension=0,
        tiled=True,
    )
    down_sums = lax.psum_scatter(
        lax.dot_general(hidden, grad_y, contract, preferred_element_type=jnp.float32).astype(
            jnp.bfloat16
        ),
        "sp",
        scatter_dimension=0,
        tiled=True,
    )
    weight_rows, down_rows = (
        lax.psum(row_sums, "dp").astype(jnp.float32),
        lax.psum(down_sums, "dp").astype(jnp.float32),
    )
    qkv_cols = model_dim + 2 * kv_width
    grad_w_qkv = weight_rows[:, :qkv_cols]
    grad_w_out = weight_rows[:, qkv_cols : qkv_cols + model_dim]
    grad_w_gate_up = weight_rows[:, qkv_cols + model_dim :]
    return (
        output,
        grad_tokens,
        grad_w_qkv,
        grad_w_out,
        grad_w_gate_up,
        down_rows,
        grad_g_attn,
        grad_g_mlp,
    )


CHIPS = 4
EXTRA = 128
BLOCK = 512
LOG2E = math.log2(math.e)
BF = jnp.bfloat16
F32 = jnp.float32
NT = (((1,), (1,)), ((), ()))
TN = (((0,), (0,)), ((), ()))


def swap_pairs(even_mask, odd_mask):
    return [(i, i ^ (odd_mask if i & 1 else even_mask)) for i in range(2 * CHIPS)]


FIRST = swap_pairs(2, 4)
SECOND = swap_pairs(4, 2)
SIBLING = swap_pairs(1, 1)
SAME_CORE = [[0, 2, 4, 6], [1, 3, 5, 7]]


def send_first(x):
    return lax.ppermute(x, "sp", FIRST)


def send_second(x):
    return lax.ppermute(x, "sp", SECOND)


def send_sibling(x):
    return lax.ppermute(x, "sp", SIBLING)


def after(value, *others):
    return lax.optimization_barrier((value,) + others)[0]


def gather_chips(own):
    first = send_first(own)
    second = send_second(after(own, first))
    far = send_second(after(first, second))
    return [own, first, second, far]


def rel_masks(core):
    first = jnp.where(core == 0, 2, 4)
    return first, 6 - first


def gather_plane(shard, me):
    core = me & 1
    first, second = rel_masks(core)
    mine = gather_chips(shard)
    theirs = [send_sibling(part) for part in mine]
    places = [me, me ^ first, me ^ second, me ^ 6]
    other = me ^ 1
    places += [other, other ^ second, other ^ first, other ^ 6]
    out = jnp.zeros((2 * CHIPS,) + shard.shape, shard.dtype)
    for part, place in zip(mine + theirs, places):
        out = lax.dynamic_update_slice_in_dim(out, part[None], place, 0)
    return out


def pick(parts, index):
    return lax.dynamic_index_in_dim(parts, index, 0, keepdims=False)


def line_scatter(parts):
    planes = parts.shape[0]
    z = lax.axis_index("dp")
    right = left = None
    for step in range(1, planes):
        ahead = pick(parts, jnp.clip(planes - step + z, 0, planes - 1))
        back = pick(parts, jnp.clip(z - planes + step, 0, planes - 1))
        if right is not None:
            ahead = (ahead.astype(F32) + right.astype(F32)).astype(BF)
            back = (back.astype(F32) + left.astype(F32)).astype(BF)
        right = lax.ppermute(ahead, "dp", [(i, i + 1) for i in range(step)])
        left = lax.ppermute(back, "dp", [(planes - 1 - i, planes - 2 - i) for i in range(step)])
    return (pick(parts, z).astype(F32) + right.astype(F32) + left.astype(F32)).astype(BF)


def line_gather(own):
    planes = lax.axis_size("dp")
    z = lax.axis_index("dp")
    rights, lefts = [own], [own]
    for step in range(1, planes):
        rights.append(lax.ppermute(rights[-1], "dp", [(i, i + 1) for i in range(step - 1, planes - 1)]))
        lefts.append(lax.ppermute(lefts[-1], "dp", [(i + 1, i) for i in range(planes - step)]))
    out = jnp.zeros((planes,) + own.shape, own.dtype)
    out = lax.dynamic_update_slice_in_dim(out, own[None], z, 0)
    for step in range(1, planes):
        block = jnp.where(z >= step, rights[step], lefts[planes - step])
        out = lax.dynamic_update_slice_in_dim(out, block[None], (z - step) % planes, 0)
    return out


def line_sum(rows):
    planes = lax.axis_size("dp")
    count, width = rows.shape
    return line_gather(line_scatter(rows.reshape(planes, count // planes, width))).reshape(count, width)


def scatter_chips(parts):
    own, first, second, far = parts
    got_first = send_first(first.astype(BF))
    got_far = send_first(far.astype(BF))
    passed = (second.astype(F32) + got_far.astype(F32)).astype(BF)
    return own.astype(F32) + got_first.astype(F32) + send_second(passed).astype(F32)


def scatter_plane(parts, me):
    core = me & 1
    chip = me // 2
    first, second = rel_masks(core)
    split = parts.reshape((CHIPS, 2) + parts.shape[1:])
    got = send_sibling(lax.dynamic_index_in_dim(split, 1 - core, 1, keepdims=False))
    kept = lax.dynamic_index_in_dim(split, core, 1, keepdims=False)

    def part(place):
        return pick(kept, place).astype(F32) + pick(got, place).astype(F32)

    return scatter_chips([part(chip), part(chip ^ (first // 2)), part(chip ^ (second // 2)), part(chip ^ 3)])


def spread_kernel(in_ref, out_ref):
    planes, _, rows, width = in_ref.shape
    out_ref[...] = in_ref[...].reshape(planes * rows, width).astype(F32)


def spread(parts, columns):
    planes, chips, rows, both = parts.shape
    return pl.pallas_call(
        spread_kernel,
        grid=(2 * chips,),
        in_specs=[pl.BlockSpec((planes, 1, rows, both // 2), lambda i: (0, i % chips, 0, i // chips))],
        out_specs=pl.BlockSpec((planes * rows, both // 2), lambda i: (0, i)),
        out_shape=jax.ShapeDtypeStruct((planes * rows, columns), F32),
        compiler_params=pltpu.CompilerParams(vmem_limit_bytes=32 * 2**20),
        cost_estimate=pl.CostEstimate(flops=0, bytes_accessed=18 * 10**6, transcendentals=0),
        name="spread",
    )(parts)


def swap_halves(values):
    width = values.shape[-1]
    lane = lax.broadcasted_iota(jnp.int32, values.shape, 1)
    ahead = pltpu.roll(values, width - HD // 2, 1)
    behind = pltpu.roll(values, HD // 2, 1)
    return jnp.where(lane % HD < HD // 2, ahead, behind)


def project_kernel(x_ref, gain_ref, cos_ref, sin_ref, wq_ref, wkv_ref, send_ref, normed_ref, inv_ref, normed_scr):
    step = pl.program_id(0)

    @pl.when(step == 0)
    def _():
        x = x_ref[...].astype(F32)
        inv = lax.rsqrt(jnp.mean(x * x, axis=-1, keepdims=True) + EPSILON)
        normed = (x * inv * gain_ref[...]).astype(BF)
        normed_scr[...] = normed
        normed_ref[...] = normed
        inv_ref[...] = inv

    normed = normed_scr[...]
    shards, depth = wq_ref.shape[:2]
    wq = wq_ref[...].reshape(shards * depth, wq_ref.shape[2])
    pq = jnp.dot(normed, wq, preferred_element_type=F32)
    wkv = wkv_ref[...].reshape(shards * depth, wkv_ref.shape[2])
    pkv = jnp.dot(normed, wkv, preferred_element_type=F32)
    cos = cos_ref[...]
    sin = sin_ref[...]
    heads = pq.shape[1]
    q_scale = LOG2E * HD**-0.5
    turned = pq * jnp.tile(cos, (1, heads // 128)) + swap_halves(pq) * jnp.tile(sin, (1, heads // 128))
    send_ref[0, :, :heads] = (turned * q_scale).astype(BF)
    lane = lax.broadcasted_iota(jnp.int32, pkv.shape, 1)
    turned_kv = jnp.where(lane < HD, pkv * cos + swap_halves(pkv) * sin, pkv)
    send_ref[0, :, heads:] = turned_kv.astype(BF)


def project(x, gain, cos, sin, w_all):
    rows, width = x.shape
    devices = 2 * CHIPS
    heads = width // devices
    out_width = heads + 2 * HD
    depth = w_all.shape[1]
    first_kv = width // (2 * HD)
    return pl.pallas_call(
        project_kernel,
        grid=(devices,),
        in_specs=[
            pl.BlockSpec((rows, width), lambda d: (0, 0)),
            pl.BlockSpec((1, width), lambda d: (0, 0)),
            pl.BlockSpec((rows, 128), lambda d: (0, 0)),
            pl.BlockSpec((rows, 128), lambda d: (0, 0)),
            pl.BlockSpec((devices, depth, heads), lambda d: (0, 0, d)),
            pl.BlockSpec((devices, depth, 2 * HD), lambda d: (0, 0, first_kv + d // 2)),
        ],
        out_specs=[
            pl.BlockSpec((1, rows, out_width), lambda d: (d, 0, 0)),
            pl.BlockSpec((rows, width), lambda d: (0, 0)),
            pl.BlockSpec((rows, 1), lambda d: (0, 0)),
        ],
        out_shape=[
            jax.ShapeDtypeStruct((devices, rows, out_width), BF),
            jax.ShapeDtypeStruct((rows, width), BF),
            jax.ShapeDtypeStruct((rows, 1), F32),
        ],
        scratch_shapes=[pltpu.VMEM((rows, width), BF)],
        compiler_params=pltpu.CompilerParams(vmem_limit_bytes=48 * 2**20),
        cost_estimate=pl.CostEstimate(flops=7 * 10**9, bytes_accessed=24 * 10**6, transcendentals=0),
        name="project",
    )(x, gain, cos, sin, w_all, w_all)


def attend_kernel(zeros_ref, q_ref, kv_ref, o_ref, send_ref, lse_ref, k_scr, v_scr, acc_ref, max_ref, *, heads):
    block = pl.program_id(0)
    zeros = zeros_ref[0]
    size = q_ref.shape[0]

    @pl.when(block == 0)
    def _():
        for part in range(kv_ref.shape[0] // size):
            rows = slice(part * size, (part + 1) * size)
            both = kv_ref[rows, :].astype(F32)
            lane = lax.broadcasted_iota(jnp.int32, both.shape, 1)
            k_scr[rows, :] = kv_ref[rows, :HD]
            v_scr[rows, :] = jnp.where(lane < HD, pltpu.roll(both, HD, 1), 1.0).astype(BF)

    first_row = block * size
    lowest = jnp.where(first_row >= zeros, zeros // size, 0)
    acc_ref[...] = jnp.zeros_like(acc_ref)
    max_ref[...] = jnp.full_like(max_ref, MASKED)
    q_heads = [q_ref[:, h * HD : (h + 1) * HD] for h in range(heads)]

    def step(index, masked):
        first_key = pl.multiple_of(index * size, size)
        keys = k_scr[pl.ds(first_key, size), :]
        values = v_scr[pl.ds(first_key, size), :]
        if masked:
            row = first_row + lax.broadcasted_iota(jnp.int32, (size, size), 0)
            col = first_key + lax.broadcasted_iota(jnp.int32, (size, size), 1)
            begin = jnp.where(row >= zeros, zeros, 0)
            refused = (col > row) | (col < begin)

        def score(h):
            return lax.dot_general(q_heads[h], keys, NT, preferred_element_type=F32)

        upcoming = score(0)
        for h in range(heads):
            scores = upcoming
            if h + 1 < heads:
                upcoming = score(h + 1)
            if masked:
                scores = jnp.where(refused, MASKED, scores)
            old_max = max_ref[h]
            new_max = jnp.maximum(old_max, jnp.max(scores, axis=-1, keepdims=True))
            weights = jnp.exp2(scores - jnp.tile(new_max, (1, size // 128)))
            shrink = jnp.exp2(old_max - new_max)
            acc_ref[h] = acc_ref[h] * shrink + jnp.dot(weights.astype(BF), values, preferred_element_type=F32)
            max_ref[h] = new_max

    def visit(index, carry):
        first_key = index * size
        mixed = (index == block) | ((first_row + size > zeros) & (first_key < zeros))

        @pl.when(mixed)
        def _():
            step(index, True)

        @pl.when(jnp.logical_not(mixed))
        def _():
            step(index, False)

        return carry

    lax.fori_loop(lowest, block + 1, visit, 0)
    for h in range(heads):
        acc = acc_ref[h]
        total = acc[:, HD : HD + 1]
        out = acc[:, :HD] / total
        o_ref[:, h * HD : (h + 1) * HD] = out
        send_ref[0, :, h * HD : (h + 1) * HD] = out.astype(BF)
        lse = max_ref[h] + jnp.log2(total)
        lse_ref[h : h + 1, :] = jnp.transpose(lse)[:1]


def attend(zeros, qkv):
    length, width = qkv.shape
    q_width = width - 2 * HD
    heads = q_width // HD
    size = BLOCK
    blocks = length // size
    return pl.pallas_call(
        functools.partial(attend_kernel, heads=heads),
        grid_spec=pltpu.PrefetchScalarGridSpec(
            num_scalar_prefetch=1,
            grid=(blocks,),
            in_specs=[
                pl.BlockSpec((size, q_width), lambda i, z: (i, 0)),
                pl.BlockSpec((length, 2 * HD), lambda i, z: (0, q_width // (2 * HD))),
            ],
            out_specs=[
                pl.BlockSpec((size, q_width), lambda i, z: (i, 0)),
                pl.BlockSpec((1, size, q_width), lambda i, z: (i, 0, 0)),
                pl.BlockSpec((heads, size), lambda i, z: (0, i)),
            ],
            scratch_shapes=[
                pltpu.VMEM((length, HD), BF),
                pltpu.VMEM((length, 2 * HD), BF),
                pltpu.VMEM((heads, size, 2 * HD), F32),
                pltpu.VMEM((heads, size, 128), F32),
            ],
        ),
        out_shape=[
            jax.ShapeDtypeStruct((length, q_width), F32),
            jax.ShapeDtypeStruct((blocks, size, q_width), BF),
            jax.ShapeDtypeStruct((heads, length), F32),
        ],
        compiler_params=pltpu.CompilerParams(vmem_limit_bytes=48 * 2**20),
        cost_estimate=pl.CostEstimate(flops=40 * 10**9, bytes_accessed=16 * 10**6, transcendentals=36 * 10**6),
        name="attend",
    )(zeros, qkv, qkv)


def attend_back_kernel(
    zeros_ref, q_ref, kv_ref, do_ref, o_ref, lse_ref, send_ref, q_scr, do_scr, delta_ref, dq_acc, *, heads
):
    block = pl.program_id(0)
    zeros = zeros_ref[0]
    size = kv_ref.shape[0]
    length = q_ref.shape[0]
    blocks = length // size

    @pl.when(block == 0)
    def _():
        dq_acc[...] = jnp.zeros_like(dq_acc)
        for part in range(blocks):
            rows = slice(part * size, (part + 1) * size)
            product = jnp.transpose(do_ref[rows, :].astype(F32) * o_ref[rows, :])
            for h in range(heads):
                cols = slice(h * HD, (h + 1) * HD)
                q_scr[h, rows, :] = q_ref[rows, cols]
                do_scr[h, rows, :] = do_ref[rows, cols]
                delta_ref[h : h + 1, rows] = jnp.sum(product[cols], axis=0, keepdims=True)

    first_key = block * size
    both = kv_ref[...]
    keys = both[:, :HD]
    values = both[:, HD:]
    keys_t = jnp.transpose(keys.astype(F32)).astype(BF)
    highest = jnp.where(first_key + size <= zeros, jnp.minimum((zeros + size - 1) // size, blocks), blocks)

    def step(index, carry, masked):
        first_row = pl.multiple_of(index * size, size)
        span = pl.ds(first_row, size)
        if masked:
            col = first_key + lax.broadcasted_iota(jnp.int32, (size, size), 0)
            row = first_row + lax.broadcasted_iota(jnp.int32, (size, size), 1)
            begin = jnp.where(row >= zeros, zeros, 0)
            refused = (col > row) | (col < begin)

        def products(h):
            q_rows = q_scr[h, span, :]
            do_rows = do_scr[h, span, :]
            scores = lax.dot_general(keys, q_rows, NT, preferred_element_type=F32)
            d_prob = lax.dot_general(values, do_rows, NT, preferred_element_type=F32)
            return q_rows, do_rows, scores, d_prob

        upcoming = products(0)
        dk_sum, dv_sum = carry
        for h in range(heads):
            q_rows, do_rows, scores, d_prob = upcoming
            if h + 1 < heads:
                upcoming = products(h + 1)
            shifted = scores - lse_ref[h : h + 1, span]
            if masked:
                shifted = jnp.where(refused, MASKED, shifted)
            prob = jnp.exp2(shifted)
            d_score = (prob * (d_prob - delta_ref[h : h + 1, span])).astype(BF)
            dv_sum = dv_sum + jnp.dot(prob.astype(BF), do_rows, preferred_element_type=F32)
            dk_sum = dk_sum + jnp.dot(d_score, q_rows, preferred_element_type=F32)
            dq_acc[h * HD : (h + 1) * HD, span] += jnp.dot(keys_t, d_score, preferred_element_type=F32)
        return dk_sum, dv_sum

    def visit(index, carry):
        first_row = index * size
        mixed = (index == block) | ((first_row + size > zeros) & (first_key < zeros))
        return lax.cond(
            mixed,
            lambda c: step(index, c, True),
            lambda c: step(index, c, False),
            carry,
        )

    zero = jnp.zeros((size, HD), F32)
    dk_sum, dv_sum = lax.fori_loop(block, highest, visit, (zero, zero))
    q_width = heads * HD
    done = pl.ds(pl.multiple_of(first_key, size), size)
    send_ref[0, :, :q_width] = (jnp.transpose(dq_acc[:, done]) * HD**-0.5).astype(BF)
    send_ref[0, :, q_width : q_width + HD] = (dk_sum * (1.0 / LOG2E)).astype(BF)
    send_ref[0, :, q_width + HD :] = dv_sum.astype(BF)


def attend_back(zeros, qkv, d_out, out, lse):
    length, width = qkv.shape
    q_width = width - 2 * HD
    heads = q_width // HD
    size = BLOCK
    blocks = length // size
    return pl.pallas_call(
        functools.partial(attend_back_kernel, heads=heads),
        grid_spec=pltpu.PrefetchScalarGridSpec(
            num_scalar_prefetch=1,
            grid=(blocks,),
            in_specs=[
                pl.BlockSpec((length, q_width), lambda j, z: (0, 0)),
                pl.BlockSpec((size, 2 * HD), lambda j, z: (j, q_width // (2 * HD))),
                pl.BlockSpec((length, q_width), lambda j, z: (0, 0)),
                pl.BlockSpec((length, q_width), lambda j, z: (0, 0)),
                pl.BlockSpec((heads, length), lambda j, z: (0, 0)),
            ],
            out_specs=pl.BlockSpec((1, size, width), lambda j, z: (j, 0, 0)),
            scratch_shapes=[
                pltpu.VMEM((heads, length, HD), BF),
                pltpu.VMEM((heads, length, HD), BF),
                pltpu.VMEM((heads, length), F32),
                pltpu.VMEM((q_width, length), F32),
            ],
        ),
        out_shape=jax.ShapeDtypeStruct((blocks, size, width), BF),
        compiler_params=pltpu.CompilerParams(vmem_limit_bytes=56 * 2**20),
        cost_estimate=pl.CostEstimate(flops=90 * 10**9, bytes_accessed=16 * 10**6, transcendentals=36 * 10**6),
        name="attend_back",
    )(zeros, qkv, qkv, d_out, out, lse)


def unturn_kernel(back_ref, cos_ref, sin_ref, out_ref):
    cos = cos_ref[...]
    sin = sin_ref[...]
    devices, _, width = back_ref.shape
    heads = width - 2 * HD
    for d in range(devices):
        dq = back_ref[d, :, :heads].astype(F32)
        turned = dq * jnp.tile(cos, (1, heads // 128)) - swap_halves(dq) * jnp.tile(sin, (1, heads // 128))
        out_ref[:, d * heads : (d + 1) * heads] = turned.astype(BF)
    base = devices * heads
    for g in range(KV):
        pair = back_ref[2 * g, :, heads:].astype(F32) + back_ref[2 * g + 1, :, heads:].astype(F32)
        lane = lax.broadcasted_iota(jnp.int32, pair.shape, 1)
        pair = jnp.where(lane < HD, pair * cos - swap_halves(pair) * sin, pair)
        out_ref[:, base + 2 * g * HD : base + 2 * (g + 1) * HD] = pair.astype(BF)
    end = base + 2 * KV * HD
    out_ref[:, end:] = jnp.zeros((out_ref.shape[0], out_ref.shape[1] - end), BF)


def unturn(back, cos, sin):
    devices, rows, width = back.shape
    return pl.pallas_call(
        unturn_kernel,
        out_shape=jax.ShapeDtypeStruct((rows, devices * (width - 2 * HD) + 2 * KV * HD + EXTRA), BF),
        compiler_params=pltpu.CompilerParams(vmem_limit_bytes=48 * 2**20),
        cost_estimate=pl.CostEstimate(flops=10**7, bytes_accessed=6 * 10**6, transcendentals=0),
        name="unturn",
    )(back, cos, sin)


def dot(left, right, dims=(((1,), (0,)), ((), ()))):
    return lax.dot_general(left, right, dims, preferred_element_type=F32)


def fast_body(tokens, segment_ids, selected, cotangent, w_qkv, w_out, w_gate_up, w_down, g_attn, g_mlp):
    _, rows, width = tokens.shape
    devices = 2 * CHIPS
    me = lax.axis_index("sp")
    core = me & 1
    planes = lax.axis_size("dp")
    share = width // devices
    kv_width = KV * HD
    qkv_width = w_qkv.shape[1]

    count = jnp.sum((segment_ids == 0).astype(jnp.int32))
    high = jnp.full((share,), count // 64, jnp.int32).astype(BF)
    low = jnp.full((share,), count % 64, jnp.int32).astype(BF)
    small = jnp.stack([g_attn, g_mlp, high, low], axis=1)
    small = jnp.concatenate([small, jnp.zeros((share, EXTRA - 4), BF)], axis=1)
    paired = [w_qkv[:, :width]]
    for head in range(KV):
        paired.append(w_qkv[:, width + head * HD : width + (head + 1) * HD])
        paired.append(w_qkv[:, width + kv_width + head * HD : width + kv_width + (head + 1) * HD])
    qkv_all = gather_plane(jnp.concatenate(paired + [small], axis=1), me)
    extras = qkv_all[:, :, qkv_width : qkv_width + 4].astype(F32)
    attn_gain = extras[:, :, 0].reshape(1, width)
    mlp_gain = extras[:, :, 1].reshape(1, width)
    zeros = jnp.sum(extras[:, 0, 2] * 64.0 + extras[:, 0, 3]).astype(jnp.int32)

    local_pos = me * rows + jnp.arange(rows, dtype=jnp.int32) - segment_ids.reshape(rows) * zeros
    cosine, sine = rope_tables(local_pos, HD)
    cos = jnp.concatenate([cosine] * 4, axis=1)
    sin = jnp.concatenate([-sine, sine, -sine, sine], axis=1)

    hidden_chip = 2 * w_down.shape[0]
    quarter = share // planes
    plane = lax.axis_index("dp")
    gu_rows = lax.dynamic_slice_in_dim(w_gate_up, plane * quarter, quarter, 0)
    gu_send = []
    for chip in range(CHIPS):
        for begin in (chip * hidden_chip, (CHIPS + chip) * hidden_chip):
            gu_send.append(gu_rows[:, begin : begin + hidden_chip])
    gu_send = jnp.stack([jnp.concatenate(gu_send[2 * c : 2 * c + 2], axis=1) for c in range(CHIPS)])
    gu_part = lax.all_to_all(gu_send, "sp", 0, 0, axis_index_groups=SAME_CORE, tiled=True)
    gu_mine = lax.all_gather(gu_part, "dp", axis=0, tiled=False)
    gu_mine = gu_mine.transpose(1, 0, 2, 3).reshape(CHIPS, 1, share, 2 * hidden_chip)
    gu_theirs = send_sibling(gu_mine)
    w_gu = jnp.where(
        core == 0, jnp.concatenate([gu_mine, gu_theirs], axis=1), jnp.concatenate([gu_theirs, gu_mine], axis=1)
    ).reshape(width, 2 * hidden_chip)
    down_theirs = send_sibling(w_down)
    w_dn = jnp.where(
        core == 0, jnp.concatenate([w_down, down_theirs], axis=0), jnp.concatenate([down_theirs, w_down], axis=0)
    )

    x_bf = tokens.reshape(rows, width)
    x = x_bf.astype(F32)
    qkv_send, normed, inv_one = project(x_bf, attn_gain, cos, sin, qkv_all)
    qkv_heads = lax.all_to_all(qkv_send, "sp", 0, 0, tiled=True)
    length = devices * rows
    qkv_heads = qkv_heads.reshape(length, qkv_send.shape[2])
    zeros_one = zeros.reshape(1)
    out_heads, out_send, lse = attend(zeros_one, qkv_heads)
    out_all = gather_plane(after(w_out, qkv_all), me).reshape(width, width)
    dy = (cotangent * selected[:, :, None].astype(BF)).reshape(rows, width)
    dy_rows = gather_chips(after(dy, qkv_heads))
    attn_tok = lax.all_to_all(out_send, "sp", 0, 0, tiled=True).transpose(1, 0, 2).reshape(rows, width)
    residual = x + dot(attn_tok, out_all)
    inv_two = lax.rsqrt(jnp.mean(residual * residual, axis=-1, keepdims=True) + EPSILON)
    inner = (residual * inv_two * mlp_gain).astype(BF)

    inner_rows = gather_chips(inner)
    hid_rows, dgu_rows, y_parts, db_parts = [], [], [], []
    for b_rows, dy_part in zip(inner_rows, dy_rows):
        gate_up = dot(b_rows, w_gu)
        d_hidden = dot(dy_part, w_dn, NT)
        gate = gate_up[:, :hidden_chip]
        up = gate_up[:, hidden_chip:]
        sigmoid_g = jax.nn.sigmoid(gate)
        silu_gate = gate * sigmoid_g
        slope = sigmoid_g * (1.0 + gate * (1.0 - sigmoid_g))
        hid = (silu_gate * up).astype(BF)
        dgu = jnp.concatenate([d_hidden * up * slope, d_hidden * silu_gate], axis=1).astype(BF)
        hid_rows.append(hid)
        dgu_rows.append(dgu)
        db_parts.append(dot(dgu, w_gu, NT))
        y_parts.append(dot(hid, w_dn))

    d_inner = scatter_chips(db_parts)
    grad_y = dy.astype(F32)
    scaled = d_inner * mlp_gain
    inner_mean = jnp.mean(scaled * residual, axis=-1, keepdims=True)
    d_resid = grad_y + inv_two * scaled - residual * inv_two**3 * inner_mean
    gain_two = jnp.sum(d_inner * residual * inv_two, axis=0)
    d_branch = d_resid.astype(BF)
    d_attn = dot(d_branch, out_all, NT).astype(BF)
    d_send = d_attn.reshape(rows, devices, share).transpose(1, 0, 2)
    d_heads = lax.all_to_all(d_send, "sp", 0, 0, tiled=True).reshape(length, share)

    all_inner = jnp.concatenate(inner_rows, axis=0)
    all_dgu = jnp.concatenate(dgu_rows, axis=0)
    grad_gu = dot(all_inner, all_dgu, TN).astype(BF).reshape(CHIPS, 2, share, 2 * hidden_chip)
    gu_keep = lax.dynamic_slice_in_dim(grad_gu, core, 1, 1)
    gu_give = lax.dynamic_slice_in_dim(grad_gu, 1 - core, 1, 1)
    gu_sum = gu_keep.astype(F32) + send_sibling(gu_give).astype(F32)
    gu_sum = gu_sum.astype(BF).reshape(CHIPS, planes, quarter, 2 * hidden_chip).transpose(1, 0, 2, 3)
    gu_z = line_scatter(gu_sum)
    gu_z = lax.all_to_all(gu_z, "sp", 0, 0, axis_index_groups=SAME_CORE, tiled=True)
    grad_w_gate_up = spread(line_gather(gu_z), 2 * CHIPS * hidden_chip)
    all_hid = jnp.concatenate(hid_rows, axis=0)
    all_dy = jnp.concatenate(dy_rows, axis=0)
    grad_dn = dot(all_hid, all_dy, TN).astype(BF).reshape(2, hidden_chip // 2, width)
    dn_keep = lax.dynamic_slice_in_dim(grad_dn, core, 1, 0)[0]
    dn_give = lax.dynamic_slice_in_dim(grad_dn, 1 - core, 1, 0)[0]
    dn_sum = (dn_keep.astype(F32) + send_sibling(dn_give).astype(F32)).astype(BF)
    grad_w_down = line_sum(dn_sum).astype(F32)

    y_sum = scatter_chips(y_parts)
    output = (residual + y_sum).astype(BF).reshape(tokens.shape)

    pad = jnp.zeros((width, 128), F32)
    grad_wo = jnp.concatenate([dot(attn_tok, d_branch, TN), pad.at[:, 0].set(gain_two)], axis=1).astype(BF)
    wo_rows = lax.psum_scatter(grad_wo, "sp", scatter_dimension=0, tiled=True)
    wo_rows = line_sum(wo_rows).astype(F32)
    grad_w_out = wo_rows[:, :width]
    grad_g_mlp = wo_rows[:, width]

    d_heads = after(d_heads, gu_sum, dn_sum)
    back_send = attend_back(zeros_one, qkv_heads, d_heads, out_heads, lse)
    back = lax.all_to_all(back_send, "sp", 0, 0, tiled=True)
    d_mixed = unturn(back, cos, sin)
    d_normed = dot(d_mixed, qkv_all.reshape(width, qkv_width + EXTRA), NT)
    scaled_one = d_normed * attn_gain
    mean_one = jnp.mean(scaled_one * x, axis=-1, keepdims=True)
    grad_in = d_resid + inv_one * scaled_one - x * inv_one**3 * mean_one
    grad_tokens = grad_in.astype(BF).reshape(tokens.shape)
    gain_one = jnp.sum(d_normed * x * inv_one, axis=0)
    column = lax.broadcasted_iota(jnp.int32, (1, qkv_width + EXTRA), 1)
    grad_wq = (dot(normed, d_mixed, TN) + jnp.where(column == qkv_width, gain_one[:, None], 0.0)).astype(BF)
    wq_rows = scatter_plane(grad_wq.reshape(devices, share, qkv_width + EXTRA), me).astype(BF)
    wq_rows = line_sum(wq_rows).astype(F32)
    pieces = [wq_rows[:, :width]]
    for kind in range(2):
        for head in range(KV):
            begin = width + (2 * head + kind) * HD
            pieces.append(wq_rows[:, begin : begin + HD])
    grad_w_qkv = jnp.concatenate(pieces, axis=1)
    return (
        output,
        grad_tokens,
        grad_w_qkv,
        grad_w_out,
        grad_w_gate_up,
        grad_w_down,
        wq_rows[:, qkv_width],
        grad_g_mlp,
    )


def solution(mesh):
    in_specs = (
        P("dp", "sp", None),
        P("dp", "sp"),
        P("dp", "sp"),
        P("dp", "sp", None),
        P("sp", None),
        P("sp", None),
        P("sp", None),
        P("sp", None),
        P("sp"),
        P("sp"),
    )
    out_specs = (
        P("dp", "sp", None),
        P("dp", "sp", None),
        P("sp", None),
        P("sp", None),
        P("sp", None),
        P("sp", None),
        P("sp"),
        P("sp"),
    )
    body = fast_body if mesh.shape["sp"] == 2 * CHIPS else general_body
    return jax.shard_map(body, mesh=mesh, in_specs=in_specs, out_specs=out_specs, check_vma=False)
```

```python
import functools
import math

import jax
import jax.numpy as jnp
from jax import lax
from jax.experimental import pallas as pl
from jax.experimental.pallas import tpu as pltpu
from jax.sharding import PartitionSpec as P

D = 2048
H = 32
KV = 4
HD = 64
FF = 5632


EPSILON = 1e-05
ROPE_BASE = 10000.0
MASKED = -1e30


def rope_tables(positions, head_size):
    half_dim = head_size // 2
    frequency = ROPE_BASE ** (-(jnp.arange(half_dim, dtype=jnp.float32) * 2.0 / head_size))
    angles = positions.astype(jnp.float32)[:, None] * frequency[None, :]
    return (jnp.cos(angles), jnp.sin(angles))


def rotate(values, cosine, sine_tab, inverse_turn):
    half_dim = values.shape[-1] // 2
    first_half = values[..., :half_dim]
    second = values[..., half_dim:]
    cos_wide = cosine[:, None, :]
    sin_wide = sine_tab[:, None, :]
    if inverse_turn:
        sin_wide = -sin_wide
    return jnp.concatenate(
        [first_half * cos_wide - second * sin_wide, second * cos_wide + first_half * sin_wide],
        axis=-1,
    )


def rms_norm(values, gain_vec):
    inverse = lax.rsqrt(jnp.mean(values * values, axis=-1, keepdims=True) + EPSILON)
    return (values * inverse * gain_vec, inverse)


def norm_back(values, inverse, gain_vec, upstream):
    scaled = upstream * gain_vec
    inner_mean = jnp.mean(scaled * values, axis=-1, keepdims=True)
    through = inverse * scaled - values * inverse**3 * inner_mean
    gain_grad = jnp.sum(upstream * values * inverse, axis=0)
    return (through, gain_grad)


def attention_inputs(flat_in, qkv_full, gain_vec, cosine, sine_tab):
    row_count = flat_in.shape[0]
    group_size = H // KV
    normed, inverse = rms_norm(flat_in, gain_vec)
    normed = normed.astype(jnp.bfloat16)
    projected = jnp.dot(normed, qkv_full, preferred_element_type=jnp.float32)
    queries = rotate(projected[:, :D].reshape(row_count, H, HD), cosine, sine_tab, False)
    key_heads = rotate(
        projected[:, D : D + KV * HD].reshape(row_count, KV, HD), cosine, sine_tab, False
    )
    value_heads = projected[:, D + KV * HD :].reshape(row_count, KV, HD)
    key_wide = jnp.broadcast_to(key_heads[:, :, None], (row_count, KV, group_size, HD)).reshape(
        row_count, D
    )
    value_wide = jnp.broadcast_to(value_heads[:, :, None], (row_count, KV, group_size, HD)).reshape(
        row_count, D
    )
    stacked = jnp.stack([queries.reshape(row_count, D), key_wide, value_wide]).astype(jnp.bfloat16)
    return (normed, inverse, stacked)


def block_mask(seg_full, position, row_begin, finish):
    row_seg = seg_full[:, row_begin:finish]
    col_seg = seg_full[:, :finish]
    same_doc = row_seg[:, :, None] == col_seg[:, None, :]
    causal = position[row_begin:finish, None] >= position[None, :finish]
    return same_doc & causal[None]


def attention_forward(queries, key_heads, value_heads, seg_full, score_scale):
    length = queries.shape[1]
    block_rows = min(512, length)
    position = jnp.arange(length, dtype=jnp.int32)
    outputs = []
    lse_parts = []
    for block_num in range(length // block_rows):
        row_begin = block_num * block_rows
        finish = row_begin + block_rows
        scores = (
            jnp.einsum(
                "sqhd,skhd->shqk",
                queries[:, row_begin:finish],
                key_heads[:, :finish],
                preferred_element_type=jnp.float32,
            )
            * score_scale
        )
        allowed = block_mask(seg_full, position, row_begin, finish)
        scores = jnp.where(allowed[:, None], scores, MASKED)
        row_max = jnp.max(scores, axis=-1, keepdims=True)
        shifted = jnp.exp(scores - row_max)
        row_total = jnp.sum(shifted, axis=-1, keepdims=True)
        softmax_w = (shifted / row_total).astype(jnp.bfloat16)
        outputs.append(
            jnp.einsum(
                "shqk,skhd->sqhd",
                softmax_w,
                value_heads[:, :finish],
                preferred_element_type=jnp.float32,
            )
        )
        lse_parts.append(row_max + jnp.log(row_total))
    return (jnp.concatenate(outputs, axis=1), jnp.concatenate(lse_parts, axis=2))


def attention_backward(queries, key_heads, value_heads, seg_full, log_sums, grad_out, score_scale):
    length = queries.shape[1]
    block_rows = min(512, length)
    position = jnp.arange(length, dtype=jnp.int32)
    grad_query = []
    grad_key = jnp.zeros(key_heads.shape, jnp.float32)
    grad_value = jnp.zeros(value_heads.shape, jnp.float32)
    for block_num in range(length // block_rows):
        row_begin = block_num * block_rows
        finish = row_begin + block_rows
        query_rows = queries[:, row_begin:finish]
        grad_rows = grad_out[:, row_begin:finish]
        key_part = key_heads[:, :finish]
        value_part = value_heads[:, :finish]
        scores = (
            jnp.einsum("sqhd,skhd->shqk", query_rows, key_part, preferred_element_type=jnp.float32)
            * score_scale
        )
        allowed = block_mask(seg_full, position, row_begin, finish)
        softmax_f = jnp.where(
            allowed[:, None], jnp.exp(scores - log_sums[:, :, row_begin:finish]), 0.0
        )
        grad_probs = jnp.einsum(
            "sqhd,skhd->shqk", grad_rows, value_part, preferred_element_type=jnp.float32
        )
        row_delta = jnp.sum(softmax_f * grad_probs, axis=-1, keepdims=True)
        grad_scores = (softmax_f * (grad_probs - row_delta)).astype(jnp.bfloat16)
        grad_query.append(
            jnp.einsum("shqk,skhd->sqhd", grad_scores, key_part, preferred_element_type=jnp.float32)
            * score_scale
        )
        grad_key = grad_key.at[:, :finish].add(
            jnp.einsum(
                "shqk,sqhd->skhd", grad_scores, query_rows, preferred_element_type=jnp.float32
            )
            * score_scale
        )
        grad_value = grad_value.at[:, :finish].add(
            jnp.einsum(
                "shqk,sqhd->skhd",
                softmax_f.astype(jnp.bfloat16),
                grad_rows,
                preferred_element_type=jnp.float32,
            )
        )
    return (jnp.concatenate(grad_query, axis=1), grad_key, grad_value)


def general_body(tokens, segment_ids, selected, cotangent, w_qkv, w_out, w_gate_up, w_down, g_attn, g_mlp):
    streams, local_len, model_dim = tokens.shape
    sp_count = lax.axis_size("sp")
    sp_index = lax.axis_index("sp")
    row_count = streams * local_len
    group_size = H // KV
    kv_width = KV * HD
    score_scale = HD ** (-0.5)
    contract = (((0,), (0,)), ((), ()))
    seg_full = lax.all_gather(segment_ids, "sp", axis=1, tiled=True)
    first_count = jnp.sum((seg_full == 0).astype(jnp.int32), axis=1, keepdims=True)
    local_pos = (
        sp_index * local_len
        + jnp.arange(local_len, dtype=jnp.int32)[None, :]
        - segment_ids * first_count
    )
    cosine, sine_tab = rope_tables(local_pos.reshape(row_count), HD)
    shards = (w_qkv, w_out, w_gate_up, w_down, g_attn, g_mlp)
    gathered = (
        lax.all_gather(shards[0], "sp", axis=0, tiled=True),
        lax.all_gather(shards[1], "sp", axis=0, tiled=True),
        lax.all_gather(shards[2], "sp", axis=0, tiled=True),
        lax.all_gather(shards[3], "sp", axis=0, tiled=True),
        lax.all_gather(shards[4], "sp", axis=0, tiled=True),
        lax.all_gather(shards[5], "sp", axis=0, tiled=True),
    )
    qkv_full, out_full, gate_up_full, down_full, attn_gain, mlp_gain = gathered
    attn_gain = attn_gain.astype(jnp.float32)
    mlp_gain = mlp_gain.astype(jnp.float32)
    flat_in = tokens.reshape(row_count, model_dim).astype(jnp.float32)
    normed, inverse_one, stacked = attention_inputs(flat_in, qkv_full, attn_gain, cosine, sine_tab)
    head_view = lax.all_to_all(
        stacked.reshape(3, streams, local_len, model_dim),
        "sp",
        split_axis=3,
        concat_axis=2,
        tiled=True,
    )
    length = head_view.shape[2]
    heads_here = head_view.shape[3] // HD
    head_shape = (streams, length, heads_here, HD)
    queries = head_view[0].reshape(head_shape)
    key_heads = head_view[1].reshape(head_shape)
    value_heads = head_view[2].reshape(head_shape)
    attn_heads, log_sums = attention_forward(queries, key_heads, value_heads, seg_full, score_scale)
    attn_send = attn_heads.astype(jnp.bfloat16).reshape(streams, length, heads_here * HD)
    attn_tok = lax.all_to_all(attn_send, "sp", split_axis=1, concat_axis=2, tiled=True).reshape(
        row_count, model_dim
    )
    branch = jnp.dot(attn_tok, out_full, preferred_element_type=jnp.float32)
    residual = flat_in + branch
    inner_f, inverse_two = rms_norm(residual, mlp_gain)
    inner_in = inner_f.astype(jnp.bfloat16)
    gate_up = jnp.dot(inner_in, gate_up_full, preferred_element_type=jnp.float32)
    gate_part = gate_up[:, :FF]
    up_part = gate_up[:, FF:]
    sigmoid_g = jax.nn.sigmoid(gate_part)
    silu_gate = gate_part * sigmoid_g
    hidden = (silu_gate * up_part).astype(jnp.bfloat16)
    result = residual + jnp.dot(hidden, down_full, preferred_element_type=jnp.float32)
    output = result.astype(jnp.bfloat16).reshape(streams, local_len, model_dim)
    qkv_back, out_back, gate_up_back, down_back, attn_gain_b, mlp_gain_b = gathered
    attn_gain_b = attn_gain_b.astype(jnp.float32)
    mlp_gain_b = mlp_gain_b.astype(jnp.float32)
    grad_y = (cotangent * selected[:, :, None].astype(jnp.bfloat16)).reshape(row_count, model_dim)
    grad_hidden = jnp.dot(grad_y, down_back.T, preferred_element_type=jnp.float32)
    silu_slope = sigmoid_g * (1.0 + gate_part * (1.0 - sigmoid_g))
    grad_both = jnp.concatenate(
        [grad_hidden * up_part * silu_slope, grad_hidden * silu_gate], axis=1
    ).astype(jnp.bfloat16)
    grad_inner = jnp.dot(grad_both, gate_up_back.T, preferred_element_type=jnp.float32)
    grad_resid, gain_two = norm_back(residual, inverse_two, mlp_gain_b, grad_inner)
    grad_resid = grad_resid + grad_y.astype(jnp.float32)
    grad_branch = grad_resid.astype(jnp.bfloat16)
    grad_attn = jnp.dot(grad_branch, out_back.T, preferred_element_type=jnp.float32).astype(
        jnp.bfloat16
    )
    grad_view = lax.all_to_all(
        grad_attn.reshape(streams, local_len, model_dim),
        "sp",
        split_axis=2,
        concat_axis=1,
        tiled=True,
    )
    grad_view = grad_view.reshape(head_shape)
    grad_q, grad_k, grad_v = attention_backward(
        queries, key_heads, value_heads, seg_full, log_sums, grad_view, score_scale
    )
    back_send = (
        jnp.stack([grad_q, grad_k, grad_v])
        .astype(jnp.bfloat16)
        .reshape(3, streams, length, heads_here * HD)
    )
    returned = lax.all_to_all(back_send, "sp", split_axis=2, concat_axis=3, tiled=True)
    returned = returned.astype(jnp.float32).reshape(3, row_count, H, HD)
    grad_pq = rotate(returned[0], cosine, sine_tab, True).reshape(row_count, model_dim)
    key_summed = jnp.sum(returned[1].reshape(row_count, KV, group_size, HD), axis=2)
    grad_pk = rotate(key_summed, cosine, sine_tab, True).reshape(row_count, kv_width)
    grad_pv = jnp.sum(returned[2].reshape(row_count, KV, group_size, HD), axis=2).reshape(
        row_count, kv_width
    )
    grad_mixed = jnp.concatenate(
        [grad_pq.astype(jnp.bfloat16), grad_pk.astype(jnp.bfloat16), grad_pv.astype(jnp.bfloat16)],
        axis=1,
    )
    grad_normed = jnp.dot(grad_mixed, qkv_back.T, preferred_element_type=jnp.float32)
    grad_in, gain_one = norm_back(flat_in, inverse_one, attn_gain_b, grad_normed)
    grad_in = grad_in + grad_resid
    grad_tokens = grad_in.astype(jnp.bfloat16).reshape(streams, local_len, model_dim)
    gain_totals = lax.psum((gain_one, gain_two), ("dp", "sp"))
    gain_share = model_dim // sp_count
    grad_g_attn = lax.dynamic_slice_in_dim(gain_totals[0], sp_index * gain_share, gain_share, 0)
    grad_g_mlp = lax.dynamic_slice_in_dim(gain_totals[1], sp_index * gain_share, gain_share, 0)
    row_sums = lax.psum_scatter(
        jnp.concatenate(
            [
                lax.dot_general(normed, grad_mixed, contract, preferred_element_type=jnp.float32),
                lax.dot_general(
                    attn_tok, grad_branch, contract, preferred_element_type=jnp.float32
                ),
                lax.dot_general(inner_in, grad_both, contract, preferred_element_type=jnp.float32),
            ],
            axis=1,
        ).astype(jnp.bfloat16),
        "sp",
        scatter_dimension=0,
        tiled=True,
    )
    down_sums = lax.psum_scatter(
        lax.dot_general(hidden, grad_y, contract, preferred_element_type=jnp.float32).astype(
            jnp.bfloat16
        ),
        "sp",
        scatter_dimension=0,
        tiled=True,
    )
    weight_rows, down_rows = (
        lax.psum(row_sums, "dp").astype(jnp.float32),
        lax.psum(down_sums, "dp").astype(jnp.float32),
    )
    qkv_cols = model_dim + 2 * kv_width
    grad_w_qkv = weight_rows[:, :qkv_cols]
    grad_w_out = weight_rows[:, qkv_cols : qkv_cols + model_dim]
    grad_w_gate_up = weight_rows[:, qkv_cols + model_dim :]
    return (
        output,
        grad_tokens,
        grad_w_qkv,
        grad_w_out,
        grad_w_gate_up,
        down_rows,
        grad_g_attn,
        grad_g_mlp,
    )


CHIPS = 4
BLOCK = 512
SHORT = pl.CostEstimate(flops=1, bytes_accessed=1, transcendentals=0)
LOG2E = math.log2(math.e)
BF = jnp.bfloat16
F32 = jnp.float32
NT = (((1,), (1,)), ((), ()))
TN = (((0,), (0,)), ((), ()))


def swap_pairs(even_mask, odd_mask):
    return [(i, i ^ (odd_mask if i & 1 else even_mask)) for i in range(2 * CHIPS)]


FIRST = swap_pairs(2, 4)
SECOND = swap_pairs(4, 2)
SIBLING = swap_pairs(1, 1)
SAME_CORE = [[0, 2, 4, 6], [1, 3, 5, 7]]


def send_first(x):
    return lax.ppermute(x, "sp", FIRST)


def send_second(x):
    return lax.ppermute(x, "sp", SECOND)


def send_sibling(x):
    return lax.ppermute(x, "sp", SIBLING)


def after(value, *others):
    return lax.optimization_barrier((value,) + others)[0]


def gather_chips(own):
    first = send_first(own)
    second = send_second(after(own, first))
    far = send_second(after(first, second))
    return [own, first, second, far]


def rel_masks(core):
    first = jnp.where(core == 0, 2, 4)
    return first, 6 - first


def fence(*values):
    return lax.optimization_barrier(values)


def gather_vectors(own, me):
    for bit in (1, 2, 4):
        got = lax.ppermute(own, "sp", swap_pairs(bit, bit))
        high = (me & bit) != 0
        own = jnp.concatenate([jnp.where(high, got, own), jnp.where(high, own, got)], axis=1)
    return own


def pick(parts, index):
    return lax.dynamic_index_in_dim(parts, index, 0, keepdims=False)


def pick_sum(parts, index, axis):
    return sum(lax.dynamic_index_in_dim(p, index, axis, keepdims=False).astype(F32) for p in parts)


def line_scatter_sends(parts, got, step, axis):
    planes = parts[0].shape[axis]
    z = lax.axis_index("dp")
    ahead = pick_sum(parts, jnp.clip(planes - step + z, 0, planes - 1), axis)
    back = pick_sum(parts, jnp.clip(z - planes + step, 0, planes - 1), axis)
    if got is not None:
        ahead = ahead + got[0].astype(F32)
        back = back + got[1].astype(F32)
    return ahead.astype(BF), back.astype(BF)


def line_scatter_move(sends, step):
    planes = lax.axis_size("dp")
    right = lax.ppermute(sends[0], "dp", [(i, i + 1) for i in range(step)])
    left = lax.ppermute(sends[1], "dp", [(planes - 1 - i, planes - 2 - i) for i in range(step)])
    return right, left


def line_scatter_end(parts, got, axis):
    own = pick_sum(parts, lax.axis_index("dp"), axis)
    return (own + got[0].astype(F32) + got[1].astype(F32)).astype(BF)


def line_gather_move(got, step):
    planes = lax.axis_size("dp")
    right = lax.ppermute(got[0], "dp", [(i, i + 1) for i in range(step - 1, planes - 1)])
    left = lax.ppermute(got[1], "dp", [(i + 1, i) for i in range(planes - step)])
    return right, left


def line_values(refs, planes, z):
    for step in range(planes):
        place = lax.rem(z - step + planes, planes)
        if step == 0:
            yield place, lambda index: refs[0][index]
        else:
            right, left = refs[step], refs[2 * planes - 1 - step]
            yield place, lambda index, right=right, left=left, step=step: jnp.where(z >= step, right[index], left[index])


def spread_kernel(in_ref, w_ref, g_ref, out_ref, gain_ref):
    planes, _, rows, width = in_ref.shape
    out = in_ref[...].reshape(planes * rows, width).astype(F32)
    out_ref[...] = out
    part = jnp.sum(out * w_ref[...].astype(F32), axis=-1, keepdims=True) / g_ref[...]

    @pl.when(pl.program_id(0) == 0)
    def _():
        gain_ref[...] = part

    @pl.when(pl.program_id(0) > 0)
    def _():
        gain_ref[...] += part


def spread(parts, weight, gain):
    planes, chips, rows, both = parts.shape
    half = both // 2
    total = planes * rows
    line = pl.BlockSpec((total, half), lambda i: (0, i))
    column = pl.BlockSpec((total, 1), lambda i: (0, 0))
    return pl.pallas_call(
        spread_kernel,
        grid=(2 * chips,),
        in_specs=[pl.BlockSpec((planes, 1, rows, half), lambda i: (0, i % chips, 0, i // chips)), line, column],
        out_specs=[line, column],
        out_shape=[jax.ShapeDtypeStruct(weight.shape, F32), jax.ShapeDtypeStruct((total, 1), F32)],
        compiler_params=pltpu.CompilerParams(vmem_limit_bytes=32 * 2**20),
        cost_estimate=SHORT,
        name="spread",
    )(parts, weight, gain)


def spread_rows_kernel(z_ref, *refs, planes):
    blocks, out_ref = refs[:-1], refs[-1]
    rows = blocks[0].shape[0]
    for place, load in line_values(blocks, planes, z_ref[0]):
        out_ref[pl.ds(pl.multiple_of(place * rows, rows), rows), :] = load(slice(None)).astype(F32)


def spread_rows(steps):
    planes = len(steps)
    rows, width = steps[0][0].shape
    blocks = [steps[0][0]] + [s[0] for s in steps[1:]] + [s[1] for s in steps[1:]]
    tile = width // 4
    return pl.pallas_call(
        functools.partial(spread_rows_kernel, planes=planes),
        grid_spec=pltpu.PrefetchScalarGridSpec(
            num_scalar_prefetch=1,
            grid=(4,),
            in_specs=[pl.BlockSpec((rows, tile), lambda i, z: (0, i))] * len(blocks),
            out_specs=pl.BlockSpec((planes * rows, tile), lambda i, z: (0, i)),
        ),
        out_shape=jax.ShapeDtypeStruct((planes * rows, width), F32),
        compiler_params=pltpu.CompilerParams(vmem_limit_bytes=32 * 2**20),
        cost_estimate=SHORT,
        name="spread_rows",
    )(lax.axis_index("dp").reshape(1), *blocks)


def spread_qkv_kernel(z_ref, *refs, planes):
    blocks, (w_ref, g_ref, out_ref, gain_ref) = refs[:-4], refs[-4:]
    devices, rows, width = blocks[0].shape
    heads = width - 2 * HD
    base = devices * heads
    z = z_ref[0]
    for place, load in line_values(blocks, planes, z):
        span = pl.ds(pl.multiple_of(place * rows, rows), rows)
        pairs = []
        for d in range(devices):
            block = load(d).astype(F32)
            out_ref[span, d * heads : (d + 1) * heads] = block[:, :heads]
            pairs.append(block[:, heads:])
        for g in range(0, KV, 2):
            low = pairs[2 * g] + pairs[2 * g + 1]
            high = pairs[2 * g + 2] + pairs[2 * g + 3]
            lane = lax.broadcasted_iota(jnp.int32, low.shape, 1)
            out_ref[span, base + g * HD : base + (g + 2) * HD] = jnp.where(lane < HD, low, pltpu.roll(high, HD, 1))
            out_ref[span, base + (KV + g) * HD : base + (KV + g + 2) * HD] = jnp.where(
                lane < HD, pltpu.roll(low, HD, 1), high
            )
    gain_ref[...] = jnp.sum(out_ref[...] * w_ref[...].astype(F32), axis=-1, keepdims=True) / g_ref[...]


def spread_qkv(steps, weight, gain):
    planes = len(steps)
    blocks = [steps[0][0]] + [s[0] for s in steps[1:]] + [s[1] for s in steps[1:]]
    vmem = pl.BlockSpec(memory_space=pltpu.VMEM)
    return pl.pallas_call(
        functools.partial(spread_qkv_kernel, planes=planes),
        in_specs=[pl.BlockSpec(memory_space=pltpu.SMEM)] + [vmem] * (len(blocks) + 2),
        out_specs=[vmem, vmem],
        out_shape=[jax.ShapeDtypeStruct(weight.shape, F32), jax.ShapeDtypeStruct((weight.shape[0], 1), F32)],
        compiler_params=pltpu.CompilerParams(vmem_limit_bytes=32 * 2**20),
        cost_estimate=SHORT,
        name="spread_qkv",
    )(lax.axis_index("dp").reshape(1), *blocks, weight, gain)


def join_kernel(core_ref, mine_ref, theirs_ref, out_ref):
    planes, _, rows, both = mine_ref.shape
    block = jnp.where(pl.program_id(1) == 0, mine_ref[...], theirs_ref[...]).reshape(planes * rows, both)
    out_ref[0, 0, 0] = block[:, : both // 2]
    out_ref[1, 0, 0] = block[:, both // 2 :]


def join(core, mine, theirs):
    planes, chips, rows, both = mine.shape
    spec = pl.BlockSpec((planes, 1, rows, both), lambda c, k, core: (0, c, 0, 0))
    out = pl.pallas_call(
        join_kernel,
        grid_spec=pltpu.PrefetchScalarGridSpec(
            num_scalar_prefetch=1,
            grid=(chips, 2),
            in_specs=[spec, spec],
            out_specs=pl.BlockSpec(
                (2, 1, 1, planes * rows, both // 2), lambda c, k, core: (0, c, (core[0] + k) % 2, 0, 0)
            ),
        ),
        out_shape=jax.ShapeDtypeStruct((2, chips, 2, planes * rows, both // 2), BF),
        compiler_params=pltpu.CompilerParams(vmem_limit_bytes=32 * 2**20),
        cost_estimate=SHORT,
        name="join",
    )(core.reshape(1), mine, theirs)
    return out.reshape(2, 2 * chips * planes * rows, both // 2)


def ffn_kernel(b_ref, dy_ref, wg_ref, wu_ref, wd_ref, hid_ref, dg_ref, du_ref, db_ref, y_ref):
    gate = jnp.dot(b_ref[...], wg_ref[...], preferred_element_type=F32)
    up = jnp.dot(b_ref[...], wu_ref[...], preferred_element_type=F32)
    d_hidden = lax.dot_general(dy_ref[...], wd_ref[...], NT, preferred_element_type=F32)
    sigmoid_g = jax.nn.sigmoid(gate)
    silu_gate = gate * sigmoid_g
    hid = (silu_gate * up).astype(BF)
    d_gate = (d_hidden * up * (sigmoid_g * (1.0 + gate * (1.0 - sigmoid_g)))).astype(BF)
    d_up = (d_hidden * silu_gate).astype(BF)
    hid_ref[...] = hid
    dg_ref[...] = d_gate
    du_ref[...] = d_up
    y_ref[...] = jnp.dot(hid, wd_ref[...], preferred_element_type=F32).astype(BF)
    d_in = lax.dot_general(d_gate, wg_ref[...], NT, preferred_element_type=F32)
    db_ref[...] = (d_in + lax.dot_general(d_up, wu_ref[...], NT, preferred_element_type=F32)).astype(BF)


def ffn(b_rows, dy_rows, w_gu, w_dn):
    rows, width = b_rows.shape
    hidden = w_dn.shape[0]
    return pl.pallas_call(
        ffn_kernel,
        grid=(1,),
        in_specs=[
            pl.BlockSpec((rows, width), lambda i: (0, 0)),
            pl.BlockSpec((rows, width), lambda i: (0, 0)),
            pl.BlockSpec((None, width, hidden), lambda i: (0, 0, 0)),
            pl.BlockSpec((None, width, hidden), lambda i: (1, 0, 0)),
            pl.BlockSpec((hidden, width), lambda i: (0, 0)),
        ],
        out_specs=[pl.BlockSpec((rows, hidden), lambda i: (0, 0))] * 3
        + [pl.BlockSpec((rows, width), lambda i: (0, 0))] * 2,
        out_shape=[jax.ShapeDtypeStruct((rows, hidden), BF)] * 3 + [jax.ShapeDtypeStruct((rows, width), BF)] * 2,
        compiler_params=pltpu.CompilerParams(vmem_limit_bytes=58 * 2**20),
        cost_estimate=SHORT,
        name="ffn",
    )(b_rows, dy_rows, w_gu, w_gu, w_dn)


def grad_gu_kernel(core_ref, *refs, count):
    left, right = refs[: 2 * count], refs[2 * count : 4 * count]
    half = right[0].shape[1]
    for side in range(2):
        for kind in range(2):
            total = None
            for r in range(count):
                a_rows = left[side * count + r][...]
                part = lax.dot_general(a_rows, right[kind * count + r][...], TN, preferred_element_type=F32)
                total = part if total is None else total + part
            refs[4 * count + side][0, :, kind * half : (kind + 1) * half] = total.astype(BF)


def grad_gu(core, b_rows, dg_rows, du_rows, share):
    count = len(b_rows)
    tokens, width = b_rows[0].shape
    hidden = dg_rows[0].shape[1]
    keep = pl.BlockSpec((tokens, share), lambda c, core: (0, 2 * c + core[0]))
    give = pl.BlockSpec((tokens, share), lambda c, core: (0, 2 * c + 1 - core[0]))
    whole = pl.BlockSpec((tokens, hidden), lambda c, core: (0, 0))
    out = pl.BlockSpec((1, share, 2 * hidden), lambda c, core: (c, 0, 0))
    return pl.pallas_call(
        functools.partial(grad_gu_kernel, count=count),
        grid_spec=pltpu.PrefetchScalarGridSpec(
            num_scalar_prefetch=1,
            grid=(width // (2 * share),),
            in_specs=[keep] * count + [give] * count + [whole] * (2 * count),
            out_specs=[out, out],
        ),
        out_shape=[jax.ShapeDtypeStruct((width // (2 * share), share, 2 * hidden), BF)] * 2,
        compiler_params=pltpu.CompilerParams(vmem_limit_bytes=58 * 2**20),
        cost_estimate=SHORT,
        name="grad_gu",
    )(core.reshape(1), *b_rows, *b_rows, *dg_rows, *du_rows)


def grad_qkv_kernel(place_ref, *refs, count):
    dp_ref, out_ref = refs[-2:]
    total = None
    for r in range(count):
        part = lax.dot_general(refs[r][...], dp_ref[place_ref[r]], TN, preferred_element_type=F32)
        total = part if total is None else total + part
    out_ref[...] = total.astype(BF)


def grad_qkv(places, a_rows, dp_heads):
    count = len(a_rows)
    tokens, width = a_rows[0].shape
    columns = dp_heads.shape[2]
    depth = 512
    return pl.pallas_call(
        functools.partial(grad_qkv_kernel, count=count),
        grid_spec=pltpu.PrefetchScalarGridSpec(
            num_scalar_prefetch=1,
            grid=(width // depth,),
            in_specs=[pl.BlockSpec((tokens, depth), lambda i, p: (0, i))] * count
            + [pl.BlockSpec(dp_heads.shape, lambda i, p: (0, 0, 0))],
            out_specs=pl.BlockSpec((depth, columns), lambda i, p: (i, 0)),
        ),
        out_shape=jax.ShapeDtypeStruct((width, columns), BF),
        compiler_params=pltpu.CompilerParams(vmem_limit_bytes=48 * 2**20),
        cost_estimate=SHORT,
        name="grad_qkv",
    )(places, *a_rows, dp_heads)


def swap_halves(values):
    width = values.shape[-1]
    lane = lax.broadcasted_iota(jnp.int32, values.shape, 1)
    ahead = pltpu.roll(values, width - HD // 2, 1)
    behind = pltpu.roll(values, HD // 2, 1)
    return jnp.where(lane % HD < HD // 2, ahead, behind)


def project_kernel(place_ref, x_ref, gain_ref, cos_ref, sin_ref, *refs, count):
    wq_refs, wkv_refs = refs[:count], refs[count : 2 * count]
    send_ref, normed_ref, inv_ref, normed_scr = refs[2 * count :]
    share = normed_scr.shape[2]

    @pl.when(pl.program_id(0) == 0)
    def _():
        x = x_ref[...].astype(F32)
        inv = lax.rsqrt(jnp.mean(x * x, axis=-1, keepdims=True) + EPSILON)
        normed = (x * inv * gain_ref[...]).astype(BF)
        normed_ref[...] = normed
        inv_ref[...] = inv
        for part in range(count):
            normed_scr[part] = normed[:, part * share : (part + 1) * share]

    pq = pkv = None
    for r in range(count):
        a_rows = normed_scr[place_ref[r]]
        q_part = jnp.dot(a_rows, wq_refs[r][...], preferred_element_type=F32)
        kv_part = jnp.dot(a_rows, wkv_refs[r][...], preferred_element_type=F32)
        pq = q_part if pq is None else pq + q_part
        pkv = kv_part if pkv is None else pkv + kv_part
    cos = cos_ref[...]
    sin = sin_ref[...]
    heads = pq.shape[1]
    q_scale = LOG2E * HD**-0.5
    turned = pq * jnp.tile(cos, (1, heads // 128)) + swap_halves(pq) * jnp.tile(sin, (1, heads // 128))
    send_ref[0, :, :heads] = (turned * q_scale).astype(BF)
    lane = lax.broadcasted_iota(jnp.int32, pkv.shape, 1)
    turned_kv = jnp.where(lane < HD, pkv * cos + swap_halves(pkv) * sin, pkv)
    send_ref[0, :, heads:] = turned_kv.astype(BF)


def project(places, x, gain, cos, sin, parts):
    rows, width = x.shape
    count = len(parts)
    heads = width // count
    out_width = heads + 2 * HD
    depth = parts[0].shape[0]
    first_kv = width // (2 * HD)
    return pl.pallas_call(
        functools.partial(project_kernel, count=count),
        grid_spec=pltpu.PrefetchScalarGridSpec(
            num_scalar_prefetch=1,
            grid=(count,),
            in_specs=[
                pl.BlockSpec((rows, width), lambda d, p: (0, 0)),
                pl.BlockSpec((1, width), lambda d, p: (0, 0)),
                pl.BlockSpec((rows, 128), lambda d, p: (0, 0)),
                pl.BlockSpec((rows, 128), lambda d, p: (0, 0)),
            ]
            + [pl.BlockSpec((depth, heads), lambda d, p: (0, d))] * count
            + [pl.BlockSpec((depth, 2 * HD), lambda d, p: (0, first_kv + d // 2))] * count,
            out_specs=[
                pl.BlockSpec((1, rows, out_width), lambda d, p: (d, 0, 0)),
                pl.BlockSpec((rows, width), lambda d, p: (0, 0)),
                pl.BlockSpec((rows, 1), lambda d, p: (0, 0)),
            ],
            scratch_shapes=[pltpu.VMEM((count, rows, width // count), BF)],
        ),
        out_shape=[
            jax.ShapeDtypeStruct((count, rows, out_width), BF),
            jax.ShapeDtypeStruct((rows, width), BF),
            jax.ShapeDtypeStruct((rows, 1), F32),
        ],
        compiler_params=pltpu.CompilerParams(vmem_limit_bytes=48 * 2**20),
        cost_estimate=SHORT,
        name="project",
    )(places, x, gain, cos, sin, *parts, *parts)


def out_proj_kernel(place_ref, attn_ref, x_ref, gain_ref, *refs, count):
    parts, (resid_ref, inv_ref, inner_ref) = refs[:count], refs[count:]
    width = x_ref.shape[1]
    tile = 512
    square = None
    for begin in range(0, width, tile):
        cols = slice(begin, begin + tile)
        total = x_ref[:, cols].astype(F32)
        for r in range(count):
            total = total + jnp.dot(attn_ref[place_ref[r]], parts[r][:, cols], preferred_element_type=F32)
        resid_ref[:, cols] = total
        part = jnp.sum(total * total, axis=-1, keepdims=True)
        square = part if square is None else square + part
    inv = lax.rsqrt(square / width + EPSILON)
    inv_ref[...] = inv
    inner_ref[...] = (resid_ref[...] * inv * gain_ref[...]).astype(BF)


def out_proj(places, attn, x, gain, parts):
    count, rows, share = attn.shape
    width = x.shape[1]
    step = rows // 2
    line = pl.BlockSpec((step, width), lambda i, p: (i, 0))
    return pl.pallas_call(
        functools.partial(out_proj_kernel, count=count),
        grid_spec=pltpu.PrefetchScalarGridSpec(
            num_scalar_prefetch=1,
            grid=(rows // step,),
            in_specs=[
                pl.BlockSpec((count, step, share), lambda i, p: (0, i, 0)),
                line,
                pl.BlockSpec((1, width), lambda i, p: (0, 0)),
            ]
            + [pl.BlockSpec((share, width), lambda i, p: (0, 0))] * count,
            out_specs=[line, pl.BlockSpec((step, 1), lambda i, p: (i, 0)), line],
        ),
        out_shape=[
            jax.ShapeDtypeStruct((rows, width), F32),
            jax.ShapeDtypeStruct((rows, 1), F32),
            jax.ShapeDtypeStruct((rows, width), BF),
        ],
        compiler_params=pltpu.CompilerParams(vmem_limit_bytes=56 * 2**20),
        cost_estimate=SHORT,
        name="out_proj",
    )(places, attn, x, gain, *parts)


def resid_back_kernel(place_ref, db_ref, first_ref, passed_ref, resid_ref, inv_ref, gain_ref, dy_ref, *refs, count):
    parts, (d_resid_ref, branch_ref, send_ref) = refs[:count], refs[count:]
    d_inner = db_ref[...].astype(F32) + first_ref[...].astype(F32) + passed_ref[...].astype(F32)
    resid = resid_ref[...]
    inv = inv_ref[...]
    scaled = d_inner * gain_ref[...]
    inner_mean = jnp.mean(scaled * resid, axis=-1, keepdims=True)
    d_resid = dy_ref[...].astype(F32) + inv * scaled - resid * (inv * inv * inv * inner_mean)
    d_resid_ref[...] = d_resid
    branch = d_resid.astype(BF)
    branch_ref[...] = branch
    for r in range(count):
        d_attn = lax.dot_general(branch, parts[r][...], NT, preferred_element_type=F32)
        send_ref[place_ref[r]] = d_attn.astype(BF)


def resid_back(places, db_own, db_first, db_passed, resid, inv, gain, dy, parts):
    rows, width = resid.shape
    count = len(parts)
    share = parts[0].shape[0]
    step = rows // 2
    line = pl.BlockSpec((step, width), lambda i, p: (i, 0))
    return pl.pallas_call(
        functools.partial(resid_back_kernel, count=count),
        grid_spec=pltpu.PrefetchScalarGridSpec(
            num_scalar_prefetch=1,
            grid=(rows // step,),
            in_specs=[line, line, line, line]
            + [pl.BlockSpec((step, 1), lambda i, p: (i, 0)), pl.BlockSpec((1, width), lambda i, p: (0, 0)), line]
            + [pl.BlockSpec((share, width), lambda i, p: (0, 0))] * count,
            out_specs=[line, line, pl.BlockSpec((count, step, share), lambda i, p: (0, i, 0))],
        ),
        out_shape=[
            jax.ShapeDtypeStruct((rows, width), F32),
            jax.ShapeDtypeStruct((rows, width), BF),
            jax.ShapeDtypeStruct((count, rows, share), BF),
        ],
        compiler_params=pltpu.CompilerParams(vmem_limit_bytes=56 * 2**20),
        cost_estimate=SHORT,
        name="resid_back",
    )(places, db_own, db_first, db_passed, resid, inv, gain, dy, *parts)


def in_back_kernel(place_ref, back_ref, x_ref, inv_ref, gain_ref, d_resid_ref, *refs, count):
    parts, (out_ref, mixed, d_scr) = refs[:count], refs[count:]
    devices, _, width = back_ref.shape
    heads = width - 2 * HD
    for d in range(devices):
        mixed[:, d * heads : (d + 1) * heads] = back_ref[d, :, :heads]
    base = devices * heads
    for g in range(KV):
        pair = back_ref[2 * g, :, heads:].astype(F32) + back_ref[2 * g + 1, :, heads:].astype(F32)
        mixed[:, base + 2 * g * HD : base + 2 * (g + 1) * HD] = pair.astype(BF)
    for r in range(count):
        d_scr[place_ref[r]] = lax.dot_general(mixed[...], parts[r][...], NT, preferred_element_type=F32)
    inv = inv_ref[...]
    share = d_scr.shape[2]
    inner = None
    for c in range(count):
        cols = slice(c * share, (c + 1) * share)
        part = jnp.sum(d_scr[c] * gain_ref[:, cols] * x_ref[:, cols].astype(F32), axis=-1, keepdims=True)
        inner = part if inner is None else inner + part
    factor = inv * inv * inv * (inner / (count * share))
    for c in range(count):
        cols = slice(c * share, (c + 1) * share)
        through = inv * (d_scr[c] * gain_ref[:, cols]) - x_ref[:, cols].astype(F32) * factor
        out_ref[:, cols] = (d_resid_ref[:, cols] + through).astype(BF)


def in_back(places, back, x, inv, gain, d_resid, parts):
    rows, width = x.shape
    count = len(parts)
    share, columns = parts[0].shape
    step = rows // 2
    line = pl.BlockSpec((step, width), lambda i, p: (i, 0))
    return pl.pallas_call(
        functools.partial(in_back_kernel, count=count),
        grid_spec=pltpu.PrefetchScalarGridSpec(
            num_scalar_prefetch=1,
            grid=(rows // step,),
            in_specs=[
                pl.BlockSpec((count, step, back.shape[2]), lambda i, p: (0, i, 0)),
                line,
                pl.BlockSpec((step, 1), lambda i, p: (i, 0)),
                pl.BlockSpec((1, width), lambda i, p: (0, 0)),
                line,
            ]
            + [pl.BlockSpec((share, columns), lambda i, p: (0, 0))] * count,
            out_specs=line,
            scratch_shapes=[pltpu.VMEM((step, columns), BF), pltpu.VMEM((count, step, share), F32)],
        ),
        out_shape=jax.ShapeDtypeStruct((rows, width), BF),
        compiler_params=pltpu.CompilerParams(vmem_limit_bytes=56 * 2**20),
        cost_estimate=SHORT,
        name="in_back",
    )(places, back, x, inv, gain, d_resid, *parts)


def grad_wo_kernel(core_ref, keep_ref, give_ref, branch_ref, keep_out, give_out):
    branch = branch_ref[...]
    keep_out[0] = lax.dot_general(keep_ref[0], branch, TN, preferred_element_type=F32).astype(BF)
    give_out[0] = lax.dot_general(give_ref[0], branch, TN, preferred_element_type=F32).astype(BF)


def grad_wo(core, attn, branch):
    devices, rows, share = attn.shape
    width = branch.shape[1]
    out = pl.BlockSpec((1, share, width), lambda c, core: (c, 0, 0))
    return pl.pallas_call(
        grad_wo_kernel,
        grid_spec=pltpu.PrefetchScalarGridSpec(
            num_scalar_prefetch=1,
            grid=(devices // 2,),
            in_specs=[
                pl.BlockSpec((1, rows, share), lambda c, core: (2 * c + core[0], 0, 0)),
                pl.BlockSpec((1, rows, share), lambda c, core: (2 * c + 1 - core[0], 0, 0)),
                pl.BlockSpec((rows, width), lambda c, core: (0, 0)),
            ],
            out_specs=[out, out],
        ),
        out_shape=[jax.ShapeDtypeStruct((devices // 2, share, width), BF)] * 2,
        compiler_params=pltpu.CompilerParams(vmem_limit_bytes=48 * 2**20),
        cost_estimate=SHORT,
        name="grad_wo",
    )(core.reshape(1), attn, attn, branch)


def grad_dn_kernel(core_ref, *refs, count):
    left, right, (keep_out, give_out) = refs[:count], refs[count : 2 * count], refs[2 * count :]
    total = None
    for r in range(count):
        part = lax.dot_general(left[r][...], right[r][...], TN, preferred_element_type=F32)
        total = part if total is None else total + part
    half = total.shape[0] // 2
    total = total.astype(BF)
    low = core_ref[0] == 0
    keep_out[...] = jnp.where(low, total[:half], total[half:])
    give_out[...] = jnp.where(low, total[half:], total[:half])


def grad_dn(core, hid_rows, dy_rows):
    count = len(hid_rows)
    tokens, hidden = hid_rows[0].shape
    width = dy_rows[0].shape[1]
    tile = 512
    out = pl.BlockSpec((hidden // 2, tile), lambda i, core: (0, i))
    return pl.pallas_call(
        functools.partial(grad_dn_kernel, count=count),
        grid_spec=pltpu.PrefetchScalarGridSpec(
            num_scalar_prefetch=1,
            grid=(width // tile,),
            in_specs=[pl.BlockSpec((tokens, hidden), lambda i, core: (0, 0))] * count
            + [pl.BlockSpec((tokens, tile), lambda i, core: (0, i))] * count,
            out_specs=[out, out],
        ),
        out_shape=[jax.ShapeDtypeStruct((hidden // 2, width), BF)] * 2,
        compiler_params=pltpu.CompilerParams(vmem_limit_bytes=56 * 2**20),
        cost_estimate=SHORT,
        name="grad_dn",
    )(core.reshape(1), *hid_rows, *dy_rows)


def attend_kernel(zeros_ref, q_ref, kv_ref, *refs, heads, start, stop):
    o_ref, send_ref, lse_ref, k_scr, v_scr, acc_ref, max_ref = refs[-7:]
    block = pl.program_id(0) + start
    zeros = zeros_ref[0]
    size = q_ref.shape[0]

    @pl.when(block == start)
    def _():
        for part in range(stop):
            rows = slice(part * size, (part + 1) * size)
            both = kv_ref[rows, :].astype(F32)
            lane = lax.broadcasted_iota(jnp.int32, both.shape, 1)
            k_scr[rows, :] = kv_ref[rows, :HD]
            v_scr[rows, :] = jnp.where(lane < HD, pltpu.roll(both, HD, 1), 1.0).astype(BF)

    first_row = block * size
    lowest = jnp.where(first_row >= zeros, zeros // size, 0)
    acc_ref[...] = jnp.zeros_like(acc_ref)
    max_ref[...] = jnp.full_like(max_ref, MASKED)
    q_heads = [q_ref[:, h * HD : (h + 1) * HD] for h in range(heads)]

    def step(index, masked):
        first_key = pl.multiple_of(index * size, size)
        keys = k_scr[pl.ds(first_key, size), :]
        values = v_scr[pl.ds(first_key, size), :]
        if masked:
            row = first_row + lax.broadcasted_iota(jnp.int32, (size, size), 0)
            col = first_key + lax.broadcasted_iota(jnp.int32, (size, size), 1)
            begin = jnp.where(row >= zeros, zeros, 0)
            refused = (col > row) | (col < begin)

        def score(h):
            return lax.dot_general(q_heads[h], keys, NT, preferred_element_type=F32)

        upcoming = score(0)
        for h in range(heads):
            scores = upcoming
            if h + 1 < heads:
                upcoming = score(h + 1)
            if masked:
                scores = jnp.where(refused, MASKED, scores)
            old_max = max_ref[h]
            new_max = jnp.maximum(old_max, jnp.max(scores, axis=-1, keepdims=True))
            weights = jnp.exp2(scores - jnp.tile(new_max, (1, size // 128)))
            shrink = jnp.exp2(old_max - new_max)
            acc_ref[h] = acc_ref[h] * shrink + jnp.dot(weights.astype(BF), values, preferred_element_type=F32)
            max_ref[h] = new_max

    def visit(index, carry):
        first_key = index * size
        mixed = (index == block) | ((first_row + size > zeros) & (first_key < zeros))

        @pl.when(mixed)
        def _():
            step(index, True)

        @pl.when(jnp.logical_not(mixed))
        def _():
            step(index, False)

        return carry

    lax.fori_loop(lowest, block + 1, visit, 0)
    for h in range(heads):
        acc = acc_ref[h]
        total = acc[:, HD : HD + 1]
        out = acc[:, :HD] / total
        o_ref[:, h * HD : (h + 1) * HD] = out
        send_ref[0, :, h * HD : (h + 1) * HD] = out.astype(BF)
        lse = max_ref[h] + jnp.log2(total)
        lse_ref[0, h : h + 1, :] = jnp.transpose(lse)[:1]


def attend(zeros, qkv, start, stop, before=None):
    length, width = qkv.shape
    q_width = width - 2 * HD
    heads = q_width // HD
    size = BLOCK
    blocks = length // size
    before = () if before is None else before
    return pl.pallas_call(
        functools.partial(attend_kernel, heads=heads, start=start, stop=stop),
        grid_spec=pltpu.PrefetchScalarGridSpec(
            num_scalar_prefetch=1,
            grid=(stop - start,),
            in_specs=[
                pl.BlockSpec((size, q_width), lambda i, z: (i + start, 0)),
                pl.BlockSpec((length, 2 * HD), lambda i, z: (0, q_width // (2 * HD))),
            ]
            + [pl.BlockSpec(memory_space=pl.ANY)] * len(before),
            out_specs=[
                pl.BlockSpec((size, q_width), lambda i, z: (i + start, 0)),
                pl.BlockSpec((1, size, q_width), lambda i, z: (i + start, 0, 0)),
                pl.BlockSpec((1, heads, size), lambda i, z: (i + start, 0, 0)),
            ],
            scratch_shapes=[
                pltpu.VMEM((length, HD), BF),
                pltpu.VMEM((length, 2 * HD), BF),
                pltpu.VMEM((heads, size, 2 * HD), F32),
                pltpu.VMEM((heads, size, 128), F32),
            ],
        ),
        out_shape=[
            jax.ShapeDtypeStruct((length, q_width), F32),
            jax.ShapeDtypeStruct((blocks, size, q_width), BF),
            jax.ShapeDtypeStruct((blocks, heads, size), F32),
        ],
        input_output_aliases={3 + i: i for i in range(len(before))},
        compiler_params=pltpu.CompilerParams(vmem_limit_bytes=48 * 2**20),
        cost_estimate=SHORT,
        name="attend",
    )(zeros, qkv, qkv, *before)


def attend_back_kernel(
    zeros_ref, q_ref, kv_ref, do_ref, lse_ref, cos_ref, sin_ref, extra_ref, *refs, heads, start
):
    send_ref, dq_acc, delta_ref, q_scr, do_scr = refs[-5:]
    block = pl.program_id(0) + start
    zeros = zeros_ref[0]
    size = kv_ref.shape[0]
    length = q_ref.shape[0]
    blocks = length // size

    @pl.when(block == start)
    def _():
        if start == 0:
            dq_acc[...] = jnp.zeros_like(dq_acc)
        else:
            dq_acc[...] = refs[0][...]
            delta_ref[...] = extra_ref[...]
        for part in range(start, blocks):
            rows = slice(part * size, (part + 1) * size)
            if start == 0:
                product = jnp.transpose(do_ref[rows, :].astype(F32) * extra_ref[rows, :])
            for h in range(heads):
                cols = slice(h * HD, (h + 1) * HD)
                q_scr[h, rows, :] = q_ref[rows, cols]
                do_scr[h, rows, :] = do_ref[rows, cols]
                if start == 0:
                    delta_ref[part, h : h + 1, :] = jnp.sum(product[cols], axis=0, keepdims=True)

    first_key = block * size
    both = kv_ref[...]
    keys = both[:, :HD]
    values = both[:, HD:]
    keys_t = jnp.transpose(keys.astype(F32)).astype(BF)
    highest = jnp.where(first_key + size <= zeros, jnp.minimum((zeros + size - 1) // size, blocks), blocks)

    def step(index, carry, masked):
        first_row = pl.multiple_of(index * size, size)
        span = pl.ds(first_row, size)
        if masked:
            col = first_key + lax.broadcasted_iota(jnp.int32, (size, size), 0)
            row = first_row + lax.broadcasted_iota(jnp.int32, (size, size), 1)
            begin = jnp.where(row >= zeros, zeros, 0)
            refused = (col > row) | (col < begin)

        def products(h):
            q_rows = q_scr[h, span, :]
            do_rows = do_scr[h, span, :]
            scores = lax.dot_general(keys, q_rows, NT, preferred_element_type=F32)
            d_prob = lax.dot_general(values, do_rows, NT, preferred_element_type=F32)
            return q_rows, do_rows, scores, d_prob

        upcoming = products(0)
        dk_sum, dv_sum = carry
        for h in range(heads):
            q_rows, do_rows, scores, d_prob = upcoming
            if h + 1 < heads:
                upcoming = products(h + 1)
            shifted = scores - lse_ref[index, h : h + 1, :]
            if masked:
                shifted = jnp.where(refused, MASKED, shifted)
            prob = jnp.exp2(shifted)
            d_score = (prob * (d_prob - delta_ref[index, h : h + 1, :])).astype(BF)
            dv_sum = dv_sum + jnp.dot(prob.astype(BF), do_rows, preferred_element_type=F32)
            dk_sum = dk_sum + jnp.dot(d_score, q_rows, preferred_element_type=F32)
            dq_acc[h * HD : (h + 1) * HD, span] += jnp.dot(keys_t, d_score, preferred_element_type=F32)
        return dk_sum, dv_sum

    def visit(index, carry):
        first_row = index * size
        mixed = (index == block) | ((first_row + size > zeros) & (first_key < zeros))
        return lax.cond(
            mixed,
            lambda c: step(index, c, True),
            lambda c: step(index, c, False),
            carry,
        )

    zero = jnp.zeros((size, HD), F32)
    dk_sum, dv_sum = lax.fori_loop(block, highest, visit, (zero, zero))
    q_width = heads * HD
    done = pl.ds(pl.multiple_of(first_key, size), size)
    cos = cos_ref[...]
    sin = sin_ref[...]
    dq = jnp.transpose(dq_acc[:, done]) * HD**-0.5
    dq = dq * jnp.tile(cos, (1, q_width // 128)) - swap_halves(dq) * jnp.tile(sin, (1, q_width // 128))
    send_ref[0, :, :q_width] = dq.astype(BF)
    dkv = jnp.concatenate([dk_sum * (1.0 / LOG2E), dv_sum], axis=1)
    lane = lax.broadcasted_iota(jnp.int32, dkv.shape, 1)
    send_ref[0, :, q_width:] = jnp.where(lane < HD, dkv * cos - swap_halves(dkv) * sin, dkv).astype(BF)


def attend_back(zeros, qkv, d_out, lse, cos, sin, start, stop, out=None, before=None):
    length, width = qkv.shape
    q_width = width - 2 * HD
    heads = q_width // HD
    size = BLOCK
    blocks = length // size
    whole = lambda *shape: pl.BlockSpec(shape, lambda j, z: (0,) * len(shape))
    if before is None:
        operands = (out,)
        specs = [whole(length, q_width)]
        aliases = {}
    else:
        send, d_query, delta = before
        operands = (delta, d_query, send)
        specs = [whole(blocks, heads, size), whole(q_width, length), pl.BlockSpec(memory_space=pl.ANY)]
        aliases = {9: 0}
    return pl.pallas_call(
        functools.partial(attend_back_kernel, heads=heads, start=start),
        grid_spec=pltpu.PrefetchScalarGridSpec(
            num_scalar_prefetch=1,
            grid=(stop - start,),
            in_specs=[
                whole(length, q_width),
                pl.BlockSpec((size, 2 * HD), lambda j, z: (j + start, q_width // (2 * HD))),
                whole(length, q_width),
                whole(blocks, heads, size),
                pl.BlockSpec((size, 128), lambda j, z: (j + start, 0)),
                pl.BlockSpec((size, 128), lambda j, z: (j + start, 0)),
            ]
            + specs,
            out_specs=[
                pl.BlockSpec((1, size, width), lambda j, z: (j + start, 0, 0)),
                whole(q_width, length),
                whole(blocks, heads, size),
            ],
            scratch_shapes=[
                pltpu.VMEM((heads, length, HD), BF),
                pltpu.VMEM((heads, length, HD), BF),
            ],
        ),
        out_shape=[
            jax.ShapeDtypeStruct((blocks, size, width), BF),
            jax.ShapeDtypeStruct((q_width, length), F32),
            jax.ShapeDtypeStruct((blocks, heads, size), F32),
        ],
        input_output_aliases=aliases,
        compiler_params=pltpu.CompilerParams(vmem_limit_bytes=58 * 2**20),
        cost_estimate=SHORT,
        name="attend_back",
    )(zeros, qkv, qkv, d_out, lse, cos, sin, *operands)


def turn_tables(positions):
    cosine, sine = rope_tables(positions, HD)
    return jnp.concatenate([cosine] * 4, axis=1), jnp.concatenate([-sine, sine, -sine, sine], axis=1)


def fast_body(tokens, segment_ids, selected, cotangent, w_qkv, w_out, w_gate_up, w_down, g_attn, g_mlp):
    _, rows, width = tokens.shape
    devices = 2 * CHIPS
    me = lax.axis_index("sp")
    core = me & 1
    planes = lax.axis_size("dp")
    share = width // devices
    kv_width = KV * HD
    first_mask, second_mask = rel_masks(core)
    other = me ^ 1
    chip = me // 2
    place_list = [me, me ^ first_mask, me ^ second_mask, me ^ 6]
    place_list += [other, other ^ second_mask, other ^ first_mask, other ^ 6]
    places = jnp.stack(place_list)
    hidden_chip = 2 * w_down.shape[0]
    quarter = share // planes
    plane = lax.axis_index("dp")
    length = devices * rows
    blocks = length // BLOCK

    count = jnp.sum((segment_ids == 0).astype(F32))
    vectors = jnp.stack([g_attn.astype(F32), g_mlp.astype(F32)] + [jnp.full((share,), count)] * 6)
    paired = [w_qkv[:, :width]]
    for head in range(KV):
        paired.append(w_qkv[:, width + head * HD : width + (head + 1) * HD])
        paired.append(w_qkv[:, width + kv_width + head * HD : width + kv_width + (head + 1) * HD])
    qkv_own = jnp.concatenate(paired, axis=1)
    gu_rows = lax.dynamic_slice_in_dim(w_gate_up, plane * quarter, quarter, 0)
    gu_send = []
    for place in range(CHIPS):
        for begin in (place * hidden_chip, (CHIPS + place) * hidden_chip):
            gu_send.append(gu_rows[:, begin : begin + hidden_chip])
    gu_send = jnp.stack([jnp.concatenate(gu_send[2 * c : 2 * c + 2], axis=1) for c in range(CHIPS)])
    vectors = gather_vectors(vectors, me)
    vectors, qkv_own, gu_send = fence(vectors, qkv_own, gu_send)
    qkv_first = send_first(qkv_own)
    attn_gain = vectors[0:1]
    mlp_gain = vectors[1:2]
    zeros = jnp.sum(vectors[2].reshape(devices, share)[:, 0]).astype(jnp.int32)
    zeros_one = zeros.reshape(1)
    local_pos = me * rows + jnp.arange(rows, dtype=jnp.int32) - segment_ids.reshape(rows) * zeros
    cos, sin = turn_tables(local_pos)
    dy = (cotangent * selected[:, :, None].astype(BF)).reshape(rows, width)
    qkv_own, qkv_first, cos, sin = fence(qkv_own, qkv_first, cos, sin)
    qkv_second = send_second(qkv_own)
    qkv_theirs = [send_sibling(qkv_own), send_sibling(qkv_first)]
    all_places = jnp.arange(length, dtype=jnp.int32)
    cos_all, sin_all = turn_tables(all_places - jnp.where(all_places >= zeros, zeros, 0))
    qkv_first, qkv_second, cos_all, sin_all, *qkv_theirs = fence(qkv_first, qkv_second, cos_all, sin_all, *qkv_theirs)
    qkv_far = send_second(qkv_first)
    qkv_theirs.append(send_sibling(qkv_second))
    qkv_far, dy, *qkv_theirs = fence(qkv_far, dy, *qkv_theirs)
    qkv_theirs.append(send_sibling(qkv_far))
    qkv_parts = [qkv_own, qkv_first, qkv_second, qkv_far] + qkv_theirs
    x_bf = tokens.reshape(rows, width)
    x_bf, w_out, gu_send, *qkv_parts = fence(x_bf, w_out, gu_send, *qkv_parts)
    out_first = send_first(w_out)
    gu_part = lax.all_to_all(gu_send, "sp", 0, 0, axis_index_groups=SAME_CORE, tiled=True)
    qkv_send, normed, inv_one = project(places, x_bf, attn_gain, cos, sin, qkv_parts)
    qkv_send, out_first = fence(qkv_send, out_first)
    gu_mine = lax.all_gather(after(gu_part, qkv_send), "dp", axis=0, tiled=False)
    gu_mine = lax.all_gather(after(gu_part, qkv_send), "dp", axis=0, tiled=False)
    down_theirs = send_sibling(w_down)
    w_dn = jnp.where(
        core == 0, jnp.concatenate([w_down, down_theirs], axis=0), jnp.concatenate([down_theirs, w_down], axis=0)
    )
    qkv_heads = lax.all_to_all(qkv_send, "sp", 0, 0, tiled=True).reshape(length, qkv_send.shape[2])

    cuts = (0, (5 * blocks) // 8, (7 * blocks) // 8, blocks)
    qkv_heads, w_dn, out_first = fence(qkv_heads, w_dn, out_first)
    out_second = send_second(after(w_out, qkv_heads))
    dy_first = send_first(after(dy, qkv_heads))
    fwd = attend(zeros_one, qkv_heads, cuts[0], cuts[1])
    qkv_heads, out_second, dy_first, out_first, dy, *fwd = fence(qkv_heads, out_second, dy_first, out_first, dy, *fwd)
    out_far = send_second(out_first)
    dy_second = send_second(dy)
    fwd = attend(zeros_one, qkv_heads, cuts[1], cuts[2], fwd)
    qkv_heads, out_far, dy_second, dy_first, *fwd = fence(qkv_heads, out_far, dy_second, dy_first, *fwd)
    dy_far = send_second(dy_first)
    gu_theirs = send_sibling(after(gu_mine, fwd[2]))
    out_heads, out_send, lse = attend(zeros_one, qkv_heads, cuts[2], cuts[3], fwd)
    out_parts = [w_out, out_first, out_second, out_far]
    out_parts = out_parts + [send_sibling(part) for part in out_parts]
    out_send, gu_mine, gu_theirs = fence(out_send, gu_mine, gu_theirs)
    attn_tok = lax.all_to_all(out_send, "sp", 0, 0, tiled=True)
    w_gu = join(core, gu_mine, gu_theirs)
    attn_tok, w_gu, dy_far, *out_parts = fence(attn_tok, w_gu, dy_far, *out_parts)
    residual, inv_two, inner = out_proj(places, attn_tok, x_bf, mlp_gain, out_parts)

    b_first = send_first(inner)
    own = ffn(inner, dy, w_gu, w_dn)
    inner, b_first, *own = fence(inner, b_first, *own)
    b_second = send_second(inner)
    first = ffn(b_first, dy_first, w_gu, w_dn)
    b_first, b_second, *first = fence(b_first, b_second, *first)
    b_far = send_second(b_first)
    second = ffn(b_second, dy_second, w_gu, w_dn)
    b_far, db_first, *second = fence(b_far, first[3], *second)
    db_got_first = send_first(db_first)
    far = ffn(b_far, dy_far, w_gu, w_dn)
    db_got_first, db_far, *hid_rows = fence(db_got_first, far[3], own[0], first[0], second[0], far[0])

    db_got_far = send_first(db_far)
    dn_keep, dn_give = grad_dn(core, hid_rows, [dy, dy_first, dy_second, dy_far])
    db_got_far, dn_keep, dn_give = fence(db_got_far, dn_keep, dn_give)
    db_pass = (second[3].astype(F32) + db_got_far.astype(F32)).astype(BF)
    b_own, db_pass, dn_give = fence(inner, db_pass, dn_give)
    db_passed = send_second(db_pass)
    dn_got = send_sibling(dn_give)
    gu_keep, gu_give = grad_gu(
        core,
        [b_own, b_first, b_second, b_far],
        [own[1], first[1], second[1], far[1]],
        [own[2], first[2], second[2], far[2]],
        share,
    )
    db_passed, dn_got, gu_keep, gu_give = fence(db_passed, dn_got, gu_keep, gu_give)
    dn_parts = [part.reshape(planes, dn_keep.shape[0] // planes, width) for part in (dn_keep, dn_got)]
    dn_moves = line_scatter_sends(dn_parts, None, 1, 0)
    db_passed, gu_give, normed, *dn_moves = fence(db_passed, gu_give, normed, *dn_moves)
    a_first = send_first(normed)
    gu_got = send_sibling(gu_give)
    dn_moves = line_scatter_move(dn_moves, 1)
    d_resid, d_branch, d_send = resid_back(
        places, own[3], db_got_first, db_passed, residual, inv_two, mlp_gain, dy, out_parts
    )
    d_send, d_branch, gu_got, *dn_moves = fence(d_send, d_branch, gu_got, *dn_moves)
    gu_sum = (gu_keep.astype(F32) + gu_got.astype(F32)).astype(BF)
    gu_sum = gu_sum.reshape(CHIPS, planes, quarter, 2 * hidden_chip).transpose(1, 0, 2, 3)
    gu_z = lax.psum_scatter(
        gu_sum.reshape(planes * CHIPS * quarter, 2 * hidden_chip), "dp", scatter_dimension=0, tiled=True
    )
    gu_z = gu_z.reshape(CHIPS, quarter, 2 * hidden_chip)
    d_heads = lax.all_to_all(d_send, "sp", 0, 0, tiled=True).reshape(length, share)
    dn_moves = line_scatter_sends(dn_parts, dn_moves, 2, 0)
    dn_moves = line_scatter_move(dn_moves, 2)
    wo_keep, wo_give = grad_wo(core, attn_tok, d_branch)
    d_heads, wo_keep, wo_give, a_first, normed, *dn_moves = fence(d_heads, wo_keep, wo_give, a_first, normed, *dn_moves)

    def back_call(heads, start, stop, **kwargs):
        return attend_back(zeros_one, qkv_heads, heads, lse, cos_all, sin_all, start, stop, **kwargs)

    turns = (0, blocks // 8, blocks // 4, blocks // 2, blocks)
    dn_moves = line_scatter_sends(dn_parts, dn_moves, 3, 0)
    d_heads, wo_give, normed, *dn_moves = fence(d_heads, wo_give, normed, *dn_moves)
    wo_got = send_sibling(wo_give)
    a_second = send_second(normed)
    a_theirs = [send_sibling(normed)]
    dn_moves = line_scatter_move(dn_moves, 3)
    bwd = back_call(d_heads, turns[0], turns[1], out=out_heads)
    d_heads, a_first, a_second, wo_got, *moves = fence(d_heads, a_first, a_second, wo_got, *a_theirs, *bwd)
    a_theirs, bwd = moves[:1], moves[1:]

    a_far = send_second(a_first)
    a_theirs.append(send_sibling(a_first))
    bwd = back_call(d_heads, turns[1], turns[2], before=bwd)
    d_heads, gu_z, a_far, *moves = fence(d_heads, gu_z, a_far, *a_theirs, *dn_moves, *bwd)
    a_theirs, dn_moves, bwd = moves[:2], moves[2:4], moves[4:]

    def wo_part(place):
        return pick(wo_keep, place).astype(F32) + pick(wo_got, place).astype(F32)

    dn_z = line_scatter_end(dn_parts, dn_moves, 0)
    wo_first = wo_part(chip ^ (first_mask // 2)).astype(BF)
    wo_far = wo_part(chip ^ 3).astype(BF)
    d_heads, dn_z, gu_z, a_second, wo_first, wo_far = fence(d_heads, dn_z, gu_z, a_second, wo_first, wo_far)
    dn_all = lax.all_gather(dn_z, "dp", axis=0, tiled=False)
    gu_z = lax.all_to_all(gu_z, "sp", 0, 0, axis_index_groups=SAME_CORE, tiled=True)
    wo_far = send_first(wo_far)
    wo_first = send_first(wo_first)
    a_theirs.append(send_sibling(a_second))
    bwd = back_call(d_heads, turns[2], turns[3], before=bwd)
    d_heads, gu_z, wo_far, wo_first, *moves = fence(d_heads, gu_z, wo_far, wo_first, *a_theirs, *bwd)
    a_theirs, bwd = moves[:3], moves[3:]

    wo_pass = (wo_part(chip ^ (second_mask // 2)) + wo_far.astype(F32)).astype(BF)
    d_heads, gu_z, wo_pass, a_far, y_far = fence(d_heads, gu_z, wo_pass, a_far, far[4])
    gu_all = lax.all_gather(gu_z, "dp", axis=0, tiled=False)
    wo_passed = send_second(wo_pass)
    y_got_far = send_first(y_far)
    a_theirs.append(send_sibling(a_far))
    bwd = back_call(d_heads, turns[3], turns[4], before=bwd)
    dp_heads, wo_passed, y_got_far, y_first, *a_theirs = fence(bwd[0], wo_passed, y_got_far, first[4], *a_theirs)

    back = lax.all_to_all(dp_heads, "sp", 0, 0, tiled=True)
    y_got_first = send_first(y_first)
    grad_wq = grad_qkv(places, [normed, a_first, a_second, a_far] + list(a_theirs), dp_heads)
    wq_parts = [grad_wq.reshape(devices, planes, quarter, dp_heads.shape[2])]
    wo_rows = (wo_part(chip) + wo_first.astype(F32) + wo_passed.astype(F32)).astype(BF)
    wo_parts = [wo_rows.reshape(planes, quarter, width)]
    y_pass = (second[4].astype(F32) + y_got_far.astype(F32)).astype(BF)
    wq_moves = wo_moves = None
    for step in range(1, planes):
        wq_moves = line_scatter_sends(wq_parts, wq_moves, step, 1)
        wo_moves = line_scatter_sends(wo_parts, wo_moves, step, 0)
        moves = fence(*wq_moves, *wo_moves, y_pass)
        wq_moves = line_scatter_move(moves[:2], step)
        wo_moves = line_scatter_move(moves[2:4], step)
        if step == planes - 1:
            y_got_first, y_pass = fence(y_got_first, moves[4])
            y_passed = send_second(y_pass)
        moves = fence(*wq_moves, *wo_moves)
        wq_moves, wo_moves = moves[:2], moves[2:]
    wq_z = line_scatter_end(wq_parts, wq_moves, 1)
    wo_z = line_scatter_end(wo_parts, wo_moves, 0)
    wq_z, wo_z, back = fence(wq_z, wo_z, back)
    wo_steps = [(wo_z, wo_z), line_gather_move((wo_z, wo_z), 1)]
    wq_z = lax.all_to_all(wq_z, "sp", 0, 0, tiled=True)
    grad_tokens = in_back(places, back, x_bf, inv_one, attn_gain, d_resid, qkv_parts).reshape(tokens.shape)
    wq_z, grad_tokens, y_passed, *moves = fence(wq_z, grad_tokens, y_passed, *wo_steps[-1])
    wo_steps[-1] = tuple(moves)
    wq_steps = [(wq_z, wq_z)]
    outs = []
    for step in range(1, planes):
        wq_steps.append(line_gather_move(wq_steps[-1], step))
        if len(wo_steps) < planes:
            wo_steps.append(line_gather_move(wo_steps[-1], len(wo_steps)))
        if step == 1:
            y_sum = own[4].astype(F32) + y_got_first.astype(F32) + y_passed.astype(F32)
            outs.append((residual + y_sum).astype(BF).reshape(tokens.shape))
            outs.append(dn_all.astype(F32).reshape(w_down.shape))
        elif step == 2:
            outs += spread(gu_all, w_gate_up, g_mlp.astype(F32).reshape(share, 1))
        if step == planes - 1:
            outs.append(spread_rows(wo_steps))
        moves = fence(*wq_steps[-1], *wo_steps[-1], *outs)
        wq_steps[-1], wo_steps[-1], outs = tuple(moves[:2]), tuple(moves[2:4]), list(moves[4:])
    output, grad_w_down, grad_w_gate_up, grad_g_mlp, grad_w_out = outs
    grad_w_qkv, grad_g_attn = spread_qkv(wq_steps, w_qkv, g_attn.astype(F32).reshape(share, 1))
    return (
        output,
        grad_tokens,
        grad_w_qkv,
        grad_w_out,
        grad_w_gate_up,
        grad_w_down,
        grad_g_attn.reshape(share),
        grad_g_mlp.reshape(share),
    )


def solution(mesh):
    in_specs = (
        P("dp", "sp", None),
        P("dp", "sp"),
        P("dp", "sp"),
        P("dp", "sp", None),
        P("sp", None),
        P("sp", None),
        P("sp", None),
        P("sp", None),
        P("sp"),
        P("sp"),
    )
    out_specs = (
        P("dp", "sp", None),
        P("dp", "sp", None),
        P("sp", None),
        P("sp", None),
        P("sp", None),
        P("sp", None),
        P("sp"),
        P("sp"),
    )
    body = fast_body if mesh.shape["sp"] == 2 * CHIPS else general_body
    return jax.shard_map(body, mesh=mesh, in_specs=in_specs, out_specs=out_specs, check_vma=False)
```

```python
import functools
import math

import jax
import jax.numpy as jnp
from jax import lax
from jax.experimental import pallas as pl
from jax.experimental.pallas import tpu as pltpu
from jax.sharding import PartitionSpec as P

D = 2048
H = 32
KV = 4
HD = 64
FF = 5632


EPSILON = 1e-05
ROPE_BASE = 10000.0
MASKED = -1e30


def rope_tables(positions, head_size):
    half_dim = head_size // 2
    frequency = ROPE_BASE ** (-(jnp.arange(half_dim, dtype=jnp.float32) * 2.0 / head_size))
    angles = positions.astype(jnp.float32)[:, None] * frequency[None, :]
    return (jnp.cos(angles), jnp.sin(angles))


def rotate(values, cosine, sine_tab, inverse_turn):
    half_dim = values.shape[-1] // 2
    first_half = values[..., :half_dim]
    second = values[..., half_dim:]
    cos_wide = cosine[:, None, :]
    sin_wide = sine_tab[:, None, :]
    if inverse_turn:
        sin_wide = -sin_wide
    return jnp.concatenate(
        [first_half * cos_wide - second * sin_wide, second * cos_wide + first_half * sin_wide],
        axis=-1,
    )


def rms_norm(values, gain_vec):
    inverse = lax.rsqrt(jnp.mean(values * values, axis=-1, keepdims=True) + EPSILON)
    return (values * inverse * gain_vec, inverse)


def norm_back(values, inverse, gain_vec, upstream):
    scaled = upstream * gain_vec
    inner_mean = jnp.mean(scaled * values, axis=-1, keepdims=True)
    through = inverse * scaled - values * inverse**3 * inner_mean
    gain_grad = jnp.sum(upstream * values * inverse, axis=0)
    return (through, gain_grad)


def attention_inputs(flat_in, qkv_full, gain_vec, cosine, sine_tab):
    row_count = flat_in.shape[0]
    group_size = H // KV
    normed, inverse = rms_norm(flat_in, gain_vec)
    normed = normed.astype(jnp.bfloat16)
    projected = jnp.dot(normed, qkv_full, preferred_element_type=jnp.float32)
    queries = rotate(projected[:, :D].reshape(row_count, H, HD), cosine, sine_tab, False)
    key_heads = rotate(
        projected[:, D : D + KV * HD].reshape(row_count, KV, HD), cosine, sine_tab, False
    )
    value_heads = projected[:, D + KV * HD :].reshape(row_count, KV, HD)
    key_wide = jnp.broadcast_to(key_heads[:, :, None], (row_count, KV, group_size, HD)).reshape(
        row_count, D
    )
    value_wide = jnp.broadcast_to(value_heads[:, :, None], (row_count, KV, group_size, HD)).reshape(
        row_count, D
    )
    stacked = jnp.stack([queries.reshape(row_count, D), key_wide, value_wide]).astype(jnp.bfloat16)
    return (normed, inverse, stacked)


def block_mask(seg_full, position, row_begin, finish):
    row_seg = seg_full[:, row_begin:finish]
    col_seg = seg_full[:, :finish]
    same_doc = row_seg[:, :, None] == col_seg[:, None, :]
    causal = position[row_begin:finish, None] >= position[None, :finish]
    return same_doc & causal[None]


def attention_forward(queries, key_heads, value_heads, seg_full, score_scale):
    length = queries.shape[1]
    block_rows = min(512, length)
    position = jnp.arange(length, dtype=jnp.int32)
    outputs = []
    lse_parts = []
    for block_num in range(length // block_rows):
        row_begin = block_num * block_rows
        finish = row_begin + block_rows
        scores = (
            jnp.einsum(
                "sqhd,skhd->shqk",
                queries[:, row_begin:finish],
                key_heads[:, :finish],
                preferred_element_type=jnp.float32,
            )
            * score_scale
        )
        allowed = block_mask(seg_full, position, row_begin, finish)
        scores = jnp.where(allowed[:, None], scores, MASKED)
        row_max = jnp.max(scores, axis=-1, keepdims=True)
        shifted = jnp.exp(scores - row_max)
        row_total = jnp.sum(shifted, axis=-1, keepdims=True)
        softmax_w = (shifted / row_total).astype(jnp.bfloat16)
        outputs.append(
            jnp.einsum(
                "shqk,skhd->sqhd",
                softmax_w,
                value_heads[:, :finish],
                preferred_element_type=jnp.float32,
            )
        )
        lse_parts.append(row_max + jnp.log(row_total))
    return (jnp.concatenate(outputs, axis=1), jnp.concatenate(lse_parts, axis=2))


def attention_backward(queries, key_heads, value_heads, seg_full, log_sums, grad_out, score_scale):
    length = queries.shape[1]
    block_rows = min(512, length)
    position = jnp.arange(length, dtype=jnp.int32)
    grad_query = []
    grad_key = jnp.zeros(key_heads.shape, jnp.float32)
    grad_value = jnp.zeros(value_heads.shape, jnp.float32)
    for block_num in range(length // block_rows):
        row_begin = block_num * block_rows
        finish = row_begin + block_rows
        query_rows = queries[:, row_begin:finish]
        grad_rows = grad_out[:, row_begin:finish]
        key_part = key_heads[:, :finish]
        value_part = value_heads[:, :finish]
        scores = (
            jnp.einsum("sqhd,skhd->shqk", query_rows, key_part, preferred_element_type=jnp.float32)
            * score_scale
        )
        allowed = block_mask(seg_full, position, row_begin, finish)
        softmax_f = jnp.where(
            allowed[:, None], jnp.exp(scores - log_sums[:, :, row_begin:finish]), 0.0
        )
        grad_probs = jnp.einsum(
            "sqhd,skhd->shqk", grad_rows, value_part, preferred_element_type=jnp.float32
        )
        row_delta = jnp.sum(softmax_f * grad_probs, axis=-1, keepdims=True)
        grad_scores = (softmax_f * (grad_probs - row_delta)).astype(jnp.bfloat16)
        grad_query.append(
            jnp.einsum("shqk,skhd->sqhd", grad_scores, key_part, preferred_element_type=jnp.float32)
            * score_scale
        )
        grad_key = grad_key.at[:, :finish].add(
            jnp.einsum(
                "shqk,sqhd->skhd", grad_scores, query_rows, preferred_element_type=jnp.float32
            )
            * score_scale
        )
        grad_value = grad_value.at[:, :finish].add(
            jnp.einsum(
                "shqk,sqhd->skhd",
                softmax_f.astype(jnp.bfloat16),
                grad_rows,
                preferred_element_type=jnp.float32,
            )
        )
    return (jnp.concatenate(grad_query, axis=1), grad_key, grad_value)


def general_body(tokens, segment_ids, selected, cotangent, w_qkv, w_out, w_gate_up, w_down, g_attn, g_mlp):
    streams, local_len, model_dim = tokens.shape
    sp_count = lax.axis_size("sp")
    sp_index = lax.axis_index("sp")
    row_count = streams * local_len
    group_size = H // KV
    kv_width = KV * HD
    score_scale = HD ** (-0.5)
    contract = (((0,), (0,)), ((), ()))
    seg_full = lax.all_gather(segment_ids, "sp", axis=1, tiled=True)
    first_count = jnp.sum((seg_full == 0).astype(jnp.int32), axis=1, keepdims=True)
    local_pos = (
        sp_index * local_len
        + jnp.arange(local_len, dtype=jnp.int32)[None, :]
        - segment_ids * first_count
    )
    cosine, sine_tab = rope_tables(local_pos.reshape(row_count), HD)
    shards = (w_qkv, w_out, w_gate_up, w_down, g_attn, g_mlp)
    gathered = (
        lax.all_gather(shards[0], "sp", axis=0, tiled=True),
        lax.all_gather(shards[1], "sp", axis=0, tiled=True),
        lax.all_gather(shards[2], "sp", axis=0, tiled=True),
        lax.all_gather(shards[3], "sp", axis=0, tiled=True),
        lax.all_gather(shards[4], "sp", axis=0, tiled=True),
        lax.all_gather(shards[5], "sp", axis=0, tiled=True),
    )
    qkv_full, out_full, gate_up_full, down_full, attn_gain, mlp_gain = gathered
    attn_gain = attn_gain.astype(jnp.float32)
    mlp_gain = mlp_gain.astype(jnp.float32)
    flat_in = tokens.reshape(row_count, model_dim).astype(jnp.float32)
    normed, inverse_one, stacked = attention_inputs(flat_in, qkv_full, attn_gain, cosine, sine_tab)
    head_view = lax.all_to_all(
        stacked.reshape(3, streams, local_len, model_dim),
        "sp",
        split_axis=3,
        concat_axis=2,
        tiled=True,
    )
    length = head_view.shape[2]
    heads_here = head_view.shape[3] // HD
    head_shape = (streams, length, heads_here, HD)
    queries = head_view[0].reshape(head_shape)
    key_heads = head_view[1].reshape(head_shape)
    value_heads = head_view[2].reshape(head_shape)
    attn_heads, log_sums = attention_forward(queries, key_heads, value_heads, seg_full, score_scale)
    attn_send = attn_heads.astype(jnp.bfloat16).reshape(streams, length, heads_here * HD)
    attn_tok = lax.all_to_all(attn_send, "sp", split_axis=1, concat_axis=2, tiled=True).reshape(
        row_count, model_dim
    )
    branch = jnp.dot(attn_tok, out_full, preferred_element_type=jnp.float32)
    residual = flat_in + branch
    inner_f, inverse_two = rms_norm(residual, mlp_gain)
    inner_in = inner_f.astype(jnp.bfloat16)
    gate_up = jnp.dot(inner_in, gate_up_full, preferred_element_type=jnp.float32)
    gate_part = gate_up[:, :FF]
    up_part = gate_up[:, FF:]
    sigmoid_g = jax.nn.sigmoid(gate_part)
    silu_gate = gate_part * sigmoid_g
    hidden = (silu_gate * up_part).astype(jnp.bfloat16)
    result = residual + jnp.dot(hidden, down_full, preferred_element_type=jnp.float32)
    output = result.astype(jnp.bfloat16).reshape(streams, local_len, model_dim)
    qkv_back, out_back, gate_up_back, down_back, attn_gain_b, mlp_gain_b = gathered
    attn_gain_b = attn_gain_b.astype(jnp.float32)
    mlp_gain_b = mlp_gain_b.astype(jnp.float32)
    grad_y = (cotangent * selected[:, :, None].astype(jnp.bfloat16)).reshape(row_count, model_dim)
    grad_hidden = jnp.dot(grad_y, down_back.T, preferred_element_type=jnp.float32)
    silu_slope = sigmoid_g * (1.0 + gate_part * (1.0 - sigmoid_g))
    grad_both = jnp.concatenate(
        [grad_hidden * up_part * silu_slope, grad_hidden * silu_gate], axis=1
    ).astype(jnp.bfloat16)
    grad_inner = jnp.dot(grad_both, gate_up_back.T, preferred_element_type=jnp.float32)
    grad_resid, gain_two = norm_back(residual, inverse_two, mlp_gain_b, grad_inner)
    grad_resid = grad_resid + grad_y.astype(jnp.float32)
    grad_branch = grad_resid.astype(jnp.bfloat16)
    grad_attn = jnp.dot(grad_branch, out_back.T, preferred_element_type=jnp.float32).astype(
        jnp.bfloat16
    )
    grad_view = lax.all_to_all(
        grad_attn.reshape(streams, local_len, model_dim),
        "sp",
        split_axis=2,
        concat_axis=1,
        tiled=True,
    )
    grad_view = grad_view.reshape(head_shape)
    grad_q, grad_k, grad_v = attention_backward(
        queries, key_heads, value_heads, seg_full, log_sums, grad_view, score_scale
    )
    back_send = (
        jnp.stack([grad_q, grad_k, grad_v])
        .astype(jnp.bfloat16)
        .reshape(3, streams, length, heads_here * HD)
    )
    returned = lax.all_to_all(back_send, "sp", split_axis=2, concat_axis=3, tiled=True)
    returned = returned.astype(jnp.float32).reshape(3, row_count, H, HD)
    grad_pq = rotate(returned[0], cosine, sine_tab, True).reshape(row_count, model_dim)
    key_summed = jnp.sum(returned[1].reshape(row_count, KV, group_size, HD), axis=2)
    grad_pk = rotate(key_summed, cosine, sine_tab, True).reshape(row_count, kv_width)
    grad_pv = jnp.sum(returned[2].reshape(row_count, KV, group_size, HD), axis=2).reshape(
        row_count, kv_width
    )
    grad_mixed = jnp.concatenate(
        [grad_pq.astype(jnp.bfloat16), grad_pk.astype(jnp.bfloat16), grad_pv.astype(jnp.bfloat16)],
        axis=1,
    )
    grad_normed = jnp.dot(grad_mixed, qkv_back.T, preferred_element_type=jnp.float32)
    grad_in, gain_one = norm_back(flat_in, inverse_one, attn_gain_b, grad_normed)
    grad_in = grad_in + grad_resid
    grad_tokens = grad_in.astype(jnp.bfloat16).reshape(streams, local_len, model_dim)
    gain_totals = lax.psum((gain_one, gain_two), ("dp", "sp"))
    gain_share = model_dim // sp_count
    grad_g_attn = lax.dynamic_slice_in_dim(gain_totals[0], sp_index * gain_share, gain_share, 0)
    grad_g_mlp = lax.dynamic_slice_in_dim(gain_totals[1], sp_index * gain_share, gain_share, 0)
    row_sums = lax.psum_scatter(
        jnp.concatenate(
            [
                lax.dot_general(normed, grad_mixed, contract, preferred_element_type=jnp.float32),
                lax.dot_general(
                    attn_tok, grad_branch, contract, preferred_element_type=jnp.float32
                ),
                lax.dot_general(inner_in, grad_both, contract, preferred_element_type=jnp.float32),
            ],
            axis=1,
        ).astype(jnp.bfloat16),
        "sp",
        scatter_dimension=0,
        tiled=True,
    )
    down_sums = lax.psum_scatter(
        lax.dot_general(hidden, grad_y, contract, preferred_element_type=jnp.float32).astype(
            jnp.bfloat16
        ),
        "sp",
        scatter_dimension=0,
        tiled=True,
    )
    weight_rows, down_rows = (
        lax.psum(row_sums, "dp").astype(jnp.float32),
        lax.psum(down_sums, "dp").astype(jnp.float32),
    )
    qkv_cols = model_dim + 2 * kv_width
    grad_w_qkv = weight_rows[:, :qkv_cols]
    grad_w_out = weight_rows[:, qkv_cols : qkv_cols + model_dim]
    grad_w_gate_up = weight_rows[:, qkv_cols + model_dim :]
    return (
        output,
        grad_tokens,
        grad_w_qkv,
        grad_w_out,
        grad_w_gate_up,
        down_rows,
        grad_g_attn,
        grad_g_mlp,
    )


CHIPS = 4
BLOCK = 512
SHORT = pl.CostEstimate(flops=1, bytes_accessed=1, transcendentals=0)
LOG2E = math.log2(math.e)
BF = jnp.bfloat16
F32 = jnp.float32
NT = (((1,), (1,)), ((), ()))
TN = (((0,), (0,)), ((), ()))


def swap_pairs(even_mask, odd_mask):
    return [(i, i ^ (odd_mask if i & 1 else even_mask)) for i in range(2 * CHIPS)]


FIRST = swap_pairs(2, 4)
SECOND = swap_pairs(4, 2)
SIBLING = swap_pairs(1, 1)
SAME_CORE = [[0, 2, 4, 6], [1, 3, 5, 7]]


def send_first(x):
    return lax.ppermute(x, "sp", FIRST)


def send_second(x):
    return lax.ppermute(x, "sp", SECOND)


def send_sibling(x):
    return lax.ppermute(x, "sp", SIBLING)


def after(value, *others):
    return lax.optimization_barrier((value,) + others)[0]


def gather_chips(own):
    first = send_first(own)
    second = send_second(after(own, first))
    far = send_second(after(first, second))
    return [own, first, second, far]


def rel_masks(core):
    first = jnp.where(core == 0, 2, 4)
    return first, 6 - first


def fence(*values):
    return lax.optimization_barrier(values)


def gather_vectors(own, me):
    for bit in (1, 2, 4):
        got = lax.ppermute(own, "sp", swap_pairs(bit, bit))
        high = (me & bit) != 0
        own = jnp.concatenate([jnp.where(high, got, own), jnp.where(high, own, got)], axis=1)
    return own


def pick(parts, index):
    return lax.dynamic_index_in_dim(parts, index, 0, keepdims=False)


def pick_sum(parts, index, axis):
    return sum(lax.dynamic_index_in_dim(p, index, axis, keepdims=False).astype(F32) for p in parts)


def line_scatter_sends(parts, got, step, axis):
    planes = parts[0].shape[axis]
    z = lax.axis_index("dp")
    ahead = pick_sum(parts, jnp.clip(planes - step + z, 0, planes - 1), axis)
    back = pick_sum(parts, jnp.clip(z - planes + step, 0, planes - 1), axis)
    if got is not None:
        ahead = ahead + got[0].astype(F32)
        back = back + got[1].astype(F32)
    return ahead.astype(BF), back.astype(BF)


def line_scatter_move(sends, step):
    planes = lax.axis_size("dp")
    right = lax.ppermute(sends[0], "dp", [(i, i + 1) for i in range(step)])
    left = lax.ppermute(sends[1], "dp", [(planes - 1 - i, planes - 2 - i) for i in range(step)])
    return right, left


def line_scatter_end(parts, got, axis):
    own = pick_sum(parts, lax.axis_index("dp"), axis)
    return (own + got[0].astype(F32) + got[1].astype(F32)).astype(BF)


def line_gather_move(got, step):
    planes = lax.axis_size("dp")
    right = lax.ppermute(got[0], "dp", [(i, i + 1) for i in range(step - 1, planes - 1)])
    left = lax.ppermute(got[1], "dp", [(i + 1, i) for i in range(planes - step)])
    return right, left


def line_values(refs, planes, z):
    for step in range(planes):
        place = lax.rem(z - step + planes, planes)
        if step == 0:
            yield place, lambda index: refs[0][index]
        else:
            right, left = refs[step], refs[2 * planes - 1 - step]
            yield place, lambda index, right=right, left=left, step=step: jnp.where(z >= step, right[index], left[index])


def spread_kernel(in_ref, w_ref, g_ref, out_ref, gain_ref):
    planes, _, rows, width = in_ref.shape
    out = in_ref[...].reshape(planes * rows, width).astype(F32)
    out_ref[...] = out
    part = jnp.sum(out * w_ref[...].astype(F32), axis=-1, keepdims=True) / g_ref[...]

    @pl.when(pl.program_id(0) == 0)
    def _():
        gain_ref[...] = part

    @pl.when(pl.program_id(0) > 0)
    def _():
        gain_ref[...] += part


def spread(parts, weight, gain):
    planes, chips, rows, both = parts.shape
    half = both // 2
    total = planes * rows
    line = pl.BlockSpec((total, half), lambda i: (0, i))
    column = pl.BlockSpec((total, 1), lambda i: (0, 0))
    return pl.pallas_call(
        spread_kernel,
        grid=(2 * chips,),
        in_specs=[pl.BlockSpec((planes, 1, rows, half), lambda i: (0, i % chips, 0, i // chips)), line, column],
        out_specs=[line, column],
        out_shape=[jax.ShapeDtypeStruct(weight.shape, F32), jax.ShapeDtypeStruct((total, 1), F32)],
        compiler_params=pltpu.CompilerParams(vmem_limit_bytes=32 * 2**20),
        cost_estimate=SHORT,
        name="spread",
    )(parts, weight, gain)


def spread_last_kernel(z_ref, *refs, planes):
    blocks, (w_ref, g_ref, out_ref, gain_ref, wo_ref) = refs[:-5], refs[-5:]
    rows = blocks[0].shape[0]
    devices = 2 * CHIPS
    width = wo_ref.shape[1]
    heads = width // devices
    each = heads + 2 * HD
    for place, load in line_values(blocks, planes, z_ref[0]):
        span = pl.ds(pl.multiple_of(place * rows, rows), rows)
        pairs = []
        for d in range(devices):
            begin = d * each
            cols = slice(begin, begin + heads)
            out_ref[span, d * heads : (d + 1) * heads] = load((slice(None), cols)).astype(F32)
            pairs.append(load((slice(None), slice(begin + heads, begin + each))).astype(F32))
        for g in range(0, KV, 2):
            low = pairs[2 * g] + pairs[2 * g + 1]
            high = pairs[2 * g + 2] + pairs[2 * g + 3]
            lane = lax.broadcasted_iota(jnp.int32, low.shape, 1)
            begin = width + g * HD
            out_ref[span, begin : begin + 2 * HD] = jnp.where(lane < HD, low, pltpu.roll(high, HD, 1))
            begin = width + (KV + g) * HD
            out_ref[span, begin : begin + 2 * HD] = jnp.where(lane < HD, pltpu.roll(low, HD, 1), high)
        wo_ref[span, :] = load((slice(None), slice(devices * each, devices * each + width))).astype(F32)
    gain_ref[...] = jnp.sum(out_ref[...] * w_ref[...].astype(F32), axis=-1, keepdims=True) / g_ref[...]


def spread_last(steps, weight, gain, width):
    planes = len(steps)
    blocks = [steps[0][0]] + [s[0] for s in steps[1:]] + [s[1] for s in steps[1:]]
    vmem = pl.BlockSpec(memory_space=pltpu.VMEM)
    total = weight.shape[0]
    return pl.pallas_call(
        functools.partial(spread_last_kernel, planes=planes),
        in_specs=[pl.BlockSpec(memory_space=pltpu.SMEM)] + [vmem] * (len(blocks) + 2),
        out_specs=[vmem] * 3,
        out_shape=[
            jax.ShapeDtypeStruct(weight.shape, F32),
            jax.ShapeDtypeStruct((total, 1), F32),
            jax.ShapeDtypeStruct((total, width), F32),
        ],
        compiler_params=pltpu.CompilerParams(vmem_limit_bytes=32 * 2**20),
        cost_estimate=SHORT,
        name="spread_last",
    )(lax.axis_index("dp").reshape(1), *blocks, weight, gain)


def join_kernel(core_ref, mine_ref, theirs_ref, out_ref):
    planes, _, rows, both = mine_ref.shape
    block = jnp.where(pl.program_id(1) == 0, mine_ref[...], theirs_ref[...]).reshape(planes * rows, both)
    out_ref[0, 0, 0] = block[:, : both // 2]
    out_ref[1, 0, 0] = block[:, both // 2 :]


def join(core, mine, theirs):
    planes, chips, rows, both = mine.shape
    spec = pl.BlockSpec((planes, 1, rows, both), lambda c, k, core: (0, c, 0, 0))
    out = pl.pallas_call(
        join_kernel,
        grid_spec=pltpu.PrefetchScalarGridSpec(
            num_scalar_prefetch=1,
            grid=(chips, 2),
            in_specs=[spec, spec],
            out_specs=pl.BlockSpec(
                (2, 1, 1, planes * rows, both // 2), lambda c, k, core: (0, c, (core[0] + k) % 2, 0, 0)
            ),
        ),
        out_shape=jax.ShapeDtypeStruct((2, chips, 2, planes * rows, both // 2), BF),
        compiler_params=pltpu.CompilerParams(vmem_limit_bytes=32 * 2**20),
        cost_estimate=SHORT,
        name="join",
    )(core.reshape(1), mine, theirs)
    return out.reshape(2, 2 * chips * planes * rows, both // 2)


def ffn_kernel(b_ref, dy_ref, wg_ref, wu_ref, wd_ref, hid_ref, dg_ref, du_ref, db_ref, y_ref):
    gate = jnp.dot(b_ref[...], wg_ref[...], preferred_element_type=F32)
    up = jnp.dot(b_ref[...], wu_ref[...], preferred_element_type=F32)
    d_hidden = lax.dot_general(dy_ref[...], wd_ref[...], NT, preferred_element_type=F32)
    sigmoid_g = jax.nn.sigmoid(gate)
    silu_gate = gate * sigmoid_g
    hid = (silu_gate * up).astype(BF)
    d_gate = (d_hidden * up * (sigmoid_g * (1.0 + gate * (1.0 - sigmoid_g)))).astype(BF)
    d_up = (d_hidden * silu_gate).astype(BF)
    hid_ref[...] = hid
    dg_ref[...] = d_gate
    du_ref[...] = d_up
    y_ref[...] = jnp.dot(hid, wd_ref[...], preferred_element_type=F32).astype(BF)
    d_in = lax.dot_general(d_gate, wg_ref[...], NT, preferred_element_type=F32)
    db_ref[...] = (d_in + lax.dot_general(d_up, wu_ref[...], NT, preferred_element_type=F32)).astype(BF)


def ffn(b_rows, dy_rows, w_gu, w_dn):
    rows, width = b_rows.shape
    hidden = w_dn.shape[0]
    return pl.pallas_call(
        ffn_kernel,
        grid=(1,),
        in_specs=[
            pl.BlockSpec((rows, width), lambda i: (0, 0)),
            pl.BlockSpec((rows, width), lambda i: (0, 0)),
            pl.BlockSpec((None, width, hidden), lambda i: (0, 0, 0)),
            pl.BlockSpec((None, width, hidden), lambda i: (1, 0, 0)),
            pl.BlockSpec((hidden, width), lambda i: (0, 0)),
        ],
        out_specs=[pl.BlockSpec((rows, hidden), lambda i: (0, 0))] * 3
        + [pl.BlockSpec((rows, width), lambda i: (0, 0))] * 2,
        out_shape=[jax.ShapeDtypeStruct((rows, hidden), BF)] * 3 + [jax.ShapeDtypeStruct((rows, width), BF)] * 2,
        compiler_params=pltpu.CompilerParams(vmem_limit_bytes=58 * 2**20),
        cost_estimate=SHORT,
        name="ffn",
    )(b_rows, dy_rows, w_gu, w_gu, w_dn)


def grad_gu_kernel(core_ref, *refs, count):
    left, right = refs[: 2 * count], refs[2 * count : 4 * count]
    half = right[0].shape[1]
    for side in range(2):
        for kind in range(2):
            total = None
            for r in range(count):
                a_rows = left[side * count + r][...]
                part = lax.dot_general(a_rows, right[kind * count + r][...], TN, preferred_element_type=F32)
                total = part if total is None else total + part
            out_ref = refs[4 * count + side]
            planes, _, rows, _ = out_ref.shape
            out_ref[:, 0, :, kind * half : (kind + 1) * half] = total.astype(BF).reshape(planes, rows, half)


def grad_gu(core, b_rows, dg_rows, du_rows, share, planes):
    count = len(b_rows)
    tokens, width = b_rows[0].shape
    hidden = dg_rows[0].shape[1]
    keep = pl.BlockSpec((tokens, share), lambda c, core: (0, 2 * c + core[0]))
    give = pl.BlockSpec((tokens, share), lambda c, core: (0, 2 * c + 1 - core[0]))
    whole = pl.BlockSpec((tokens, hidden), lambda c, core: (0, 0))
    rows = share // planes
    out = pl.BlockSpec((planes, 1, rows, 2 * hidden), lambda c, core: (0, c, 0, 0))
    return pl.pallas_call(
        functools.partial(grad_gu_kernel, count=count),
        grid_spec=pltpu.PrefetchScalarGridSpec(
            num_scalar_prefetch=1,
            grid=(width // (2 * share),),
            in_specs=[keep] * count + [give] * count + [whole] * (2 * count),
            out_specs=[out, out],
        ),
        out_shape=[jax.ShapeDtypeStruct((planes, width // (2 * share), rows, 2 * hidden), BF)] * 2,
        compiler_params=pltpu.CompilerParams(vmem_limit_bytes=58 * 2**20),
        cost_estimate=SHORT,
        name="grad_gu",
    )(core.reshape(1), *b_rows, *b_rows, *dg_rows, *du_rows)


def grad_qkv_kernel(place_ref, *refs, count):
    dp_ref, out_ref = refs[-2:]
    total = None
    for r in range(count):
        part = lax.dot_general(refs[r][...], dp_ref[place_ref[r]], TN, preferred_element_type=F32)
        total = part if total is None else total + part
    planes, rows, wide = out_ref.shape
    columns = total.shape[1]
    for k in range(wide // columns):
        block = total[k * planes * rows : (k + 1) * planes * rows].astype(BF)
        out_ref[:, :, k * columns : (k + 1) * columns] = block.reshape(planes, rows, columns)


def grad_qkv(places, a_rows, dp_heads, planes):
    count = len(a_rows)
    tokens, width = a_rows[0].shape
    columns = dp_heads.shape[2]
    share = width // count
    depth = 2 * share
    return pl.pallas_call(
        functools.partial(grad_qkv_kernel, count=count),
        grid_spec=pltpu.PrefetchScalarGridSpec(
            num_scalar_prefetch=1,
            grid=(width // depth,),
            in_specs=[pl.BlockSpec((tokens, depth), lambda i, p: (0, i))] * count
            + [pl.BlockSpec(dp_heads.shape, lambda i, p: (0, 0, 0))],
            out_specs=pl.BlockSpec((planes, share // planes, 2 * columns), lambda i, p: (0, 0, i)),
        ),
        out_shape=jax.ShapeDtypeStruct((planes, share // planes, count * columns), BF),
        compiler_params=pltpu.CompilerParams(vmem_limit_bytes=48 * 2**20),
        cost_estimate=SHORT,
        name="grad_qkv",
    )(places, *a_rows, dp_heads)


def swap_halves(values):
    width = values.shape[-1]
    lane = lax.broadcasted_iota(jnp.int32, values.shape, 1)
    ahead = pltpu.roll(values, width - HD // 2, 1)
    behind = pltpu.roll(values, HD // 2, 1)
    return jnp.where(lane % HD < HD // 2, ahead, behind)


def project_kernel(place_ref, x_ref, gain_ref, cos_ref, sin_ref, *refs, count):
    wq_refs, wkv_refs = refs[:count], refs[count : 2 * count]
    send_ref, normed_ref, inv_ref, normed_scr = refs[2 * count :]
    share = normed_scr.shape[2]

    @pl.when(pl.program_id(0) == 0)
    def _():
        x = x_ref[...].astype(F32)
        inv = lax.rsqrt(jnp.mean(x * x, axis=-1, keepdims=True) + EPSILON)
        normed = (x * inv * gain_ref[...]).astype(BF)
        normed_ref[...] = normed
        inv_ref[...] = inv
        for part in range(count):
            normed_scr[part] = normed[:, part * share : (part + 1) * share]

    pq = pkv = None
    for r in range(count):
        a_rows = normed_scr[place_ref[r]]
        q_part = jnp.dot(a_rows, wq_refs[r][...], preferred_element_type=F32)
        kv_part = jnp.dot(a_rows, wkv_refs[r][...], preferred_element_type=F32)
        pq = q_part if pq is None else pq + q_part
        pkv = kv_part if pkv is None else pkv + kv_part
    cos = cos_ref[...]
    sin = sin_ref[...]
    heads = pq.shape[1]
    q_scale = LOG2E * HD**-0.5
    turned = pq * jnp.tile(cos, (1, heads // 128)) + swap_halves(pq) * jnp.tile(sin, (1, heads // 128))
    send_ref[0, :, :heads] = (turned * q_scale).astype(BF)
    lane = lax.broadcasted_iota(jnp.int32, pkv.shape, 1)
    turned_kv = jnp.where(lane < HD, pkv * cos + swap_halves(pkv) * sin, pkv)
    send_ref[0, :, heads:] = turned_kv.astype(BF)


def project(places, x, gain, cos, sin, parts):
    rows, width = x.shape
    count = len(parts)
    heads = width // count
    out_width = heads + 2 * HD
    depth = parts[0].shape[0]
    first_kv = width // (2 * HD)
    return pl.pallas_call(
        functools.partial(project_kernel, count=count),
        grid_spec=pltpu.PrefetchScalarGridSpec(
            num_scalar_prefetch=1,
            grid=(count,),
            in_specs=[
                pl.BlockSpec((rows, width), lambda d, p: (0, 0)),
                pl.BlockSpec((1, width), lambda d, p: (0, 0)),
                pl.BlockSpec((rows, 128), lambda d, p: (0, 0)),
                pl.BlockSpec((rows, 128), lambda d, p: (0, 0)),
            ]
            + [pl.BlockSpec((depth, heads), lambda d, p: (0, d))] * count
            + [pl.BlockSpec((depth, 2 * HD), lambda d, p: (0, first_kv + d // 2))] * count,
            out_specs=[
                pl.BlockSpec((1, rows, out_width), lambda d, p: (d, 0, 0)),
                pl.BlockSpec((rows, width), lambda d, p: (0, 0)),
                pl.BlockSpec((rows, 1), lambda d, p: (0, 0)),
            ],
            scratch_shapes=[pltpu.VMEM((count, rows, width // count), BF)],
        ),
        out_shape=[
            jax.ShapeDtypeStruct((count, rows, out_width), BF),
            jax.ShapeDtypeStruct((rows, width), BF),
            jax.ShapeDtypeStruct((rows, 1), F32),
        ],
        compiler_params=pltpu.CompilerParams(vmem_limit_bytes=48 * 2**20),
        cost_estimate=SHORT,
        name="project",
    )(places, x, gain, cos, sin, *parts, *parts)


def out_proj_kernel(place_ref, attn_ref, x_ref, gain_ref, *refs, count):
    parts, (resid_ref, inv_ref, inner_ref) = refs[:count], refs[count:]
    width = x_ref.shape[1]
    tile = 512
    square = None
    for begin in range(0, width, tile):
        cols = slice(begin, begin + tile)
        total = x_ref[:, cols].astype(F32)
        for r in range(count):
            total = total + jnp.dot(attn_ref[place_ref[r]], parts[r][:, cols], preferred_element_type=F32)
        resid_ref[:, cols] = total
        part = jnp.sum(total * total, axis=-1, keepdims=True)
        square = part if square is None else square + part
    inv = lax.rsqrt(square / width + EPSILON)
    inv_ref[...] = inv
    inner_ref[...] = (resid_ref[...] * inv * gain_ref[...]).astype(BF)


def out_proj(places, attn, x, gain, parts):
    count, rows, share = attn.shape
    width = x.shape[1]
    step = rows // 2
    line = pl.BlockSpec((step, width), lambda i, p: (i, 0))
    return pl.pallas_call(
        functools.partial(out_proj_kernel, count=count),
        grid_spec=pltpu.PrefetchScalarGridSpec(
            num_scalar_prefetch=1,
            grid=(rows // step,),
            in_specs=[
                pl.BlockSpec((count, step, share), lambda i, p: (0, i, 0)),
                line,
                pl.BlockSpec((1, width), lambda i, p: (0, 0)),
            ]
            + [pl.BlockSpec((share, width), lambda i, p: (0, 0))] * count,
            out_specs=[line, pl.BlockSpec((step, 1), lambda i, p: (i, 0)), line],
        ),
        out_shape=[
            jax.ShapeDtypeStruct((rows, width), F32),
            jax.ShapeDtypeStruct((rows, 1), F32),
            jax.ShapeDtypeStruct((rows, width), BF),
        ],
        compiler_params=pltpu.CompilerParams(vmem_limit_bytes=56 * 2**20),
        cost_estimate=SHORT,
        name="out_proj",
    )(places, attn, x, gain, *parts)


def resid_back_kernel(place_ref, db_ref, first_ref, passed_ref, resid_ref, inv_ref, gain_ref, dy_ref, *refs, count):
    parts, (d_resid_ref, branch_ref, send_ref) = refs[:count], refs[count:]
    d_inner = db_ref[...].astype(F32) + first_ref[...].astype(F32) + passed_ref[...].astype(F32)
    resid = resid_ref[...]
    inv = inv_ref[...]
    scaled = d_inner * gain_ref[...]
    inner_mean = jnp.mean(scaled * resid, axis=-1, keepdims=True)
    d_resid = dy_ref[...].astype(F32) + inv * scaled - resid * (inv * inv * inv * inner_mean)
    d_resid_ref[...] = d_resid
    branch = d_resid.astype(BF)
    branch_ref[...] = branch
    for r in range(count):
        d_attn = lax.dot_general(branch, parts[r][...], NT, preferred_element_type=F32)
        send_ref[place_ref[r]] = d_attn.astype(BF)


def resid_back(places, db_own, db_first, db_passed, resid, inv, gain, dy, parts):
    rows, width = resid.shape
    count = len(parts)
    share = parts[0].shape[0]
    step = rows // 2
    line = pl.BlockSpec((step, width), lambda i, p: (i, 0))
    return pl.pallas_call(
        functools.partial(resid_back_kernel, count=count),
        grid_spec=pltpu.PrefetchScalarGridSpec(
            num_scalar_prefetch=1,
            grid=(rows // step,),
            in_specs=[line, line, line, line]
            + [pl.BlockSpec((step, 1), lambda i, p: (i, 0)), pl.BlockSpec((1, width), lambda i, p: (0, 0)), line]
            + [pl.BlockSpec((share, width), lambda i, p: (0, 0))] * count,
            out_specs=[line, line, pl.BlockSpec((count, step, share), lambda i, p: (0, i, 0))],
        ),
        out_shape=[
            jax.ShapeDtypeStruct((rows, width), F32),
            jax.ShapeDtypeStruct((rows, width), BF),
            jax.ShapeDtypeStruct((count, rows, share), BF),
        ],
        compiler_params=pltpu.CompilerParams(vmem_limit_bytes=56 * 2**20),
        cost_estimate=SHORT,
        name="resid_back",
    )(places, db_own, db_first, db_passed, resid, inv, gain, dy, *parts)


def in_back_kernel(place_ref, back_ref, x_ref, inv_ref, gain_ref, d_resid_ref, *refs, count):
    parts, (out_ref, mixed, d_scr) = refs[:count], refs[count:]
    devices, _, width = back_ref.shape
    heads = width - 2 * HD
    for d in range(devices):
        mixed[:, d * heads : (d + 1) * heads] = back_ref[d, :, :heads]
    base = devices * heads
    for g in range(KV):
        pair = back_ref[2 * g, :, heads:].astype(F32) + back_ref[2 * g + 1, :, heads:].astype(F32)
        mixed[:, base + 2 * g * HD : base + 2 * (g + 1) * HD] = pair.astype(BF)
    for r in range(count):
        d_scr[place_ref[r]] = lax.dot_general(mixed[...], parts[r][...], NT, preferred_element_type=F32)
    inv = inv_ref[...]
    share = d_scr.shape[2]
    inner = None
    for c in range(count):
        cols = slice(c * share, (c + 1) * share)
        part = jnp.sum(d_scr[c] * gain_ref[:, cols] * x_ref[:, cols].astype(F32), axis=-1, keepdims=True)
        inner = part if inner is None else inner + part
    factor = inv * inv * inv * (inner / (count * share))
    for c in range(count):
        cols = slice(c * share, (c + 1) * share)
        through = inv * (d_scr[c] * gain_ref[:, cols]) - x_ref[:, cols].astype(F32) * factor
        out_ref[:, cols] = (d_resid_ref[:, cols] + through).astype(BF)


def in_back(places, back, x, inv, gain, d_resid, parts):
    rows, width = x.shape
    count = len(parts)
    share, columns = parts[0].shape
    step = rows // 2
    line = pl.BlockSpec((step, width), lambda i, p: (i, 0))
    return pl.pallas_call(
        functools.partial(in_back_kernel, count=count),
        grid_spec=pltpu.PrefetchScalarGridSpec(
            num_scalar_prefetch=1,
            grid=(rows // step,),
            in_specs=[
                pl.BlockSpec((count, step, back.shape[2]), lambda i, p: (0, i, 0)),
                line,
                pl.BlockSpec((step, 1), lambda i, p: (i, 0)),
                pl.BlockSpec((1, width), lambda i, p: (0, 0)),
                line,
            ]
            + [pl.BlockSpec((share, columns), lambda i, p: (0, 0))] * count,
            out_specs=line,
            scratch_shapes=[pltpu.VMEM((step, columns), BF), pltpu.VMEM((count, step, share), F32)],
        ),
        out_shape=jax.ShapeDtypeStruct((rows, width), BF),
        compiler_params=pltpu.CompilerParams(vmem_limit_bytes=56 * 2**20),
        cost_estimate=SHORT,
        name="in_back",
    )(places, back, x, inv, gain, d_resid, *parts)


def grad_wo_kernel(core_ref, keep_ref, give_ref, branch_ref, keep_out, give_out):
    branch = branch_ref[...]
    keep_out[0] = lax.dot_general(keep_ref[0], branch, TN, preferred_element_type=F32).astype(BF)
    give_out[0] = lax.dot_general(give_ref[0], branch, TN, preferred_element_type=F32).astype(BF)


def grad_wo(core, attn, branch):
    devices, rows, share = attn.shape
    width = branch.shape[1]
    out = pl.BlockSpec((1, share, width), lambda c, core: (c, 0, 0))
    return pl.pallas_call(
        grad_wo_kernel,
        grid_spec=pltpu.PrefetchScalarGridSpec(
            num_scalar_prefetch=1,
            grid=(devices // 2,),
            in_specs=[
                pl.BlockSpec((1, rows, share), lambda c, core: (2 * c + core[0], 0, 0)),
                pl.BlockSpec((1, rows, share), lambda c, core: (2 * c + 1 - core[0], 0, 0)),
                pl.BlockSpec((rows, width), lambda c, core: (0, 0)),
            ],
            out_specs=[out, out],
        ),
        out_shape=[jax.ShapeDtypeStruct((devices // 2, share, width), BF)] * 2,
        compiler_params=pltpu.CompilerParams(vmem_limit_bytes=48 * 2**20),
        cost_estimate=SHORT,
        name="grad_wo",
    )(core.reshape(1), attn, attn, branch)


def grad_dn_kernel(core_ref, *refs, count):
    left, right, (keep_out, give_out) = refs[:count], refs[count : 2 * count], refs[2 * count :]
    total = None
    for r in range(count):
        part = lax.dot_general(left[r][...], right[r][...], TN, preferred_element_type=F32)
        total = part if total is None else total + part
    half = total.shape[0] // 2
    total = total.astype(BF)
    low = core_ref[0] == 0
    keep_out[...] = jnp.where(low, total[:half], total[half:])
    give_out[...] = jnp.where(low, total[half:], total[:half])


def grad_dn(core, hid_rows, dy_rows):
    count = len(hid_rows)
    tokens, hidden = hid_rows[0].shape
    width = dy_rows[0].shape[1]
    tile = 512
    out = pl.BlockSpec((hidden // 2, tile), lambda i, core: (0, i))
    return pl.pallas_call(
        functools.partial(grad_dn_kernel, count=count),
        grid_spec=pltpu.PrefetchScalarGridSpec(
            num_scalar_prefetch=1,
            grid=(width // tile,),
            in_specs=[pl.BlockSpec((tokens, hidden), lambda i, core: (0, 0))] * count
            + [pl.BlockSpec((tokens, tile), lambda i, core: (0, i))] * count,
            out_specs=[out, out],
        ),
        out_shape=[jax.ShapeDtypeStruct((hidden // 2, width), BF)] * 2,
        compiler_params=pltpu.CompilerParams(vmem_limit_bytes=56 * 2**20),
        cost_estimate=SHORT,
        name="grad_dn",
    )(core.reshape(1), *hid_rows, *dy_rows)


def attend_kernel(zeros_ref, q_ref, kv_ref, *refs, heads, start, stop):
    o_ref, send_ref, lse_ref, k_scr, v_scr, acc_ref, max_ref = refs[-7:]
    block = pl.program_id(0) + start
    zeros = zeros_ref[0]
    size = q_ref.shape[0]

    @pl.when(block == start)
    def _():
        for part in range(stop):
            rows = slice(part * size, (part + 1) * size)
            both = kv_ref[rows, :].astype(F32)
            lane = lax.broadcasted_iota(jnp.int32, both.shape, 1)
            k_scr[rows, :] = kv_ref[rows, :HD]
            v_scr[rows, :] = jnp.where(lane < HD, pltpu.roll(both, HD, 1), 1.0).astype(BF)

    first_row = block * size
    lowest = jnp.where(first_row >= zeros, zeros // size, 0)
    acc_ref[...] = jnp.zeros_like(acc_ref)
    max_ref[...] = jnp.full_like(max_ref, MASKED)
    q_heads = [q_ref[:, h * HD : (h + 1) * HD] for h in range(heads)]

    def step(index, masked):
        first_key = pl.multiple_of(index * size, size)
        keys = k_scr[pl.ds(first_key, size), :]
        values = v_scr[pl.ds(first_key, size), :]
        if masked:
            row = first_row + lax.broadcasted_iota(jnp.int32, (size, size), 0)
            col = first_key + lax.broadcasted_iota(jnp.int32, (size, size), 1)
            begin = jnp.where(row >= zeros, zeros, 0)
            refused = (col > row) | (col < begin)

        def score(h):
            return lax.dot_general(q_heads[h], keys, NT, preferred_element_type=F32)

        upcoming = score(0)
        for h in range(heads):
            scores = upcoming
            if h + 1 < heads:
                upcoming = score(h + 1)
            if masked:
                scores = jnp.where(refused, MASKED, scores)
            old_max = max_ref[h]
            new_max = jnp.maximum(old_max, jnp.max(scores, axis=-1, keepdims=True))
            weights = jnp.exp2(scores - jnp.tile(new_max, (1, size // 128)))
            shrink = jnp.exp2(old_max - new_max)
            acc_ref[h] = acc_ref[h] * shrink + jnp.dot(weights.astype(BF), values, preferred_element_type=F32)
            max_ref[h] = new_max

    def visit(index, carry):
        first_key = index * size
        mixed = (index == block) | ((first_row + size > zeros) & (first_key < zeros))

        @pl.when(mixed)
        def _():
            step(index, True)

        @pl.when(jnp.logical_not(mixed))
        def _():
            step(index, False)

        return carry

    lax.fori_loop(lowest, block + 1, visit, 0)
    for h in range(heads):
        acc = acc_ref[h]
        total = acc[:, HD : HD + 1]
        out = acc[:, :HD] / total
        o_ref[:, h * HD : (h + 1) * HD] = out
        send_ref[0, :, h * HD : (h + 1) * HD] = out.astype(BF)
        lse = max_ref[h] + jnp.log2(total)
        lse_ref[0, h : h + 1, :] = jnp.transpose(lse)[:1]


def attend(zeros, qkv, start, stop, before=None):
    length, width = qkv.shape
    q_width = width - 2 * HD
    heads = q_width // HD
    size = BLOCK
    blocks = length // size
    before = () if before is None else before
    return pl.pallas_call(
        functools.partial(attend_kernel, heads=heads, start=start, stop=stop),
        grid_spec=pltpu.PrefetchScalarGridSpec(
            num_scalar_prefetch=1,
            grid=(stop - start,),
            in_specs=[
                pl.BlockSpec((size, q_width), lambda i, z: (i + start, 0)),
                pl.BlockSpec((length, 2 * HD), lambda i, z: (0, q_width // (2 * HD))),
            ]
            + [pl.BlockSpec(memory_space=pl.ANY)] * len(before),
            out_specs=[
                pl.BlockSpec((size, q_width), lambda i, z: (i + start, 0)),
                pl.BlockSpec((1, size, q_width), lambda i, z: (i + start, 0, 0)),
                pl.BlockSpec((1, heads, size), lambda i, z: (i + start, 0, 0)),
            ],
            scratch_shapes=[
                pltpu.VMEM((length, HD), BF),
                pltpu.VMEM((length, 2 * HD), BF),
                pltpu.VMEM((heads, size, 2 * HD), F32),
                pltpu.VMEM((heads, size, 128), F32),
            ],
        ),
        out_shape=[
            jax.ShapeDtypeStruct((length, q_width), F32),
            jax.ShapeDtypeStruct((blocks, size, q_width), BF),
            jax.ShapeDtypeStruct((blocks, heads, size), F32),
        ],
        input_output_aliases={3 + i: i for i in range(len(before))},
        compiler_params=pltpu.CompilerParams(vmem_limit_bytes=48 * 2**20),
        cost_estimate=SHORT,
        name="attend",
    )(zeros, qkv, qkv, *before)


def attend_back_kernel(
    zeros_ref, q_ref, kv_ref, do_ref, lse_ref, cos_ref, sin_ref, extra_ref, *refs, heads, start
):
    send_ref, dq_acc, delta_ref, q_scr, do_scr = refs[-5:]
    block = pl.program_id(0) + start
    zeros = zeros_ref[0]
    size = kv_ref.shape[0]
    length = q_ref.shape[0]
    blocks = length // size

    @pl.when(block == start)
    def _():
        if start == 0:
            dq_acc[...] = jnp.zeros_like(dq_acc)
        else:
            dq_acc[...] = refs[0][...]
            delta_ref[...] = extra_ref[...]
        for part in range(start, blocks):
            rows = slice(part * size, (part + 1) * size)
            if start == 0:
                product = jnp.transpose(do_ref[rows, :].astype(F32) * extra_ref[rows, :])
            for h in range(heads):
                cols = slice(h * HD, (h + 1) * HD)
                q_scr[h, rows, :] = q_ref[rows, cols]
                do_scr[h, rows, :] = do_ref[rows, cols]
                if start == 0:
                    delta_ref[part, h : h + 1, :] = jnp.sum(product[cols], axis=0, keepdims=True)

    first_key = block * size
    both = kv_ref[...]
    keys = both[:, :HD]
    values = both[:, HD:]
    keys_t = jnp.transpose(keys.astype(F32)).astype(BF)
    highest = jnp.where(first_key + size <= zeros, jnp.minimum((zeros + size - 1) // size, blocks), blocks)

    def step(index, carry, masked):
        first_row = pl.multiple_of(index * size, size)
        span = pl.ds(first_row, size)
        if masked:
            col = first_key + lax.broadcasted_iota(jnp.int32, (size, size), 0)
            row = first_row + lax.broadcasted_iota(jnp.int32, (size, size), 1)
            begin = jnp.where(row >= zeros, zeros, 0)
            refused = (col > row) | (col < begin)

        def products(h):
            q_rows = q_scr[h, span, :]
            do_rows = do_scr[h, span, :]
            scores = lax.dot_general(keys, q_rows, NT, preferred_element_type=F32)
            d_prob = lax.dot_general(values, do_rows, NT, preferred_element_type=F32)
            return q_rows, do_rows, scores, d_prob

        upcoming = products(0)
        dk_sum, dv_sum = carry
        for h in range(heads):
            q_rows, do_rows, scores, d_prob = upcoming
            if h + 1 < heads:
                upcoming = products(h + 1)
            shifted = scores - lse_ref[index, h : h + 1, :]
            if masked:
                shifted = jnp.where(refused, MASKED, shifted)
            prob = jnp.exp2(shifted)
            d_score = (prob * (d_prob - delta_ref[index, h : h + 1, :])).astype(BF)
            dv_sum = dv_sum + jnp.dot(prob.astype(BF), do_rows, preferred_element_type=F32)
            dk_sum = dk_sum + jnp.dot(d_score, q_rows, preferred_element_type=F32)
            dq_acc[h * HD : (h + 1) * HD, span] += jnp.dot(keys_t, d_score, preferred_element_type=F32)
        return dk_sum, dv_sum

    def visit(index, carry):
        first_row = index * size
        mixed = (index == block) | ((first_row + size > zeros) & (first_key < zeros))
        return lax.cond(
            mixed,
            lambda c: step(index, c, True),
            lambda c: step(index, c, False),
            carry,
        )

    zero = jnp.zeros((size, HD), F32)
    dk_sum, dv_sum = lax.fori_loop(block, highest, visit, (zero, zero))
    q_width = heads * HD
    done = pl.ds(pl.multiple_of(first_key, size), size)
    cos = cos_ref[...]
    sin = sin_ref[...]
    dq = jnp.transpose(dq_acc[:, done]) * HD**-0.5
    dq = dq * jnp.tile(cos, (1, q_width // 128)) - swap_halves(dq) * jnp.tile(sin, (1, q_width // 128))
    send_ref[0, :, :q_width] = dq.astype(BF)
    dkv = jnp.concatenate([dk_sum * (1.0 / LOG2E), dv_sum], axis=1)
    lane = lax.broadcasted_iota(jnp.int32, dkv.shape, 1)
    send_ref[0, :, q_width:] = jnp.where(lane < HD, dkv * cos - swap_halves(dkv) * sin, dkv).astype(BF)


def attend_back(zeros, qkv, d_out, lse, cos, sin, start, stop, out=None, before=None):
    length, width = qkv.shape
    q_width = width - 2 * HD
    heads = q_width // HD
    size = BLOCK
    blocks = length // size
    whole = lambda *shape: pl.BlockSpec(shape, lambda j, z: (0,) * len(shape))
    if before is None:
        operands = (out,)
        specs = [whole(length, q_width)]
        aliases = {}
    else:
        send, d_query, delta = before
        operands = (delta, d_query, send)
        specs = [whole(blocks, heads, size), whole(q_width, length), pl.BlockSpec(memory_space=pl.ANY)]
        aliases = {9: 0}
    return pl.pallas_call(
        functools.partial(attend_back_kernel, heads=heads, start=start),
        grid_spec=pltpu.PrefetchScalarGridSpec(
            num_scalar_prefetch=1,
            grid=(stop - start,),
            in_specs=[
                whole(length, q_width),
                pl.BlockSpec((size, 2 * HD), lambda j, z: (j + start, q_width // (2 * HD))),
                whole(length, q_width),
                whole(blocks, heads, size),
                pl.BlockSpec((size, 128), lambda j, z: (j + start, 0)),
                pl.BlockSpec((size, 128), lambda j, z: (j + start, 0)),
            ]
            + specs,
            out_specs=[
                pl.BlockSpec((1, size, width), lambda j, z: (j + start, 0, 0)),
                whole(q_width, length),
                whole(blocks, heads, size),
            ],
            scratch_shapes=[
                pltpu.VMEM((heads, length, HD), BF),
                pltpu.VMEM((heads, length, HD), BF),
            ],
        ),
        out_shape=[
            jax.ShapeDtypeStruct((blocks, size, width), BF),
            jax.ShapeDtypeStruct((q_width, length), F32),
            jax.ShapeDtypeStruct((blocks, heads, size), F32),
        ],
        input_output_aliases=aliases,
        compiler_params=pltpu.CompilerParams(vmem_limit_bytes=58 * 2**20),
        cost_estimate=SHORT,
        name="attend_back",
    )(zeros, qkv, qkv, d_out, lse, cos, sin, *operands)


def turn_tables(positions):
    cosine, sine = rope_tables(positions, HD)
    return jnp.concatenate([cosine] * 4, axis=1), jnp.concatenate([-sine, sine, -sine, sine], axis=1)


def fast_body(tokens, segment_ids, selected, cotangent, w_qkv, w_out, w_gate_up, w_down, g_attn, g_mlp):
    _, rows, width = tokens.shape
    devices = 2 * CHIPS
    me = lax.axis_index("sp")
    core = me & 1
    planes = lax.axis_size("dp")
    share = width // devices
    kv_width = KV * HD
    first_mask, second_mask = rel_masks(core)
    other = me ^ 1
    chip = me // 2
    place_list = [me, me ^ first_mask, me ^ second_mask, me ^ 6]
    place_list += [other, other ^ second_mask, other ^ first_mask, other ^ 6]
    places = jnp.stack(place_list)
    hidden_chip = 2 * w_down.shape[0]
    quarter = share // planes
    plane = lax.axis_index("dp")
    length = devices * rows
    blocks = length // BLOCK

    count = jnp.sum((segment_ids == 0).astype(F32))
    vectors = jnp.stack([g_attn.astype(F32), g_mlp.astype(F32)] + [jnp.full((share,), count)] * 6)
    paired = [w_qkv[:, :width]]
    for head in range(KV):
        paired.append(w_qkv[:, width + head * HD : width + (head + 1) * HD])
        paired.append(w_qkv[:, width + kv_width + head * HD : width + kv_width + (head + 1) * HD])
    qkv_own = jnp.concatenate(paired, axis=1)
    gu_rows = lax.dynamic_slice_in_dim(w_gate_up, plane * quarter, quarter, 0)
    gu_send = []
    for place in range(CHIPS):
        for begin in (place * hidden_chip, (CHIPS + place) * hidden_chip):
            gu_send.append(gu_rows[:, begin : begin + hidden_chip])
    gu_send = jnp.stack([jnp.concatenate(gu_send[2 * c : 2 * c + 2], axis=1) for c in range(CHIPS)])
    vectors = gather_vectors(vectors, me)
    vectors, qkv_own, gu_send = fence(vectors, qkv_own, gu_send)
    qkv_first = send_first(qkv_own)
    attn_gain = vectors[0:1]
    mlp_gain = vectors[1:2]
    zeros = jnp.sum(vectors[2].reshape(devices, share)[:, 0]).astype(jnp.int32)
    zeros_one = zeros.reshape(1)
    local_pos = me * rows + jnp.arange(rows, dtype=jnp.int32) - segment_ids.reshape(rows) * zeros
    cos, sin = turn_tables(local_pos)
    dy = (cotangent * selected[:, :, None].astype(BF)).reshape(rows, width)
    qkv_own, qkv_first, cos, sin = fence(qkv_own, qkv_first, cos, sin)
    qkv_second = send_second(qkv_own)
    qkv_theirs = [send_sibling(qkv_own), send_sibling(qkv_first)]
    all_places = jnp.arange(length, dtype=jnp.int32)
    cos_all, sin_all = turn_tables(all_places - jnp.where(all_places >= zeros, zeros, 0))
    qkv_first, qkv_second, cos_all, sin_all, *qkv_theirs = fence(qkv_first, qkv_second, cos_all, sin_all, *qkv_theirs)
    qkv_far = send_second(qkv_first)
    qkv_theirs.append(send_sibling(qkv_second))
    qkv_far, dy, *qkv_theirs = fence(qkv_far, dy, *qkv_theirs)
    qkv_theirs.append(send_sibling(qkv_far))
    qkv_parts = [qkv_own, qkv_first, qkv_second, qkv_far] + qkv_theirs
    x_bf = tokens.reshape(rows, width)
    x_bf, w_out, gu_send, *qkv_parts = fence(x_bf, w_out, gu_send, *qkv_parts)
    out_first = send_first(w_out)
    gu_part = lax.all_to_all(gu_send, "sp", 0, 0, axis_index_groups=SAME_CORE, tiled=True)
    qkv_send, normed, inv_one = project(places, x_bf, attn_gain, cos, sin, qkv_parts)
    qkv_send, out_first = fence(qkv_send, out_first)
    gu_mine = lax.all_gather(after(gu_part, qkv_send), "dp", axis=0, tiled=False)
    gu_mine = lax.all_gather(after(gu_part, qkv_send), "dp", axis=0, tiled=False)
    down_theirs = send_sibling(w_down)
    w_dn = jnp.where(
        core == 0, jnp.concatenate([w_down, down_theirs], axis=0), jnp.concatenate([down_theirs, w_down], axis=0)
    )
    qkv_heads = lax.all_to_all(qkv_send, "sp", 0, 0, tiled=True).reshape(length, qkv_send.shape[2])

    cuts = (0, (5 * blocks) // 8, (7 * blocks) // 8, blocks)
    qkv_heads, w_dn, out_first = fence(qkv_heads, w_dn, out_first)
    out_second = send_second(after(w_out, qkv_heads))
    dy_first = send_first(after(dy, qkv_heads))
    fwd = attend(zeros_one, qkv_heads, cuts[0], cuts[1])
    qkv_heads, out_second, dy_first, out_first, dy, *fwd = fence(qkv_heads, out_second, dy_first, out_first, dy, *fwd)
    out_far = send_second(out_first)
    dy_second = send_second(dy)
    fwd = attend(zeros_one, qkv_heads, cuts[1], cuts[2], fwd)
    qkv_heads, out_far, dy_second, dy_first, *fwd = fence(qkv_heads, out_far, dy_second, dy_first, *fwd)
    dy_far = send_second(dy_first)
    gu_theirs = send_sibling(after(gu_mine, fwd[2]))
    out_heads, out_send, lse = attend(zeros_one, qkv_heads, cuts[2], cuts[3], fwd)
    out_parts = [w_out, out_first, out_second, out_far]
    out_parts = out_parts + [send_sibling(part) for part in out_parts]
    out_send, gu_mine, gu_theirs = fence(out_send, gu_mine, gu_theirs)
    attn_tok = lax.all_to_all(out_send, "sp", 0, 0, tiled=True)
    w_gu = join(core, gu_mine, gu_theirs)
    attn_tok, w_gu, dy_far, *out_parts = fence(attn_tok, w_gu, dy_far, *out_parts)
    residual, inv_two, inner = out_proj(places, attn_tok, x_bf, mlp_gain, out_parts)

    b_first = send_first(inner)
    own = ffn(inner, dy, w_gu, w_dn)
    inner, b_first, *own = fence(inner, b_first, *own)
    b_second = send_second(inner)
    first = ffn(b_first, dy_first, w_gu, w_dn)
    b_first, b_second, *first = fence(b_first, b_second, *first)
    b_far = send_second(b_first)
    second = ffn(b_second, dy_second, w_gu, w_dn)
    b_far, db_first, *second = fence(b_far, first[3], *second)
    db_got_first = send_first(db_first)
    far = ffn(b_far, dy_far, w_gu, w_dn)
    db_got_first, db_far, *hid_rows = fence(db_got_first, far[3], own[0], first[0], second[0], far[0])

    db_got_far = send_first(db_far)
    dn_keep, dn_give = grad_dn(core, hid_rows, [dy, dy_first, dy_second, dy_far])
    db_got_far, dn_keep, dn_give = fence(db_got_far, dn_keep, dn_give)
    db_pass = (second[3].astype(F32) + db_got_far.astype(F32)).astype(BF)
    b_own, db_pass, dn_give = fence(inner, db_pass, dn_give)
    db_passed = send_second(db_pass)
    dn_got = send_sibling(dn_give)
    gu_keep, gu_give = grad_gu(
        core,
        [b_own, b_first, b_second, b_far],
        [own[1], first[1], second[1], far[1]],
        [own[2], first[2], second[2], far[2]],
        share,
        planes,
    )
    db_passed, dn_got, gu_keep, gu_give = fence(db_passed, dn_got, gu_keep, gu_give)
    dn_parts = [part.reshape(planes, dn_keep.shape[0] // planes, width) for part in (dn_keep, dn_got)]
    dn_moves = line_scatter_sends(dn_parts, None, 1, 0)
    db_passed, gu_give, *dn_moves = fence(db_passed, gu_give, *dn_moves)
    gu_got = send_sibling(gu_give)
    dn_moves = line_scatter_move(dn_moves, 1)
    d_resid, d_branch, d_send = resid_back(
        places, own[3], db_got_first, db_passed, residual, inv_two, mlp_gain, dy, out_parts
    )
    d_send, d_branch, gu_got, *dn_moves = fence(d_send, d_branch, gu_got, *dn_moves)
    gu_sum = (gu_keep.astype(F32) + gu_got.astype(F32)).astype(BF)
    gu_z = lax.psum_scatter(
        gu_sum.reshape(planes * CHIPS * quarter, 2 * hidden_chip), "dp", scatter_dimension=0, tiled=True
    )
    gu_z = gu_z.reshape(CHIPS, quarter, 2 * hidden_chip)
    d_heads = lax.all_to_all(d_send, "sp", 0, 0, tiled=True).reshape(length, share)
    dn_moves = line_scatter_sends(dn_parts, dn_moves, 2, 0)
    dn_moves = line_scatter_move(dn_moves, 2)
    wo_keep, wo_give = grad_wo(core, attn_tok, d_branch)
    d_heads, wo_keep, wo_give, normed = fence(d_heads, wo_keep, wo_give, normed)

    def back_call(heads, start, stop, **kwargs):
        return attend_back(zeros_one, qkv_heads, heads, lse, cos_all, sin_all, start, stop, **kwargs)

    turns = (0, blocks // 8, blocks // 4, blocks // 2, blocks)
    wo_got = send_sibling(wo_give)
    a_first = send_first(normed)
    bwd = back_call(d_heads, turns[0], turns[1], out=out_heads)
    d_heads, a_first, wo_got, normed, *moves = fence(d_heads, a_first, wo_got, normed, *dn_moves, *bwd)
    dn_moves, bwd = moves[:2], moves[2:]

    dn_moves = line_scatter_sends(dn_parts, dn_moves, 3, 0)
    d_heads, normed, a_first, *dn_moves = fence(d_heads, normed, a_first, *dn_moves)
    a_second = send_second(normed)
    a_theirs = [send_sibling(normed), send_sibling(a_first)]
    dn_moves = line_scatter_move(dn_moves, 3)
    bwd = back_call(d_heads, turns[1], turns[2], before=bwd)
    d_heads, gu_z, a_second, *moves = fence(d_heads, gu_z, a_second, *a_theirs, *dn_moves, *bwd)
    a_theirs, dn_moves, bwd = moves[:2], moves[2:4], moves[4:]

    def wo_part(place):
        return pick(wo_keep, place).astype(F32) + pick(wo_got, place).astype(F32)

    dn_z = line_scatter_end(dn_parts, dn_moves, 0)
    d_heads, dn_z, gu_z, a_first, a_second = fence(d_heads, dn_z, gu_z, a_first, a_second)
    dn_all = lax.all_gather(dn_z, "dp", axis=0, tiled=False)
    gu_z = lax.all_to_all(gu_z, "sp", 0, 0, axis_index_groups=SAME_CORE, tiled=True)
    a_far = send_second(a_first)
    a_theirs.append(send_sibling(a_second))
    bwd = back_call(d_heads, turns[2], turns[3], before=bwd)
    d_heads, gu_z, a_far, *moves = fence(d_heads, gu_z, a_far, *a_theirs, *bwd)
    a_theirs, bwd = moves[:3], moves[3:]

    wo_first = wo_part(chip ^ (first_mask // 2)).astype(BF)
    wo_far = wo_part(chip ^ 3).astype(BF)
    d_heads, gu_z, a_far, wo_first, wo_far = fence(d_heads, gu_z, a_far, wo_first, wo_far)
    gu_all = lax.all_gather(gu_z, "dp", axis=0, tiled=False)
    wo_far = send_first(wo_far)
    wo_first = send_first(wo_first)
    a_theirs.append(send_sibling(a_far))
    bwd = back_call(d_heads, turns[3], turns[4], before=bwd)
    wo_pass = (wo_part(chip ^ (second_mask // 2)) + wo_far.astype(F32)).astype(BF)
    dp_heads, wo_first, wo_pass, *a_theirs = fence(bwd[0], wo_first, wo_pass, *a_theirs)

    wo_passed = send_second(wo_pass)
    back = lax.all_to_all(dp_heads, "sp", 0, 0, tiled=True)
    grad_wq = grad_qkv(places, [normed, a_first, a_second, a_far] + list(a_theirs), dp_heads, planes)
    wo_rows = (wo_part(chip) + wo_first.astype(F32) + wo_passed.astype(F32)).astype(BF)
    split = grad_wq.shape[2]
    last_parts = [jnp.concatenate([grad_wq, wo_rows.reshape(planes, quarter, width)], axis=2)]
    y_far, y_first = far[4], first[4]
    moves = None
    for step in range(1, planes):
        moves = line_scatter_sends(last_parts, moves, step, 0)
        y_far, y_first, *moves = fence(y_far, y_first, *moves)
        moves = line_scatter_move(moves, step)
        if step == 1:
            y_got_far = send_first(y_far)
        elif step == 2:
            y_got_first = send_first(y_first)
        moves = fence(*moves)
    last_z = line_scatter_end(last_parts, moves, 0)
    wq_z = last_z[:, :split].reshape(quarter, devices, split // devices).transpose(1, 0, 2)
    wq_z, wo_z, back = fence(wq_z, last_z[:, split:], back)
    wq_z = lax.all_to_all(wq_z, "sp", 0, 0, tiled=True)
    grad_tokens = in_back(places, back, x_bf, inv_one, attn_gain, d_resid, qkv_parts).reshape(tokens.shape)
    y_pass = (second[4].astype(F32) + y_got_far.astype(F32)).astype(BF)
    last_z = jnp.concatenate([wq_z.transpose(1, 0, 2).reshape(quarter, split), wo_z], axis=1)
    last_z, grad_tokens, y_pass, y_got_first = fence(last_z, grad_tokens, y_pass, y_got_first)
    y_passed = send_second(y_pass)
    last_steps = [(last_z, last_z)]
    outs = []
    for step in range(1, planes):
        last_steps.append(line_gather_move(last_steps[-1], step))
        if step == 1:
            outs.append(dn_all.astype(F32).reshape(w_down.shape))
        elif step == 2:
            outs += spread(gu_all, w_gate_up, g_mlp.astype(F32).reshape(share, 1))
        if step == planes - 1:
            y_sum = own[4].astype(F32) + y_got_first.astype(F32) + y_passed.astype(F32)
            outs.append((residual + y_sum).astype(BF).reshape(tokens.shape))
        moves = fence(*last_steps[-1], *outs)
        last_steps[-1], outs = tuple(moves[:2]), list(moves[2:])
    grad_w_down, grad_w_gate_up, grad_g_mlp, output = outs
    grad_w_qkv, grad_g_attn, grad_w_out = spread_last(last_steps, w_qkv, g_attn.astype(F32).reshape(share, 1), width)
    return (
        output,
        grad_tokens,
        grad_w_qkv,
        grad_w_out,
        grad_w_gate_up,
        grad_w_down,
        grad_g_attn.reshape(share),
        grad_g_mlp.reshape(share),
    )


def solution(mesh):
    in_specs = (
        P("dp", "sp", None),
        P("dp", "sp"),
        P("dp", "sp"),
        P("dp", "sp", None),
        P("sp", None),
        P("sp", None),
        P("sp", None),
        P("sp", None),
        P("sp"),
        P("sp"),
    )
    out_specs = (
        P("dp", "sp", None),
        P("dp", "sp", None),
        P("sp", None),
        P("sp", None),
        P("sp", None),
        P("sp", None),
        P("sp"),
        P("sp"),
    )
    body = fast_body if mesh.shape["sp"] == 2 * CHIPS else general_body
    return jax.shard_map(body, mesh=mesh, in_specs=in_specs, out_specs=out_specs, check_vma=False)
```

```python
import functools
import math

import jax
import jax.numpy as jnp
from jax import lax
from jax.experimental import pallas as pl
from jax.experimental.pallas import tpu as pltpu
from jax.sharding import PartitionSpec as P

D = 2048
H = 32
KV = 4
HD = 64
FF = 5632


EPSILON = 1e-05
ROPE_BASE = 10000.0
MASKED = -1e30


def rope_tables(positions, head_size):
    half_dim = head_size // 2
    frequency = ROPE_BASE ** (-(jnp.arange(half_dim, dtype=jnp.float32) * 2.0 / head_size))
    angles = positions.astype(jnp.float32)[:, None] * frequency[None, :]
    return (jnp.cos(angles), jnp.sin(angles))


def rotate(values, cosine, sine_tab, inverse_turn):
    half_dim = values.shape[-1] // 2
    first_half = values[..., :half_dim]
    second = values[..., half_dim:]
    cos_wide = cosine[:, None, :]
    sin_wide = sine_tab[:, None, :]
    if inverse_turn:
        sin_wide = -sin_wide
    return jnp.concatenate(
        [first_half * cos_wide - second * sin_wide, second * cos_wide + first_half * sin_wide],
        axis=-1,
    )


def rms_norm(values, gain_vec):
    inverse = lax.rsqrt(jnp.mean(values * values, axis=-1, keepdims=True) + EPSILON)
    return (values * inverse * gain_vec, inverse)


def norm_back(values, inverse, gain_vec, upstream):
    scaled = upstream * gain_vec
    inner_mean = jnp.mean(scaled * values, axis=-1, keepdims=True)
    through = inverse * scaled - values * inverse**3 * inner_mean
    gain_grad = jnp.sum(upstream * values * inverse, axis=0)
    return (through, gain_grad)


def attention_inputs(flat_in, qkv_full, gain_vec, cosine, sine_tab):
    row_count = flat_in.shape[0]
    group_size = H // KV
    normed, inverse = rms_norm(flat_in, gain_vec)
    normed = normed.astype(jnp.bfloat16)
    projected = jnp.dot(normed, qkv_full, preferred_element_type=jnp.float32)
    queries = rotate(projected[:, :D].reshape(row_count, H, HD), cosine, sine_tab, False)
    key_heads = rotate(
        projected[:, D : D + KV * HD].reshape(row_count, KV, HD), cosine, sine_tab, False
    )
    value_heads = projected[:, D + KV * HD :].reshape(row_count, KV, HD)
    key_wide = jnp.broadcast_to(key_heads[:, :, None], (row_count, KV, group_size, HD)).reshape(
        row_count, D
    )
    value_wide = jnp.broadcast_to(value_heads[:, :, None], (row_count, KV, group_size, HD)).reshape(
        row_count, D
    )
    stacked = jnp.stack([queries.reshape(row_count, D), key_wide, value_wide]).astype(jnp.bfloat16)
    return (normed, inverse, stacked)


def block_mask(seg_full, position, row_begin, finish):
    row_seg = seg_full[:, row_begin:finish]
    col_seg = seg_full[:, :finish]
    same_doc = row_seg[:, :, None] == col_seg[:, None, :]
    causal = position[row_begin:finish, None] >= position[None, :finish]
    return same_doc & causal[None]


def attention_forward(queries, key_heads, value_heads, seg_full, score_scale):
    length = queries.shape[1]
    block_rows = min(512, length)
    position = jnp.arange(length, dtype=jnp.int32)
    outputs = []
    lse_parts = []
    for block_num in range(length // block_rows):
        row_begin = block_num * block_rows
        finish = row_begin + block_rows
        scores = (
            jnp.einsum(
                "sqhd,skhd->shqk",
                queries[:, row_begin:finish],
                key_heads[:, :finish],
                preferred_element_type=jnp.float32,
            )
            * score_scale
        )
        allowed = block_mask(seg_full, position, row_begin, finish)
        scores = jnp.where(allowed[:, None], scores, MASKED)
        row_max = jnp.max(scores, axis=-1, keepdims=True)
        shifted = jnp.exp(scores - row_max)
        row_total = jnp.sum(shifted, axis=-1, keepdims=True)
        softmax_w = (shifted / row_total).astype(jnp.bfloat16)
        outputs.append(
            jnp.einsum(
                "shqk,skhd->sqhd",
                softmax_w,
                value_heads[:, :finish],
                preferred_element_type=jnp.float32,
            )
        )
        lse_parts.append(row_max + jnp.log(row_total))
    return (jnp.concatenate(outputs, axis=1), jnp.concatenate(lse_parts, axis=2))


def attention_backward(queries, key_heads, value_heads, seg_full, log_sums, grad_out, score_scale):
    length = queries.shape[1]
    block_rows = min(512, length)
    position = jnp.arange(length, dtype=jnp.int32)
    grad_query = []
    grad_key = jnp.zeros(key_heads.shape, jnp.float32)
    grad_value = jnp.zeros(value_heads.shape, jnp.float32)
    for block_num in range(length // block_rows):
        row_begin = block_num * block_rows
        finish = row_begin + block_rows
        query_rows = queries[:, row_begin:finish]
        grad_rows = grad_out[:, row_begin:finish]
        key_part = key_heads[:, :finish]
        value_part = value_heads[:, :finish]
        scores = (
            jnp.einsum("sqhd,skhd->shqk", query_rows, key_part, preferred_element_type=jnp.float32)
            * score_scale
        )
        allowed = block_mask(seg_full, position, row_begin, finish)
        softmax_f = jnp.where(
            allowed[:, None], jnp.exp(scores - log_sums[:, :, row_begin:finish]), 0.0
        )
        grad_probs = jnp.einsum(
            "sqhd,skhd->shqk", grad_rows, value_part, preferred_element_type=jnp.float32
        )
        row_delta = jnp.sum(softmax_f * grad_probs, axis=-1, keepdims=True)
        grad_scores = (softmax_f * (grad_probs - row_delta)).astype(jnp.bfloat16)
        grad_query.append(
            jnp.einsum("shqk,skhd->sqhd", grad_scores, key_part, preferred_element_type=jnp.float32)
            * score_scale
        )
        grad_key = grad_key.at[:, :finish].add(
            jnp.einsum(
                "shqk,sqhd->skhd", grad_scores, query_rows, preferred_element_type=jnp.float32
            )
            * score_scale
        )
        grad_value = grad_value.at[:, :finish].add(
            jnp.einsum(
                "shqk,sqhd->skhd",
                softmax_f.astype(jnp.bfloat16),
                grad_rows,
                preferred_element_type=jnp.float32,
            )
        )
    return (jnp.concatenate(grad_query, axis=1), grad_key, grad_value)


def general_body(tokens, segment_ids, selected, cotangent, w_qkv, w_out, w_gate_up, w_down, g_attn, g_mlp):
    streams, local_len, model_dim = tokens.shape
    sp_count = lax.axis_size("sp")
    sp_index = lax.axis_index("sp")
    row_count = streams * local_len
    group_size = H // KV
    kv_width = KV * HD
    score_scale = HD ** (-0.5)
    contract = (((0,), (0,)), ((), ()))
    seg_full = lax.all_gather(segment_ids, "sp", axis=1, tiled=True)
    first_count = jnp.sum((seg_full == 0).astype(jnp.int32), axis=1, keepdims=True)
    local_pos = (
        sp_index * local_len
        + jnp.arange(local_len, dtype=jnp.int32)[None, :]
        - segment_ids * first_count
    )
    cosine, sine_tab = rope_tables(local_pos.reshape(row_count), HD)
    shards = (w_qkv, w_out, w_gate_up, w_down, g_attn, g_mlp)
    gathered = (
        lax.all_gather(shards[0], "sp", axis=0, tiled=True),
        lax.all_gather(shards[1], "sp", axis=0, tiled=True),
        lax.all_gather(shards[2], "sp", axis=0, tiled=True),
        lax.all_gather(shards[3], "sp", axis=0, tiled=True),
        lax.all_gather(shards[4], "sp", axis=0, tiled=True),
        lax.all_gather(shards[5], "sp", axis=0, tiled=True),
    )
    qkv_full, out_full, gate_up_full, down_full, attn_gain, mlp_gain = gathered
    attn_gain = attn_gain.astype(jnp.float32)
    mlp_gain = mlp_gain.astype(jnp.float32)
    flat_in = tokens.reshape(row_count, model_dim).astype(jnp.float32)
    normed, inverse_one, stacked = attention_inputs(flat_in, qkv_full, attn_gain, cosine, sine_tab)
    head_view = lax.all_to_all(
        stacked.reshape(3, streams, local_len, model_dim),
        "sp",
        split_axis=3,
        concat_axis=2,
        tiled=True,
    )
    length = head_view.shape[2]
    heads_here = head_view.shape[3] // HD
    head_shape = (streams, length, heads_here, HD)
    queries = head_view[0].reshape(head_shape)
    key_heads = head_view[1].reshape(head_shape)
    value_heads = head_view[2].reshape(head_shape)
    attn_heads, log_sums = attention_forward(queries, key_heads, value_heads, seg_full, score_scale)
    attn_send = attn_heads.astype(jnp.bfloat16).reshape(streams, length, heads_here * HD)
    attn_tok = lax.all_to_all(attn_send, "sp", split_axis=1, concat_axis=2, tiled=True).reshape(
        row_count, model_dim
    )
    branch = jnp.dot(attn_tok, out_full, preferred_element_type=jnp.float32)
    residual = flat_in + branch
    inner_f, inverse_two = rms_norm(residual, mlp_gain)
    inner_in = inner_f.astype(jnp.bfloat16)
    gate_up = jnp.dot(inner_in, gate_up_full, preferred_element_type=jnp.float32)
    gate_part = gate_up[:, :FF]
    up_part = gate_up[:, FF:]
    sigmoid_g = jax.nn.sigmoid(gate_part)
    silu_gate = gate_part * sigmoid_g
    hidden = (silu_gate * up_part).astype(jnp.bfloat16)
    result = residual + jnp.dot(hidden, down_full, preferred_element_type=jnp.float32)
    output = result.astype(jnp.bfloat16).reshape(streams, local_len, model_dim)
    qkv_back, out_back, gate_up_back, down_back, attn_gain_b, mlp_gain_b = gathered
    attn_gain_b = attn_gain_b.astype(jnp.float32)
    mlp_gain_b = mlp_gain_b.astype(jnp.float32)
    grad_y = (cotangent * selected[:, :, None].astype(jnp.bfloat16)).reshape(row_count, model_dim)
    grad_hidden = jnp.dot(grad_y, down_back.T, preferred_element_type=jnp.float32)
    silu_slope = sigmoid_g * (1.0 + gate_part * (1.0 - sigmoid_g))
    grad_both = jnp.concatenate(
        [grad_hidden * up_part * silu_slope, grad_hidden * silu_gate], axis=1
    ).astype(jnp.bfloat16)
    grad_inner = jnp.dot(grad_both, gate_up_back.T, preferred_element_type=jnp.float32)
    grad_resid, gain_two = norm_back(residual, inverse_two, mlp_gain_b, grad_inner)
    grad_resid = grad_resid + grad_y.astype(jnp.float32)
    grad_branch = grad_resid.astype(jnp.bfloat16)
    grad_attn = jnp.dot(grad_branch, out_back.T, preferred_element_type=jnp.float32).astype(
        jnp.bfloat16
    )
    grad_view = lax.all_to_all(
        grad_attn.reshape(streams, local_len, model_dim),
        "sp",
        split_axis=2,
        concat_axis=1,
        tiled=True,
    )
    grad_view = grad_view.reshape(head_shape)
    grad_q, grad_k, grad_v = attention_backward(
        queries, key_heads, value_heads, seg_full, log_sums, grad_view, score_scale
    )
    back_send = (
        jnp.stack([grad_q, grad_k, grad_v])
        .astype(jnp.bfloat16)
        .reshape(3, streams, length, heads_here * HD)
    )
    returned = lax.all_to_all(back_send, "sp", split_axis=2, concat_axis=3, tiled=True)
    returned = returned.astype(jnp.float32).reshape(3, row_count, H, HD)
    grad_pq = rotate(returned[0], cosine, sine_tab, True).reshape(row_count, model_dim)
    key_summed = jnp.sum(returned[1].reshape(row_count, KV, group_size, HD), axis=2)
    grad_pk = rotate(key_summed, cosine, sine_tab, True).reshape(row_count, kv_width)
    grad_pv = jnp.sum(returned[2].reshape(row_count, KV, group_size, HD), axis=2).reshape(
        row_count, kv_width
    )
    grad_mixed = jnp.concatenate(
        [grad_pq.astype(jnp.bfloat16), grad_pk.astype(jnp.bfloat16), grad_pv.astype(jnp.bfloat16)],
        axis=1,
    )
    grad_normed = jnp.dot(grad_mixed, qkv_back.T, preferred_element_type=jnp.float32)
    grad_in, gain_one = norm_back(flat_in, inverse_one, attn_gain_b, grad_normed)
    grad_in = grad_in + grad_resid
    grad_tokens = grad_in.astype(jnp.bfloat16).reshape(streams, local_len, model_dim)
    gain_totals = lax.psum((gain_one, gain_two), ("dp", "sp"))
    gain_share = model_dim // sp_count
    grad_g_attn = lax.dynamic_slice_in_dim(gain_totals[0], sp_index * gain_share, gain_share, 0)
    grad_g_mlp = lax.dynamic_slice_in_dim(gain_totals[1], sp_index * gain_share, gain_share, 0)
    row_sums = lax.psum_scatter(
        jnp.concatenate(
            [
                lax.dot_general(normed, grad_mixed, contract, preferred_element_type=jnp.float32),
                lax.dot_general(
                    attn_tok, grad_branch, contract, preferred_element_type=jnp.float32
                ),
                lax.dot_general(inner_in, grad_both, contract, preferred_element_type=jnp.float32),
            ],
            axis=1,
        ).astype(jnp.bfloat16),
        "sp",
        scatter_dimension=0,
        tiled=True,
    )
    down_sums = lax.psum_scatter(
        lax.dot_general(hidden, grad_y, contract, preferred_element_type=jnp.float32).astype(
            jnp.bfloat16
        ),
        "sp",
        scatter_dimension=0,
        tiled=True,
    )
    weight_rows, down_rows = (
        lax.psum(row_sums, "dp").astype(jnp.float32),
        lax.psum(down_sums, "dp").astype(jnp.float32),
    )
    qkv_cols = model_dim + 2 * kv_width
    grad_w_qkv = weight_rows[:, :qkv_cols]
    grad_w_out = weight_rows[:, qkv_cols : qkv_cols + model_dim]
    grad_w_gate_up = weight_rows[:, qkv_cols + model_dim :]
    return (
        output,
        grad_tokens,
        grad_w_qkv,
        grad_w_out,
        grad_w_gate_up,
        down_rows,
        grad_g_attn,
        grad_g_mlp,
    )


CHIPS = 4
BLOCK = 512
SHORT = pl.CostEstimate(flops=1, bytes_accessed=1, transcendentals=0)
LOG2E = math.log2(math.e)
BF = jnp.bfloat16
F32 = jnp.float32
NT = (((1,), (1,)), ((), ()))
TN = (((0,), (0,)), ((), ()))


def swap_pairs(even_mask, odd_mask):
    return [(i, i ^ (odd_mask if i & 1 else even_mask)) for i in range(2 * CHIPS)]


FIRST = swap_pairs(2, 4)
SECOND = swap_pairs(4, 2)
SIBLING = swap_pairs(1, 1)
SAME_CORE = [[0, 2, 4, 6], [1, 3, 5, 7]]


def send_first(x):
    return lax.ppermute(x, "sp", FIRST)


def send_second(x):
    return lax.ppermute(x, "sp", SECOND)


def send_sibling(x):
    return lax.ppermute(x, "sp", SIBLING)


def after(value, *others):
    return lax.optimization_barrier((value,) + others)[0]


def gather_chips(own):
    first = send_first(own)
    second = send_second(after(own, first))
    far = send_second(after(first, second))
    return [own, first, second, far]


def rel_masks(core):
    first = jnp.where(core == 0, 2, 4)
    return first, 6 - first


def fence(*values):
    return lax.optimization_barrier(values)


def gather_vectors(own, me):
    for bit in (1, 2, 4):
        got = lax.ppermute(own, "sp", swap_pairs(bit, bit))
        high = (me & bit) != 0
        own = jnp.concatenate([jnp.where(high, got, own), jnp.where(high, own, got)], axis=1)
    return own


def pick(parts, index):
    return lax.dynamic_index_in_dim(parts, index, 0, keepdims=False)


def pick_sum(parts, index, axis):
    return sum(lax.dynamic_index_in_dim(p, index, axis, keepdims=False).astype(F32) for p in parts)


def line_scatter_sends(parts, got, step, axis):
    planes = parts[0].shape[axis]
    z = lax.axis_index("dp")
    ahead = pick_sum(parts, jnp.clip(planes - step + z, 0, planes - 1), axis)
    back = pick_sum(parts, jnp.clip(z - planes + step, 0, planes - 1), axis)
    if got is not None:
        ahead = ahead + got[0].astype(F32)
        back = back + got[1].astype(F32)
    return ahead.astype(BF), back.astype(BF)


def line_scatter_move(sends, step):
    planes = lax.axis_size("dp")
    right = lax.ppermute(sends[0], "dp", [(i, i + 1) for i in range(step)])
    left = lax.ppermute(sends[1], "dp", [(planes - 1 - i, planes - 2 - i) for i in range(step)])
    return right, left


def line_scatter_end(parts, got, axis):
    own = pick_sum(parts, lax.axis_index("dp"), axis)
    return (own + got[0].astype(F32) + got[1].astype(F32)).astype(BF)


def line_gather_move(got, step):
    planes = lax.axis_size("dp")
    right = lax.ppermute(got[0], "dp", [(i, i + 1) for i in range(step - 1, planes - 1)])
    left = lax.ppermute(got[1], "dp", [(i + 1, i) for i in range(planes - step)])
    return right, left


def line_values(refs, planes, z):
    for step in range(planes):
        place = lax.rem(z - step + planes, planes)
        if step == 0:
            yield place, lambda index: refs[0][index]
        else:
            right, left = refs[step], refs[2 * planes - 1 - step]
            yield place, lambda index, right=right, left=left, step=step: jnp.where(z >= step, right[index], left[index])


def spread_kernel(in_ref, w_ref, g_ref, out_ref, gain_ref):
    planes, _, rows, width = in_ref.shape
    out = in_ref[...].reshape(planes * rows, width).astype(F32)
    out_ref[...] = out
    part = jnp.sum(out * w_ref[...].astype(F32), axis=-1, keepdims=True) / g_ref[...]

    @pl.when(pl.program_id(0) == 0)
    def _():
        gain_ref[...] = part

    @pl.when(pl.program_id(0) > 0)
    def _():
        gain_ref[...] += part


def spread(parts, weight, gain):
    planes, chips, rows, both = parts.shape
    half = both // 2
    total = planes * rows
    line = pl.BlockSpec((total, half), lambda i: (0, i))
    column = pl.BlockSpec((total, 1), lambda i: (0, 0))
    return pl.pallas_call(
        spread_kernel,
        grid=(2 * chips,),
        in_specs=[pl.BlockSpec((planes, 1, rows, half), lambda i: (0, i % chips, 0, i // chips)), line, column],
        out_specs=[line, column],
        out_shape=[jax.ShapeDtypeStruct(weight.shape, F32), jax.ShapeDtypeStruct((total, 1), F32)],
        compiler_params=pltpu.CompilerParams(vmem_limit_bytes=32 * 2**20),
        cost_estimate=SHORT,
        name="spread",
    )(parts, weight, gain)


def spread_rows_kernel(z_ref, *refs, planes):
    blocks, out_ref = refs[:-1], refs[-1]
    rows = blocks[0].shape[0]
    for place, load in line_values(blocks, planes, z_ref[0]):
        out_ref[pl.ds(pl.multiple_of(place * rows, rows), rows), :] = load(slice(None)).astype(F32)


def spread_rows(steps):
    planes = len(steps)
    rows, width = steps[0][0].shape
    blocks = [steps[0][0]] + [s[0] for s in steps[1:]] + [s[1] for s in steps[1:]]
    tile = width // 4
    return pl.pallas_call(
        functools.partial(spread_rows_kernel, planes=planes),
        grid_spec=pltpu.PrefetchScalarGridSpec(
            num_scalar_prefetch=1,
            grid=(4,),
            in_specs=[pl.BlockSpec((rows, tile), lambda i, z: (0, i))] * len(blocks),
            out_specs=pl.BlockSpec((planes * rows, tile), lambda i, z: (0, i)),
        ),
        out_shape=jax.ShapeDtypeStruct((planes * rows, width), F32),
        compiler_params=pltpu.CompilerParams(vmem_limit_bytes=32 * 2**20),
        cost_estimate=SHORT,
        name="spread_rows",
    )(lax.axis_index("dp").reshape(1), *blocks)


def spread_last_kernel(z_ref, *refs, planes):
    blocks, (w_ref, g_ref, out_ref, gain_ref, wo_ref) = refs[:-5], refs[-5:]
    rows = blocks[0].shape[0]
    devices = 2 * CHIPS
    width = wo_ref.shape[1]
    heads = width // devices
    each = heads + 2 * HD
    for place, load in line_values(blocks, planes, z_ref[0]):
        span = pl.ds(pl.multiple_of(place * rows, rows), rows)
        pairs = []
        for d in range(devices):
            begin = d * each
            cols = slice(begin, begin + heads)
            out_ref[span, d * heads : (d + 1) * heads] = load((slice(None), cols)).astype(F32)
            pairs.append(load((slice(None), slice(begin + heads, begin + each))).astype(F32))
        for g in range(0, KV, 2):
            low = pairs[2 * g] + pairs[2 * g + 1]
            high = pairs[2 * g + 2] + pairs[2 * g + 3]
            lane = lax.broadcasted_iota(jnp.int32, low.shape, 1)
            begin = width + g * HD
            out_ref[span, begin : begin + 2 * HD] = jnp.where(lane < HD, low, pltpu.roll(high, HD, 1))
            begin = width + (KV + g) * HD
            out_ref[span, begin : begin + 2 * HD] = jnp.where(lane < HD, pltpu.roll(low, HD, 1), high)
        wo_ref[span, :] = load((slice(None), slice(devices * each, devices * each + width))).astype(F32)
    gain_ref[...] = jnp.sum(out_ref[...] * w_ref[...].astype(F32), axis=-1, keepdims=True) / g_ref[...]


def spread_last(steps, weight, gain, width):
    planes = len(steps)
    blocks = [steps[0][0]] + [s[0] for s in steps[1:]] + [s[1] for s in steps[1:]]
    vmem = pl.BlockSpec(memory_space=pltpu.VMEM)
    total = weight.shape[0]
    return pl.pallas_call(
        functools.partial(spread_last_kernel, planes=planes),
        in_specs=[pl.BlockSpec(memory_space=pltpu.SMEM)] + [vmem] * (len(blocks) + 2),
        out_specs=[vmem] * 3,
        out_shape=[
            jax.ShapeDtypeStruct(weight.shape, F32),
            jax.ShapeDtypeStruct((total, 1), F32),
            jax.ShapeDtypeStruct((total, width), F32),
        ],
        compiler_params=pltpu.CompilerParams(vmem_limit_bytes=32 * 2**20),
        cost_estimate=SHORT,
        name="spread_last",
    )(lax.axis_index("dp").reshape(1), *blocks, weight, gain)


def join_kernel(core_ref, mine_ref, theirs_ref, out_ref):
    planes, _, rows, both = mine_ref.shape
    block = jnp.where(pl.program_id(1) == 0, mine_ref[...], theirs_ref[...]).reshape(planes * rows, both)
    out_ref[0, 0, 0] = block[:, : both // 2]
    out_ref[1, 0, 0] = block[:, both // 2 :]


def join(core, mine, theirs):
    planes, chips, rows, both = mine.shape
    spec = pl.BlockSpec((planes, 1, rows, both), lambda c, k, core: (0, c, 0, 0))
    out = pl.pallas_call(
        join_kernel,
        grid_spec=pltpu.PrefetchScalarGridSpec(
            num_scalar_prefetch=1,
            grid=(chips, 2),
            in_specs=[spec, spec],
            out_specs=pl.BlockSpec(
                (2, 1, 1, planes * rows, both // 2), lambda c, k, core: (0, c, (core[0] + k) % 2, 0, 0)
            ),
        ),
        out_shape=jax.ShapeDtypeStruct((2, chips, 2, planes * rows, both // 2), BF),
        compiler_params=pltpu.CompilerParams(vmem_limit_bytes=32 * 2**20),
        cost_estimate=SHORT,
        name="join",
    )(core.reshape(1), mine, theirs)
    return out.reshape(2, 2 * chips * planes * rows, both // 2)


def ffn_kernel(*refs, cuts):
    b_hbm, dy_hbm, wgu_hbm, wd_hbm, hid_hbm, dg_hbm, du_hbm, db_hbm, y_hbm = refs[:9]
    b_ref, dy_ref, wg_ref, wu_ref, wd_ref, hid_ref, dg_ref, du_ref, db_ref, y_ref, sems = refs[9:]
    count = len(cuts) - 1

    def move(source, target, index):
        copy = pltpu.make_async_copy(source, target, sems.at[index])
        copy.start()
        return copy

    b_copy = move(b_hbm, b_ref, 3 * count)
    weights = []
    for c in range(count):
        span = slice(cuts[c], cuts[c + 1])
        gate_copy = move(wgu_hbm.at[0, :, span], wg_ref.at[:, span], 3 * c)
        up_copy = move(wgu_hbm.at[1, :, span], wu_ref.at[:, span], 3 * c + 1)
        weights.append([gate_copy, up_copy])
        if c == 0:
            dy_copy = move(dy_hbm, dy_ref, 3 * count + 1)
        weights[-1].append(move(wd_hbm.at[span, :], wd_ref.at[span, :], 3 * c + 2))
    b_copy.wait()
    for c in range(count):
        span = slice(cuts[c], cuts[c + 1])
        for copy in weights[c][:2]:
            copy.wait()
        gate = jnp.dot(b_ref[...], wg_ref[:, span], preferred_element_type=F32)
        up = jnp.dot(b_ref[...], wu_ref[:, span], preferred_element_type=F32)
        if c == 0:
            dy_copy.wait()
        weights[c][2].wait()
        d_hidden = lax.dot_general(dy_ref[...], wd_ref[span, :], NT, preferred_element_type=F32)
        sigmoid_g = jax.nn.sigmoid(gate)
        silu_gate = gate * sigmoid_g
        hid_ref[:, span] = (silu_gate * up).astype(BF)
        dg_ref[:, span] = (d_hidden * up * (sigmoid_g * (1.0 + gate * (1.0 - sigmoid_g)))).astype(BF)
        du_ref[:, span] = (d_hidden * silu_gate).astype(BF)
    base = 3 * count + 2
    outs = [move(hid_ref, hid_hbm, base), move(dg_ref, dg_hbm, base + 1), move(du_ref, du_hbm, base + 2)]
    y_ref[...] = jnp.dot(hid_ref[...], wd_ref[...], preferred_element_type=F32).astype(BF)
    outs.append(move(y_ref, y_hbm, base + 3))
    d_in = lax.dot_general(dg_ref[...], wg_ref[...], NT, preferred_element_type=F32)
    db_ref[...] = (d_in + lax.dot_general(du_ref[...], wu_ref[...], NT, preferred_element_type=F32)).astype(BF)
    outs.append(move(db_ref, db_hbm, base + 4))
    for copy in outs:
        copy.wait()


def ffn(b_rows, dy_rows, w_gu, w_dn):
    rows, width = b_rows.shape
    hidden = w_dn.shape[0]
    pieces = 3
    cuts = tuple(round(hidden * c / pieces / 128) * 128 for c in range(pieces)) + (hidden,)
    hbm = pl.BlockSpec(memory_space=pl.ANY)
    return pl.pallas_call(
        functools.partial(ffn_kernel, cuts=cuts),
        in_specs=[hbm] * 4,
        out_specs=[hbm] * 5,
        out_shape=[jax.ShapeDtypeStruct((rows, hidden), BF)] * 3 + [jax.ShapeDtypeStruct((rows, width), BF)] * 2,
        scratch_shapes=[pltpu.VMEM((rows, width), BF)] * 2
        + [pltpu.VMEM((width, hidden), BF)] * 2
        + [pltpu.VMEM((hidden, width), BF)]
        + [pltpu.VMEM((rows, hidden), BF)] * 3
        + [pltpu.VMEM((rows, width), BF)] * 2
        + [pltpu.SemaphoreType.DMA((3 * pieces + 7,))],
        compiler_params=pltpu.CompilerParams(vmem_limit_bytes=58 * 2**20),
        cost_estimate=SHORT,
        name="ffn",
    )(b_rows, dy_rows, w_gu, w_dn)


def grad_gu_kernel(core_ref, *refs, count):
    left, right = refs[: 2 * count], refs[2 * count : 4 * count]
    half = right[0].shape[1]
    for side in range(2):
        for kind in range(2):
            total = None
            for r in range(count):
                a_rows = left[side * count + r][...]
                part = lax.dot_general(a_rows, right[kind * count + r][...], TN, preferred_element_type=F32)
                total = part if total is None else total + part
            out_ref = refs[4 * count + side]
            planes, _, rows, _ = out_ref.shape
            out_ref[:, 0, :, kind * half : (kind + 1) * half] = total.astype(BF).reshape(planes, rows, half)


def grad_gu(core, b_rows, dg_rows, du_rows, share, planes):
    count = len(b_rows)
    tokens, width = b_rows[0].shape
    hidden = dg_rows[0].shape[1]
    keep = pl.BlockSpec((tokens, share), lambda c, core: (0, 2 * c + core[0]))
    give = pl.BlockSpec((tokens, share), lambda c, core: (0, 2 * c + 1 - core[0]))
    whole = pl.BlockSpec((tokens, hidden), lambda c, core: (0, 0))
    rows = share // planes
    out = pl.BlockSpec((planes, 1, rows, 2 * hidden), lambda c, core: (0, c, 0, 0))
    return pl.pallas_call(
        functools.partial(grad_gu_kernel, count=count),
        grid_spec=pltpu.PrefetchScalarGridSpec(
            num_scalar_prefetch=1,
            grid=(width // (2 * share),),
            in_specs=[keep] * count + [give] * count + [whole] * (2 * count),
            out_specs=[out, out],
        ),
        out_shape=[jax.ShapeDtypeStruct((planes, width // (2 * share), rows, 2 * hidden), BF)] * 2,
        compiler_params=pltpu.CompilerParams(vmem_limit_bytes=58 * 2**20),
        cost_estimate=SHORT,
        name="grad_gu",
    )(core.reshape(1), *b_rows, *b_rows, *dg_rows, *du_rows)


def grad_qkv_kernel(place_ref, *refs, count):
    dp_ref, out_ref = refs[-2:]
    total = None
    for r in range(count):
        part = lax.dot_general(refs[r][...], dp_ref[place_ref[r]], TN, preferred_element_type=F32)
        total = part if total is None else total + part
    planes, rows, wide = out_ref.shape
    columns = total.shape[1]
    for k in range(wide // columns):
        block = total[k * planes * rows : (k + 1) * planes * rows].astype(BF)
        out_ref[:, :, k * columns : (k + 1) * columns] = block.reshape(planes, rows, columns)


def grad_qkv(places, a_rows, dp_heads, planes):
    count = len(a_rows)
    tokens, width = a_rows[0].shape
    columns = dp_heads.shape[2]
    share = width // count
    depth = 2 * share
    return pl.pallas_call(
        functools.partial(grad_qkv_kernel, count=count),
        grid_spec=pltpu.PrefetchScalarGridSpec(
            num_scalar_prefetch=1,
            grid=(width // depth,),
            in_specs=[pl.BlockSpec((tokens, depth), lambda i, p: (0, i))] * count
            + [pl.BlockSpec(dp_heads.shape, lambda i, p: (0, 0, 0))],
            out_specs=pl.BlockSpec((planes, share // planes, 2 * columns), lambda i, p: (0, 0, i)),
        ),
        out_shape=jax.ShapeDtypeStruct((planes, share // planes, count * columns), BF),
        compiler_params=pltpu.CompilerParams(vmem_limit_bytes=48 * 2**20),
        cost_estimate=SHORT,
        name="grad_qkv",
    )(places, *a_rows, dp_heads)


def swap_halves(values):
    width = values.shape[-1]
    lane = lax.broadcasted_iota(jnp.int32, values.shape, 1)
    ahead = pltpu.roll(values, width - HD // 2, 1)
    behind = pltpu.roll(values, HD // 2, 1)
    return jnp.where(lane % HD < HD // 2, ahead, behind)


def project_kernel(place_ref, x_ref, gain_ref, cos_ref, sin_ref, *refs, count):
    wq_refs, wkv_refs = refs[:count], refs[count : 2 * count]
    send_ref, normed_ref, inv_ref, normed_scr = refs[2 * count :]
    share = normed_scr.shape[2]

    @pl.when(pl.program_id(0) == 0)
    def _():
        x = x_ref[...].astype(F32)
        inv = lax.rsqrt(jnp.mean(x * x, axis=-1, keepdims=True) + EPSILON)
        normed = (x * inv * gain_ref[...]).astype(BF)
        normed_ref[...] = normed
        inv_ref[...] = inv
        for part in range(count):
            normed_scr[part] = normed[:, part * share : (part + 1) * share]

    pq = pkv = None
    for r in range(count):
        a_rows = normed_scr[place_ref[r]]
        q_part = jnp.dot(a_rows, wq_refs[r][...], preferred_element_type=F32)
        kv_part = jnp.dot(a_rows, wkv_refs[r][...], preferred_element_type=F32)
        pq = q_part if pq is None else pq + q_part
        pkv = kv_part if pkv is None else pkv + kv_part
    cos = cos_ref[...]
    sin = sin_ref[...]
    heads = pq.shape[1]
    q_scale = LOG2E * HD**-0.5
    turned = pq * jnp.tile(cos, (1, heads // 128)) + swap_halves(pq) * jnp.tile(sin, (1, heads // 128))
    send_ref[0, :, :heads] = (turned * q_scale).astype(BF)
    lane = lax.broadcasted_iota(jnp.int32, pkv.shape, 1)
    turned_kv = jnp.where(lane < HD, pkv * cos + swap_halves(pkv) * sin, pkv)
    send_ref[0, :, heads:] = turned_kv.astype(BF)


def project(places, x, gain, cos, sin, parts):
    rows, width = x.shape
    count = len(parts)
    heads = width // count
    out_width = heads + 2 * HD
    depth = parts[0].shape[0]
    first_kv = width // (2 * HD)
    return pl.pallas_call(
        functools.partial(project_kernel, count=count),
        grid_spec=pltpu.PrefetchScalarGridSpec(
            num_scalar_prefetch=1,
            grid=(count,),
            in_specs=[
                pl.BlockSpec((rows, width), lambda d, p: (0, 0)),
                pl.BlockSpec((1, width), lambda d, p: (0, 0)),
                pl.BlockSpec((rows, 128), lambda d, p: (0, 0)),
                pl.BlockSpec((rows, 128), lambda d, p: (0, 0)),
            ]
            + [pl.BlockSpec((depth, heads), lambda d, p: (0, d))] * count
            + [pl.BlockSpec((depth, 2 * HD), lambda d, p: (0, first_kv + d // 2))] * count,
            out_specs=[
                pl.BlockSpec((1, rows, out_width), lambda d, p: (d, 0, 0)),
                pl.BlockSpec((rows, width), lambda d, p: (0, 0)),
                pl.BlockSpec((rows, 1), lambda d, p: (0, 0)),
            ],
            scratch_shapes=[pltpu.VMEM((count, rows, width // count), BF)],
        ),
        out_shape=[
            jax.ShapeDtypeStruct((count, rows, out_width), BF),
            jax.ShapeDtypeStruct((rows, width), BF),
            jax.ShapeDtypeStruct((rows, 1), F32),
        ],
        compiler_params=pltpu.CompilerParams(vmem_limit_bytes=48 * 2**20),
        cost_estimate=SHORT,
        name="project",
    )(places, x, gain, cos, sin, *parts, *parts)


def out_proj_kernel(place_ref, attn_ref, x_ref, gain_ref, *refs, count):
    parts, (resid_ref, inv_ref, inner_ref) = refs[:count], refs[count:]
    width = x_ref.shape[1]
    tile = 512
    square = None
    for begin in range(0, width, tile):
        cols = slice(begin, begin + tile)
        total = x_ref[:, cols].astype(F32)
        for r in range(count):
            total = total + jnp.dot(attn_ref[place_ref[r]], parts[r][:, cols], preferred_element_type=F32)
        resid_ref[:, cols] = total
        part = jnp.sum(total * total, axis=-1, keepdims=True)
        square = part if square is None else square + part
    inv = lax.rsqrt(square / width + EPSILON)
    inv_ref[...] = inv
    inner_ref[...] = (resid_ref[...] * inv * gain_ref[...]).astype(BF)


def out_proj(places, attn, x, gain, parts):
    count, rows, share = attn.shape
    width = x.shape[1]
    step = rows // 2
    line = pl.BlockSpec((step, width), lambda i, p: (i, 0))
    return pl.pallas_call(
        functools.partial(out_proj_kernel, count=count),
        grid_spec=pltpu.PrefetchScalarGridSpec(
            num_scalar_prefetch=1,
            grid=(rows // step,),
            in_specs=[
                pl.BlockSpec((count, step, share), lambda i, p: (0, i, 0)),
                line,
                pl.BlockSpec((1, width), lambda i, p: (0, 0)),
            ]
            + [pl.BlockSpec((share, width), lambda i, p: (0, 0))] * count,
            out_specs=[line, pl.BlockSpec((step, 1), lambda i, p: (i, 0)), line],
        ),
        out_shape=[
            jax.ShapeDtypeStruct((rows, width), F32),
            jax.ShapeDtypeStruct((rows, 1), F32),
            jax.ShapeDtypeStruct((rows, width), BF),
        ],
        compiler_params=pltpu.CompilerParams(vmem_limit_bytes=56 * 2**20),
        cost_estimate=SHORT,
        name="out_proj",
    )(places, attn, x, gain, *parts)


def resid_back_kernel(place_ref, db_ref, first_ref, passed_ref, resid_ref, inv_ref, gain_ref, dy_ref, *refs, count):
    parts, (d_resid_ref, branch_ref, send_ref) = refs[:count], refs[count:]
    d_inner = db_ref[...].astype(F32) + first_ref[...].astype(F32) + passed_ref[...].astype(F32)
    resid = resid_ref[...]
    inv = inv_ref[...]
    scaled = d_inner * gain_ref[...]
    inner_mean = jnp.mean(scaled * resid, axis=-1, keepdims=True)
    d_resid = dy_ref[...].astype(F32) + inv * scaled - resid * (inv * inv * inv * inner_mean)
    d_resid_ref[...] = d_resid
    branch = d_resid.astype(BF)
    branch_ref[...] = branch
    for r in range(count):
        d_attn = lax.dot_general(branch, parts[r][...], NT, preferred_element_type=F32)
        send_ref[place_ref[r]] = d_attn.astype(BF)


def resid_back(places, db_own, db_first, db_passed, resid, inv, gain, dy, parts):
    rows, width = resid.shape
    count = len(parts)
    share = parts[0].shape[0]
    step = rows // 2
    line = pl.BlockSpec((step, width), lambda i, p: (i, 0))
    return pl.pallas_call(
        functools.partial(resid_back_kernel, count=count),
        grid_spec=pltpu.PrefetchScalarGridSpec(
            num_scalar_prefetch=1,
            grid=(rows // step,),
            in_specs=[line, line, line, line]
            + [pl.BlockSpec((step, 1), lambda i, p: (i, 0)), pl.BlockSpec((1, width), lambda i, p: (0, 0)), line]
            + [pl.BlockSpec((share, width), lambda i, p: (0, 0))] * count,
            out_specs=[line, line, pl.BlockSpec((count, step, share), lambda i, p: (0, i, 0))],
        ),
        out_shape=[
            jax.ShapeDtypeStruct((rows, width), F32),
            jax.ShapeDtypeStruct((rows, width), BF),
            jax.ShapeDtypeStruct((count, rows, share), BF),
        ],
        compiler_params=pltpu.CompilerParams(vmem_limit_bytes=56 * 2**20),
        cost_estimate=SHORT,
        name="resid_back",
    )(places, db_own, db_first, db_passed, resid, inv, gain, dy, *parts)


def in_back_kernel(place_ref, back_ref, x_ref, inv_ref, gain_ref, d_resid_ref, *refs, count):
    parts, (out_ref, mixed, d_scr) = refs[:count], refs[count:]
    devices, _, width = back_ref.shape
    heads = width - 2 * HD
    for d in range(devices):
        mixed[:, d * heads : (d + 1) * heads] = back_ref[d, :, :heads]
    base = devices * heads
    for g in range(KV):
        pair = back_ref[2 * g, :, heads:].astype(F32) + back_ref[2 * g + 1, :, heads:].astype(F32)
        mixed[:, base + 2 * g * HD : base + 2 * (g + 1) * HD] = pair.astype(BF)
    for r in range(count):
        d_scr[place_ref[r]] = lax.dot_general(mixed[...], parts[r][...], NT, preferred_element_type=F32)
    inv = inv_ref[...]
    share = d_scr.shape[2]
    inner = None
    for c in range(count):
        cols = slice(c * share, (c + 1) * share)
        part = jnp.sum(d_scr[c] * gain_ref[:, cols] * x_ref[:, cols].astype(F32), axis=-1, keepdims=True)
        inner = part if inner is None else inner + part
    factor = inv * inv * inv * (inner / (count * share))
    for c in range(count):
        cols = slice(c * share, (c + 1) * share)
        through = inv * (d_scr[c] * gain_ref[:, cols]) - x_ref[:, cols].astype(F32) * factor
        out_ref[:, cols] = (d_resid_ref[:, cols] + through).astype(BF)


def in_back(places, back, x, inv, gain, d_resid, parts):
    rows, width = x.shape
    count = len(parts)
    share, columns = parts[0].shape
    step = rows // 2
    line = pl.BlockSpec((step, width), lambda i, p: (i, 0))
    return pl.pallas_call(
        functools.partial(in_back_kernel, count=count),
        grid_spec=pltpu.PrefetchScalarGridSpec(
            num_scalar_prefetch=1,
            grid=(rows // step,),
            in_specs=[
                pl.BlockSpec((count, step, back.shape[2]), lambda i, p: (0, i, 0)),
                line,
                pl.BlockSpec((step, 1), lambda i, p: (i, 0)),
                pl.BlockSpec((1, width), lambda i, p: (0, 0)),
                line,
            ]
            + [pl.BlockSpec((share, columns), lambda i, p: (0, 0))] * count,
            out_specs=line,
            scratch_shapes=[pltpu.VMEM((step, columns), BF), pltpu.VMEM((count, step, share), F32)],
        ),
        out_shape=jax.ShapeDtypeStruct((rows, width), BF),
        compiler_params=pltpu.CompilerParams(vmem_limit_bytes=56 * 2**20),
        cost_estimate=SHORT,
        name="in_back",
    )(places, back, x, inv, gain, d_resid, *parts)


def grad_wo_kernel(core_ref, keep_ref, give_ref, branch_ref, keep_out, give_out):
    branch = branch_ref[...]
    keep_out[0] = lax.dot_general(keep_ref[0], branch, TN, preferred_element_type=F32).astype(BF)
    give_out[0] = lax.dot_general(give_ref[0], branch, TN, preferred_element_type=F32).astype(BF)


def grad_wo(core, attn, branch):
    devices, rows, share = attn.shape
    width = branch.shape[1]
    out = pl.BlockSpec((1, share, width), lambda c, core: (c, 0, 0))
    return pl.pallas_call(
        grad_wo_kernel,
        grid_spec=pltpu.PrefetchScalarGridSpec(
            num_scalar_prefetch=1,
            grid=(devices // 2,),
            in_specs=[
                pl.BlockSpec((1, rows, share), lambda c, core: (2 * c + core[0], 0, 0)),
                pl.BlockSpec((1, rows, share), lambda c, core: (2 * c + 1 - core[0], 0, 0)),
                pl.BlockSpec((rows, width), lambda c, core: (0, 0)),
            ],
            out_specs=[out, out],
        ),
        out_shape=[jax.ShapeDtypeStruct((devices // 2, share, width), BF)] * 2,
        compiler_params=pltpu.CompilerParams(vmem_limit_bytes=48 * 2**20),
        cost_estimate=SHORT,
        name="grad_wo",
    )(core.reshape(1), attn, attn, branch)


def grad_dn_kernel(core_ref, *refs, count):
    left, right, (keep_out, give_out) = refs[:count], refs[count : 2 * count], refs[2 * count :]
    total = None
    for r in range(count):
        part = lax.dot_general(left[r][...], right[r][...], TN, preferred_element_type=F32)
        total = part if total is None else total + part
    half = total.shape[0] // 2
    total = total.astype(BF)
    low = core_ref[0] == 0
    keep_out[...] = jnp.where(low, total[:half], total[half:])
    give_out[...] = jnp.where(low, total[half:], total[:half])


def grad_dn(core, hid_rows, dy_rows):
    count = len(hid_rows)
    tokens, hidden = hid_rows[0].shape
    width = dy_rows[0].shape[1]
    tile = 512
    out = pl.BlockSpec((hidden // 2, tile), lambda i, core: (0, i))
    return pl.pallas_call(
        functools.partial(grad_dn_kernel, count=count),
        grid_spec=pltpu.PrefetchScalarGridSpec(
            num_scalar_prefetch=1,
            grid=(width // tile,),
            in_specs=[pl.BlockSpec((tokens, hidden), lambda i, core: (0, 0))] * count
            + [pl.BlockSpec((tokens, tile), lambda i, core: (0, i))] * count,
            out_specs=[out, out],
        ),
        out_shape=[jax.ShapeDtypeStruct((hidden // 2, width), BF)] * 2,
        compiler_params=pltpu.CompilerParams(vmem_limit_bytes=56 * 2**20),
        cost_estimate=SHORT,
        name="grad_dn",
    )(core.reshape(1), *hid_rows, *dy_rows)


def attend_kernel(zeros_ref, q_ref, kv_ref, *refs, heads, start, stop):
    o_ref, send_ref, lse_ref, k_scr, v_scr, acc_ref, max_ref = refs[-7:]
    block = pl.program_id(0) + start
    zeros = zeros_ref[0]
    size = q_ref.shape[0]

    @pl.when(block == start)
    def _():
        for part in range(stop):
            rows = slice(part * size, (part + 1) * size)
            both = kv_ref[rows, :].astype(F32)
            lane = lax.broadcasted_iota(jnp.int32, both.shape, 1)
            k_scr[rows, :] = kv_ref[rows, :HD]
            v_scr[rows, :] = jnp.where(lane < HD, pltpu.roll(both, HD, 1), 1.0).astype(BF)

    first_row = block * size
    lowest = jnp.where(first_row >= zeros, zeros // size, 0)
    acc_ref[...] = jnp.zeros_like(acc_ref)
    max_ref[...] = jnp.full_like(max_ref, MASKED)
    q_heads = [q_ref[:, h * HD : (h + 1) * HD] for h in range(heads)]

    def step(index, masked):
        first_key = pl.multiple_of(index * size, size)
        keys = k_scr[pl.ds(first_key, size), :]
        values = v_scr[pl.ds(first_key, size), :]
        if masked:
            row = first_row + lax.broadcasted_iota(jnp.int32, (size, size), 0)
            col = first_key + lax.broadcasted_iota(jnp.int32, (size, size), 1)
            begin = jnp.where(row >= zeros, zeros, 0)
            refused = (col > row) | (col < begin)

        def score(h):
            return lax.dot_general(q_heads[h], keys, NT, preferred_element_type=F32)

        upcoming = score(0)
        for h in range(heads):
            scores = upcoming
            if h + 1 < heads:
                upcoming = score(h + 1)
            if masked:
                scores = jnp.where(refused, MASKED, scores)
            old_max = max_ref[h]
            new_max = jnp.maximum(old_max, jnp.max(scores, axis=-1, keepdims=True))
            weights = jnp.exp2(scores - jnp.tile(new_max, (1, size // 128)))
            shrink = jnp.exp2(old_max - new_max)
            acc_ref[h] = acc_ref[h] * shrink + jnp.dot(weights.astype(BF), values, preferred_element_type=F32)
            max_ref[h] = new_max

    def visit(index, carry):
        first_key = index * size
        mixed = (index == block) | ((first_row + size > zeros) & (first_key < zeros))

        @pl.when(mixed)
        def _():
            step(index, True)

        @pl.when(jnp.logical_not(mixed))
        def _():
            step(index, False)

        return carry

    lax.fori_loop(lowest, block + 1, visit, 0)
    for h in range(heads):
        acc = acc_ref[h]
        total = acc[:, HD : HD + 1]
        out = acc[:, :HD] / total
        o_ref[:, h * HD : (h + 1) * HD] = out
        send_ref[0, :, h * HD : (h + 1) * HD] = out.astype(BF)
        lse = max_ref[h] + jnp.log2(total)
        lse_ref[0, h : h + 1, :] = jnp.transpose(lse)[:1]


def attend(zeros, qkv, start, stop, before=None):
    length, width = qkv.shape
    q_width = width - 2 * HD
    heads = q_width // HD
    size = BLOCK
    blocks = length // size
    before = () if before is None else before
    return pl.pallas_call(
        functools.partial(attend_kernel, heads=heads, start=start, stop=stop),
        grid_spec=pltpu.PrefetchScalarGridSpec(
            num_scalar_prefetch=1,
            grid=(stop - start,),
            in_specs=[
                pl.BlockSpec((size, q_width), lambda i, z: (i + start, 0)),
                pl.BlockSpec((length, 2 * HD), lambda i, z: (0, q_width // (2 * HD))),
            ]
            + [pl.BlockSpec(memory_space=pl.ANY)] * len(before),
            out_specs=[
                pl.BlockSpec((size, q_width), lambda i, z: (i + start, 0)),
                pl.BlockSpec((1, size, q_width), lambda i, z: (i + start, 0, 0)),
                pl.BlockSpec((1, heads, size), lambda i, z: (i + start, 0, 0)),
            ],
            scratch_shapes=[
                pltpu.VMEM((length, HD), BF),
                pltpu.VMEM((length, 2 * HD), BF),
                pltpu.VMEM((heads, size, 2 * HD), F32),
                pltpu.VMEM((heads, size, 128), F32),
            ],
        ),
        out_shape=[
            jax.ShapeDtypeStruct((length, q_width), F32),
            jax.ShapeDtypeStruct((blocks, size, q_width), BF),
            jax.ShapeDtypeStruct((blocks, heads, size), F32),
        ],
        input_output_aliases={3 + i: i for i in range(len(before))},
        compiler_params=pltpu.CompilerParams(vmem_limit_bytes=48 * 2**20),
        cost_estimate=SHORT,
        name="attend",
    )(zeros, qkv, qkv, *before)


def attend_back_kernel(
    zeros_ref, q_ref, kv_ref, do_ref, lse_ref, cos_ref, sin_ref, extra_ref, *refs, heads, start
):
    send_ref, dq_acc, delta_ref, q_scr, do_scr = refs[-5:]
    block = pl.program_id(0) + start
    zeros = zeros_ref[0]
    size = kv_ref.shape[0]
    length = q_ref.shape[0]
    blocks = length // size

    @pl.when(block == start)
    def _():
        if start == 0:
            dq_acc[...] = jnp.zeros_like(dq_acc)
        else:
            dq_acc[...] = refs[0][...]
            delta_ref[...] = extra_ref[...]
        for part in range(start, blocks):
            rows = slice(part * size, (part + 1) * size)
            if start == 0:
                product = jnp.transpose(do_ref[rows, :].astype(F32) * extra_ref[rows, :])
            for h in range(heads):
                cols = slice(h * HD, (h + 1) * HD)
                q_scr[h, rows, :] = q_ref[rows, cols]
                do_scr[h, rows, :] = do_ref[rows, cols]
                if start == 0:
                    delta_ref[part, h : h + 1, :] = jnp.sum(product[cols], axis=0, keepdims=True)

    first_key = block * size
    both = kv_ref[...]
    keys = both[:, :HD]
    values = both[:, HD:]
    keys_t = jnp.transpose(keys.astype(F32)).astype(BF)
    highest = jnp.where(first_key + size <= zeros, jnp.minimum((zeros + size - 1) // size, blocks), blocks)

    def step(index, carry, masked):
        first_row = pl.multiple_of(index * size, size)
        span = pl.ds(first_row, size)
        if masked:
            col = first_key + lax.broadcasted_iota(jnp.int32, (size, size), 0)
            row = first_row + lax.broadcasted_iota(jnp.int32, (size, size), 1)
            begin = jnp.where(row >= zeros, zeros, 0)
            refused = (col > row) | (col < begin)

        def products(h):
            q_rows = q_scr[h, span, :]
            do_rows = do_scr[h, span, :]
            scores = lax.dot_general(keys, q_rows, NT, preferred_element_type=F32)
            d_prob = lax.dot_general(values, do_rows, NT, preferred_element_type=F32)
            return q_rows, do_rows, scores, d_prob

        upcoming = products(0)
        dk_sum, dv_sum = carry
        for h in range(heads):
            q_rows, do_rows, scores, d_prob = upcoming
            if h + 1 < heads:
                upcoming = products(h + 1)
            shifted = scores - lse_ref[index, h : h + 1, :]
            if masked:
                shifted = jnp.where(refused, MASKED, shifted)
            prob = jnp.exp2(shifted)
            d_score = (prob * (d_prob - delta_ref[index, h : h + 1, :])).astype(BF)
            dv_sum = dv_sum + jnp.dot(prob.astype(BF), do_rows, preferred_element_type=F32)
            dk_sum = dk_sum + jnp.dot(d_score, q_rows, preferred_element_type=F32)
            dq_acc[h * HD : (h + 1) * HD, span] += jnp.dot(keys_t, d_score, preferred_element_type=F32)
        return dk_sum, dv_sum

    def visit(index, carry):
        first_row = index * size
        mixed = (index == block) | ((first_row + size > zeros) & (first_key < zeros))
        return lax.cond(
            mixed,
            lambda c: step(index, c, True),
            lambda c: step(index, c, False),
            carry,
        )

    zero = jnp.zeros((size, HD), F32)
    dk_sum, dv_sum = lax.fori_loop(block, highest, visit, (zero, zero))
    q_width = heads * HD
    done = pl.ds(pl.multiple_of(first_key, size), size)
    cos = cos_ref[...]
    sin = sin_ref[...]
    dq = jnp.transpose(dq_acc[:, done]) * HD**-0.5
    dq = dq * jnp.tile(cos, (1, q_width // 128)) - swap_halves(dq) * jnp.tile(sin, (1, q_width // 128))
    send_ref[0, :, :q_width] = dq.astype(BF)
    dkv = jnp.concatenate([dk_sum * (1.0 / LOG2E), dv_sum], axis=1)
    lane = lax.broadcasted_iota(jnp.int32, dkv.shape, 1)
    send_ref[0, :, q_width:] = jnp.where(lane < HD, dkv * cos - swap_halves(dkv) * sin, dkv).astype(BF)


def attend_back(zeros, qkv, d_out, lse, cos, sin, start, stop, out=None, before=None):
    length, width = qkv.shape
    q_width = width - 2 * HD
    heads = q_width // HD
    size = BLOCK
    blocks = length // size
    whole = lambda *shape: pl.BlockSpec(shape, lambda j, z: (0,) * len(shape))
    if before is None:
        operands = (out,)
        specs = [whole(length, q_width)]
        aliases = {}
    else:
        send, d_query, delta = before
        operands = (delta, d_query, send)
        specs = [whole(blocks, heads, size), whole(q_width, length), pl.BlockSpec(memory_space=pl.ANY)]
        aliases = {9: 0}
    return pl.pallas_call(
        functools.partial(attend_back_kernel, heads=heads, start=start),
        grid_spec=pltpu.PrefetchScalarGridSpec(
            num_scalar_prefetch=1,
            grid=(stop - start,),
            in_specs=[
                whole(length, q_width),
                pl.BlockSpec((size, 2 * HD), lambda j, z: (j + start, q_width // (2 * HD))),
                whole(length, q_width),
                whole(blocks, heads, size),
                pl.BlockSpec((size, 128), lambda j, z: (j + start, 0)),
                pl.BlockSpec((size, 128), lambda j, z: (j + start, 0)),
            ]
            + specs,
            out_specs=[
                pl.BlockSpec((1, size, width), lambda j, z: (j + start, 0, 0)),
                whole(q_width, length),
                whole(blocks, heads, size),
            ],
            scratch_shapes=[
                pltpu.VMEM((heads, length, HD), BF),
                pltpu.VMEM((heads, length, HD), BF),
            ],
        ),
        out_shape=[
            jax.ShapeDtypeStruct((blocks, size, width), BF),
            jax.ShapeDtypeStruct((q_width, length), F32),
            jax.ShapeDtypeStruct((blocks, heads, size), F32),
        ],
        input_output_aliases=aliases,
        compiler_params=pltpu.CompilerParams(vmem_limit_bytes=58 * 2**20),
        cost_estimate=SHORT,
        name="attend_back",
    )(zeros, qkv, qkv, d_out, lse, cos, sin, *operands)


def turn_tables(positions):
    cosine, sine = rope_tables(positions, HD)
    return jnp.concatenate([cosine] * 4, axis=1), jnp.concatenate([-sine, sine, -sine, sine], axis=1)


def fast_body(tokens, segment_ids, selected, cotangent, w_qkv, w_out, w_gate_up, w_down, g_attn, g_mlp):
    _, rows, width = tokens.shape
    devices = 2 * CHIPS
    me = lax.axis_index("sp")
    core = me & 1
    planes = lax.axis_size("dp")
    share = width // devices
    kv_width = KV * HD
    first_mask, second_mask = rel_masks(core)
    other = me ^ 1
    chip = me // 2
    place_list = [me, me ^ first_mask, me ^ second_mask, me ^ 6]
    place_list += [other, other ^ second_mask, other ^ first_mask, other ^ 6]
    places = jnp.stack(place_list)
    hidden_chip = 2 * w_down.shape[0]
    quarter = share // planes
    plane = lax.axis_index("dp")
    length = devices * rows
    blocks = length // BLOCK

    count = jnp.sum((segment_ids == 0).astype(F32))
    vectors = jnp.stack([g_attn.astype(F32), g_mlp.astype(F32)] + [jnp.full((share,), count)] * 6)
    paired = [w_qkv[:, :width]]
    for head in range(KV):
        paired.append(w_qkv[:, width + head * HD : width + (head + 1) * HD])
        paired.append(w_qkv[:, width + kv_width + head * HD : width + kv_width + (head + 1) * HD])
    qkv_own = jnp.concatenate(paired, axis=1)
    gu_rows = lax.dynamic_slice_in_dim(w_gate_up, plane * quarter, quarter, 0)
    gu_send = []
    for place in range(CHIPS):
        for begin in (place * hidden_chip, (CHIPS + place) * hidden_chip):
            gu_send.append(gu_rows[:, begin : begin + hidden_chip])
    gu_send = jnp.stack([jnp.concatenate(gu_send[2 * c : 2 * c + 2], axis=1) for c in range(CHIPS)])
    vectors = gather_vectors(vectors, me)
    vectors, qkv_own, gu_send = fence(vectors, qkv_own, gu_send)
    qkv_first = send_first(qkv_own)
    attn_gain = vectors[0:1]
    mlp_gain = vectors[1:2]
    zeros = jnp.sum(vectors[2].reshape(devices, share)[:, 0]).astype(jnp.int32)
    zeros_one = zeros.reshape(1)
    local_pos = me * rows + jnp.arange(rows, dtype=jnp.int32) - segment_ids.reshape(rows) * zeros
    cos, sin = turn_tables(local_pos)
    dy = (cotangent * selected[:, :, None].astype(BF)).reshape(rows, width)
    qkv_own, qkv_first, cos, sin = fence(qkv_own, qkv_first, cos, sin)
    qkv_second = send_second(qkv_own)
    qkv_theirs = [send_sibling(qkv_own), send_sibling(qkv_first)]
    all_places = jnp.arange(length, dtype=jnp.int32)
    cos_all, sin_all = turn_tables(all_places - jnp.where(all_places >= zeros, zeros, 0))
    qkv_first, qkv_second, cos_all, sin_all, *qkv_theirs = fence(qkv_first, qkv_second, cos_all, sin_all, *qkv_theirs)
    qkv_far = send_second(qkv_first)
    qkv_theirs.append(send_sibling(qkv_second))
    qkv_far, dy, *qkv_theirs = fence(qkv_far, dy, *qkv_theirs)
    qkv_theirs.append(send_sibling(qkv_far))
    qkv_parts = [qkv_own, qkv_first, qkv_second, qkv_far] + qkv_theirs
    x_bf = tokens.reshape(rows, width)
    x_bf, w_out, gu_send, *qkv_parts = fence(x_bf, w_out, gu_send, *qkv_parts)
    out_first = send_first(w_out)
    gu_part = lax.all_to_all(gu_send, "sp", 0, 0, axis_index_groups=SAME_CORE, tiled=True)
    qkv_send, normed, inv_one = project(places, x_bf, attn_gain, cos, sin, qkv_parts)
    qkv_send, out_first = fence(qkv_send, out_first)
    gu_mine = lax.all_gather(after(gu_part, qkv_send), "dp", axis=0, tiled=False)
    gu_mine = lax.all_gather(after(gu_part, qkv_send), "dp", axis=0, tiled=False)
    down_theirs = send_sibling(w_down)
    w_dn = jnp.where(
        core == 0, jnp.concatenate([w_down, down_theirs], axis=0), jnp.concatenate([down_theirs, w_down], axis=0)
    )
    qkv_heads = lax.all_to_all(qkv_send, "sp", 0, 0, tiled=True).reshape(length, qkv_send.shape[2])

    cuts = (0, (5 * blocks) // 8, (7 * blocks) // 8, blocks)
    qkv_heads, w_dn, out_first = fence(qkv_heads, w_dn, out_first)
    out_second = send_second(after(w_out, qkv_heads))
    dy_first = send_first(after(dy, qkv_heads))
    fwd = attend(zeros_one, qkv_heads, cuts[0], cuts[1])
    qkv_heads, out_second, dy_first, out_first, dy, *fwd = fence(qkv_heads, out_second, dy_first, out_first, dy, *fwd)
    out_far = send_second(out_first)
    dy_second = send_second(dy)
    fwd = attend(zeros_one, qkv_heads, cuts[1], cuts[2], fwd)
    qkv_heads, out_far, dy_second, dy_first, *fwd = fence(qkv_heads, out_far, dy_second, dy_first, *fwd)
    dy_far = send_second(dy_first)
    gu_theirs = send_sibling(after(gu_mine, fwd[2]))
    out_heads, out_send, lse = attend(zeros_one, qkv_heads, cuts[2], cuts[3], fwd)
    out_parts = [w_out, out_first, out_second, out_far]
    out_parts = out_parts + [send_sibling(part) for part in out_parts]
    out_send, gu_mine, gu_theirs = fence(out_send, gu_mine, gu_theirs)
    attn_tok = lax.all_to_all(out_send, "sp", 0, 0, tiled=True)
    w_gu = join(core, gu_mine, gu_theirs)
    attn_tok, w_gu, dy_far, *out_parts = fence(attn_tok, w_gu, dy_far, *out_parts)
    residual, inv_two, inner = out_proj(places, attn_tok, x_bf, mlp_gain, out_parts)

    b_first = send_first(inner)
    own = ffn(inner, dy, w_gu, w_dn)
    inner, b_first, *own = fence(inner, b_first, *own)
    b_second = send_second(inner)
    first = ffn(b_first, dy_first, w_gu, w_dn)
    b_first, b_second, *first = fence(b_first, b_second, *first)
    b_far = send_second(b_first)
    second = ffn(b_second, dy_second, w_gu, w_dn)
    b_far, db_first, *second = fence(b_far, first[3], *second)
    db_got_first = send_first(db_first)
    far = ffn(b_far, dy_far, w_gu, w_dn)
    db_got_first, db_far, *hid_rows = fence(db_got_first, far[3], own[0], first[0], second[0], far[0])

    db_got_far = send_first(db_far)
    dn_keep, dn_give = grad_dn(core, hid_rows, [dy, dy_first, dy_second, dy_far])
    db_got_far, dn_keep, dn_give = fence(db_got_far, dn_keep, dn_give)
    db_pass = (second[3].astype(F32) + db_got_far.astype(F32)).astype(BF)
    b_own, db_pass, dn_give = fence(inner, db_pass, dn_give)
    db_passed = send_second(db_pass)
    dn_got = send_sibling(dn_give)
    gu_keep, gu_give = grad_gu(
        core,
        [b_own, b_first, b_second, b_far],
        [own[1], first[1], second[1], far[1]],
        [own[2], first[2], second[2], far[2]],
        share,
        planes,
    )
    db_passed, dn_got, gu_keep, gu_give = fence(db_passed, dn_got, gu_keep, gu_give)
    dn_parts = [part.reshape(planes, dn_keep.shape[0] // planes, width) for part in (dn_keep, dn_got)]
    dn_moves = line_scatter_sends(dn_parts, None, 1, 0)
    db_passed, gu_give, *dn_moves = fence(db_passed, gu_give, *dn_moves)
    gu_got = send_sibling(gu_give)
    dn_moves = line_scatter_move(dn_moves, 1)
    d_resid, d_branch, d_send = resid_back(
        places, own[3], db_got_first, db_passed, residual, inv_two, mlp_gain, dy, out_parts
    )
    d_send, d_branch, gu_got, *dn_moves = fence(d_send, d_branch, gu_got, *dn_moves)
    gu_sum = (gu_keep.astype(F32) + gu_got.astype(F32)).astype(BF)
    gu_z = lax.psum_scatter(
        gu_sum.reshape(planes * CHIPS * quarter, 2 * hidden_chip), "dp", scatter_dimension=0, tiled=True
    )
    gu_z = gu_z.reshape(CHIPS, quarter, 2 * hidden_chip)
    d_heads = lax.all_to_all(d_send, "sp", 0, 0, tiled=True).reshape(length, share)
    dn_moves = line_scatter_sends(dn_parts, dn_moves, 2, 0)
    dn_moves = line_scatter_move(dn_moves, 2)
    wo_keep, wo_give = grad_wo(core, attn_tok, d_branch)
    d_heads, wo_keep, wo_give, normed = fence(d_heads, wo_keep, wo_give, normed)

    def back_call(heads, start, stop, **kwargs):
        return attend_back(zeros_one, qkv_heads, heads, lse, cos_all, sin_all, start, stop, **kwargs)

    turns = (0, blocks // 8, blocks // 4, (3 * blocks) // 8, blocks)
    wo_got = send_sibling(wo_give)
    a_first = send_first(normed)
    bwd = back_call(d_heads, turns[0], turns[1], out=out_heads)
    d_heads, a_first, wo_got, normed, *moves = fence(d_heads, a_first, wo_got, normed, *dn_moves, *bwd)
    dn_moves, bwd = moves[:2], moves[2:]

    dn_moves = line_scatter_sends(dn_parts, dn_moves, 3, 0)
    d_heads, normed, a_first, *dn_moves = fence(d_heads, normed, a_first, *dn_moves)
    a_second = send_second(normed)
    a_theirs = [send_sibling(normed), send_sibling(a_first)]
    dn_moves = line_scatter_move(dn_moves, 3)
    bwd = back_call(d_heads, turns[1], turns[2], before=bwd)
    d_heads, gu_z, a_second, *moves = fence(d_heads, gu_z, a_second, *a_theirs, *dn_moves, *bwd)
    a_theirs, dn_moves, bwd = moves[:2], moves[2:4], moves[4:]

    def wo_part(place):
        return pick(wo_keep, place).astype(F32) + pick(wo_got, place).astype(F32)

    dn_z = line_scatter_end(dn_parts, dn_moves, 0)
    d_heads, dn_z, gu_z, a_second = fence(d_heads, dn_z, gu_z, a_second)
    dn_steps = [(dn_z, dn_z), line_gather_move((dn_z, dn_z), 1)]
    gu_z = lax.all_to_all(gu_z, "sp", 0, 0, axis_index_groups=SAME_CORE, tiled=True)
    a_theirs.append(send_sibling(a_second))
    bwd = back_call(d_heads, turns[2], turns[3], before=bwd)
    d_heads, gu_z, a_first, *moves = fence(d_heads, gu_z, a_first, *a_theirs, *dn_steps[-1], *bwd)
    a_theirs, dn_steps[-1], bwd = moves[:3], tuple(moves[3:5]), moves[5:]

    wo_first = wo_part(chip ^ (first_mask // 2)).astype(BF)
    wo_far = wo_part(chip ^ 3).astype(BF)
    d_heads, gu_z, a_first, wo_first, wo_far = fence(d_heads, gu_z, a_first, wo_first, wo_far)
    gu_all = lax.all_gather(gu_z, "dp", axis=0, tiled=False)
    a_far = send_second(a_first)
    wo_far = send_first(wo_far)
    wo_first = send_first(wo_first)
    dn_steps.append(line_gather_move(dn_steps[-1], 2))
    bwd = back_call(d_heads, turns[3], turns[4], before=bwd)
    wo_pass = (wo_part(chip ^ (second_mask // 2)) + wo_far.astype(F32)).astype(BF)
    dp_heads, wo_first, wo_pass, a_far, *moves = fence(bwd[0], wo_first, wo_pass, a_far, *dn_steps[-1])
    dn_steps[-1] = tuple(moves)

    wo_passed = send_second(wo_pass)
    a_theirs.append(send_sibling(a_far))
    dn_steps.append(line_gather_move(dn_steps[-1], 3))
    back = lax.all_to_all(dp_heads, "sp", 0, 0, tiled=True)
    grad_wq = grad_qkv(places, [normed, a_first, a_second, a_far] + list(a_theirs), dp_heads, planes)
    wo_rows = (wo_part(chip) + wo_first.astype(F32) + wo_passed.astype(F32)).astype(BF)
    split = grad_wq.shape[2]
    last_parts = [jnp.concatenate([grad_wq, wo_rows.reshape(planes, quarter, width)], axis=2)]
    y_far, y_first = far[4], first[4]
    moves = None
    for step in range(1, planes):
        moves = line_scatter_sends(last_parts, moves, step, 0)
        y_far, y_first, *moves = fence(y_far, y_first, *moves)
        moves = line_scatter_move(moves, step)
        if step == 1:
            y_got_far = send_first(y_far)
            moves = fence(*moves, *dn_steps[-1])
            moves, dn_steps[-1] = moves[:2], tuple(moves[2:])
        elif step == 2:
            y_got_first = send_first(y_first)
        moves = fence(*moves)
    last_z = line_scatter_end(last_parts, moves, 0)
    wq_z = last_z[:, :split].reshape(quarter, devices, split // devices).transpose(1, 0, 2)
    wq_z, wo_z, back = fence(wq_z, last_z[:, split:], back)
    wq_z = lax.all_to_all(wq_z, "sp", 0, 0, tiled=True)
    grad_tokens = in_back(places, back, x_bf, inv_one, attn_gain, d_resid, qkv_parts).reshape(tokens.shape)
    y_pass = (second[4].astype(F32) + y_got_far.astype(F32)).astype(BF)
    last_z = jnp.concatenate([wq_z.transpose(1, 0, 2).reshape(quarter, split), wo_z], axis=1)
    last_z, grad_tokens, y_pass, y_got_first = fence(last_z, grad_tokens, y_pass, y_got_first)
    y_passed = send_second(y_pass)
    last_steps = [(last_z, last_z)]
    outs = []
    for step in range(1, planes):
        last_steps.append(line_gather_move(last_steps[-1], step))
        if step == 1:
            outs.append(spread_rows(dn_steps))
        elif step == 2:
            outs += spread(gu_all, w_gate_up, g_mlp.astype(F32).reshape(share, 1))
        if step == planes - 1:
            y_sum = own[4].astype(F32) + y_got_first.astype(F32) + y_passed.astype(F32)
            outs.append((residual + y_sum).astype(BF).reshape(tokens.shape))
        moves = fence(*last_steps[-1], *outs)
        last_steps[-1], outs = tuple(moves[:2]), list(moves[2:])
    grad_w_down, grad_w_gate_up, grad_g_mlp, output = outs
    grad_w_qkv, grad_g_attn, grad_w_out = spread_last(last_steps, w_qkv, g_attn.astype(F32).reshape(share, 1), width)
    return (
        output,
        grad_tokens,
        grad_w_qkv,
        grad_w_out,
        grad_w_gate_up,
        grad_w_down,
        grad_g_attn.reshape(share),
        grad_g_mlp.reshape(share),
    )


def solution(mesh):
    in_specs = (
        P("dp", "sp", None),
        P("dp", "sp"),
        P("dp", "sp"),
        P("dp", "sp", None),
        P("sp", None),
        P("sp", None),
        P("sp", None),
        P("sp", None),
        P("sp"),
        P("sp"),
    )
    out_specs = (
        P("dp", "sp", None),
        P("dp", "sp", None),
        P("sp", None),
        P("sp", None),
        P("sp", None),
        P("sp", None),
        P("sp"),
        P("sp"),
    )
    body = fast_body if mesh.shape["sp"] == 2 * CHIPS else general_body
    return jax.shard_map(body, mesh=mesh, in_specs=in_specs, out_specs=out_specs, check_vma=False)
```

```python
import functools
import math

import jax
import jax.numpy as jnp
from jax import lax
from jax.experimental import pallas as pl
from jax.experimental.pallas import tpu as pltpu
from jax.sharding import PartitionSpec as P

D = 2048
H = 32
KV = 4
HD = 64
FF = 5632


EPSILON = 1e-05
ROPE_BASE = 10000.0
MASKED = -1e30


def rope_tables(positions, head_size):
    half_dim = head_size // 2
    frequency = ROPE_BASE ** (-(jnp.arange(half_dim, dtype=jnp.float32) * 2.0 / head_size))
    angles = positions.astype(jnp.float32)[:, None] * frequency[None, :]
    return (jnp.cos(angles), jnp.sin(angles))


def rotate(values, cosine, sine_tab, inverse_turn):
    half_dim = values.shape[-1] // 2
    first_half = values[..., :half_dim]
    second = values[..., half_dim:]
    cos_wide = cosine[:, None, :]
    sin_wide = sine_tab[:, None, :]
    if inverse_turn:
        sin_wide = -sin_wide
    return jnp.concatenate(
        [first_half * cos_wide - second * sin_wide, second * cos_wide + first_half * sin_wide],
        axis=-1,
    )


def rms_norm(values, gain_vec):
    inverse = lax.rsqrt(jnp.mean(values * values, axis=-1, keepdims=True) + EPSILON)
    return (values * inverse * gain_vec, inverse)


def norm_back(values, inverse, gain_vec, upstream):
    scaled = upstream * gain_vec
    inner_mean = jnp.mean(scaled * values, axis=-1, keepdims=True)
    through = inverse * scaled - values * inverse**3 * inner_mean
    gain_grad = jnp.sum(upstream * values * inverse, axis=0)
    return (through, gain_grad)


def attention_inputs(flat_in, qkv_full, gain_vec, cosine, sine_tab):
    row_count = flat_in.shape[0]
    group_size = H // KV
    normed, inverse = rms_norm(flat_in, gain_vec)
    normed = normed.astype(jnp.bfloat16)
    projected = jnp.dot(normed, qkv_full, preferred_element_type=jnp.float32)
    queries = rotate(projected[:, :D].reshape(row_count, H, HD), cosine, sine_tab, False)
    key_heads = rotate(
        projected[:, D : D + KV * HD].reshape(row_count, KV, HD), cosine, sine_tab, False
    )
    value_heads = projected[:, D + KV * HD :].reshape(row_count, KV, HD)
    key_wide = jnp.broadcast_to(key_heads[:, :, None], (row_count, KV, group_size, HD)).reshape(
        row_count, D
    )
    value_wide = jnp.broadcast_to(value_heads[:, :, None], (row_count, KV, group_size, HD)).reshape(
        row_count, D
    )
    stacked = jnp.stack([queries.reshape(row_count, D), key_wide, value_wide]).astype(jnp.bfloat16)
    return (normed, inverse, stacked)


def block_mask(seg_full, position, row_begin, finish):
    row_seg = seg_full[:, row_begin:finish]
    col_seg = seg_full[:, :finish]
    same_doc = row_seg[:, :, None] == col_seg[:, None, :]
    causal = position[row_begin:finish, None] >= position[None, :finish]
    return same_doc & causal[None]


def attention_forward(queries, key_heads, value_heads, seg_full, score_scale):
    length = queries.shape[1]
    block_rows = min(512, length)
    position = jnp.arange(length, dtype=jnp.int32)
    outputs = []
    lse_parts = []
    for block_num in range(length // block_rows):
        row_begin = block_num * block_rows
        finish = row_begin + block_rows
        scores = (
            jnp.einsum(
                "sqhd,skhd->shqk",
                queries[:, row_begin:finish],
                key_heads[:, :finish],
                preferred_element_type=jnp.float32,
            )
            * score_scale
        )
        allowed = block_mask(seg_full, position, row_begin, finish)
        scores = jnp.where(allowed[:, None], scores, MASKED)
        row_max = jnp.max(scores, axis=-1, keepdims=True)
        shifted = jnp.exp(scores - row_max)
        row_total = jnp.sum(shifted, axis=-1, keepdims=True)
        softmax_w = (shifted / row_total).astype(jnp.bfloat16)
        outputs.append(
            jnp.einsum(
                "shqk,skhd->sqhd",
                softmax_w,
                value_heads[:, :finish],
                preferred_element_type=jnp.float32,
            )
        )
        lse_parts.append(row_max + jnp.log(row_total))
    return (jnp.concatenate(outputs, axis=1), jnp.concatenate(lse_parts, axis=2))


def attention_backward(queries, key_heads, value_heads, seg_full, log_sums, grad_out, score_scale):
    length = queries.shape[1]
    block_rows = min(512, length)
    position = jnp.arange(length, dtype=jnp.int32)
    grad_query = []
    grad_key = jnp.zeros(key_heads.shape, jnp.float32)
    grad_value = jnp.zeros(value_heads.shape, jnp.float32)
    for block_num in range(length // block_rows):
        row_begin = block_num * block_rows
        finish = row_begin + block_rows
        query_rows = queries[:, row_begin:finish]
        grad_rows = grad_out[:, row_begin:finish]
        key_part = key_heads[:, :finish]
        value_part = value_heads[:, :finish]
        scores = (
            jnp.einsum("sqhd,skhd->shqk", query_rows, key_part, preferred_element_type=jnp.float32)
            * score_scale
        )
        allowed = block_mask(seg_full, position, row_begin, finish)
        softmax_f = jnp.where(
            allowed[:, None], jnp.exp(scores - log_sums[:, :, row_begin:finish]), 0.0
        )
        grad_probs = jnp.einsum(
            "sqhd,skhd->shqk", grad_rows, value_part, preferred_element_type=jnp.float32
        )
        row_delta = jnp.sum(softmax_f * grad_probs, axis=-1, keepdims=True)
        grad_scores = (softmax_f * (grad_probs - row_delta)).astype(jnp.bfloat16)
        grad_query.append(
            jnp.einsum("shqk,skhd->sqhd", grad_scores, key_part, preferred_element_type=jnp.float32)
            * score_scale
        )
        grad_key = grad_key.at[:, :finish].add(
            jnp.einsum(
                "shqk,sqhd->skhd", grad_scores, query_rows, preferred_element_type=jnp.float32
            )
            * score_scale
        )
        grad_value = grad_value.at[:, :finish].add(
            jnp.einsum(
                "shqk,sqhd->skhd",
                softmax_f.astype(jnp.bfloat16),
                grad_rows,
                preferred_element_type=jnp.float32,
            )
        )
    return (jnp.concatenate(grad_query, axis=1), grad_key, grad_value)


def general_body(tokens, segment_ids, selected, cotangent, w_qkv, w_out, w_gate_up, w_down, g_attn, g_mlp):
    streams, local_len, model_dim = tokens.shape
    sp_count = lax.axis_size("sp")
    sp_index = lax.axis_index("sp")
    row_count = streams * local_len
    group_size = H // KV
    kv_width = KV * HD
    score_scale = HD ** (-0.5)
    contract = (((0,), (0,)), ((), ()))
    seg_full = lax.all_gather(segment_ids, "sp", axis=1, tiled=True)
    first_count = jnp.sum((seg_full == 0).astype(jnp.int32), axis=1, keepdims=True)
    local_pos = (
        sp_index * local_len
        + jnp.arange(local_len, dtype=jnp.int32)[None, :]
        - segment_ids * first_count
    )
    cosine, sine_tab = rope_tables(local_pos.reshape(row_count), HD)
    shards = (w_qkv, w_out, w_gate_up, w_down, g_attn, g_mlp)
    gathered = (
        lax.all_gather(shards[0], "sp", axis=0, tiled=True),
        lax.all_gather(shards[1], "sp", axis=0, tiled=True),
        lax.all_gather(shards[2], "sp", axis=0, tiled=True),
        lax.all_gather(shards[3], "sp", axis=0, tiled=True),
        lax.all_gather(shards[4], "sp", axis=0, tiled=True),
        lax.all_gather(shards[5], "sp", axis=0, tiled=True),
    )
    qkv_full, out_full, gate_up_full, down_full, attn_gain, mlp_gain = gathered
    attn_gain = attn_gain.astype(jnp.float32)
    mlp_gain = mlp_gain.astype(jnp.float32)
    flat_in = tokens.reshape(row_count, model_dim).astype(jnp.float32)
    normed, inverse_one, stacked = attention_inputs(flat_in, qkv_full, attn_gain, cosine, sine_tab)
    head_view = lax.all_to_all(
        stacked.reshape(3, streams, local_len, model_dim),
        "sp",
        split_axis=3,
        concat_axis=2,
        tiled=True,
    )
    length = head_view.shape[2]
    heads_here = head_view.shape[3] // HD
    head_shape = (streams, length, heads_here, HD)
    queries = head_view[0].reshape(head_shape)
    key_heads = head_view[1].reshape(head_shape)
    value_heads = head_view[2].reshape(head_shape)
    attn_heads, log_sums = attention_forward(queries, key_heads, value_heads, seg_full, score_scale)
    attn_send = attn_heads.astype(jnp.bfloat16).reshape(streams, length, heads_here * HD)
    attn_tok = lax.all_to_all(attn_send, "sp", split_axis=1, concat_axis=2, tiled=True).reshape(
        row_count, model_dim
    )
    branch = jnp.dot(attn_tok, out_full, preferred_element_type=jnp.float32)
    residual = flat_in + branch
    inner_f, inverse_two = rms_norm(residual, mlp_gain)
    inner_in = inner_f.astype(jnp.bfloat16)
    gate_up = jnp.dot(inner_in, gate_up_full, preferred_element_type=jnp.float32)
    gate_part = gate_up[:, :FF]
    up_part = gate_up[:, FF:]
    sigmoid_g = jax.nn.sigmoid(gate_part)
    silu_gate = gate_part * sigmoid_g
    hidden = (silu_gate * up_part).astype(jnp.bfloat16)
    result = residual + jnp.dot(hidden, down_full, preferred_element_type=jnp.float32)
    output = result.astype(jnp.bfloat16).reshape(streams, local_len, model_dim)
    qkv_back, out_back, gate_up_back, down_back, attn_gain_b, mlp_gain_b = gathered
    attn_gain_b = attn_gain_b.astype(jnp.float32)
    mlp_gain_b = mlp_gain_b.astype(jnp.float32)
    grad_y = (cotangent * selected[:, :, None].astype(jnp.bfloat16)).reshape(row_count, model_dim)
    grad_hidden = jnp.dot(grad_y, down_back.T, preferred_element_type=jnp.float32)
    silu_slope = sigmoid_g * (1.0 + gate_part * (1.0 - sigmoid_g))
    grad_both = jnp.concatenate(
        [grad_hidden * up_part * silu_slope, grad_hidden * silu_gate], axis=1
    ).astype(jnp.bfloat16)
    grad_inner = jnp.dot(grad_both, gate_up_back.T, preferred_element_type=jnp.float32)
    grad_resid, gain_two = norm_back(residual, inverse_two, mlp_gain_b, grad_inner)
    grad_resid = grad_resid + grad_y.astype(jnp.float32)
    grad_branch = grad_resid.astype(jnp.bfloat16)
    grad_attn = jnp.dot(grad_branch, out_back.T, preferred_element_type=jnp.float32).astype(
        jnp.bfloat16
    )
    grad_view = lax.all_to_all(
        grad_attn.reshape(streams, local_len, model_dim),
        "sp",
        split_axis=2,
        concat_axis=1,
        tiled=True,
    )
    grad_view = grad_view.reshape(head_shape)
    grad_q, grad_k, grad_v = attention_backward(
        queries, key_heads, value_heads, seg_full, log_sums, grad_view, score_scale
    )
    back_send = (
        jnp.stack([grad_q, grad_k, grad_v])
        .astype(jnp.bfloat16)
        .reshape(3, streams, length, heads_here * HD)
    )
    returned = lax.all_to_all(back_send, "sp", split_axis=2, concat_axis=3, tiled=True)
    returned = returned.astype(jnp.float32).reshape(3, row_count, H, HD)
    grad_pq = rotate(returned[0], cosine, sine_tab, True).reshape(row_count, model_dim)
    key_summed = jnp.sum(returned[1].reshape(row_count, KV, group_size, HD), axis=2)
    grad_pk = rotate(key_summed, cosine, sine_tab, True).reshape(row_count, kv_width)
    grad_pv = jnp.sum(returned[2].reshape(row_count, KV, group_size, HD), axis=2).reshape(
        row_count, kv_width
    )
    grad_mixed = jnp.concatenate(
        [grad_pq.astype(jnp.bfloat16), grad_pk.astype(jnp.bfloat16), grad_pv.astype(jnp.bfloat16)],
        axis=1,
    )
    grad_normed = jnp.dot(grad_mixed, qkv_back.T, preferred_element_type=jnp.float32)
    grad_in, gain_one = norm_back(flat_in, inverse_one, attn_gain_b, grad_normed)
    grad_in = grad_in + grad_resid
    grad_tokens = grad_in.astype(jnp.bfloat16).reshape(streams, local_len, model_dim)
    gain_totals = lax.psum((gain_one, gain_two), ("dp", "sp"))
    gain_share = model_dim // sp_count
    grad_g_attn = lax.dynamic_slice_in_dim(gain_totals[0], sp_index * gain_share, gain_share, 0)
    grad_g_mlp = lax.dynamic_slice_in_dim(gain_totals[1], sp_index * gain_share, gain_share, 0)
    row_sums = lax.psum_scatter(
        jnp.concatenate(
            [
                lax.dot_general(normed, grad_mixed, contract, preferred_element_type=jnp.float32),
                lax.dot_general(
                    attn_tok, grad_branch, contract, preferred_element_type=jnp.float32
                ),
                lax.dot_general(inner_in, grad_both, contract, preferred_element_type=jnp.float32),
            ],
            axis=1,
        ).astype(jnp.bfloat16),
        "sp",
        scatter_dimension=0,
        tiled=True,
    )
    down_sums = lax.psum_scatter(
        lax.dot_general(hidden, grad_y, contract, preferred_element_type=jnp.float32).astype(
            jnp.bfloat16
        ),
        "sp",
        scatter_dimension=0,
        tiled=True,
    )
    weight_rows, down_rows = (
        lax.psum(row_sums, "dp").astype(jnp.float32),
        lax.psum(down_sums, "dp").astype(jnp.float32),
    )
    qkv_cols = model_dim + 2 * kv_width
    grad_w_qkv = weight_rows[:, :qkv_cols]
    grad_w_out = weight_rows[:, qkv_cols : qkv_cols + model_dim]
    grad_w_gate_up = weight_rows[:, qkv_cols + model_dim :]
    return (
        output,
        grad_tokens,
        grad_w_qkv,
        grad_w_out,
        grad_w_gate_up,
        down_rows,
        grad_g_attn,
        grad_g_mlp,
    )


CHIPS = 4
BLOCK = 512
SHORT = pl.CostEstimate(flops=1, bytes_accessed=1, transcendentals=0)
LOG2E = math.log2(math.e)
BF = jnp.bfloat16
F32 = jnp.float32
NT = (((1,), (1,)), ((), ()))
TN = (((0,), (0,)), ((), ()))


def swap_pairs(even_mask, odd_mask):
    return [(i, i ^ (odd_mask if i & 1 else even_mask)) for i in range(2 * CHIPS)]


FIRST = swap_pairs(2, 4)
SECOND = swap_pairs(4, 2)
SIBLING = swap_pairs(1, 1)
SAME_CORE = [[0, 2, 4, 6], [1, 3, 5, 7]]
LINE_NEAR = [(z, z ^ 1) for z in range(4)]
LINE_FAR = [(z, z ^ 2) for z in range(4)]


def send_first(x):
    return lax.ppermute(x, "sp", FIRST)


def send_second(x):
    return lax.ppermute(x, "sp", SECOND)


def send_sibling(x):
    return lax.ppermute(x, "sp", SIBLING)


def after(value, *others):
    return lax.optimization_barrier((value,) + others)[0]


def gather_chips(own):
    first = send_first(own)
    second = send_second(after(own, first))
    far = send_second(after(first, second))
    return [own, first, second, far]


def rel_masks(core):
    first = jnp.where(core == 0, 2, 4)
    return first, 6 - first


def fence(*values):
    return lax.optimization_barrier(values)


def gather_vectors(own, me):
    for bit in (1, 2, 4):
        got = lax.ppermute(own, "sp", swap_pairs(bit, bit))
        high = (me & bit) != 0
        own = jnp.concatenate([jnp.where(high, got, own), jnp.where(high, own, got)], axis=1)
    return own


def pick(parts, index):
    return lax.dynamic_index_in_dim(parts, index, 0, keepdims=False)


def pick_sum(parts, index, axis):
    return sum(lax.dynamic_index_in_dim(p, index, axis, keepdims=False).astype(F32) for p in parts)


def line_scatter_sends(parts, got, step, axis):
    planes = parts[0].shape[axis]
    z = lax.axis_index("dp")
    ahead = pick_sum(parts, jnp.clip(planes - step + z, 0, planes - 1), axis)
    back = pick_sum(parts, jnp.clip(z - planes + step, 0, planes - 1), axis)
    if got is not None:
        ahead = ahead + got[0].astype(F32)
        back = back + got[1].astype(F32)
    return ahead.astype(BF), back.astype(BF)


def line_scatter_move(sends, step):
    planes = lax.axis_size("dp")
    right = lax.ppermute(sends[0], "dp", [(i, i + 1) for i in range(step)])
    left = lax.ppermute(sends[1], "dp", [(planes - 1 - i, planes - 2 - i) for i in range(step)])
    return right, left


def line_scatter_end(parts, got, axis):
    own = pick_sum(parts, lax.axis_index("dp"), axis)
    return (own + got[0].astype(F32) + got[1].astype(F32)).astype(BF)


def line_gather_move(got, step):
    planes = lax.axis_size("dp")
    right = lax.ppermute(got[0], "dp", [(i, i + 1) for i in range(step - 1, planes - 1)])
    left = lax.ppermute(got[1], "dp", [(i + 1, i) for i in range(planes - step)])
    return right, left


def line_values(refs, planes, z):
    for step in range(planes):
        place = lax.rem(z - step + planes, planes)
        if step == 0:
            yield place, lambda index: refs[0][index]
        else:
            right, left = refs[step], refs[2 * planes - 1 - step]
            yield place, lambda index, right=right, left=left, step=step: jnp.where(z >= step, right[index], left[index])


def spread_kernel(in_ref, w_ref, g_ref, out_ref, gain_ref):
    planes, _, rows, width = in_ref.shape
    out = in_ref[...].reshape(planes * rows, width).astype(F32)
    out_ref[...] = out
    part = jnp.sum(out * w_ref[...].astype(F32), axis=-1, keepdims=True) / g_ref[...]

    @pl.when(pl.program_id(0) == 0)
    def _():
        gain_ref[...] = part

    @pl.when(pl.program_id(0) > 0)
    def _():
        gain_ref[...] += part


def spread(parts, weight, gain):
    planes, chips, rows, both = parts.shape
    half = both // 2
    total = planes * rows
    line = pl.BlockSpec((total, half), lambda i: (0, i))
    column = pl.BlockSpec((total, 1), lambda i: (0, 0))
    return pl.pallas_call(
        spread_kernel,
        grid=(2 * chips,),
        in_specs=[pl.BlockSpec((planes, 1, rows, half), lambda i: (0, i % chips, 0, i // chips)), line, column],
        out_specs=[line, column],
        out_shape=[jax.ShapeDtypeStruct(weight.shape, F32), jax.ShapeDtypeStruct((total, 1), F32)],
        compiler_params=pltpu.CompilerParams(vmem_limit_bytes=32 * 2**20),
        cost_estimate=SHORT,
        name="spread",
    )(parts, weight, gain)


def spread_last_kernel(z_ref, *refs, planes):
    blocks, (w_ref, g_ref, out_ref, gain_ref, wo_ref) = refs[:-5], refs[-5:]
    rows = blocks[0].shape[0]
    devices = 2 * CHIPS
    width = wo_ref.shape[1]
    heads = width // devices
    each = heads + 2 * HD
    for place, load in line_values(blocks, planes, z_ref[0]):
        span = pl.ds(pl.multiple_of(place * rows, rows), rows)
        pairs = []
        for d in range(devices):
            begin = d * each
            cols = slice(begin, begin + heads)
            out_ref[span, d * heads : (d + 1) * heads] = load((slice(None), cols)).astype(F32)
            pairs.append(load((slice(None), slice(begin + heads, begin + each))).astype(F32))
        for g in range(0, KV, 2):
            low = pairs[2 * g] + pairs[2 * g + 1]
            high = pairs[2 * g + 2] + pairs[2 * g + 3]
            lane = lax.broadcasted_iota(jnp.int32, low.shape, 1)
            begin = width + g * HD
            out_ref[span, begin : begin + 2 * HD] = jnp.where(lane < HD, low, pltpu.roll(high, HD, 1))
            begin = width + (KV + g) * HD
            out_ref[span, begin : begin + 2 * HD] = jnp.where(lane < HD, pltpu.roll(low, HD, 1), high)
        wo_ref[span, :] = load((slice(None), slice(devices * each, devices * each + width))).astype(F32)
    gain_ref[...] = jnp.sum(out_ref[...] * w_ref[...].astype(F32), axis=-1, keepdims=True) / g_ref[...]


def spread_last(steps, weight, gain, width):
    planes = len(steps)
    blocks = [steps[0][0]] + [s[0] for s in steps[1:]] + [s[1] for s in steps[1:]]
    vmem = pl.BlockSpec(memory_space=pltpu.VMEM)
    total = weight.shape[0]
    return pl.pallas_call(
        functools.partial(spread_last_kernel, planes=planes),
        in_specs=[pl.BlockSpec(memory_space=pltpu.SMEM)] + [vmem] * (len(blocks) + 2),
        out_specs=[vmem] * 3,
        out_shape=[
            jax.ShapeDtypeStruct(weight.shape, F32),
            jax.ShapeDtypeStruct((total, 1), F32),
            jax.ShapeDtypeStruct((total, width), F32),
        ],
        compiler_params=pltpu.CompilerParams(vmem_limit_bytes=32 * 2**20),
        cost_estimate=SHORT,
        name="spread_last",
    )(lax.axis_index("dp").reshape(1), *blocks, weight, gain)


def join_kernel(core_ref, mine_ref, theirs_ref, out_ref):
    planes, _, rows, both = mine_ref.shape
    block = jnp.where(pl.program_id(1) == 0, mine_ref[...], theirs_ref[...]).reshape(planes * rows, both)
    out_ref[0, 0, 0] = block[:, : both // 2]
    out_ref[1, 0, 0] = block[:, both // 2 :]


def join(core, mine, theirs):
    planes, chips, rows, both = mine.shape
    spec = pl.BlockSpec((planes, 1, rows, both), lambda c, k, core: (0, c, 0, 0))
    out = pl.pallas_call(
        join_kernel,
        grid_spec=pltpu.PrefetchScalarGridSpec(
            num_scalar_prefetch=1,
            grid=(chips, 2),
            in_specs=[spec, spec],
            out_specs=pl.BlockSpec(
                (2, 1, 1, planes * rows, both // 2), lambda c, k, core: (0, c, (core[0] + k) % 2, 0, 0)
            ),
        ),
        out_shape=jax.ShapeDtypeStruct((2, chips, 2, planes * rows, both // 2), BF),
        compiler_params=pltpu.CompilerParams(vmem_limit_bytes=32 * 2**20),
        cost_estimate=SHORT,
        name="join",
    )(core.reshape(1), mine, theirs)
    return out.reshape(2, 2 * chips * planes * rows, both // 2)


def ffn_kernel(*refs, cuts):
    b_hbm, dy_hbm, wgu_hbm, wd_hbm, hid_hbm, dg_hbm, du_hbm, db_hbm, y_hbm = refs[:9]
    b_ref, dy_ref, wg_ref, wu_ref, wd_ref, hid_ref, dg_ref, du_ref, db_ref, y_ref, sems = refs[9:]
    count = len(cuts) - 1

    def move(source, target, index):
        copy = pltpu.make_async_copy(source, target, sems.at[index])
        copy.start()
        return copy

    b_copy = move(b_hbm, b_ref, 3 * count)
    weights = []
    for c in range(count):
        span = slice(cuts[c], cuts[c + 1])
        gate_copy = move(wgu_hbm.at[0, :, span], wg_ref.at[:, span], 3 * c)
        up_copy = move(wgu_hbm.at[1, :, span], wu_ref.at[:, span], 3 * c + 1)
        weights.append([gate_copy, up_copy])
        if c == 0:
            dy_copy = move(dy_hbm, dy_ref, 3 * count + 1)
        weights[-1].append(move(wd_hbm.at[span, :], wd_ref.at[span, :], 3 * c + 2))
    b_copy.wait()
    for c in range(count):
        span = slice(cuts[c], cuts[c + 1])
        for copy in weights[c][:2]:
            copy.wait()
        gate = jnp.dot(b_ref[...], wg_ref[:, span], preferred_element_type=F32)
        up = jnp.dot(b_ref[...], wu_ref[:, span], preferred_element_type=F32)
        if c == 0:
            dy_copy.wait()
        weights[c][2].wait()
        d_hidden = lax.dot_general(dy_ref[...], wd_ref[span, :], NT, preferred_element_type=F32)
        sigmoid_g = jax.nn.sigmoid(gate)
        silu_gate = gate * sigmoid_g
        hid_ref[:, span] = (silu_gate * up).astype(BF)
        dg_ref[:, span] = (d_hidden * up * (sigmoid_g * (1.0 + gate * (1.0 - sigmoid_g)))).astype(BF)
        du_ref[:, span] = (d_hidden * silu_gate).astype(BF)
    base = 3 * count + 2
    outs = [move(hid_ref, hid_hbm, base), move(dg_ref, dg_hbm, base + 1), move(du_ref, du_hbm, base + 2)]
    y_ref[...] = jnp.dot(hid_ref[...], wd_ref[...], preferred_element_type=F32).astype(BF)
    outs.append(move(y_ref, y_hbm, base + 3))
    d_in = lax.dot_general(dg_ref[...], wg_ref[...], NT, preferred_element_type=F32)
    db_ref[...] = (d_in + lax.dot_general(du_ref[...], wu_ref[...], NT, preferred_element_type=F32)).astype(BF)
    outs.append(move(db_ref, db_hbm, base + 4))
    for copy in outs:
        copy.wait()


def ffn(b_rows, dy_rows, w_gu, w_dn):
    rows, width = b_rows.shape
    hidden = w_dn.shape[0]
    pieces = 3
    cuts = tuple(round(hidden * c / pieces / 128) * 128 for c in range(pieces)) + (hidden,)
    hbm = pl.BlockSpec(memory_space=pl.ANY)
    return pl.pallas_call(
        functools.partial(ffn_kernel, cuts=cuts),
        in_specs=[hbm] * 4,
        out_specs=[hbm] * 5,
        out_shape=[jax.ShapeDtypeStruct((rows, hidden), BF)] * 3 + [jax.ShapeDtypeStruct((rows, width), BF)] * 2,
        scratch_shapes=[pltpu.VMEM((rows, width), BF)] * 2
        + [pltpu.VMEM((width, hidden), BF)] * 2
        + [pltpu.VMEM((hidden, width), BF)]
        + [pltpu.VMEM((rows, hidden), BF)] * 3
        + [pltpu.VMEM((rows, width), BF)] * 2
        + [pltpu.SemaphoreType.DMA((3 * pieces + 7,))],
        compiler_params=pltpu.CompilerParams(vmem_limit_bytes=58 * 2**20),
        cost_estimate=SHORT,
        name="ffn",
    )(b_rows, dy_rows, w_gu, w_dn)


def grad_gu_kernel(core_ref, *refs, count):
    left, right = refs[: 2 * count], refs[2 * count : 4 * count]
    half = right[0].shape[1]
    for side in range(2):
        for kind in range(2):
            total = None
            for r in range(count):
                a_rows = left[side * count + r][...]
                part = lax.dot_general(a_rows, right[kind * count + r][...], TN, preferred_element_type=F32)
                total = part if total is None else total + part
            out_ref = refs[4 * count + side]
            planes, _, rows, _ = out_ref.shape
            out_ref[:, 0, :, kind * half : (kind + 1) * half] = total.astype(BF).reshape(planes, rows, half)


def grad_gu(core, b_rows, dg_rows, du_rows, share, planes):
    count = len(b_rows)
    tokens, width = b_rows[0].shape
    hidden = dg_rows[0].shape[1]
    keep = pl.BlockSpec((tokens, share), lambda c, core: (0, 2 * c + core[0]))
    give = pl.BlockSpec((tokens, share), lambda c, core: (0, 2 * c + 1 - core[0]))
    whole = pl.BlockSpec((tokens, hidden), lambda c, core: (0, 0))
    rows = share // planes
    out = pl.BlockSpec((planes, 1, rows, 2 * hidden), lambda c, core: (0, c, 0, 0))
    return pl.pallas_call(
        functools.partial(grad_gu_kernel, count=count),
        grid_spec=pltpu.PrefetchScalarGridSpec(
            num_scalar_prefetch=1,
            grid=(width // (2 * share),),
            in_specs=[keep] * count + [give] * count + [whole] * (2 * count),
            out_specs=[out, out],
        ),
        out_shape=[jax.ShapeDtypeStruct((planes, width // (2 * share), rows, 2 * hidden), BF)] * 2,
        compiler_params=pltpu.CompilerParams(vmem_limit_bytes=58 * 2**20),
        cost_estimate=SHORT,
        name="grad_gu",
    )(core.reshape(1), *b_rows, *b_rows, *dg_rows, *du_rows)


def grad_qkv_kernel(place_ref, *refs, count):
    dp_ref, out_ref = refs[-2:]
    total = None
    for r in range(count):
        part = lax.dot_general(refs[r][...], dp_ref[place_ref[r]], TN, preferred_element_type=F32)
        total = part if total is None else total + part
    planes, rows, wide = out_ref.shape
    columns = total.shape[1]
    for k in range(wide // columns):
        block = total[k * planes * rows : (k + 1) * planes * rows].astype(BF)
        out_ref[:, :, k * columns : (k + 1) * columns] = block.reshape(planes, rows, columns)


def grad_qkv(places, a_rows, dp_heads, planes):
    count = len(a_rows)
    tokens, width = a_rows[0].shape
    columns = dp_heads.shape[2]
    share = width // count
    depth = 2 * share
    return pl.pallas_call(
        functools.partial(grad_qkv_kernel, count=count),
        grid_spec=pltpu.PrefetchScalarGridSpec(
            num_scalar_prefetch=1,
            grid=(width // depth,),
            in_specs=[pl.BlockSpec((tokens, depth), lambda i, p: (0, i))] * count
            + [pl.BlockSpec(dp_heads.shape, lambda i, p: (0, 0, 0))],
            out_specs=pl.BlockSpec((planes, share // planes, 2 * columns), lambda i, p: (0, 0, i)),
        ),
        out_shape=jax.ShapeDtypeStruct((planes, share // planes, count * columns), BF),
        compiler_params=pltpu.CompilerParams(vmem_limit_bytes=48 * 2**20),
        cost_estimate=SHORT,
        name="grad_qkv",
    )(places, *a_rows, dp_heads)


def swap_halves(values):
    width = values.shape[-1]
    lane = lax.broadcasted_iota(jnp.int32, values.shape, 1)
    ahead = pltpu.roll(values, width - HD // 2, 1)
    behind = pltpu.roll(values, HD // 2, 1)
    return jnp.where(lane % HD < HD // 2, ahead, behind)


def project_kernel(place_ref, x_ref, gain_ref, cos_ref, sin_ref, *refs, count):
    wq_refs, wkv_refs = refs[:count], refs[count : 2 * count]
    send_ref, normed_ref, inv_ref, normed_scr = refs[2 * count :]
    share = normed_scr.shape[2]

    @pl.when(pl.program_id(0) == 0)
    def _():
        x = x_ref[...].astype(F32)
        inv = lax.rsqrt(jnp.mean(x * x, axis=-1, keepdims=True) + EPSILON)
        normed = (x * inv * gain_ref[...]).astype(BF)
        normed_ref[...] = normed
        inv_ref[...] = inv
        for part in range(count):
            normed_scr[part] = normed[:, part * share : (part + 1) * share]

    pq = pkv = None
    for r in range(count):
        a_rows = normed_scr[place_ref[r]]
        q_part = jnp.dot(a_rows, wq_refs[r][...], preferred_element_type=F32)
        kv_part = jnp.dot(a_rows, wkv_refs[r][...], preferred_element_type=F32)
        pq = q_part if pq is None else pq + q_part
        pkv = kv_part if pkv is None else pkv + kv_part
    cos = cos_ref[...]
    sin = sin_ref[...]
    heads = pq.shape[1]
    q_scale = LOG2E * HD**-0.5
    turned = pq * jnp.tile(cos, (1, heads // 128)) + swap_halves(pq) * jnp.tile(sin, (1, heads // 128))
    send_ref[0, :, :heads] = (turned * q_scale).astype(BF)
    lane = lax.broadcasted_iota(jnp.int32, pkv.shape, 1)
    turned_kv = jnp.where(lane < HD, pkv * cos + swap_halves(pkv) * sin, pkv)
    send_ref[0, :, heads:] = turned_kv.astype(BF)


def project(places, x, gain, cos, sin, parts):
    rows, width = x.shape
    count = len(parts)
    heads = width // count
    out_width = heads + 2 * HD
    depth = parts[0].shape[0]
    first_kv = width // (2 * HD)
    return pl.pallas_call(
        functools.partial(project_kernel, count=count),
        grid_spec=pltpu.PrefetchScalarGridSpec(
            num_scalar_prefetch=1,
            grid=(count,),
            in_specs=[
                pl.BlockSpec((rows, width), lambda d, p: (0, 0)),
                pl.BlockSpec((1, width), lambda d, p: (0, 0)),
                pl.BlockSpec((rows, 128), lambda d, p: (0, 0)),
                pl.BlockSpec((rows, 128), lambda d, p: (0, 0)),
            ]
            + [pl.BlockSpec((depth, heads), lambda d, p: (0, d))] * count
            + [pl.BlockSpec((depth, 2 * HD), lambda d, p: (0, first_kv + d // 2))] * count,
            out_specs=[
                pl.BlockSpec((1, rows, out_width), lambda d, p: (d, 0, 0)),
                pl.BlockSpec((rows, width), lambda d, p: (0, 0)),
                pl.BlockSpec((rows, 1), lambda d, p: (0, 0)),
            ],
            scratch_shapes=[pltpu.VMEM((count, rows, width // count), BF)],
        ),
        out_shape=[
            jax.ShapeDtypeStruct((count, rows, out_width), BF),
            jax.ShapeDtypeStruct((rows, width), BF),
            jax.ShapeDtypeStruct((rows, 1), F32),
        ],
        compiler_params=pltpu.CompilerParams(vmem_limit_bytes=48 * 2**20),
        cost_estimate=SHORT,
        name="project",
    )(places, x, gain, cos, sin, *parts, *parts)


def out_proj_kernel(place_ref, attn_ref, x_ref, gain_ref, *refs, count):
    parts, (resid_ref, inv_ref, inner_ref) = refs[:count], refs[count:]
    width = x_ref.shape[1]
    tile = 512
    square = None
    for begin in range(0, width, tile):
        cols = slice(begin, begin + tile)
        total = x_ref[:, cols].astype(F32)
        for r in range(count):
            total = total + jnp.dot(attn_ref[place_ref[r]], parts[r][:, cols], preferred_element_type=F32)
        resid_ref[:, cols] = total
        part = jnp.sum(total * total, axis=-1, keepdims=True)
        square = part if square is None else square + part
    inv = lax.rsqrt(square / width + EPSILON)
    inv_ref[...] = inv
    inner_ref[...] = (resid_ref[...] * inv * gain_ref[...]).astype(BF)


def out_proj(places, attn, x, gain, parts):
    count, rows, share = attn.shape
    width = x.shape[1]
    step = rows // 2
    line = pl.BlockSpec((step, width), lambda i, p: (i, 0))
    return pl.pallas_call(
        functools.partial(out_proj_kernel, count=count),
        grid_spec=pltpu.PrefetchScalarGridSpec(
            num_scalar_prefetch=1,
            grid=(rows // step,),
            in_specs=[
                pl.BlockSpec((count, step, share), lambda i, p: (0, i, 0)),
                line,
                pl.BlockSpec((1, width), lambda i, p: (0, 0)),
            ]
            + [pl.BlockSpec((share, width), lambda i, p: (0, 0))] * count,
            out_specs=[line, pl.BlockSpec((step, 1), lambda i, p: (i, 0)), line],
        ),
        out_shape=[
            jax.ShapeDtypeStruct((rows, width), F32),
            jax.ShapeDtypeStruct((rows, 1), F32),
            jax.ShapeDtypeStruct((rows, width), BF),
        ],
        compiler_params=pltpu.CompilerParams(vmem_limit_bytes=56 * 2**20),
        cost_estimate=SHORT,
        name="out_proj",
    )(places, attn, x, gain, *parts)


def resid_back_kernel(place_ref, db_ref, first_ref, passed_ref, resid_ref, inv_ref, gain_ref, dy_ref, *refs, count):
    parts, (d_resid_ref, branch_ref, send_ref) = refs[:count], refs[count:]
    d_inner = db_ref[...].astype(F32) + first_ref[...].astype(F32) + passed_ref[...].astype(F32)
    resid = resid_ref[...]
    inv = inv_ref[...]
    scaled = d_inner * gain_ref[...]
    inner_mean = jnp.mean(scaled * resid, axis=-1, keepdims=True)
    d_resid = dy_ref[...].astype(F32) + inv * scaled - resid * (inv * inv * inv * inner_mean)
    d_resid_ref[...] = d_resid
    branch = d_resid.astype(BF)
    branch_ref[...] = branch
    for r in range(count):
        d_attn = lax.dot_general(branch, parts[r][...], NT, preferred_element_type=F32)
        send_ref[place_ref[r]] = d_attn.astype(BF)


def resid_back(places, db_own, db_first, db_passed, resid, inv, gain, dy, parts):
    rows, width = resid.shape
    count = len(parts)
    share = parts[0].shape[0]
    step = rows // 2
    line = pl.BlockSpec((step, width), lambda i, p: (i, 0))
    return pl.pallas_call(
        functools.partial(resid_back_kernel, count=count),
        grid_spec=pltpu.PrefetchScalarGridSpec(
            num_scalar_prefetch=1,
            grid=(rows // step,),
            in_specs=[line, line, line, line]
            + [pl.BlockSpec((step, 1), lambda i, p: (i, 0)), pl.BlockSpec((1, width), lambda i, p: (0, 0)), line]
            + [pl.BlockSpec((share, width), lambda i, p: (0, 0))] * count,
            out_specs=[line, line, pl.BlockSpec((count, step, share), lambda i, p: (0, i, 0))],
        ),
        out_shape=[
            jax.ShapeDtypeStruct((rows, width), F32),
            jax.ShapeDtypeStruct((rows, width), BF),
            jax.ShapeDtypeStruct((count, rows, share), BF),
        ],
        compiler_params=pltpu.CompilerParams(vmem_limit_bytes=56 * 2**20),
        cost_estimate=SHORT,
        name="resid_back",
    )(places, db_own, db_first, db_passed, resid, inv, gain, dy, *parts)


def in_back_kernel(place_ref, back_ref, x_ref, inv_ref, gain_ref, d_resid_ref, *refs, count):
    parts, (out_ref, mixed, d_scr) = refs[:count], refs[count:]
    devices, _, width = back_ref.shape
    heads = width - 2 * HD
    for d in range(devices):
        mixed[:, d * heads : (d + 1) * heads] = back_ref[d, :, :heads]
    base = devices * heads
    for g in range(KV):
        pair = back_ref[2 * g, :, heads:].astype(F32) + back_ref[2 * g + 1, :, heads:].astype(F32)
        mixed[:, base + 2 * g * HD : base + 2 * (g + 1) * HD] = pair.astype(BF)
    for r in range(count):
        d_scr[place_ref[r]] = lax.dot_general(mixed[...], parts[r][...], NT, preferred_element_type=F32)
    inv = inv_ref[...]
    share = d_scr.shape[2]
    inner = None
    for c in range(count):
        cols = slice(c * share, (c + 1) * share)
        part = jnp.sum(d_scr[c] * gain_ref[:, cols] * x_ref[:, cols].astype(F32), axis=-1, keepdims=True)
        inner = part if inner is None else inner + part
    factor = inv * inv * inv * (inner / (count * share))
    for c in range(count):
        cols = slice(c * share, (c + 1) * share)
        through = inv * (d_scr[c] * gain_ref[:, cols]) - x_ref[:, cols].astype(F32) * factor
        out_ref[:, cols] = (d_resid_ref[:, cols] + through).astype(BF)


def in_back(places, back, x, inv, gain, d_resid, parts):
    rows, width = x.shape
    count = len(parts)
    share, columns = parts[0].shape
    step = rows // 2
    line = pl.BlockSpec((step, width), lambda i, p: (i, 0))
    return pl.pallas_call(
        functools.partial(in_back_kernel, count=count),
        grid_spec=pltpu.PrefetchScalarGridSpec(
            num_scalar_prefetch=1,
            grid=(rows // step,),
            in_specs=[
                pl.BlockSpec((count, step, back.shape[2]), lambda i, p: (0, i, 0)),
                line,
                pl.BlockSpec((step, 1), lambda i, p: (i, 0)),
                pl.BlockSpec((1, width), lambda i, p: (0, 0)),
                line,
            ]
            + [pl.BlockSpec((share, columns), lambda i, p: (0, 0))] * count,
            out_specs=line,
            scratch_shapes=[pltpu.VMEM((step, columns), BF), pltpu.VMEM((count, step, share), F32)],
        ),
        out_shape=jax.ShapeDtypeStruct((rows, width), BF),
        compiler_params=pltpu.CompilerParams(vmem_limit_bytes=56 * 2**20),
        cost_estimate=SHORT,
        name="in_back",
    )(places, back, x, inv, gain, d_resid, *parts)


def grad_wo_kernel(core_ref, keep_ref, give_ref, branch_ref, keep_out, give_out):
    branch = branch_ref[...]
    keep_out[0] = lax.dot_general(keep_ref[0], branch, TN, preferred_element_type=F32).astype(BF)
    give_out[0] = lax.dot_general(give_ref[0], branch, TN, preferred_element_type=F32).astype(BF)


def grad_wo(core, attn, branch):
    devices, rows, share = attn.shape
    width = branch.shape[1]
    out = pl.BlockSpec((1, share, width), lambda c, core: (c, 0, 0))
    return pl.pallas_call(
        grad_wo_kernel,
        grid_spec=pltpu.PrefetchScalarGridSpec(
            num_scalar_prefetch=1,
            grid=(devices // 2,),
            in_specs=[
                pl.BlockSpec((1, rows, share), lambda c, core: (2 * c + core[0], 0, 0)),
                pl.BlockSpec((1, rows, share), lambda c, core: (2 * c + 1 - core[0], 0, 0)),
                pl.BlockSpec((rows, width), lambda c, core: (0, 0)),
            ],
            out_specs=[out, out],
        ),
        out_shape=[jax.ShapeDtypeStruct((devices // 2, share, width), BF)] * 2,
        compiler_params=pltpu.CompilerParams(vmem_limit_bytes=48 * 2**20),
        cost_estimate=SHORT,
        name="grad_wo",
    )(core.reshape(1), attn, attn, branch)


def grad_dn_kernel(core_ref, *refs, count):
    left, right, (keep_out, give_out) = refs[:count], refs[count : 2 * count], refs[2 * count :]
    total = None
    for r in range(count):
        part = lax.dot_general(left[r][...], right[r][...], TN, preferred_element_type=F32)
        total = part if total is None else total + part
    half = total.shape[0] // 2
    total = total.astype(BF)
    low = core_ref[0] == 0
    keep_out[...] = jnp.where(low, total[:half], total[half:])
    give_out[...] = jnp.where(low, total[half:], total[:half])


def grad_dn(core, hid_rows, dy_rows):
    count = len(hid_rows)
    tokens, hidden = hid_rows[0].shape
    width = dy_rows[0].shape[1]
    tile = 512
    out = pl.BlockSpec((hidden // 2, tile), lambda i, core: (0, i))
    return pl.pallas_call(
        functools.partial(grad_dn_kernel, count=count),
        grid_spec=pltpu.PrefetchScalarGridSpec(
            num_scalar_prefetch=1,
            grid=(width // tile,),
            in_specs=[pl.BlockSpec((tokens, hidden), lambda i, core: (0, 0))] * count
            + [pl.BlockSpec((tokens, tile), lambda i, core: (0, i))] * count,
            out_specs=[out, out],
        ),
        out_shape=[jax.ShapeDtypeStruct((hidden // 2, width), BF)] * 2,
        compiler_params=pltpu.CompilerParams(vmem_limit_bytes=56 * 2**20),
        cost_estimate=SHORT,
        name="grad_dn",
    )(core.reshape(1), *hid_rows, *dy_rows)


def attend_kernel(zeros_ref, q_ref, kv_ref, *refs, heads, start, stop):
    o_ref, send_ref, lse_ref, k_scr, v_scr, acc_ref, max_ref = refs[-7:]
    block = pl.program_id(0) + start
    zeros = zeros_ref[0]
    size = q_ref.shape[0]

    @pl.when(block == start)
    def _():
        for part in range(stop):
            rows = slice(part * size, (part + 1) * size)
            both = kv_ref[rows, :].astype(F32)
            lane = lax.broadcasted_iota(jnp.int32, both.shape, 1)
            k_scr[rows, :] = kv_ref[rows, :HD]
            v_scr[rows, :] = jnp.where(lane < HD, pltpu.roll(both, HD, 1), 1.0).astype(BF)

    first_row = block * size
    lowest = jnp.where(first_row >= zeros, zeros // size, 0)
    acc_ref[...] = jnp.zeros_like(acc_ref)
    max_ref[...] = jnp.full_like(max_ref, MASKED)
    q_heads = [q_ref[:, h * HD : (h + 1) * HD] for h in range(heads)]

    def step(index, masked):
        first_key = pl.multiple_of(index * size, size)
        keys = k_scr[pl.ds(first_key, size), :]
        values = v_scr[pl.ds(first_key, size), :]
        if masked:
            row = first_row + lax.broadcasted_iota(jnp.int32, (size, size), 0)
            col = first_key + lax.broadcasted_iota(jnp.int32, (size, size), 1)
            begin = jnp.where(row >= zeros, zeros, 0)
            refused = (col > row) | (col < begin)

        def score(h):
            return lax.dot_general(q_heads[h], keys, NT, preferred_element_type=F32)

        upcoming = score(0)
        for h in range(heads):
            scores = upcoming
            if h + 1 < heads:
                upcoming = score(h + 1)
            if masked:
                scores = jnp.where(refused, MASKED, scores)
            old_max = max_ref[h]
            new_max = jnp.maximum(old_max, jnp.max(scores, axis=-1, keepdims=True))
            weights = jnp.exp2(scores - jnp.tile(new_max, (1, size // 128)))
            shrink = jnp.exp2(old_max - new_max)
            acc_ref[h] = acc_ref[h] * shrink + jnp.dot(weights.astype(BF), values, preferred_element_type=F32)
            max_ref[h] = new_max

    def visit(index, carry):
        first_key = index * size
        mixed = (index == block) | ((first_row + size > zeros) & (first_key < zeros))

        @pl.when(mixed)
        def _():
            step(index, True)

        @pl.when(jnp.logical_not(mixed))
        def _():
            step(index, False)

        return carry

    lax.fori_loop(lowest, block + 1, visit, 0)
    for h in range(heads):
        acc = acc_ref[h]
        total = acc[:, HD : HD + 1]
        out = acc[:, :HD] / total
        o_ref[:, h * HD : (h + 1) * HD] = out
        send_ref[0, :, h * HD : (h + 1) * HD] = out.astype(BF)
        lse = max_ref[h] + jnp.log2(total)
        lse_ref[0, h : h + 1, :] = jnp.transpose(lse)[:1]


def attend(zeros, qkv, start, stop, before=None):
    length, width = qkv.shape
    q_width = width - 2 * HD
    heads = q_width // HD
    size = BLOCK
    blocks = length // size
    before = () if before is None else before
    return pl.pallas_call(
        functools.partial(attend_kernel, heads=heads, start=start, stop=stop),
        grid_spec=pltpu.PrefetchScalarGridSpec(
            num_scalar_prefetch=1,
            grid=(stop - start,),
            in_specs=[
                pl.BlockSpec((size, q_width), lambda i, z: (i + start, 0)),
                pl.BlockSpec((length, 2 * HD), lambda i, z: (0, q_width // (2 * HD))),
            ]
            + [pl.BlockSpec(memory_space=pl.ANY)] * len(before),
            out_specs=[
                pl.BlockSpec((size, q_width), lambda i, z: (i + start, 0)),
                pl.BlockSpec((1, size, q_width), lambda i, z: (i + start, 0, 0)),
                pl.BlockSpec((1, heads, size), lambda i, z: (i + start, 0, 0)),
            ],
            scratch_shapes=[
                pltpu.VMEM((length, HD), BF),
                pltpu.VMEM((length, 2 * HD), BF),
                pltpu.VMEM((heads, size, 2 * HD), F32),
                pltpu.VMEM((heads, size, 128), F32),
            ],
        ),
        out_shape=[
            jax.ShapeDtypeStruct((length, q_width), F32),
            jax.ShapeDtypeStruct((blocks, size, q_width), BF),
            jax.ShapeDtypeStruct((blocks, heads, size), F32),
        ],
        input_output_aliases={3 + i: i for i in range(len(before))},
        compiler_params=pltpu.CompilerParams(vmem_limit_bytes=48 * 2**20),
        cost_estimate=SHORT,
        name="attend",
    )(zeros, qkv, qkv, *before)


def attend_back_kernel(
    zeros_ref, q_ref, kv_ref, do_ref, lse_ref, cos_ref, sin_ref, extra_ref, *refs, heads, start
):
    send_ref, dq_acc, delta_ref, q_scr, do_scr = refs[-5:]
    block = pl.program_id(0) + start
    zeros = zeros_ref[0]
    size = kv_ref.shape[0]
    length = q_ref.shape[0]
    blocks = length // size

    @pl.when(block == start)
    def _():
        if start == 0:
            dq_acc[...] = jnp.zeros_like(dq_acc)
        else:
            dq_acc[...] = refs[0][...]
            delta_ref[...] = extra_ref[...]
        for part in range(start, blocks):
            rows = slice(part * size, (part + 1) * size)
            if start == 0:
                product = jnp.transpose(do_ref[rows, :].astype(F32) * extra_ref[rows, :])
            for h in range(heads):
                cols = slice(h * HD, (h + 1) * HD)
                q_scr[h, rows, :] = q_ref[rows, cols]
                do_scr[h, rows, :] = do_ref[rows, cols]
                if start == 0:
                    delta_ref[part, h : h + 1, :] = jnp.sum(product[cols], axis=0, keepdims=True)

    first_key = block * size
    both = kv_ref[...]
    keys = both[:, :HD]
    values = both[:, HD:]
    keys_t = jnp.transpose(keys.astype(F32)).astype(BF)
    highest = jnp.where(first_key + size <= zeros, jnp.minimum((zeros + size - 1) // size, blocks), blocks)

    def step(index, carry, masked):
        first_row = pl.multiple_of(index * size, size)
        span = pl.ds(first_row, size)
        if masked:
            col = first_key + lax.broadcasted_iota(jnp.int32, (size, size), 0)
            row = first_row + lax.broadcasted_iota(jnp.int32, (size, size), 1)
            begin = jnp.where(row >= zeros, zeros, 0)
            refused = (col > row) | (col < begin)

        def products(h):
            q_rows = q_scr[h, span, :]
            do_rows = do_scr[h, span, :]
            scores = lax.dot_general(keys, q_rows, NT, preferred_element_type=F32)
            d_prob = lax.dot_general(values, do_rows, NT, preferred_element_type=F32)
            return q_rows, do_rows, scores, d_prob

        upcoming = products(0)
        dk_sum, dv_sum = carry
        for h in range(heads):
            q_rows, do_rows, scores, d_prob = upcoming
            if h + 1 < heads:
                upcoming = products(h + 1)
            shifted = scores - lse_ref[index, h : h + 1, :]
            if masked:
                shifted = jnp.where(refused, MASKED, shifted)
            prob = jnp.exp2(shifted)
            d_score = (prob * (d_prob - delta_ref[index, h : h + 1, :])).astype(BF)
            dv_sum = dv_sum + jnp.dot(prob.astype(BF), do_rows, preferred_element_type=F32)
            dk_sum = dk_sum + jnp.dot(d_score, q_rows, preferred_element_type=F32)
            dq_acc[h * HD : (h + 1) * HD, span] += jnp.dot(keys_t, d_score, preferred_element_type=F32)
        return dk_sum, dv_sum

    def visit(index, carry):
        first_row = index * size
        mixed = (index == block) | ((first_row + size > zeros) & (first_key < zeros))
        return lax.cond(
            mixed,
            lambda c: step(index, c, True),
            lambda c: step(index, c, False),
            carry,
        )

    zero = jnp.zeros((size, HD), F32)
    dk_sum, dv_sum = lax.fori_loop(block, highest, visit, (zero, zero))
    q_width = heads * HD
    done = pl.ds(pl.multiple_of(first_key, size), size)
    cos = cos_ref[...]
    sin = sin_ref[...]
    dq = jnp.transpose(dq_acc[:, done]) * HD**-0.5
    dq = dq * jnp.tile(cos, (1, q_width // 128)) - swap_halves(dq) * jnp.tile(sin, (1, q_width // 128))
    send_ref[0, :, :q_width] = dq.astype(BF)
    dkv = jnp.concatenate([dk_sum * (1.0 / LOG2E), dv_sum], axis=1)
    lane = lax.broadcasted_iota(jnp.int32, dkv.shape, 1)
    send_ref[0, :, q_width:] = jnp.where(lane < HD, dkv * cos - swap_halves(dkv) * sin, dkv).astype(BF)


def attend_back(zeros, qkv, d_out, lse, cos, sin, start, stop, out=None, before=None):
    length, width = qkv.shape
    q_width = width - 2 * HD
    heads = q_width // HD
    size = BLOCK
    blocks = length // size
    whole = lambda *shape: pl.BlockSpec(shape, lambda j, z: (0,) * len(shape))
    if before is None:
        operands = (out,)
        specs = [whole(length, q_width)]
        aliases = {}
    else:
        send, d_query, delta = before
        operands = (delta, d_query, send)
        specs = [whole(blocks, heads, size), whole(q_width, length), pl.BlockSpec(memory_space=pl.ANY)]
        aliases = {9: 0}
    return pl.pallas_call(
        functools.partial(attend_back_kernel, heads=heads, start=start),
        grid_spec=pltpu.PrefetchScalarGridSpec(
            num_scalar_prefetch=1,
            grid=(stop - start,),
            in_specs=[
                whole(length, q_width),
                pl.BlockSpec((size, 2 * HD), lambda j, z: (j + start, q_width // (2 * HD))),
                whole(length, q_width),
                whole(blocks, heads, size),
                pl.BlockSpec((size, 128), lambda j, z: (j + start, 0)),
                pl.BlockSpec((size, 128), lambda j, z: (j + start, 0)),
            ]
            + specs,
            out_specs=[
                pl.BlockSpec((1, size, width), lambda j, z: (j + start, 0, 0)),
                whole(q_width, length),
                whole(blocks, heads, size),
            ],
            scratch_shapes=[
                pltpu.VMEM((heads, length, HD), BF),
                pltpu.VMEM((heads, length, HD), BF),
            ],
        ),
        out_shape=[
            jax.ShapeDtypeStruct((blocks, size, width), BF),
            jax.ShapeDtypeStruct((q_width, length), F32),
            jax.ShapeDtypeStruct((blocks, heads, size), F32),
        ],
        input_output_aliases=aliases,
        compiler_params=pltpu.CompilerParams(vmem_limit_bytes=58 * 2**20),
        cost_estimate=SHORT,
        name="attend_back",
    )(zeros, qkv, qkv, d_out, lse, cos, sin, *operands)


def turn_tables(positions):
    cosine, sine = rope_tables(positions, HD)
    return jnp.concatenate([cosine] * 4, axis=1), jnp.concatenate([-sine, sine, -sine, sine], axis=1)


def fast_body(tokens, segment_ids, selected, cotangent, w_qkv, w_out, w_gate_up, w_down, g_attn, g_mlp):
    _, rows, width = tokens.shape
    devices = 2 * CHIPS
    me = lax.axis_index("sp")
    core = me & 1
    planes = lax.axis_size("dp")
    share = width // devices
    kv_width = KV * HD
    first_mask, second_mask = rel_masks(core)
    other = me ^ 1
    chip = me // 2
    place_list = [me, me ^ first_mask, me ^ second_mask, me ^ 6]
    place_list += [other, other ^ second_mask, other ^ first_mask, other ^ 6]
    places = jnp.stack(place_list)
    hidden_chip = 2 * w_down.shape[0]
    quarter = share // planes
    plane = lax.axis_index("dp")
    length = devices * rows
    blocks = length // BLOCK

    count = jnp.sum((segment_ids == 0).astype(F32))
    vectors = jnp.stack([g_attn.astype(F32), g_mlp.astype(F32)] + [jnp.full((share,), count)] * 6)
    paired = [w_qkv[:, :width]]
    for head in range(KV):
        paired.append(w_qkv[:, width + head * HD : width + (head + 1) * HD])
        paired.append(w_qkv[:, width + kv_width + head * HD : width + kv_width + (head + 1) * HD])
    qkv_own = jnp.concatenate(paired, axis=1)
    gu_rows = lax.dynamic_slice_in_dim(w_gate_up, plane * quarter, quarter, 0)
    gu_send = []
    for place in range(CHIPS):
        for begin in (place * hidden_chip, (CHIPS + place) * hidden_chip):
            gu_send.append(gu_rows[:, begin : begin + hidden_chip])
    gu_send = jnp.stack([jnp.concatenate(gu_send[2 * c : 2 * c + 2], axis=1) for c in range(CHIPS)])
    vectors = gather_vectors(vectors, me)
    vectors, qkv_own, gu_send = fence(vectors, qkv_own, gu_send)
    qkv_first = send_first(qkv_own)
    attn_gain = vectors[0:1]
    mlp_gain = vectors[1:2]
    zeros = jnp.sum(vectors[2].reshape(devices, share)[:, 0]).astype(jnp.int32)
    zeros_one = zeros.reshape(1)
    local_pos = me * rows + jnp.arange(rows, dtype=jnp.int32) - segment_ids.reshape(rows) * zeros
    cos, sin = turn_tables(local_pos)
    dy = (cotangent * selected[:, :, None].astype(BF)).reshape(rows, width)
    qkv_own, qkv_first, cos, sin = fence(qkv_own, qkv_first, cos, sin)
    qkv_second = send_second(qkv_own)
    qkv_theirs = [send_sibling(qkv_own), send_sibling(qkv_first)]
    all_places = jnp.arange(length, dtype=jnp.int32)
    cos_all, sin_all = turn_tables(all_places - jnp.where(all_places >= zeros, zeros, 0))
    qkv_first, qkv_second, cos_all, sin_all, *qkv_theirs = fence(qkv_first, qkv_second, cos_all, sin_all, *qkv_theirs)
    qkv_far = send_second(qkv_first)
    qkv_theirs.append(send_sibling(qkv_second))
    qkv_far, dy, *qkv_theirs = fence(qkv_far, dy, *qkv_theirs)
    qkv_theirs.append(send_sibling(qkv_far))
    qkv_parts = [qkv_own, qkv_first, qkv_second, qkv_far] + qkv_theirs
    x_bf = tokens.reshape(rows, width)
    x_bf, w_out, gu_send, *qkv_parts = fence(x_bf, w_out, gu_send, *qkv_parts)
    out_first = send_first(w_out)
    gu_part = lax.all_to_all(gu_send, "sp", 0, 0, axis_index_groups=SAME_CORE, tiled=True)
    qkv_send, normed, inv_one = project(places, x_bf, attn_gain, cos, sin, qkv_parts)
    qkv_send, out_first = fence(qkv_send, out_first)
    gu_mine = lax.all_gather(after(gu_part, qkv_send), "dp", axis=0, tiled=False)
    gu_mine = lax.all_gather(after(gu_part, qkv_send), "dp", axis=0, tiled=False)
    down_theirs = send_sibling(w_down)
    w_dn = jnp.where(
        core == 0, jnp.concatenate([w_down, down_theirs], axis=0), jnp.concatenate([down_theirs, w_down], axis=0)
    )
    qkv_heads = lax.all_to_all(qkv_send, "sp", 0, 0, tiled=True).reshape(length, qkv_send.shape[2])

    cuts = (0, (5 * blocks) // 8, (7 * blocks) // 8, blocks)
    qkv_heads, w_dn, out_first = fence(qkv_heads, w_dn, out_first)
    out_second = send_second(after(w_out, qkv_heads))
    dy_first = send_first(after(dy, qkv_heads))
    fwd = attend(zeros_one, qkv_heads, cuts[0], cuts[1])
    qkv_heads, out_second, dy_first, out_first, dy, *fwd = fence(qkv_heads, out_second, dy_first, out_first, dy, *fwd)
    out_far = send_second(out_first)
    dy_second = send_second(dy)
    fwd = attend(zeros_one, qkv_heads, cuts[1], cuts[2], fwd)
    qkv_heads, out_far, dy_second, dy_first, *fwd = fence(qkv_heads, out_far, dy_second, dy_first, *fwd)
    dy_far = send_second(dy_first)
    gu_theirs = send_sibling(after(gu_mine, fwd[2]))
    out_heads, out_send, lse = attend(zeros_one, qkv_heads, cuts[2], cuts[3], fwd)
    out_parts = [w_out, out_first, out_second, out_far]
    out_parts = out_parts + [send_sibling(part) for part in out_parts]
    out_send, gu_mine, gu_theirs = fence(out_send, gu_mine, gu_theirs)
    attn_tok = lax.all_to_all(out_send, "sp", 0, 0, tiled=True)
    w_gu = join(core, gu_mine, gu_theirs)
    attn_tok, w_gu, dy_far, *out_parts = fence(attn_tok, w_gu, dy_far, *out_parts)
    residual, inv_two, inner = out_proj(places, attn_tok, x_bf, mlp_gain, out_parts)

    b_first = send_first(inner)
    own = ffn(inner, dy, w_gu, w_dn)
    inner, b_first, *own = fence(inner, b_first, *own)
    b_second = send_second(inner)
    first = ffn(b_first, dy_first, w_gu, w_dn)
    b_first, b_second, *first = fence(b_first, b_second, *first)
    b_far = send_second(b_first)
    second = ffn(b_second, dy_second, w_gu, w_dn)
    b_far, db_first, *second = fence(b_far, first[3], *second)
    db_got_first = send_first(db_first)
    far = ffn(b_far, dy_far, w_gu, w_dn)
    db_got_first, db_far, *hid_rows = fence(db_got_first, far[3], own[0], first[0], second[0], far[0])

    b_rows = [inner, b_first, b_second, b_far]
    db_got_far = send_first(db_far)
    gu_keep, gu_give = grad_gu(
        core,
        b_rows,
        [own[1], first[1], second[1], far[1]],
        [own[2], first[2], second[2], far[2]],
        share,
        planes,
    )
    db_got_far, gu_keep, gu_give, *hid_rows = fence(db_got_far, gu_keep, gu_give, *hid_rows)
    db_pass = (second[3].astype(F32) + db_got_far.astype(F32)).astype(BF)
    db_pass, gu_give, *hid_rows = fence(db_pass, gu_give, *hid_rows)
    db_passed = send_second(db_pass)
    gu_got = send_sibling(gu_give)
    dn_keep, dn_give = grad_dn(core, hid_rows, [dy, dy_first, dy_second, dy_far])
    db_passed, gu_got, dn_keep, dn_give = fence(db_passed, gu_got, dn_keep, dn_give)
    gu_sum = (gu_keep.astype(F32) + gu_got.astype(F32)).astype(BF)
    gu_sum, db_passed, dn_give = fence(gu_sum, db_passed, dn_give)
    gu_z = lax.psum_scatter(
        gu_sum.reshape(planes * CHIPS * quarter, 2 * hidden_chip), "dp", scatter_dimension=0, tiled=True
    )
    gu_z = gu_z.reshape(CHIPS, quarter, 2 * hidden_chip)
    dn_got = send_sibling(dn_give)
    d_resid, d_branch, d_send = resid_back(
        places, own[3], db_got_first, db_passed, residual, inv_two, mlp_gain, dy, out_parts
    )
    d_send, d_branch, dn_got = fence(d_send, d_branch, dn_got)
    d_heads = lax.all_to_all(d_send, "sp", 0, 0, tiled=True).reshape(length, share)
    dn_parts = [part.reshape(2, 2, dn_keep.shape[0] // planes, width) for part in (dn_keep, dn_got)]
    dn_own = pick_sum(dn_parts, plane & 1, 1)
    dn_move = lax.ppermute(pick_sum(dn_parts, 1 - (plane & 1), 1).astype(BF), "dp", LINE_NEAR)
    wo_keep, wo_give = grad_wo(core, attn_tok, d_branch)
    d_heads, wo_keep, wo_give, normed = fence(d_heads, wo_keep, wo_give, normed)

    def back_call(heads, start, stop, **kwargs):
        return attend_back(zeros_one, qkv_heads, heads, lse, cos_all, sin_all, start, stop, **kwargs)

    turns = (0, blocks // 8, blocks // 4, (3 * blocks) // 8, blocks)
    wo_got = send_sibling(wo_give)
    a_first = send_first(normed)
    bwd = back_call(d_heads, turns[0], turns[1], out=out_heads)
    d_heads, a_first, wo_got, normed, dn_move, *bwd = fence(d_heads, a_first, wo_got, normed, dn_move, *bwd)

    dn_own = dn_own + dn_move.astype(F32)
    far_side = plane // 2
    dn_move = pick(dn_own, 1 - far_side).astype(BF)
    d_heads, normed, a_first, dn_move = fence(d_heads, normed, a_first, dn_move)
    a_second = send_second(normed)
    a_theirs = [send_sibling(normed), send_sibling(a_first)]
    dn_move = lax.ppermute(dn_move, "dp", LINE_FAR)
    bwd = back_call(d_heads, turns[1], turns[2], before=bwd)
    d_heads, gu_z, a_second, dn_move, *moves = fence(d_heads, gu_z, a_second, dn_move, *a_theirs, *bwd)
    a_theirs, bwd = moves[:2], moves[2:]

    def wo_part(place):
        return pick(wo_keep, place).astype(F32) + pick(wo_got, place).astype(F32)

    dn_z = (pick(dn_own, far_side) + dn_move.astype(F32)).astype(BF)
    d_heads, dn_z, gu_z, a_second = fence(d_heads, dn_z, gu_z, a_second)
    dn_move = lax.ppermute(dn_z, "dp", LINE_FAR)
    gu_z = lax.all_to_all(gu_z, "sp", 0, 0, axis_index_groups=SAME_CORE, tiled=True)
    a_theirs.append(send_sibling(a_second))
    bwd = back_call(d_heads, turns[2], turns[3], before=bwd)
    d_heads, gu_z, a_first, dn_move, *moves = fence(d_heads, gu_z, a_first, dn_move, *a_theirs, *bwd)
    a_theirs, bwd = moves[:3], moves[3:]

    dn_pair = jnp.where(far_side == 0, jnp.stack([dn_z, dn_move]), jnp.stack([dn_move, dn_z]))
    wo_first = wo_part(chip ^ (first_mask // 2)).astype(BF)
    wo_far = wo_part(chip ^ 3).astype(BF)
    d_heads, gu_z, a_first, wo_first, wo_far, dn_pair = fence(d_heads, gu_z, a_first, wo_first, wo_far, dn_pair)
    gu_all = lax.all_gather(gu_z, "dp", axis=0, tiled=False)
    a_far = send_second(a_first)
    wo_far = send_first(wo_far)
    wo_first = send_first(wo_first)
    dn_other = lax.ppermute(dn_pair, "dp", LINE_NEAR)
    bwd = back_call(d_heads, turns[3], turns[4], before=bwd)
    wo_pass = (wo_part(chip ^ (second_mask // 2)) + wo_far.astype(F32)).astype(BF)
    dp_heads, wo_first, wo_pass, a_far, dn_other = fence(bwd[0], wo_first, wo_pass, a_far, dn_other)

    wo_passed = send_second(wo_pass)
    a_theirs.append(send_sibling(a_far))
    back = lax.all_to_all(dp_heads, "sp", 0, 0, tiled=True)
    grad_wq = grad_qkv(places, [normed, a_first, a_second, a_far] + list(a_theirs), dp_heads, planes)
    wo_rows = (wo_part(chip) + wo_first.astype(F32) + wo_passed.astype(F32)).astype(BF)
    split = grad_wq.shape[2]
    last_parts = [jnp.concatenate([grad_wq, wo_rows.reshape(planes, quarter, width)], axis=2)]
    y_far, y_first = far[4], first[4]
    moves = None
    for step in range(1, planes):
        moves = line_scatter_sends(last_parts, moves, step, 0)
        y_far, y_first, *moves = fence(y_far, y_first, *moves)
        moves = line_scatter_move(moves, step)
        if step == 1:
            y_got_far = send_first(y_far)
        elif step == 2:
            y_got_first = send_first(y_first)
        moves = fence(*moves)
    last_z = line_scatter_end(last_parts, moves, 0)
    wq_z = last_z[:, :split].reshape(quarter, devices, split // devices).transpose(1, 0, 2)
    wq_z, wo_z, back, gu_all = fence(wq_z, last_z[:, split:], back, gu_all)
    wq_z = lax.all_to_all(wq_z, "sp", 0, 0, tiled=True)
    grad_tokens = in_back(places, back, x_bf, inv_one, attn_gain, d_resid, qkv_parts).reshape(tokens.shape)
    y_pass = (second[4].astype(F32) + y_got_far.astype(F32)).astype(BF)
    last_z = jnp.concatenate([wq_z.transpose(1, 0, 2).reshape(quarter, split), wo_z], axis=1)
    last_z, grad_tokens, y_pass, y_got_first = fence(last_z, grad_tokens, y_pass, y_got_first)
    y_passed = send_second(y_pass)
    last_steps = [(last_z, last_z)]
    outs = []
    for step in range(1, planes):
        last_steps.append(line_gather_move(last_steps[-1], step))
        if step == 1:
            low, high = jnp.stack([dn_pair, dn_other], axis=1), jnp.stack([dn_other, dn_pair], axis=1)
            outs.append(jnp.where((plane & 1) == 0, low, high).astype(F32).reshape(w_down.shape))
        elif step == 2:
            outs += spread(gu_all, w_gate_up, g_mlp.astype(F32).reshape(share, 1))
        if step == planes - 1:
            y_sum = own[4].astype(F32) + y_got_first.astype(F32) + y_passed.astype(F32)
            outs.append((residual + y_sum).astype(BF).reshape(tokens.shape))
        moves = fence(*last_steps[-1], *outs)
        last_steps[-1], outs = tuple(moves[:2]), list(moves[2:])
    grad_w_down, grad_w_gate_up, grad_g_mlp, output = outs
    grad_w_qkv, grad_g_attn, grad_w_out = spread_last(last_steps, w_qkv, g_attn.astype(F32).reshape(share, 1), width)
    return (
        output,
        grad_tokens,
        grad_w_qkv,
        grad_w_out,
        grad_w_gate_up,
        grad_w_down,
        grad_g_attn.reshape(share),
        grad_g_mlp.reshape(share),
    )


def solution(mesh):
    in_specs = (
        P("dp", "sp", None),
        P("dp", "sp"),
        P("dp", "sp"),
        P("dp", "sp", None),
        P("sp", None),
        P("sp", None),
        P("sp", None),
        P("sp", None),
        P("sp"),
        P("sp"),
    )
    out_specs = (
        P("dp", "sp", None),
        P("dp", "sp", None),
        P("sp", None),
        P("sp", None),
        P("sp", None),
        P("sp", None),
        P("sp"),
        P("sp"),
    )
    body = fast_body if dict(mesh.shape) == {"dp": 4, "sp": 2 * CHIPS} else general_body
    return jax.shard_map(body, mesh=mesh, in_specs=in_specs, out_specs=out_specs, check_vma=False)
```

```python
import functools
import math

import jax
import jax.numpy as jnp
from jax import lax
from jax.experimental import pallas as pl
from jax.experimental.pallas import tpu as pltpu
from jax.sharding import PartitionSpec as P

D = 2048
H = 32
KV = 4
HD = 64
FF = 5632


EPSILON = 1e-05
ROPE_BASE = 10000.0
MASKED = -1e30


def rope_tables(positions, head_size):
    half_dim = head_size // 2
    frequency = ROPE_BASE ** (-(jnp.arange(half_dim, dtype=jnp.float32) * 2.0 / head_size))
    angles = positions.astype(jnp.float32)[:, None] * frequency[None, :]
    return (jnp.cos(angles), jnp.sin(angles))


def rotate(values, cosine, sine_tab, inverse_turn):
    half_dim = values.shape[-1] // 2
    first_half = values[..., :half_dim]
    second = values[..., half_dim:]
    cos_wide = cosine[:, None, :]
    sin_wide = sine_tab[:, None, :]
    if inverse_turn:
        sin_wide = -sin_wide
    return jnp.concatenate(
        [first_half * cos_wide - second * sin_wide, second * cos_wide + first_half * sin_wide],
        axis=-1,
    )


def rms_norm(values, gain_vec):
    inverse = lax.rsqrt(jnp.mean(values * values, axis=-1, keepdims=True) + EPSILON)
    return (values * inverse * gain_vec, inverse)


def norm_back(values, inverse, gain_vec, upstream):
    scaled = upstream * gain_vec
    inner_mean = jnp.mean(scaled * values, axis=-1, keepdims=True)
    through = inverse * scaled - values * inverse**3 * inner_mean
    gain_grad = jnp.sum(upstream * values * inverse, axis=0)
    return (through, gain_grad)


def attention_inputs(flat_in, qkv_full, gain_vec, cosine, sine_tab):
    row_count = flat_in.shape[0]
    group_size = H // KV
    normed, inverse = rms_norm(flat_in, gain_vec)
    normed = normed.astype(jnp.bfloat16)
    projected = jnp.dot(normed, qkv_full, preferred_element_type=jnp.float32)
    queries = rotate(projected[:, :D].reshape(row_count, H, HD), cosine, sine_tab, False)
    key_heads = rotate(
        projected[:, D : D + KV * HD].reshape(row_count, KV, HD), cosine, sine_tab, False
    )
    value_heads = projected[:, D + KV * HD :].reshape(row_count, KV, HD)
    key_wide = jnp.broadcast_to(key_heads[:, :, None], (row_count, KV, group_size, HD)).reshape(
        row_count, D
    )
    value_wide = jnp.broadcast_to(value_heads[:, :, None], (row_count, KV, group_size, HD)).reshape(
        row_count, D
    )
    stacked = jnp.stack([queries.reshape(row_count, D), key_wide, value_wide]).astype(jnp.bfloat16)
    return (normed, inverse, stacked)


def block_mask(seg_full, position, row_begin, finish):
    row_seg = seg_full[:, row_begin:finish]
    col_seg = seg_full[:, :finish]
    same_doc = row_seg[:, :, None] == col_seg[:, None, :]
    causal = position[row_begin:finish, None] >= position[None, :finish]
    return same_doc & causal[None]


def attention_forward(queries, key_heads, value_heads, seg_full, score_scale):
    length = queries.shape[1]
    block_rows = min(512, length)
    position = jnp.arange(length, dtype=jnp.int32)
    outputs = []
    lse_parts = []
    for block_num in range(length // block_rows):
        row_begin = block_num * block_rows
        finish = row_begin + block_rows
        scores = (
            jnp.einsum(
                "sqhd,skhd->shqk",
                queries[:, row_begin:finish],
                key_heads[:, :finish],
                preferred_element_type=jnp.float32,
            )
            * score_scale
        )
        allowed = block_mask(seg_full, position, row_begin, finish)
        scores = jnp.where(allowed[:, None], scores, MASKED)
        row_max = jnp.max(scores, axis=-1, keepdims=True)
        shifted = jnp.exp(scores - row_max)
        row_total = jnp.sum(shifted, axis=-1, keepdims=True)
        softmax_w = (shifted / row_total).astype(jnp.bfloat16)
        outputs.append(
            jnp.einsum(
                "shqk,skhd->sqhd",
                softmax_w,
                value_heads[:, :finish],
                preferred_element_type=jnp.float32,
            )
        )
        lse_parts.append(row_max + jnp.log(row_total))
    return (jnp.concatenate(outputs, axis=1), jnp.concatenate(lse_parts, axis=2))


def attention_backward(queries, key_heads, value_heads, seg_full, log_sums, grad_out, score_scale):
    length = queries.shape[1]
    block_rows = min(512, length)
    position = jnp.arange(length, dtype=jnp.int32)
    grad_query = []
    grad_key = jnp.zeros(key_heads.shape, jnp.float32)
    grad_value = jnp.zeros(value_heads.shape, jnp.float32)
    for block_num in range(length // block_rows):
        row_begin = block_num * block_rows
        finish = row_begin + block_rows
        query_rows = queries[:, row_begin:finish]
        grad_rows = grad_out[:, row_begin:finish]
        key_part = key_heads[:, :finish]
        value_part = value_heads[:, :finish]
        scores = (
            jnp.einsum("sqhd,skhd->shqk", query_rows, key_part, preferred_element_type=jnp.float32)
            * score_scale
        )
        allowed = block_mask(seg_full, position, row_begin, finish)
        softmax_f = jnp.where(
            allowed[:, None], jnp.exp(scores - log_sums[:, :, row_begin:finish]), 0.0
        )
        grad_probs = jnp.einsum(
            "sqhd,skhd->shqk", grad_rows, value_part, preferred_element_type=jnp.float32
        )
        row_delta = jnp.sum(softmax_f * grad_probs, axis=-1, keepdims=True)
        grad_scores = (softmax_f * (grad_probs - row_delta)).astype(jnp.bfloat16)
        grad_query.append(
            jnp.einsum("shqk,skhd->sqhd", grad_scores, key_part, preferred_element_type=jnp.float32)
            * score_scale
        )
        grad_key = grad_key.at[:, :finish].add(
            jnp.einsum(
                "shqk,sqhd->skhd", grad_scores, query_rows, preferred_element_type=jnp.float32
            )
            * score_scale
        )
        grad_value = grad_value.at[:, :finish].add(
            jnp.einsum(
                "shqk,sqhd->skhd",
                softmax_f.astype(jnp.bfloat16),
                grad_rows,
                preferred_element_type=jnp.float32,
            )
        )
    return (jnp.concatenate(grad_query, axis=1), grad_key, grad_value)


def general_body(tokens, segment_ids, selected, cotangent, w_qkv, w_out, w_gate_up, w_down, g_attn, g_mlp):
    streams, local_len, model_dim = tokens.shape
    sp_count = lax.axis_size("sp")
    sp_index = lax.axis_index("sp")
    row_count = streams * local_len
    group_size = H // KV
    kv_width = KV * HD
    score_scale = HD ** (-0.5)
    contract = (((0,), (0,)), ((), ()))
    seg_full = lax.all_gather(segment_ids, "sp", axis=1, tiled=True)
    first_count = jnp.sum((seg_full == 0).astype(jnp.int32), axis=1, keepdims=True)
    local_pos = (
        sp_index * local_len
        + jnp.arange(local_len, dtype=jnp.int32)[None, :]
        - segment_ids * first_count
    )
    cosine, sine_tab = rope_tables(local_pos.reshape(row_count), HD)
    shards = (w_qkv, w_out, w_gate_up, w_down, g_attn, g_mlp)
    gathered = (
        lax.all_gather(shards[0], "sp", axis=0, tiled=True),
        lax.all_gather(shards[1], "sp", axis=0, tiled=True),
        lax.all_gather(shards[2], "sp", axis=0, tiled=True),
        lax.all_gather(shards[3], "sp", axis=0, tiled=True),
        lax.all_gather(shards[4], "sp", axis=0, tiled=True),
        lax.all_gather(shards[5], "sp", axis=0, tiled=True),
    )
    qkv_full, out_full, gate_up_full, down_full, attn_gain, mlp_gain = gathered
    attn_gain = attn_gain.astype(jnp.float32)
    mlp_gain = mlp_gain.astype(jnp.float32)
    flat_in = tokens.reshape(row_count, model_dim).astype(jnp.float32)
    normed, inverse_one, stacked = attention_inputs(flat_in, qkv_full, attn_gain, cosine, sine_tab)
    head_view = lax.all_to_all(
        stacked.reshape(3, streams, local_len, model_dim),
        "sp",
        split_axis=3,
        concat_axis=2,
        tiled=True,
    )
    length = head_view.shape[2]
    heads_here = head_view.shape[3] // HD
    head_shape = (streams, length, heads_here, HD)
    queries = head_view[0].reshape(head_shape)
    key_heads = head_view[1].reshape(head_shape)
    value_heads = head_view[2].reshape(head_shape)
    attn_heads, log_sums = attention_forward(queries, key_heads, value_heads, seg_full, score_scale)
    attn_send = attn_heads.astype(jnp.bfloat16).reshape(streams, length, heads_here * HD)
    attn_tok = lax.all_to_all(attn_send, "sp", split_axis=1, concat_axis=2, tiled=True).reshape(
        row_count, model_dim
    )
    branch = jnp.dot(attn_tok, out_full, preferred_element_type=jnp.float32)
    residual = flat_in + branch
    inner_f, inverse_two = rms_norm(residual, mlp_gain)
    inner_in = inner_f.astype(jnp.bfloat16)
    gate_up = jnp.dot(inner_in, gate_up_full, preferred_element_type=jnp.float32)
    gate_part = gate_up[:, :FF]
    up_part = gate_up[:, FF:]
    sigmoid_g = jax.nn.sigmoid(gate_part)
    silu_gate = gate_part * sigmoid_g
    hidden = (silu_gate * up_part).astype(jnp.bfloat16)
    result = residual + jnp.dot(hidden, down_full, preferred_element_type=jnp.float32)
    output = result.astype(jnp.bfloat16).reshape(streams, local_len, model_dim)
    qkv_back, out_back, gate_up_back, down_back, attn_gain_b, mlp_gain_b = gathered
    attn_gain_b = attn_gain_b.astype(jnp.float32)
    mlp_gain_b = mlp_gain_b.astype(jnp.float32)
    grad_y = (cotangent * selected[:, :, None].astype(jnp.bfloat16)).reshape(row_count, model_dim)
    grad_hidden = jnp.dot(grad_y, down_back.T, preferred_element_type=jnp.float32)
    silu_slope = sigmoid_g * (1.0 + gate_part * (1.0 - sigmoid_g))
    grad_both = jnp.concatenate(
        [grad_hidden * up_part * silu_slope, grad_hidden * silu_gate], axis=1
    ).astype(jnp.bfloat16)
    grad_inner = jnp.dot(grad_both, gate_up_back.T, preferred_element_type=jnp.float32)
    grad_resid, gain_two = norm_back(residual, inverse_two, mlp_gain_b, grad_inner)
    grad_resid = grad_resid + grad_y.astype(jnp.float32)
    grad_branch = grad_resid.astype(jnp.bfloat16)
    grad_attn = jnp.dot(grad_branch, out_back.T, preferred_element_type=jnp.float32).astype(
        jnp.bfloat16
    )
    grad_view = lax.all_to_all(
        grad_attn.reshape(streams, local_len, model_dim),
        "sp",
        split_axis=2,
        concat_axis=1,
        tiled=True,
    )
    grad_view = grad_view.reshape(head_shape)
    grad_q, grad_k, grad_v = attention_backward(
        queries, key_heads, value_heads, seg_full, log_sums, grad_view, score_scale
    )
    back_send = (
        jnp.stack([grad_q, grad_k, grad_v])
        .astype(jnp.bfloat16)
        .reshape(3, streams, length, heads_here * HD)
    )
    returned = lax.all_to_all(back_send, "sp", split_axis=2, concat_axis=3, tiled=True)
    returned = returned.astype(jnp.float32).reshape(3, row_count, H, HD)
    grad_pq = rotate(returned[0], cosine, sine_tab, True).reshape(row_count, model_dim)
    key_summed = jnp.sum(returned[1].reshape(row_count, KV, group_size, HD), axis=2)
    grad_pk = rotate(key_summed, cosine, sine_tab, True).reshape(row_count, kv_width)
    grad_pv = jnp.sum(returned[2].reshape(row_count, KV, group_size, HD), axis=2).reshape(
        row_count, kv_width
    )
    grad_mixed = jnp.concatenate(
        [grad_pq.astype(jnp.bfloat16), grad_pk.astype(jnp.bfloat16), grad_pv.astype(jnp.bfloat16)],
        axis=1,
    )
    grad_normed = jnp.dot(grad_mixed, qkv_back.T, preferred_element_type=jnp.float32)
    grad_in, gain_one = norm_back(flat_in, inverse_one, attn_gain_b, grad_normed)
    grad_in = grad_in + grad_resid
    grad_tokens = grad_in.astype(jnp.bfloat16).reshape(streams, local_len, model_dim)
    gain_totals = lax.psum((gain_one, gain_two), ("dp", "sp"))
    gain_share = model_dim // sp_count
    grad_g_attn = lax.dynamic_slice_in_dim(gain_totals[0], sp_index * gain_share, gain_share, 0)
    grad_g_mlp = lax.dynamic_slice_in_dim(gain_totals[1], sp_index * gain_share, gain_share, 0)
    row_sums = lax.psum_scatter(
        jnp.concatenate(
            [
                lax.dot_general(normed, grad_mixed, contract, preferred_element_type=jnp.float32),
                lax.dot_general(
                    attn_tok, grad_branch, contract, preferred_element_type=jnp.float32
                ),
                lax.dot_general(inner_in, grad_both, contract, preferred_element_type=jnp.float32),
            ],
            axis=1,
        ).astype(jnp.bfloat16),
        "sp",
        scatter_dimension=0,
        tiled=True,
    )
    down_sums = lax.psum_scatter(
        lax.dot_general(hidden, grad_y, contract, preferred_element_type=jnp.float32).astype(
            jnp.bfloat16
        ),
        "sp",
        scatter_dimension=0,
        tiled=True,
    )
    weight_rows, down_rows = (
        lax.psum(row_sums, "dp").astype(jnp.float32),
        lax.psum(down_sums, "dp").astype(jnp.float32),
    )
    qkv_cols = model_dim + 2 * kv_width
    grad_w_qkv = weight_rows[:, :qkv_cols]
    grad_w_out = weight_rows[:, qkv_cols : qkv_cols + model_dim]
    grad_w_gate_up = weight_rows[:, qkv_cols + model_dim :]
    return (
        output,
        grad_tokens,
        grad_w_qkv,
        grad_w_out,
        grad_w_gate_up,
        down_rows,
        grad_g_attn,
        grad_g_mlp,
    )


CHIPS = 4
BLOCK = 512
SHORT = pl.CostEstimate(flops=1, bytes_accessed=1, transcendentals=0)
LOG2E = math.log2(math.e)
BF = jnp.bfloat16
F32 = jnp.float32
NT = (((1,), (1,)), ((), ()))
TN = (((0,), (0,)), ((), ()))


def swap_pairs(even_mask, odd_mask):
    return [(i, i ^ (odd_mask if i & 1 else even_mask)) for i in range(2 * CHIPS)]


FIRST = swap_pairs(2, 4)
SECOND = swap_pairs(4, 2)
SIBLING = swap_pairs(1, 1)
SAME_CORE = [[0, 2, 4, 6], [1, 3, 5, 7]]
LINE_NEAR = [(z, z ^ 1) for z in range(4)]
LINE_FAR = [(z, z ^ 2) for z in range(4)]


def send_first(x):
    return lax.ppermute(x, "sp", FIRST)


def send_second(x):
    return lax.ppermute(x, "sp", SECOND)


def send_sibling(x):
    return lax.ppermute(x, "sp", SIBLING)


def after(value, *others):
    return lax.optimization_barrier((value,) + others)[0]


def gather_chips(own):
    first = send_first(own)
    second = send_second(after(own, first))
    far = send_second(after(first, second))
    return [own, first, second, far]


def rel_masks(core):
    first = jnp.where(core == 0, 2, 4)
    return first, 6 - first


def fence(*values):
    return lax.optimization_barrier(values)


def gather_vectors(own, me):
    for bit in (1, 2, 4):
        got = lax.ppermute(own, "sp", swap_pairs(bit, bit))
        high = (me & bit) != 0
        own = jnp.concatenate([jnp.where(high, got, own), jnp.where(high, own, got)], axis=1)
    return own


def pick(parts, index):
    return lax.dynamic_index_in_dim(parts, index, 0, keepdims=False)


def pick_sum(parts, index, axis):
    return sum(lax.dynamic_index_in_dim(p, index, axis, keepdims=False).astype(F32) for p in parts)


def line_scatter_sends(parts, got, step, axis):
    planes = parts[0].shape[axis]
    z = lax.axis_index("dp")
    ahead = pick_sum(parts, jnp.clip(planes - step + z, 0, planes - 1), axis)
    back = pick_sum(parts, jnp.clip(z - planes + step, 0, planes - 1), axis)
    if got is not None:
        ahead = ahead + got[0].astype(F32)
        back = back + got[1].astype(F32)
    return ahead.astype(BF), back.astype(BF)


def line_scatter_move(sends, step):
    planes = lax.axis_size("dp")
    right = lax.ppermute(sends[0], "dp", [(i, i + 1) for i in range(step)])
    left = lax.ppermute(sends[1], "dp", [(planes - 1 - i, planes - 2 - i) for i in range(step)])
    return right, left


def line_scatter_end(parts, got, axis):
    own = pick_sum(parts, lax.axis_index("dp"), axis)
    return (own + got[0].astype(F32) + got[1].astype(F32)).astype(BF)


def line_gather_move(got, step):
    planes = lax.axis_size("dp")
    right = lax.ppermute(got[0], "dp", [(i, i + 1) for i in range(step - 1, planes - 1)])
    left = lax.ppermute(got[1], "dp", [(i + 1, i) for i in range(planes - step)])
    return right, left


def line_values(refs, planes, z):
    for step in range(planes):
        place = lax.rem(z - step + planes, planes)
        if step == 0:
            yield place, lambda index: refs[0][index]
        else:
            right, left = refs[step], refs[2 * planes - 1 - step]
            yield place, lambda index, right=right, left=left, step=step: jnp.where(z >= step, right[index], left[index])


def spread_kernel(in_ref, w_ref, g_ref, out_ref, gain_ref):
    planes, _, rows, width = in_ref.shape
    out = in_ref[...].reshape(planes * rows, width).astype(F32)
    out_ref[...] = out
    part = jnp.sum(out * w_ref[...].astype(F32), axis=-1, keepdims=True) / g_ref[...]

    @pl.when(pl.program_id(0) == 0)
    def _():
        gain_ref[...] = part

    @pl.when(pl.program_id(0) > 0)
    def _():
        gain_ref[...] += part


def spread(parts, weight, gain):
    planes, chips, rows, both = parts.shape
    half = both // 2
    total = planes * rows
    line = pl.BlockSpec((total, half), lambda i: (0, i))
    column = pl.BlockSpec((total, 1), lambda i: (0, 0))
    return pl.pallas_call(
        spread_kernel,
        grid=(2 * chips,),
        in_specs=[pl.BlockSpec((planes, 1, rows, half), lambda i: (0, i % chips, 0, i // chips)), line, column],
        out_specs=[line, column],
        out_shape=[jax.ShapeDtypeStruct(weight.shape, F32), jax.ShapeDtypeStruct((total, 1), F32)],
        compiler_params=pltpu.CompilerParams(vmem_limit_bytes=32 * 2**20),
        cost_estimate=SHORT,
        name="spread",
    )(parts, weight, gain)


def spread_last_kernel(z_ref, *refs, planes):
    blocks, (w_ref, g_ref, out_ref, gain_ref, wo_ref) = refs[:-5], refs[-5:]
    rows = blocks[0].shape[0]
    devices = 2 * CHIPS
    width = wo_ref.shape[1]
    heads = width // devices
    each = heads + 2 * HD
    for place, load in line_values(blocks, planes, z_ref[0]):
        span = pl.ds(pl.multiple_of(place * rows, rows), rows)
        pairs = []
        for d in range(devices):
            begin = d * each
            cols = slice(begin, begin + heads)
            out_ref[span, d * heads : (d + 1) * heads] = load((slice(None), cols)).astype(F32)
            pairs.append(load((slice(None), slice(begin + heads, begin + each))).astype(F32))
        for g in range(0, KV, 2):
            low = pairs[2 * g] + pairs[2 * g + 1]
            high = pairs[2 * g + 2] + pairs[2 * g + 3]
            lane = lax.broadcasted_iota(jnp.int32, low.shape, 1)
            begin = width + g * HD
            out_ref[span, begin : begin + 2 * HD] = jnp.where(lane < HD, low, pltpu.roll(high, HD, 1))
            begin = width + (KV + g) * HD
            out_ref[span, begin : begin + 2 * HD] = jnp.where(lane < HD, pltpu.roll(low, HD, 1), high)
        wo_ref[span, :] = load((slice(None), slice(devices * each, devices * each + width))).astype(F32)
    gain_ref[...] = jnp.sum(out_ref[...] * w_ref[...].astype(F32), axis=-1, keepdims=True) / g_ref[...]


def spread_last(steps, weight, gain, width):
    planes = len(steps)
    blocks = [steps[0][0]] + [s[0] for s in steps[1:]] + [s[1] for s in steps[1:]]
    vmem = pl.BlockSpec(memory_space=pltpu.VMEM)
    total = weight.shape[0]
    return pl.pallas_call(
        functools.partial(spread_last_kernel, planes=planes),
        in_specs=[pl.BlockSpec(memory_space=pltpu.SMEM)] + [vmem] * (len(blocks) + 2),
        out_specs=[vmem] * 3,
        out_shape=[
            jax.ShapeDtypeStruct(weight.shape, F32),
            jax.ShapeDtypeStruct((total, 1), F32),
            jax.ShapeDtypeStruct((total, width), F32),
        ],
        compiler_params=pltpu.CompilerParams(vmem_limit_bytes=32 * 2**20),
        cost_estimate=SHORT,
        name="spread_last",
    )(lax.axis_index("dp").reshape(1), *blocks, weight, gain)


def join_kernel(core_ref, mine_ref, theirs_ref, out_ref):
    planes, _, rows, both = mine_ref.shape
    block = jnp.where(pl.program_id(1) == 0, mine_ref[...], theirs_ref[...]).reshape(planes * rows, both)
    out_ref[0, 0, 0] = block[:, : both // 2]
    out_ref[1, 0, 0] = block[:, both // 2 :]


def join(core, mine, theirs):
    planes, chips, rows, both = mine.shape
    spec = pl.BlockSpec((planes, 1, rows, both), lambda c, k, core: (0, c, 0, 0))
    out = pl.pallas_call(
        join_kernel,
        grid_spec=pltpu.PrefetchScalarGridSpec(
            num_scalar_prefetch=1,
            grid=(chips, 2),
            in_specs=[spec, spec],
            out_specs=pl.BlockSpec(
                (2, 1, 1, planes * rows, both // 2), lambda c, k, core: (0, c, (core[0] + k) % 2, 0, 0)
            ),
        ),
        out_shape=jax.ShapeDtypeStruct((2, chips, 2, planes * rows, both // 2), BF),
        compiler_params=pltpu.CompilerParams(vmem_limit_bytes=32 * 2**20),
        cost_estimate=SHORT,
        name="join",
    )(core.reshape(1), mine, theirs)
    return out.reshape(2, 2 * chips * planes * rows, both // 2)


def ffn_kernel(*refs, cuts):
    b_hbm, dy_hbm, wgu_hbm, wd_hbm, hid_hbm, dg_hbm, du_hbm, db_hbm, y_hbm = refs[:9]
    b_ref, dy_ref, wg_ref, wu_ref, wd_ref, hid_ref, dg_ref, du_ref, db_ref, y_ref, sems = refs[9:]
    count = len(cuts) - 1

    def move(source, target, index):
        copy = pltpu.make_async_copy(source, target, sems.at[index])
        copy.start()
        return copy

    b_copy = move(b_hbm, b_ref, 3 * count)
    weights = []
    for c in range(count):
        span = slice(cuts[c], cuts[c + 1])
        gate_copy = move(wgu_hbm.at[0, :, span], wg_ref.at[:, span], 3 * c)
        up_copy = move(wgu_hbm.at[1, :, span], wu_ref.at[:, span], 3 * c + 1)
        weights.append([gate_copy, up_copy])
        if c == 0:
            dy_copy = move(dy_hbm, dy_ref, 3 * count + 1)
        weights[-1].append(move(wd_hbm.at[span, :], wd_ref.at[span, :], 3 * c + 2))
    b_copy.wait()
    for c in range(count):
        span = slice(cuts[c], cuts[c + 1])
        for copy in weights[c][:2]:
            copy.wait()
        gate = jnp.dot(b_ref[...], wg_ref[:, span], preferred_element_type=F32)
        up = jnp.dot(b_ref[...], wu_ref[:, span], preferred_element_type=F32)
        if c == 0:
            dy_copy.wait()
        weights[c][2].wait()
        d_hidden = lax.dot_general(dy_ref[...], wd_ref[span, :], NT, preferred_element_type=F32)
        sigmoid_g = jax.nn.sigmoid(gate)
        silu_gate = gate * sigmoid_g
        hid_ref[:, span] = (silu_gate * up).astype(BF)
        dg_ref[:, span] = (d_hidden * up * (sigmoid_g * (1.0 + gate * (1.0 - sigmoid_g)))).astype(BF)
        du_ref[:, span] = (d_hidden * silu_gate).astype(BF)
    base = 3 * count + 2
    outs = [move(hid_ref, hid_hbm, base), move(dg_ref, dg_hbm, base + 1), move(du_ref, du_hbm, base + 2)]
    y_ref[...] = jnp.dot(hid_ref[...], wd_ref[...], preferred_element_type=F32).astype(BF)
    outs.append(move(y_ref, y_hbm, base + 3))
    d_in = lax.dot_general(dg_ref[...], wg_ref[...], NT, preferred_element_type=F32)
    db_ref[...] = (d_in + lax.dot_general(du_ref[...], wu_ref[...], NT, preferred_element_type=F32)).astype(BF)
    outs.append(move(db_ref, db_hbm, base + 4))
    for copy in outs:
        copy.wait()


def ffn(b_rows, dy_rows, w_gu, w_dn):
    rows, width = b_rows.shape
    hidden = w_dn.shape[0]
    pieces = 3
    cuts = tuple(round(hidden * c / pieces / 128) * 128 for c in range(pieces)) + (hidden,)
    hbm = pl.BlockSpec(memory_space=pl.ANY)
    return pl.pallas_call(
        functools.partial(ffn_kernel, cuts=cuts),
        in_specs=[hbm] * 4,
        out_specs=[hbm] * 5,
        out_shape=[jax.ShapeDtypeStruct((rows, hidden), BF)] * 3 + [jax.ShapeDtypeStruct((rows, width), BF)] * 2,
        scratch_shapes=[pltpu.VMEM((rows, width), BF)] * 2
        + [pltpu.VMEM((width, hidden), BF)] * 2
        + [pltpu.VMEM((hidden, width), BF)]
        + [pltpu.VMEM((rows, hidden), BF)] * 3
        + [pltpu.VMEM((rows, width), BF)] * 2
        + [pltpu.SemaphoreType.DMA((3 * pieces + 7,))],
        compiler_params=pltpu.CompilerParams(vmem_limit_bytes=58 * 2**20),
        cost_estimate=SHORT,
        name="ffn",
    )(b_rows, dy_rows, w_gu, w_dn)


def grad_gu_kernel(core_ref, *refs, count):
    left, right = refs[: 2 * count], refs[2 * count : 4 * count]
    half = right[0].shape[1]
    for side in range(2):
        for kind in range(2):
            total = None
            for r in range(count):
                a_rows = left[side * count + r][...]
                part = lax.dot_general(a_rows, right[kind * count + r][...], TN, preferred_element_type=F32)
                total = part if total is None else total + part
            out_ref = refs[4 * count + side]
            planes, _, rows, _ = out_ref.shape
            out_ref[:, 0, :, kind * half : (kind + 1) * half] = total.astype(BF).reshape(planes, rows, half)


def grad_gu(core, b_rows, dg_rows, du_rows, share, planes):
    count = len(b_rows)
    tokens, width = b_rows[0].shape
    hidden = dg_rows[0].shape[1]
    keep = pl.BlockSpec((tokens, share), lambda c, core: (0, 2 * c + core[0]))
    give = pl.BlockSpec((tokens, share), lambda c, core: (0, 2 * c + 1 - core[0]))
    whole = pl.BlockSpec((tokens, hidden), lambda c, core: (0, 0))
    rows = share // planes
    out = pl.BlockSpec((planes, 1, rows, 2 * hidden), lambda c, core: (0, c, 0, 0))
    return pl.pallas_call(
        functools.partial(grad_gu_kernel, count=count),
        grid_spec=pltpu.PrefetchScalarGridSpec(
            num_scalar_prefetch=1,
            grid=(width // (2 * share),),
            in_specs=[keep] * count + [give] * count + [whole] * (2 * count),
            out_specs=[out, out],
        ),
        out_shape=[jax.ShapeDtypeStruct((planes, width // (2 * share), rows, 2 * hidden), BF)] * 2,
        compiler_params=pltpu.CompilerParams(vmem_limit_bytes=58 * 2**20),
        cost_estimate=SHORT,
        name="grad_gu",
    )(core.reshape(1), *b_rows, *b_rows, *dg_rows, *du_rows)


def grad_qkv_kernel(place_ref, *refs, count):
    dp_ref, out_ref = refs[-2:]
    total = None
    for r in range(count):
        part = lax.dot_general(refs[r][...], dp_ref[place_ref[r]], TN, preferred_element_type=F32)
        total = part if total is None else total + part
    planes, rows, wide = out_ref.shape
    columns = total.shape[1]
    for k in range(wide // columns):
        block = total[k * planes * rows : (k + 1) * planes * rows].astype(BF)
        out_ref[:, :, k * columns : (k + 1) * columns] = block.reshape(planes, rows, columns)


def grad_qkv(places, a_rows, dp_heads, planes):
    count = len(a_rows)
    tokens, width = a_rows[0].shape
    columns = dp_heads.shape[2]
    share = width // count
    depth = 2 * share
    return pl.pallas_call(
        functools.partial(grad_qkv_kernel, count=count),
        grid_spec=pltpu.PrefetchScalarGridSpec(
            num_scalar_prefetch=1,
            grid=(width // depth,),
            in_specs=[pl.BlockSpec((tokens, depth), lambda i, p: (0, i))] * count
            + [pl.BlockSpec(dp_heads.shape, lambda i, p: (0, 0, 0))],
            out_specs=pl.BlockSpec((planes, share // planes, 2 * columns), lambda i, p: (0, 0, i)),
        ),
        out_shape=jax.ShapeDtypeStruct((planes, share // planes, count * columns), BF),
        compiler_params=pltpu.CompilerParams(vmem_limit_bytes=48 * 2**20),
        cost_estimate=SHORT,
        name="grad_qkv",
    )(places, *a_rows, dp_heads)


def swap_halves(values):
    width = values.shape[-1]
    lane = lax.broadcasted_iota(jnp.int32, values.shape, 1)
    ahead = pltpu.roll(values, width - HD // 2, 1)
    behind = pltpu.roll(values, HD // 2, 1)
    return jnp.where(lane % HD < HD // 2, ahead, behind)


def project_kernel(place_ref, x_ref, gain_ref, cos_ref, sin_ref, *refs, count):
    wq_refs, wkv_refs = refs[:count], refs[count : 2 * count]
    send_ref, normed_ref, inv_ref, normed_scr = refs[2 * count :]
    share = normed_scr.shape[2]

    @pl.when(pl.program_id(0) == 0)
    def _():
        x = x_ref[...].astype(F32)
        inv = lax.rsqrt(jnp.mean(x * x, axis=-1, keepdims=True) + EPSILON)
        normed = (x * inv * gain_ref[...]).astype(BF)
        normed_ref[...] = normed
        inv_ref[...] = inv
        for part in range(count):
            normed_scr[part] = normed[:, part * share : (part + 1) * share]

    pq = pkv = None
    for r in range(count):
        a_rows = normed_scr[place_ref[r]]
        q_part = jnp.dot(a_rows, wq_refs[r][...], preferred_element_type=F32)
        kv_part = jnp.dot(a_rows, wkv_refs[r][...], preferred_element_type=F32)
        pq = q_part if pq is None else pq + q_part
        pkv = kv_part if pkv is None else pkv + kv_part
    cos = cos_ref[...]
    sin = sin_ref[...]
    heads = pq.shape[1]
    q_scale = LOG2E * HD**-0.5
    turned = pq * jnp.tile(cos, (1, heads // 128)) + swap_halves(pq) * jnp.tile(sin, (1, heads // 128))
    send_ref[0, :, :heads] = (turned * q_scale).astype(BF)
    lane = lax.broadcasted_iota(jnp.int32, pkv.shape, 1)
    turned_kv = jnp.where(lane < HD, pkv * cos + swap_halves(pkv) * sin, pkv)
    send_ref[0, :, heads:] = turned_kv.astype(BF)


def project(places, x, gain, cos, sin, parts):
    rows, width = x.shape
    count = len(parts)
    heads = width // count
    out_width = heads + 2 * HD
    depth = parts[0].shape[0]
    first_kv = width // (2 * HD)
    return pl.pallas_call(
        functools.partial(project_kernel, count=count),
        grid_spec=pltpu.PrefetchScalarGridSpec(
            num_scalar_prefetch=1,
            grid=(count,),
            in_specs=[
                pl.BlockSpec((rows, width), lambda d, p: (0, 0)),
                pl.BlockSpec((1, width), lambda d, p: (0, 0)),
                pl.BlockSpec((rows, 128), lambda d, p: (0, 0)),
                pl.BlockSpec((rows, 128), lambda d, p: (0, 0)),
            ]
            + [pl.BlockSpec((depth, heads), lambda d, p: (0, d))] * count
            + [pl.BlockSpec((depth, 2 * HD), lambda d, p: (0, first_kv + d // 2))] * count,
            out_specs=[
                pl.BlockSpec((1, rows, out_width), lambda d, p: (d, 0, 0)),
                pl.BlockSpec((rows, width), lambda d, p: (0, 0)),
                pl.BlockSpec((rows, 1), lambda d, p: (0, 0)),
            ],
            scratch_shapes=[pltpu.VMEM((count, rows, width // count), BF)],
        ),
        out_shape=[
            jax.ShapeDtypeStruct((count, rows, out_width), BF),
            jax.ShapeDtypeStruct((rows, width), BF),
            jax.ShapeDtypeStruct((rows, 1), F32),
        ],
        compiler_params=pltpu.CompilerParams(vmem_limit_bytes=48 * 2**20),
        cost_estimate=SHORT,
        name="project",
    )(places, x, gain, cos, sin, *parts, *parts)


def out_proj_kernel(place_ref, attn_ref, x_ref, gain_ref, *refs, count):
    parts, (resid_ref, inv_ref, inner_ref) = refs[:count], refs[count:]
    width = x_ref.shape[1]
    tile = 512
    square = None
    for begin in range(0, width, tile):
        cols = slice(begin, begin + tile)
        total = x_ref[:, cols].astype(F32)
        for r in range(count):
            total = total + jnp.dot(attn_ref[place_ref[r]], parts[r][:, cols], preferred_element_type=F32)
        resid_ref[:, cols] = total
        part = jnp.sum(total * total, axis=-1, keepdims=True)
        square = part if square is None else square + part
    inv = lax.rsqrt(square / width + EPSILON)
    inv_ref[...] = inv
    inner_ref[...] = (resid_ref[...] * inv * gain_ref[...]).astype(BF)


def out_proj(places, attn, x, gain, parts):
    count, rows, share = attn.shape
    width = x.shape[1]
    step = rows // 2
    line = pl.BlockSpec((step, width), lambda i, p: (i, 0))
    return pl.pallas_call(
        functools.partial(out_proj_kernel, count=count),
        grid_spec=pltpu.PrefetchScalarGridSpec(
            num_scalar_prefetch=1,
            grid=(rows // step,),
            in_specs=[
                pl.BlockSpec((count, step, share), lambda i, p: (0, i, 0)),
                line,
                pl.BlockSpec((1, width), lambda i, p: (0, 0)),
            ]
            + [pl.BlockSpec((share, width), lambda i, p: (0, 0))] * count,
            out_specs=[line, pl.BlockSpec((step, 1), lambda i, p: (i, 0)), line],
        ),
        out_shape=[
            jax.ShapeDtypeStruct((rows, width), F32),
            jax.ShapeDtypeStruct((rows, 1), F32),
            jax.ShapeDtypeStruct((rows, width), BF),
        ],
        compiler_params=pltpu.CompilerParams(vmem_limit_bytes=56 * 2**20),
        cost_estimate=SHORT,
        name="out_proj",
    )(places, attn, x, gain, *parts)


def resid_back_kernel(place_ref, db_ref, first_ref, passed_ref, resid_ref, inv_ref, gain_ref, dy_ref, *refs, count):
    parts, (d_resid_ref, branch_ref, send_ref) = refs[:count], refs[count:]
    d_inner = db_ref[...].astype(F32) + first_ref[...].astype(F32) + passed_ref[...].astype(F32)
    resid = resid_ref[...]
    inv = inv_ref[...]
    scaled = d_inner * gain_ref[...]
    inner_mean = jnp.mean(scaled * resid, axis=-1, keepdims=True)
    d_resid = dy_ref[...].astype(F32) + inv * scaled - resid * (inv * inv * inv * inner_mean)
    d_resid_ref[...] = d_resid
    branch = d_resid.astype(BF)
    branch_ref[...] = branch
    for r in range(count):
        d_attn = lax.dot_general(branch, parts[r][...], NT, preferred_element_type=F32)
        send_ref[place_ref[r]] = d_attn.astype(BF)


def resid_back(places, db_own, db_first, db_passed, resid, inv, gain, dy, parts):
    rows, width = resid.shape
    count = len(parts)
    share = parts[0].shape[0]
    step = rows // 2
    line = pl.BlockSpec((step, width), lambda i, p: (i, 0))
    return pl.pallas_call(
        functools.partial(resid_back_kernel, count=count),
        grid_spec=pltpu.PrefetchScalarGridSpec(
            num_scalar_prefetch=1,
            grid=(rows // step,),
            in_specs=[line, line, line, line]
            + [pl.BlockSpec((step, 1), lambda i, p: (i, 0)), pl.BlockSpec((1, width), lambda i, p: (0, 0)), line]
            + [pl.BlockSpec((share, width), lambda i, p: (0, 0))] * count,
            out_specs=[line, line, pl.BlockSpec((count, step, share), lambda i, p: (0, i, 0))],
        ),
        out_shape=[
            jax.ShapeDtypeStruct((rows, width), F32),
            jax.ShapeDtypeStruct((rows, width), BF),
            jax.ShapeDtypeStruct((count, rows, share), BF),
        ],
        compiler_params=pltpu.CompilerParams(vmem_limit_bytes=56 * 2**20),
        cost_estimate=SHORT,
        name="resid_back",
    )(places, db_own, db_first, db_passed, resid, inv, gain, dy, *parts)


def in_back_kernel(place_ref, back_ref, x_ref, inv_ref, gain_ref, d_resid_ref, *refs, count):
    parts, (out_ref, mixed, d_scr) = refs[:count], refs[count:]
    devices, _, width = back_ref.shape
    heads = width - 2 * HD
    for d in range(devices):
        mixed[:, d * heads : (d + 1) * heads] = back_ref[d, :, :heads]
    base = devices * heads
    for g in range(KV):
        pair = back_ref[2 * g, :, heads:].astype(F32) + back_ref[2 * g + 1, :, heads:].astype(F32)
        mixed[:, base + 2 * g * HD : base + 2 * (g + 1) * HD] = pair.astype(BF)
    for r in range(count):
        d_scr[place_ref[r]] = lax.dot_general(mixed[...], parts[r][...], NT, preferred_element_type=F32)
    inv = inv_ref[...]
    share = d_scr.shape[2]
    inner = None
    for c in range(count):
        cols = slice(c * share, (c + 1) * share)
        part = jnp.sum(d_scr[c] * gain_ref[:, cols] * x_ref[:, cols].astype(F32), axis=-1, keepdims=True)
        inner = part if inner is None else inner + part
    factor = inv * inv * inv * (inner / (count * share))
    for c in range(count):
        cols = slice(c * share, (c + 1) * share)
        through = inv * (d_scr[c] * gain_ref[:, cols]) - x_ref[:, cols].astype(F32) * factor
        out_ref[:, cols] = (d_resid_ref[:, cols] + through).astype(BF)


def in_back(places, back, x, inv, gain, d_resid, parts):
    rows, width = x.shape
    count = len(parts)
    share, columns = parts[0].shape
    step = rows // 2
    line = pl.BlockSpec((step, width), lambda i, p: (i, 0))
    return pl.pallas_call(
        functools.partial(in_back_kernel, count=count),
        grid_spec=pltpu.PrefetchScalarGridSpec(
            num_scalar_prefetch=1,
            grid=(rows // step,),
            in_specs=[
                pl.BlockSpec((count, step, back.shape[2]), lambda i, p: (0, i, 0)),
                line,
                pl.BlockSpec((step, 1), lambda i, p: (i, 0)),
                pl.BlockSpec((1, width), lambda i, p: (0, 0)),
                line,
            ]
            + [pl.BlockSpec((share, columns), lambda i, p: (0, 0))] * count,
            out_specs=line,
            scratch_shapes=[pltpu.VMEM((step, columns), BF), pltpu.VMEM((count, step, share), F32)],
        ),
        out_shape=jax.ShapeDtypeStruct((rows, width), BF),
        compiler_params=pltpu.CompilerParams(vmem_limit_bytes=56 * 2**20),
        cost_estimate=SHORT,
        name="in_back",
    )(places, back, x, inv, gain, d_resid, *parts)


def grad_wo_kernel(core_ref, keep_ref, give_ref, branch_ref, keep_out, give_out):
    branch = branch_ref[...]
    keep_out[0] = lax.dot_general(keep_ref[0], branch, TN, preferred_element_type=F32).astype(BF)
    give_out[0] = lax.dot_general(give_ref[0], branch, TN, preferred_element_type=F32).astype(BF)


def grad_wo(core, attn, branch):
    devices, rows, share = attn.shape
    width = branch.shape[1]
    out = pl.BlockSpec((1, share, width), lambda c, core: (c, 0, 0))
    return pl.pallas_call(
        grad_wo_kernel,
        grid_spec=pltpu.PrefetchScalarGridSpec(
            num_scalar_prefetch=1,
            grid=(devices // 2,),
            in_specs=[
                pl.BlockSpec((1, rows, share), lambda c, core: (2 * c + core[0], 0, 0)),
                pl.BlockSpec((1, rows, share), lambda c, core: (2 * c + 1 - core[0], 0, 0)),
                pl.BlockSpec((rows, width), lambda c, core: (0, 0)),
            ],
            out_specs=[out, out],
        ),
        out_shape=[jax.ShapeDtypeStruct((devices // 2, share, width), BF)] * 2,
        compiler_params=pltpu.CompilerParams(vmem_limit_bytes=48 * 2**20),
        cost_estimate=SHORT,
        name="grad_wo",
    )(core.reshape(1), attn, attn, branch)


def grad_dn_kernel(core_ref, *refs, count):
    left, right, (keep_out, give_out) = refs[:count], refs[count : 2 * count], refs[2 * count :]
    total = None
    for r in range(count):
        part = lax.dot_general(left[r][...], right[r][...], TN, preferred_element_type=F32)
        total = part if total is None else total + part
    half = total.shape[0] // 2
    total = total.astype(BF)
    low = core_ref[0] == 0
    keep_out[...] = jnp.where(low, total[:half], total[half:])
    give_out[...] = jnp.where(low, total[half:], total[:half])


def grad_dn(core, hid_rows, dy_rows):
    count = len(hid_rows)
    tokens, hidden = hid_rows[0].shape
    width = dy_rows[0].shape[1]
    tile = 512
    out = pl.BlockSpec((hidden // 2, tile), lambda i, core: (0, i))
    return pl.pallas_call(
        functools.partial(grad_dn_kernel, count=count),
        grid_spec=pltpu.PrefetchScalarGridSpec(
            num_scalar_prefetch=1,
            grid=(width // tile,),
            in_specs=[pl.BlockSpec((tokens, hidden), lambda i, core: (0, 0))] * count
            + [pl.BlockSpec((tokens, tile), lambda i, core: (0, i))] * count,
            out_specs=[out, out],
        ),
        out_shape=[jax.ShapeDtypeStruct((hidden // 2, width), BF)] * 2,
        compiler_params=pltpu.CompilerParams(vmem_limit_bytes=56 * 2**20),
        cost_estimate=SHORT,
        name="grad_dn",
    )(core.reshape(1), *hid_rows, *dy_rows)


def attend_kernel(zeros_ref, q_ref, kv_ref, *refs, heads, start, stop):
    o_ref, send_ref, lse_ref, k_scr, v_scr, acc_ref, max_ref = refs[-7:]
    block = pl.program_id(0) + start
    zeros = zeros_ref[0]
    size = q_ref.shape[0]

    @pl.when(block == start)
    def _():
        for part in range(stop):
            rows = slice(part * size, (part + 1) * size)
            both = kv_ref[rows, :].astype(F32)
            lane = lax.broadcasted_iota(jnp.int32, both.shape, 1)
            k_scr[rows, :] = kv_ref[rows, :HD]
            v_scr[rows, :] = jnp.where(lane < HD, pltpu.roll(both, HD, 1), 1.0).astype(BF)

    first_row = block * size
    lowest = jnp.where(first_row >= zeros, zeros // size, 0)
    acc_ref[...] = jnp.zeros_like(acc_ref)
    max_ref[...] = jnp.full_like(max_ref, MASKED)
    q_heads = [q_ref[:, h * HD : (h + 1) * HD] for h in range(heads)]

    def step(index, masked):
        first_key = pl.multiple_of(index * size, size)
        keys = k_scr[pl.ds(first_key, size), :]
        values = v_scr[pl.ds(first_key, size), :]
        if masked:
            row = first_row + lax.broadcasted_iota(jnp.int32, (size, size), 0)
            col = first_key + lax.broadcasted_iota(jnp.int32, (size, size), 1)
            begin = jnp.where(row >= zeros, zeros, 0)
            refused = (col > row) | (col < begin)

        def score(h):
            return lax.dot_general(q_heads[h], keys, NT, preferred_element_type=F32)

        upcoming = score(0)
        for h in range(heads):
            scores = upcoming
            if h + 1 < heads:
                upcoming = score(h + 1)
            if masked:
                scores = jnp.where(refused, MASKED, scores)
            old_max = max_ref[h]
            new_max = jnp.maximum(old_max, jnp.max(scores, axis=-1, keepdims=True))
            weights = jnp.exp2(scores - jnp.tile(new_max, (1, size // 128)))
            shrink = jnp.exp2(old_max - new_max)
            acc_ref[h] = acc_ref[h] * shrink + jnp.dot(weights.astype(BF), values, preferred_element_type=F32)
            max_ref[h] = new_max

    def visit(index, carry):
        first_key = index * size
        mixed = (index == block) | ((first_row + size > zeros) & (first_key < zeros))

        @pl.when(mixed)
        def _():
            step(index, True)

        @pl.when(jnp.logical_not(mixed))
        def _():
            step(index, False)

        return carry

    lax.fori_loop(lowest, block + 1, visit, 0)
    for h in range(heads):
        acc = acc_ref[h]
        total = acc[:, HD : HD + 1]
        out = acc[:, :HD] / total
        o_ref[:, h * HD : (h + 1) * HD] = out
        send_ref[0, :, h * HD : (h + 1) * HD] = out.astype(BF)
        lse = max_ref[h] + jnp.log2(total)
        lse_ref[0, h : h + 1, :] = jnp.transpose(lse)[:1]


def attend(zeros, qkv, start, stop, before=None):
    length, width = qkv.shape
    q_width = width - 2 * HD
    heads = q_width // HD
    size = BLOCK
    blocks = length // size
    before = () if before is None else before
    return pl.pallas_call(
        functools.partial(attend_kernel, heads=heads, start=start, stop=stop),
        grid_spec=pltpu.PrefetchScalarGridSpec(
            num_scalar_prefetch=1,
            grid=(stop - start,),
            in_specs=[
                pl.BlockSpec((size, q_width), lambda i, z: (i + start, 0)),
                pl.BlockSpec((length, 2 * HD), lambda i, z: (0, q_width // (2 * HD))),
            ]
            + [pl.BlockSpec(memory_space=pl.ANY)] * len(before),
            out_specs=[
                pl.BlockSpec((size, q_width), lambda i, z: (i + start, 0)),
                pl.BlockSpec((1, size, q_width), lambda i, z: (i + start, 0, 0)),
                pl.BlockSpec((1, heads, size), lambda i, z: (i + start, 0, 0)),
            ],
            scratch_shapes=[
                pltpu.VMEM((length, HD), BF),
                pltpu.VMEM((length, 2 * HD), BF),
                pltpu.VMEM((heads, size, 2 * HD), F32),
                pltpu.VMEM((heads, size, 128), F32),
            ],
        ),
        out_shape=[
            jax.ShapeDtypeStruct((length, q_width), F32),
            jax.ShapeDtypeStruct((blocks, size, q_width), BF),
            jax.ShapeDtypeStruct((blocks, heads, size), F32),
        ],
        input_output_aliases={3 + i: i for i in range(len(before))},
        compiler_params=pltpu.CompilerParams(vmem_limit_bytes=48 * 2**20),
        cost_estimate=SHORT,
        name="attend",
    )(zeros, qkv, qkv, *before)


def attend_back_kernel(
    zeros_ref, q_ref, kv_ref, do_ref, lse_ref, cos_ref, sin_ref, extra_ref, *refs, heads, start
):
    send_ref, dq_acc, delta_ref, q_scr, do_scr = refs[-5:]
    block = pl.program_id(0) + start
    zeros = zeros_ref[0]
    size = kv_ref.shape[0]
    length = q_ref.shape[0]
    blocks = length // size

    @pl.when(block == start)
    def _():
        if start == 0:
            dq_acc[...] = jnp.zeros_like(dq_acc)
        else:
            dq_acc[...] = refs[0][...]
            delta_ref[...] = extra_ref[...]
        for part in range(start, blocks):
            rows = slice(part * size, (part + 1) * size)
            if start == 0:
                product = jnp.transpose(do_ref[rows, :].astype(F32) * extra_ref[rows, :])
            for h in range(heads):
                cols = slice(h * HD, (h + 1) * HD)
                q_scr[h, rows, :] = q_ref[rows, cols]
                do_scr[h, rows, :] = do_ref[rows, cols]
                if start == 0:
                    delta_ref[part, h : h + 1, :] = jnp.sum(product[cols], axis=0, keepdims=True)

    first_key = block * size
    both = kv_ref[...]
    keys = both[:, :HD]
    values = both[:, HD:]
    keys_t = jnp.transpose(keys.astype(F32)).astype(BF)
    highest = jnp.where(first_key + size <= zeros, jnp.minimum((zeros + size - 1) // size, blocks), blocks)

    def step(index, carry, masked):
        first_row = pl.multiple_of(index * size, size)
        span = pl.ds(first_row, size)
        if masked:
            col = first_key + lax.broadcasted_iota(jnp.int32, (size, size), 0)
            row = first_row + lax.broadcasted_iota(jnp.int32, (size, size), 1)
            begin = jnp.where(row >= zeros, zeros, 0)
            refused = (col > row) | (col < begin)

        def products(h):
            q_rows = q_scr[h, span, :]
            do_rows = do_scr[h, span, :]
            scores = lax.dot_general(keys, q_rows, NT, preferred_element_type=F32)
            d_prob = lax.dot_general(values, do_rows, NT, preferred_element_type=F32)
            return q_rows, do_rows, scores, d_prob

        upcoming = products(0)
        dk_sum, dv_sum = carry
        for h in range(heads):
            q_rows, do_rows, scores, d_prob = upcoming
            if h + 1 < heads:
                upcoming = products(h + 1)
            shifted = scores - lse_ref[index, h : h + 1, :]
            if masked:
                shifted = jnp.where(refused, MASKED, shifted)
            prob = jnp.exp2(shifted)
            d_score = (prob * (d_prob - delta_ref[index, h : h + 1, :])).astype(BF)
            dv_sum = dv_sum + jnp.dot(prob.astype(BF), do_rows, preferred_element_type=F32)
            dk_sum = dk_sum + jnp.dot(d_score, q_rows, preferred_element_type=F32)
            dq_acc[h * HD : (h + 1) * HD, span] += jnp.dot(keys_t, d_score, preferred_element_type=F32)
        return dk_sum, dv_sum

    def visit(index, carry):
        first_row = index * size
        mixed = (index == block) | ((first_row + size > zeros) & (first_key < zeros))
        return lax.cond(
            mixed,
            lambda c: step(index, c, True),
            lambda c: step(index, c, False),
            carry,
        )

    zero = jnp.zeros((size, HD), F32)
    dk_sum, dv_sum = lax.fori_loop(block, highest, visit, (zero, zero))
    q_width = heads * HD
    done = pl.ds(pl.multiple_of(first_key, size), size)
    cos = cos_ref[...]
    sin = sin_ref[...]
    dq = jnp.transpose(dq_acc[:, done]) * HD**-0.5
    dq = dq * jnp.tile(cos, (1, q_width // 128)) - swap_halves(dq) * jnp.tile(sin, (1, q_width // 128))
    send_ref[0, :, :q_width] = dq.astype(BF)
    dkv = jnp.concatenate([dk_sum * (1.0 / LOG2E), dv_sum], axis=1)
    lane = lax.broadcasted_iota(jnp.int32, dkv.shape, 1)
    send_ref[0, :, q_width:] = jnp.where(lane < HD, dkv * cos - swap_halves(dkv) * sin, dkv).astype(BF)


def attend_back(zeros, qkv, d_out, lse, cos, sin, start, stop, out=None, before=None):
    length, width = qkv.shape
    q_width = width - 2 * HD
    heads = q_width // HD
    size = BLOCK
    blocks = length // size
    whole = lambda *shape: pl.BlockSpec(shape, lambda j, z: (0,) * len(shape))
    if before is None:
        operands = (out,)
        specs = [whole(length, q_width)]
        aliases = {}
    else:
        send, d_query, delta = before
        operands = (delta, d_query, send)
        specs = [whole(blocks, heads, size), whole(q_width, length), pl.BlockSpec(memory_space=pl.ANY)]
        aliases = {9: 0}
    return pl.pallas_call(
        functools.partial(attend_back_kernel, heads=heads, start=start),
        grid_spec=pltpu.PrefetchScalarGridSpec(
            num_scalar_prefetch=1,
            grid=(stop - start,),
            in_specs=[
                whole(length, q_width),
                pl.BlockSpec((size, 2 * HD), lambda j, z: (j + start, q_width // (2 * HD))),
                whole(length, q_width),
                whole(blocks, heads, size),
                pl.BlockSpec((size, 128), lambda j, z: (j + start, 0)),
                pl.BlockSpec((size, 128), lambda j, z: (j + start, 0)),
            ]
            + specs,
            out_specs=[
                pl.BlockSpec((1, size, width), lambda j, z: (j + start, 0, 0)),
                whole(q_width, length),
                whole(blocks, heads, size),
            ],
            scratch_shapes=[
                pltpu.VMEM((heads, length, HD), BF),
                pltpu.VMEM((heads, length, HD), BF),
            ],
        ),
        out_shape=[
            jax.ShapeDtypeStruct((blocks, size, width), BF),
            jax.ShapeDtypeStruct((q_width, length), F32),
            jax.ShapeDtypeStruct((blocks, heads, size), F32),
        ],
        input_output_aliases=aliases,
        compiler_params=pltpu.CompilerParams(vmem_limit_bytes=58 * 2**20),
        cost_estimate=SHORT,
        name="attend_back",
    )(zeros, qkv, qkv, d_out, lse, cos, sin, *operands)


def turn_tables(positions):
    cosine, sine = rope_tables(positions, HD)
    return jnp.concatenate([cosine] * 4, axis=1), jnp.concatenate([-sine, sine, -sine, sine], axis=1)


def fast_body(tokens, segment_ids, selected, cotangent, w_qkv, w_out, w_gate_up, w_down, g_attn, g_mlp):
    _, rows, width = tokens.shape
    devices = 2 * CHIPS
    me = lax.axis_index("sp")
    core = me & 1
    planes = lax.axis_size("dp")
    share = width // devices
    kv_width = KV * HD
    first_mask, second_mask = rel_masks(core)
    other = me ^ 1
    chip = me // 2
    place_list = [me, me ^ first_mask, me ^ second_mask, me ^ 6]
    place_list += [other, other ^ second_mask, other ^ first_mask, other ^ 6]
    places = jnp.stack(place_list)
    hidden_chip = 2 * w_down.shape[0]
    quarter = share // planes
    plane = lax.axis_index("dp")
    length = devices * rows
    blocks = length // BLOCK

    count = jnp.sum((segment_ids == 0).astype(F32))
    vectors = jnp.stack([g_attn.astype(F32), g_mlp.astype(F32)] + [jnp.full((share,), count)] * 6)
    paired = [w_qkv[:, :width]]
    for head in range(KV):
        paired.append(w_qkv[:, width + head * HD : width + (head + 1) * HD])
        paired.append(w_qkv[:, width + kv_width + head * HD : width + kv_width + (head + 1) * HD])
    qkv_own = jnp.concatenate(paired, axis=1)
    gu_rows = lax.dynamic_slice_in_dim(w_gate_up, plane * quarter, quarter, 0)
    gu_send = []
    for place in range(CHIPS):
        for begin in (place * hidden_chip, (CHIPS + place) * hidden_chip):
            gu_send.append(gu_rows[:, begin : begin + hidden_chip])
    gu_send = jnp.stack([jnp.concatenate(gu_send[2 * c : 2 * c + 2], axis=1) for c in range(CHIPS)])
    vectors = gather_vectors(vectors, me)
    vectors, qkv_own, gu_send = fence(vectors, qkv_own, gu_send)
    qkv_first = send_first(qkv_own)
    attn_gain = vectors[0:1]
    mlp_gain = vectors[1:2]
    zeros = jnp.sum(vectors[2].reshape(devices, share)[:, 0]).astype(jnp.int32)
    zeros_one = zeros.reshape(1)
    local_pos = me * rows + jnp.arange(rows, dtype=jnp.int32) - segment_ids.reshape(rows) * zeros
    cos, sin = turn_tables(local_pos)
    dy = (cotangent * selected[:, :, None].astype(BF)).reshape(rows, width)
    qkv_own, qkv_first, cos, sin = fence(qkv_own, qkv_first, cos, sin)
    qkv_second = send_second(qkv_own)
    qkv_theirs = [send_sibling(qkv_own), send_sibling(qkv_first)]
    all_places = jnp.arange(length, dtype=jnp.int32)
    cos_all, sin_all = turn_tables(all_places - jnp.where(all_places >= zeros, zeros, 0))
    qkv_first, qkv_second, cos_all, sin_all, *qkv_theirs = fence(qkv_first, qkv_second, cos_all, sin_all, *qkv_theirs)
    qkv_far = send_second(qkv_first)
    qkv_theirs.append(send_sibling(qkv_second))
    qkv_far, dy, *qkv_theirs = fence(qkv_far, dy, *qkv_theirs)
    qkv_theirs.append(send_sibling(qkv_far))
    qkv_parts = [qkv_own, qkv_first, qkv_second, qkv_far] + qkv_theirs
    x_bf = tokens.reshape(rows, width)
    x_bf, w_out, gu_send, *qkv_parts = fence(x_bf, w_out, gu_send, *qkv_parts)
    out_first = send_first(w_out)
    gu_part = lax.all_to_all(gu_send, "sp", 0, 0, axis_index_groups=SAME_CORE, tiled=True)
    qkv_send, normed, inv_one = project(places, x_bf, attn_gain, cos, sin, qkv_parts)
    qkv_send, out_first = fence(qkv_send, out_first)
    gu_mine = lax.all_gather(after(gu_part, qkv_send), "dp", axis=0, tiled=False)
    gu_mine = lax.all_gather(after(gu_part, qkv_send), "dp", axis=0, tiled=False)
    down_theirs = send_sibling(w_down)
    w_dn = jnp.where(
        core == 0, jnp.concatenate([w_down, down_theirs], axis=0), jnp.concatenate([down_theirs, w_down], axis=0)
    )
    qkv_heads = lax.all_to_all(qkv_send, "sp", 0, 0, tiled=True).reshape(length, qkv_send.shape[2])

    cuts = (0, (5 * blocks) // 8, (7 * blocks) // 8, blocks)
    qkv_heads, w_dn, out_first = fence(qkv_heads, w_dn, out_first)
    out_second = send_second(after(w_out, qkv_heads))
    dy_first = send_first(after(dy, qkv_heads))
    fwd = attend(zeros_one, qkv_heads, cuts[0], cuts[1])
    qkv_heads, out_second, dy_first, out_first, dy, *fwd = fence(qkv_heads, out_second, dy_first, out_first, dy, *fwd)
    out_far = send_second(out_first)
    dy_second = send_second(dy)
    fwd = attend(zeros_one, qkv_heads, cuts[1], cuts[2], fwd)
    qkv_heads, out_far, dy_second, dy_first, *fwd = fence(qkv_heads, out_far, dy_second, dy_first, *fwd)
    dy_far = send_second(dy_first)
    gu_theirs = send_sibling(after(gu_mine, fwd[2]))
    out_heads, out_send, lse = attend(zeros_one, qkv_heads, cuts[2], cuts[3], fwd)
    out_parts = [w_out, out_first, out_second, out_far]
    out_parts = out_parts + [send_sibling(part) for part in out_parts]
    out_send, gu_mine, gu_theirs = fence(out_send, gu_mine, gu_theirs)
    attn_tok = lax.all_to_all(out_send, "sp", 0, 0, tiled=True)
    w_gu = join(core, gu_mine, gu_theirs)
    attn_tok, w_gu, dy_far, *out_parts = fence(attn_tok, w_gu, dy_far, *out_parts)
    residual, inv_two, inner = out_proj(places, attn_tok, x_bf, mlp_gain, out_parts)

    b_first = send_first(inner)
    own = ffn(inner, dy, w_gu, w_dn)
    inner, b_first, *own = fence(inner, b_first, *own)
    b_second = send_second(inner)
    first = ffn(b_first, dy_first, w_gu, w_dn)
    b_first, b_second, *first = fence(b_first, b_second, *first)
    b_far = send_second(b_first)
    second = ffn(b_second, dy_second, w_gu, w_dn)
    b_far, db_first, *second = fence(b_far, first[3], *second)
    db_got_first = send_first(db_first)
    far = ffn(b_far, dy_far, w_gu, w_dn)
    db_got_first, db_far, *hid_rows = fence(db_got_first, far[3], own[0], first[0], second[0], far[0])

    b_rows = [inner, b_first, b_second, b_far]
    db_got_far = send_first(db_far)
    gu_keep, gu_give = grad_gu(
        core,
        b_rows,
        [own[1], first[1], second[1], far[1]],
        [own[2], first[2], second[2], far[2]],
        share,
        planes,
    )
    db_got_far, gu_keep, gu_give, *hid_rows = fence(db_got_far, gu_keep, gu_give, *hid_rows)
    db_pass = (second[3].astype(F32) + db_got_far.astype(F32)).astype(BF)
    db_pass, gu_give, *hid_rows = fence(db_pass, gu_give, *hid_rows)
    db_passed = send_second(db_pass)
    gu_got = send_sibling(gu_give)
    dn_keep, dn_give = grad_dn(core, hid_rows, [dy, dy_first, dy_second, dy_far])
    gu_got, dn_keep, dn_give = fence(gu_got, dn_keep, dn_give)
    gu_sum = (gu_keep.astype(F32) + gu_got.astype(F32)).astype(BF)
    gu_sum, db_passed, dn_give = fence(gu_sum, db_passed, dn_give)
    gu_z = lax.psum_scatter(
        gu_sum.reshape(planes * CHIPS * quarter, 2 * hidden_chip), "dp", scatter_dimension=0, tiled=True
    )
    gu_z = gu_z.reshape(CHIPS, quarter, 2 * hidden_chip)
    dn_got = send_sibling(dn_give)
    d_resid, d_branch, d_send = resid_back(
        places, own[3], db_got_first, db_passed, residual, inv_two, mlp_gain, dy, out_parts
    )
    d_send, d_branch, dn_got = fence(d_send, d_branch, dn_got)
    d_heads = lax.all_to_all(d_send, "sp", 0, 0, tiled=True).reshape(length, share)
    wo_keep, wo_give = grad_wo(core, attn_tok, d_branch)
    d_heads, wo_keep, wo_give, normed = fence(d_heads, wo_keep, wo_give, normed)

    def back_call(heads, start, stop, **kwargs):
        return attend_back(zeros_one, qkv_heads, heads, lse, cos_all, sin_all, start, stop, **kwargs)

    turns = (0, blocks // 8, blocks // 4, (3 * blocks) // 8, blocks)
    wo_got = send_sibling(wo_give)
    a_first = send_first(normed)
    bwd = back_call(d_heads, turns[0], turns[1], out=out_heads)
    d_heads, a_first, wo_got, normed, *bwd = fence(d_heads, a_first, wo_got, normed, *bwd)
    a_second = send_second(normed)
    a_theirs = [send_sibling(normed), send_sibling(a_first)]
    bwd = back_call(d_heads, turns[1], turns[2], before=bwd)
    dn_parts = [part.reshape(2, 2, dn_keep.shape[0] // planes, width) for part in (dn_keep, dn_got)]
    dn_move = pick_sum(dn_parts, 1 - (plane & 1), 1).astype(BF)
    d_heads, gu_z, a_second, dn_move, *moves = fence(d_heads, gu_z, a_second, dn_move, *a_theirs, *bwd)
    a_theirs, bwd = moves[:2], moves[2:]

    def wo_part(place):
        return pick(wo_keep, place).astype(F32) + pick(wo_got, place).astype(F32)

    dn_move = lax.ppermute(dn_move, "dp", LINE_NEAR)
    gu_z = lax.all_to_all(gu_z, "sp", 0, 0, axis_index_groups=SAME_CORE, tiled=True)
    a_theirs.append(send_sibling(a_second))
    bwd = back_call(d_heads, turns[2], turns[3], before=bwd)
    d_heads, gu_z, a_first, dn_move, *moves = fence(d_heads, gu_z, a_first, dn_move, *a_theirs, *bwd)
    a_theirs, bwd = moves[:3], moves[3:]

    dn_own = pick_sum(dn_parts, plane & 1, 1) + dn_move.astype(F32)
    dn_move = pick(dn_own, 1 - plane // 2).astype(BF)
    wo_first = wo_part(chip ^ (first_mask // 2)).astype(BF)
    wo_far = wo_part(chip ^ 3).astype(BF)
    d_heads, gu_z, a_first, wo_first, wo_far, dn_move = fence(d_heads, gu_z, a_first, wo_first, wo_far, dn_move)
    gu_all = lax.all_gather(gu_z, "dp", axis=0, tiled=False)
    a_far = send_second(a_first)
    wo_far = send_first(wo_far)
    wo_first = send_first(wo_first)
    dn_move = lax.ppermute(dn_move, "dp", LINE_FAR)
    bwd = back_call(d_heads, turns[3], turns[4], before=bwd)
    wo_pass = (wo_part(chip ^ (second_mask // 2)) + wo_far.astype(F32)).astype(BF)
    dn_z = (pick(dn_own, plane // 2) + dn_move.astype(F32)).astype(BF)
    dp_heads, wo_first, wo_pass, a_far, dn_z = fence(bwd[0], wo_first, wo_pass, a_far, dn_z)

    wo_passed = send_second(wo_pass)
    dn_all = lax.all_gather(dn_z, "dp", axis=0, tiled=False)
    a_theirs.append(send_sibling(a_far))
    back = lax.all_to_all(dp_heads, "sp", 0, 0, tiled=True)
    grad_wq = grad_qkv(places, [normed, a_first, a_second, a_far] + list(a_theirs), dp_heads, planes)
    wo_rows = (wo_part(chip) + wo_first.astype(F32) + wo_passed.astype(F32)).astype(BF)
    split = grad_wq.shape[2]
    last_parts = [jnp.concatenate([grad_wq, wo_rows.reshape(planes, quarter, width)], axis=2)]
    y_far, y_first = far[4], first[4]
    moves = None
    for step in range(1, planes):
        moves = line_scatter_sends(last_parts, moves, step, 0)
        y_far, y_first, *moves = fence(y_far, y_first, *moves)
        moves = line_scatter_move(moves, step)
        if step == 1:
            back, *moves = fence(back, *moves)
        elif step == 2:
            y_got_far = send_first(y_far)
        elif step == 3:
            y_got_first = send_first(y_first)
        moves = fence(*moves)
    last_z = line_scatter_end(last_parts, moves, 0)
    wq_z = last_z[:, :split].reshape(quarter, devices, split // devices).transpose(1, 0, 2)
    wq_z, wo_z, gu_all, y_got_far = fence(wq_z, last_z[:, split:], gu_all, y_got_far)
    wq_z = lax.all_to_all(wq_z, "sp", 0, 0, tiled=True)
    grad_tokens = in_back(places, back, x_bf, inv_one, attn_gain, d_resid, qkv_parts).reshape(tokens.shape)
    y_pass = (second[4].astype(F32) + y_got_far.astype(F32)).astype(BF)
    last_z = jnp.concatenate([wq_z.transpose(1, 0, 2).reshape(quarter, split), wo_z], axis=1)
    last_z, grad_tokens, y_pass = fence(last_z, grad_tokens, y_pass)
    y_passed = send_second(y_pass)
    last_steps = [(last_z, last_z)]
    outs = []
    for step in range(1, planes):
        last_steps.append(line_gather_move(last_steps[-1], step))
        if step == 1:
            outs += spread(gu_all, w_gate_up, g_mlp.astype(F32).reshape(share, 1))
        if step == planes - 1:
            y_sum = own[4].astype(F32) + y_got_first.astype(F32) + y_passed.astype(F32)
            outs.append((residual + y_sum).astype(BF).reshape(tokens.shape))
            break
        moves = fence(*last_steps[-1], *outs)
        last_steps[-1], outs = tuple(moves[:2]), list(moves[2:])
    grad_w_gate_up, grad_g_mlp, output = outs
    grad_w_down = dn_all.astype(F32).reshape(w_down.shape)
    grad_w_qkv, grad_g_attn, grad_w_out = spread_last(last_steps, w_qkv, g_attn.astype(F32).reshape(share, 1), width)
    return (
        output,
        grad_tokens,
        grad_w_qkv,
        grad_w_out,
        grad_w_gate_up,
        grad_w_down,
        grad_g_attn.reshape(share),
        grad_g_mlp.reshape(share),
    )


def solution(mesh):
    in_specs = (
        P("dp", "sp", None),
        P("dp", "sp"),
        P("dp", "sp"),
        P("dp", "sp", None),
        P("sp", None),
        P("sp", None),
        P("sp", None),
        P("sp", None),
        P("sp"),
        P("sp"),
    )
    out_specs = (
        P("dp", "sp", None),
        P("dp", "sp", None),
        P("sp", None),
        P("sp", None),
        P("sp", None),
        P("sp", None),
        P("sp"),
        P("sp"),
    )
    body = fast_body if dict(mesh.shape) == {"dp": 4, "sp": 2 * CHIPS} else general_body
    return jax.shard_map(body, mesh=mesh, in_specs=in_specs, out_specs=out_specs, check_vma=False)
```

```python
import functools
import math

import jax
import jax.numpy as jnp
from jax import lax
from jax.experimental import pallas as pl
from jax.experimental.pallas import tpu as pltpu
from jax.sharding import PartitionSpec as P

D = 2048
H = 32
KV = 4
HD = 64
FF = 5632


EPSILON = 1e-05
ROPE_BASE = 10000.0
MASKED = -1e30


def rope_tables(positions, head_size):
    half_dim = head_size // 2
    frequency = ROPE_BASE ** (-(jnp.arange(half_dim, dtype=jnp.float32) * 2.0 / head_size))
    angles = positions.astype(jnp.float32)[:, None] * frequency[None, :]
    return (jnp.cos(angles), jnp.sin(angles))


def rotate(values, cosine, sine_tab, inverse_turn):
    half_dim = values.shape[-1] // 2
    first_half = values[..., :half_dim]
    second = values[..., half_dim:]
    cos_wide = cosine[:, None, :]
    sin_wide = sine_tab[:, None, :]
    if inverse_turn:
        sin_wide = -sin_wide
    return jnp.concatenate(
        [first_half * cos_wide - second * sin_wide, second * cos_wide + first_half * sin_wide],
        axis=-1,
    )


def rms_norm(values, gain_vec):
    inverse = lax.rsqrt(jnp.mean(values * values, axis=-1, keepdims=True) + EPSILON)
    return (values * inverse * gain_vec, inverse)


def norm_back(values, inverse, gain_vec, upstream):
    scaled = upstream * gain_vec
    inner_mean = jnp.mean(scaled * values, axis=-1, keepdims=True)
    through = inverse * scaled - values * inverse**3 * inner_mean
    gain_grad = jnp.sum(upstream * values * inverse, axis=0)
    return (through, gain_grad)


def attention_inputs(flat_in, qkv_full, gain_vec, cosine, sine_tab):
    row_count = flat_in.shape[0]
    group_size = H // KV
    normed, inverse = rms_norm(flat_in, gain_vec)
    normed = normed.astype(jnp.bfloat16)
    projected = jnp.dot(normed, qkv_full, preferred_element_type=jnp.float32)
    queries = rotate(projected[:, :D].reshape(row_count, H, HD), cosine, sine_tab, False)
    key_heads = rotate(
        projected[:, D : D + KV * HD].reshape(row_count, KV, HD), cosine, sine_tab, False
    )
    value_heads = projected[:, D + KV * HD :].reshape(row_count, KV, HD)
    key_wide = jnp.broadcast_to(key_heads[:, :, None], (row_count, KV, group_size, HD)).reshape(
        row_count, D
    )
    value_wide = jnp.broadcast_to(value_heads[:, :, None], (row_count, KV, group_size, HD)).reshape(
        row_count, D
    )
    stacked = jnp.stack([queries.reshape(row_count, D), key_wide, value_wide]).astype(jnp.bfloat16)
    return (normed, inverse, stacked)


def block_mask(seg_full, position, row_begin, finish):
    row_seg = seg_full[:, row_begin:finish]
    col_seg = seg_full[:, :finish]
    same_doc = row_seg[:, :, None] == col_seg[:, None, :]
    causal = position[row_begin:finish, None] >= position[None, :finish]
    return same_doc & causal[None]


def attention_forward(queries, key_heads, value_heads, seg_full, score_scale):
    length = queries.shape[1]
    block_rows = min(512, length)
    position = jnp.arange(length, dtype=jnp.int32)
    outputs = []
    lse_parts = []
    for block_num in range(length // block_rows):
        row_begin = block_num * block_rows
        finish = row_begin + block_rows
        scores = (
            jnp.einsum(
                "sqhd,skhd->shqk",
                queries[:, row_begin:finish],
                key_heads[:, :finish],
                preferred_element_type=jnp.float32,
            )
            * score_scale
        )
        allowed = block_mask(seg_full, position, row_begin, finish)
        scores = jnp.where(allowed[:, None], scores, MASKED)
        row_max = jnp.max(scores, axis=-1, keepdims=True)
        shifted = jnp.exp(scores - row_max)
        row_total = jnp.sum(shifted, axis=-1, keepdims=True)
        softmax_w = (shifted / row_total).astype(jnp.bfloat16)
        outputs.append(
            jnp.einsum(
                "shqk,skhd->sqhd",
                softmax_w,
                value_heads[:, :finish],
                preferred_element_type=jnp.float32,
            )
        )
        lse_parts.append(row_max + jnp.log(row_total))
    return (jnp.concatenate(outputs, axis=1), jnp.concatenate(lse_parts, axis=2))


def attention_backward(queries, key_heads, value_heads, seg_full, log_sums, grad_out, score_scale):
    length = queries.shape[1]
    block_rows = min(512, length)
    position = jnp.arange(length, dtype=jnp.int32)
    grad_query = []
    grad_key = jnp.zeros(key_heads.shape, jnp.float32)
    grad_value = jnp.zeros(value_heads.shape, jnp.float32)
    for block_num in range(length // block_rows):
        row_begin = block_num * block_rows
        finish = row_begin + block_rows
        query_rows = queries[:, row_begin:finish]
        grad_rows = grad_out[:, row_begin:finish]
        key_part = key_heads[:, :finish]
        value_part = value_heads[:, :finish]
        scores = (
            jnp.einsum("sqhd,skhd->shqk", query_rows, key_part, preferred_element_type=jnp.float32)
            * score_scale
        )
        allowed = block_mask(seg_full, position, row_begin, finish)
        softmax_f = jnp.where(
            allowed[:, None], jnp.exp(scores - log_sums[:, :, row_begin:finish]), 0.0
        )
        grad_probs = jnp.einsum(
            "sqhd,skhd->shqk", grad_rows, value_part, preferred_element_type=jnp.float32
        )
        row_delta = jnp.sum(softmax_f * grad_probs, axis=-1, keepdims=True)
        grad_scores = (softmax_f * (grad_probs - row_delta)).astype(jnp.bfloat16)
        grad_query.append(
            jnp.einsum("shqk,skhd->sqhd", grad_scores, key_part, preferred_element_type=jnp.float32)
            * score_scale
        )
        grad_key = grad_key.at[:, :finish].add(
            jnp.einsum(
                "shqk,sqhd->skhd", grad_scores, query_rows, preferred_element_type=jnp.float32
            )
            * score_scale
        )
        grad_value = grad_value.at[:, :finish].add(
            jnp.einsum(
                "shqk,sqhd->skhd",
                softmax_f.astype(jnp.bfloat16),
                grad_rows,
                preferred_element_type=jnp.float32,
            )
        )
    return (jnp.concatenate(grad_query, axis=1), grad_key, grad_value)


def general_body(tokens, segment_ids, selected, cotangent, w_qkv, w_out, w_gate_up, w_down, g_attn, g_mlp):
    streams, local_len, model_dim = tokens.shape
    sp_count = lax.axis_size("sp")
    sp_index = lax.axis_index("sp")
    row_count = streams * local_len
    group_size = H // KV
    kv_width = KV * HD
    score_scale = HD ** (-0.5)
    contract = (((0,), (0,)), ((), ()))
    seg_full = lax.all_gather(segment_ids, "sp", axis=1, tiled=True)
    first_count = jnp.sum((seg_full == 0).astype(jnp.int32), axis=1, keepdims=True)
    local_pos = (
        sp_index * local_len
        + jnp.arange(local_len, dtype=jnp.int32)[None, :]
        - segment_ids * first_count
    )
    cosine, sine_tab = rope_tables(local_pos.reshape(row_count), HD)
    shards = (w_qkv, w_out, w_gate_up, w_down, g_attn, g_mlp)
    gathered = (
        lax.all_gather(shards[0], "sp", axis=0, tiled=True),
        lax.all_gather(shards[1], "sp", axis=0, tiled=True),
        lax.all_gather(shards[2], "sp", axis=0, tiled=True),
        lax.all_gather(shards[3], "sp", axis=0, tiled=True),
        lax.all_gather(shards[4], "sp", axis=0, tiled=True),
        lax.all_gather(shards[5], "sp", axis=0, tiled=True),
    )
    qkv_full, out_full, gate_up_full, down_full, attn_gain, mlp_gain = gathered
    attn_gain = attn_gain.astype(jnp.float32)
    mlp_gain = mlp_gain.astype(jnp.float32)
    flat_in = tokens.reshape(row_count, model_dim).astype(jnp.float32)
    normed, inverse_one, stacked = attention_inputs(flat_in, qkv_full, attn_gain, cosine, sine_tab)
    head_view = lax.all_to_all(
        stacked.reshape(3, streams, local_len, model_dim),
        "sp",
        split_axis=3,
        concat_axis=2,
        tiled=True,
    )
    length = head_view.shape[2]
    heads_here = head_view.shape[3] // HD
    head_shape = (streams, length, heads_here, HD)
    queries = head_view[0].reshape(head_shape)
    key_heads = head_view[1].reshape(head_shape)
    value_heads = head_view[2].reshape(head_shape)
    attn_heads, log_sums = attention_forward(queries, key_heads, value_heads, seg_full, score_scale)
    attn_send = attn_heads.astype(jnp.bfloat16).reshape(streams, length, heads_here * HD)
    attn_tok = lax.all_to_all(attn_send, "sp", split_axis=1, concat_axis=2, tiled=True).reshape(
        row_count, model_dim
    )
    branch = jnp.dot(attn_tok, out_full, preferred_element_type=jnp.float32)
    residual = flat_in + branch
    inner_f, inverse_two = rms_norm(residual, mlp_gain)
    inner_in = inner_f.astype(jnp.bfloat16)
    gate_up = jnp.dot(inner_in, gate_up_full, preferred_element_type=jnp.float32)
    gate_part = gate_up[:, :FF]
    up_part = gate_up[:, FF:]
    sigmoid_g = jax.nn.sigmoid(gate_part)
    silu_gate = gate_part * sigmoid_g
    hidden = (silu_gate * up_part).astype(jnp.bfloat16)
    result = residual + jnp.dot(hidden, down_full, preferred_element_type=jnp.float32)
    output = result.astype(jnp.bfloat16).reshape(streams, local_len, model_dim)
    qkv_back, out_back, gate_up_back, down_back, attn_gain_b, mlp_gain_b = gathered
    attn_gain_b = attn_gain_b.astype(jnp.float32)
    mlp_gain_b = mlp_gain_b.astype(jnp.float32)
    grad_y = (cotangent * selected[:, :, None].astype(jnp.bfloat16)).reshape(row_count, model_dim)
    grad_hidden = jnp.dot(grad_y, down_back.T, preferred_element_type=jnp.float32)
    silu_slope = sigmoid_g * (1.0 + gate_part * (1.0 - sigmoid_g))
    grad_both = jnp.concatenate(
        [grad_hidden * up_part * silu_slope, grad_hidden * silu_gate], axis=1
    ).astype(jnp.bfloat16)
    grad_inner = jnp.dot(grad_both, gate_up_back.T, preferred_element_type=jnp.float32)
    grad_resid, gain_two = norm_back(residual, inverse_two, mlp_gain_b, grad_inner)
    grad_resid = grad_resid + grad_y.astype(jnp.float32)
    grad_branch = grad_resid.astype(jnp.bfloat16)
    grad_attn = jnp.dot(grad_branch, out_back.T, preferred_element_type=jnp.float32).astype(
        jnp.bfloat16
    )
    grad_view = lax.all_to_all(
        grad_attn.reshape(streams, local_len, model_dim),
        "sp",
        split_axis=2,
        concat_axis=1,
        tiled=True,
    )
    grad_view = grad_view.reshape(head_shape)
    grad_q, grad_k, grad_v = attention_backward(
        queries, key_heads, value_heads, seg_full, log_sums, grad_view, score_scale
    )
    back_send = (
        jnp.stack([grad_q, grad_k, grad_v])
        .astype(jnp.bfloat16)
        .reshape(3, streams, length, heads_here * HD)
    )
    returned = lax.all_to_all(back_send, "sp", split_axis=2, concat_axis=3, tiled=True)
    returned = returned.astype(jnp.float32).reshape(3, row_count, H, HD)
    grad_pq = rotate(returned[0], cosine, sine_tab, True).reshape(row_count, model_dim)
    key_summed = jnp.sum(returned[1].reshape(row_count, KV, group_size, HD), axis=2)
    grad_pk = rotate(key_summed, cosine, sine_tab, True).reshape(row_count, kv_width)
    grad_pv = jnp.sum(returned[2].reshape(row_count, KV, group_size, HD), axis=2).reshape(
        row_count, kv_width
    )
    grad_mixed = jnp.concatenate(
        [grad_pq.astype(jnp.bfloat16), grad_pk.astype(jnp.bfloat16), grad_pv.astype(jnp.bfloat16)],
        axis=1,
    )
    grad_normed = jnp.dot(grad_mixed, qkv_back.T, preferred_element_type=jnp.float32)
    grad_in, gain_one = norm_back(flat_in, inverse_one, attn_gain_b, grad_normed)
    grad_in = grad_in + grad_resid
    grad_tokens = grad_in.astype(jnp.bfloat16).reshape(streams, local_len, model_dim)
    gain_totals = lax.psum((gain_one, gain_two), ("dp", "sp"))
    gain_share = model_dim // sp_count
    grad_g_attn = lax.dynamic_slice_in_dim(gain_totals[0], sp_index * gain_share, gain_share, 0)
    grad_g_mlp = lax.dynamic_slice_in_dim(gain_totals[1], sp_index * gain_share, gain_share, 0)
    row_sums = lax.psum_scatter(
        jnp.concatenate(
            [
                lax.dot_general(normed, grad_mixed, contract, preferred_element_type=jnp.float32),
                lax.dot_general(
                    attn_tok, grad_branch, contract, preferred_element_type=jnp.float32
                ),
                lax.dot_general(inner_in, grad_both, contract, preferred_element_type=jnp.float32),
            ],
            axis=1,
        ).astype(jnp.bfloat16),
        "sp",
        scatter_dimension=0,
        tiled=True,
    )
    down_sums = lax.psum_scatter(
        lax.dot_general(hidden, grad_y, contract, preferred_element_type=jnp.float32).astype(
            jnp.bfloat16
        ),
        "sp",
        scatter_dimension=0,
        tiled=True,
    )
    weight_rows, down_rows = (
        lax.psum(row_sums, "dp").astype(jnp.float32),
        lax.psum(down_sums, "dp").astype(jnp.float32),
    )
    qkv_cols = model_dim + 2 * kv_width
    grad_w_qkv = weight_rows[:, :qkv_cols]
    grad_w_out = weight_rows[:, qkv_cols : qkv_cols + model_dim]
    grad_w_gate_up = weight_rows[:, qkv_cols + model_dim :]
    return (
        output,
        grad_tokens,
        grad_w_qkv,
        grad_w_out,
        grad_w_gate_up,
        down_rows,
        grad_g_attn,
        grad_g_mlp,
    )


CHIPS = 4
BLOCK = 512
SHORT = pl.CostEstimate(flops=1, bytes_accessed=1, transcendentals=0)
LOG2E = math.log2(math.e)
BF = jnp.bfloat16
F32 = jnp.float32
NT = (((1,), (1,)), ((), ()))
TN = (((0,), (0,)), ((), ()))


def swap_pairs(even_mask, odd_mask):
    return [(i, i ^ (odd_mask if i & 1 else even_mask)) for i in range(2 * CHIPS)]


FIRST = swap_pairs(2, 4)
SECOND = swap_pairs(4, 2)
SIBLING = swap_pairs(1, 1)
SAME_CORE = [[0, 2, 4, 6], [1, 3, 5, 7]]
LINE_NEAR = [(z, z ^ 1) for z in range(4)]
LINE_FAR = [(z, z ^ 2) for z in range(4)]


def send_first(x):
    return lax.ppermute(x, "sp", FIRST)


def send_second(x):
    return lax.ppermute(x, "sp", SECOND)


def send_sibling(x):
    return lax.ppermute(x, "sp", SIBLING)


def after(value, *others):
    return lax.optimization_barrier((value,) + others)[0]


def gather_chips(own):
    first = send_first(own)
    second = send_second(after(own, first))
    far = send_second(after(first, second))
    return [own, first, second, far]


def rel_masks(core):
    first = jnp.where(core == 0, 2, 4)
    return first, 6 - first


def fence(*values):
    return lax.optimization_barrier(values)


def gather_vectors(own, me):
    for bit in (1, 2, 4):
        got = lax.ppermute(own, "sp", swap_pairs(bit, bit))
        high = (me & bit) != 0
        own = jnp.concatenate([jnp.where(high, got, own), jnp.where(high, own, got)], axis=1)
    return own


def pick(parts, index):
    return lax.dynamic_index_in_dim(parts, index, 0, keepdims=False)


def pick_sum(parts, index, axis):
    return sum(lax.dynamic_index_in_dim(p, index, axis, keepdims=False).astype(F32) for p in parts)


def line_scatter_sends(parts, got, step, axis):
    planes = parts[0].shape[axis]
    z = lax.axis_index("dp")
    ahead = pick_sum(parts, jnp.clip(planes - step + z, 0, planes - 1), axis)
    back = pick_sum(parts, jnp.clip(z - planes + step, 0, planes - 1), axis)
    if got is not None:
        ahead = ahead + got[0].astype(F32)
        back = back + got[1].astype(F32)
    return ahead.astype(BF), back.astype(BF)


def line_scatter_move(sends, step):
    planes = lax.axis_size("dp")
    right = lax.ppermute(sends[0], "dp", [(i, i + 1) for i in range(step)])
    left = lax.ppermute(sends[1], "dp", [(planes - 1 - i, planes - 2 - i) for i in range(step)])
    return right, left


def line_scatter_end(parts, got, axis):
    own = pick_sum(parts, lax.axis_index("dp"), axis)
    return (own + got[0].astype(F32) + got[1].astype(F32)).astype(BF)


def line_gather_move(got, step):
    planes = lax.axis_size("dp")
    right = lax.ppermute(got[0], "dp", [(i, i + 1) for i in range(step - 1, planes - 1)])
    left = lax.ppermute(got[1], "dp", [(i + 1, i) for i in range(planes - step)])
    return right, left


def line_values(refs, planes, z):
    for step in range(planes):
        place = lax.rem(z - step + planes, planes)
        if step == 0:
            yield place, lambda index: refs[0][index]
        else:
            right, left = refs[step], refs[2 * planes - 1 - step]
            yield place, lambda index, right=right, left=left, step=step: jnp.where(z >= step, right[index], left[index])


def spread_kernel(in_ref, w_ref, g_ref, out_ref, gain_ref):
    planes, _, rows, width = in_ref.shape
    out = in_ref[...].reshape(planes * rows, width).astype(F32)
    out_ref[...] = out
    part = jnp.sum(out * w_ref[...].astype(F32), axis=-1, keepdims=True) / g_ref[...]

    @pl.when(pl.program_id(0) == 0)
    def _():
        gain_ref[...] = part

    @pl.when(pl.program_id(0) > 0)
    def _():
        gain_ref[...] += part


def spread(parts, weight, gain):
    planes, chips, rows, both = parts.shape
    half = both // 2
    total = planes * rows
    line = pl.BlockSpec((total, half), lambda i: (0, i))
    column = pl.BlockSpec((total, 1), lambda i: (0, 0))
    return pl.pallas_call(
        spread_kernel,
        grid=(2 * chips,),
        in_specs=[pl.BlockSpec((planes, 1, rows, half), lambda i: (0, i % chips, 0, i // chips)), line, column],
        out_specs=[line, column],
        out_shape=[jax.ShapeDtypeStruct(weight.shape, F32), jax.ShapeDtypeStruct((total, 1), F32)],
        compiler_params=pltpu.CompilerParams(vmem_limit_bytes=32 * 2**20),
        cost_estimate=SHORT,
        name="spread",
    )(parts, weight, gain)


def spread_last_kernel(z_ref, *refs, planes):
    blocks, (w_ref, g_ref, out_ref, gain_ref, wo_ref) = refs[:-5], refs[-5:]
    rows = blocks[0].shape[0]
    devices = 2 * CHIPS
    width = wo_ref.shape[1]
    heads = width // devices
    each = heads + 2 * HD
    for place, load in line_values(blocks, planes, z_ref[0]):
        span = pl.ds(pl.multiple_of(place * rows, rows), rows)
        pairs = []
        for d in range(devices):
            begin = d * each
            cols = slice(begin, begin + heads)
            out_ref[span, d * heads : (d + 1) * heads] = load((slice(None), cols)).astype(F32)
            pairs.append(load((slice(None), slice(begin + heads, begin + each))).astype(F32))
        for g in range(0, KV, 2):
            low = pairs[2 * g] + pairs[2 * g + 1]
            high = pairs[2 * g + 2] + pairs[2 * g + 3]
            lane = lax.broadcasted_iota(jnp.int32, low.shape, 1)
            begin = width + g * HD
            out_ref[span, begin : begin + 2 * HD] = jnp.where(lane < HD, low, pltpu.roll(high, HD, 1))
            begin = width + (KV + g) * HD
            out_ref[span, begin : begin + 2 * HD] = jnp.where(lane < HD, pltpu.roll(low, HD, 1), high)
        wo_ref[span, :] = load((slice(None), slice(devices * each, devices * each + width))).astype(F32)
    gain_ref[...] = jnp.sum(out_ref[...] * w_ref[...].astype(F32), axis=-1, keepdims=True) / g_ref[...]


def spread_last(steps, weight, gain, width):
    planes = len(steps)
    blocks = [steps[0][0]] + [s[0] for s in steps[1:]] + [s[1] for s in steps[1:]]
    vmem = pl.BlockSpec(memory_space=pltpu.VMEM)
    total = weight.shape[0]
    return pl.pallas_call(
        functools.partial(spread_last_kernel, planes=planes),
        in_specs=[pl.BlockSpec(memory_space=pltpu.SMEM)] + [vmem] * (len(blocks) + 2),
        out_specs=[vmem] * 3,
        out_shape=[
            jax.ShapeDtypeStruct(weight.shape, F32),
            jax.ShapeDtypeStruct((total, 1), F32),
            jax.ShapeDtypeStruct((total, width), F32),
        ],
        compiler_params=pltpu.CompilerParams(vmem_limit_bytes=32 * 2**20),
        cost_estimate=SHORT,
        name="spread_last",
    )(lax.axis_index("dp").reshape(1), *blocks, weight, gain)


def join_kernel(core_ref, mine_ref, theirs_ref, out_ref):
    planes, _, rows, both = mine_ref.shape
    block = jnp.where(pl.program_id(1) == 0, mine_ref[...], theirs_ref[...]).reshape(planes * rows, both)
    out_ref[0, 0, 0] = block[:, : both // 2]
    out_ref[1, 0, 0] = block[:, both // 2 :]


def join(core, mine, theirs):
    planes, chips, rows, both = mine.shape
    spec = pl.BlockSpec((planes, 1, rows, both), lambda c, k, core: (0, c, 0, 0))
    out = pl.pallas_call(
        join_kernel,
        grid_spec=pltpu.PrefetchScalarGridSpec(
            num_scalar_prefetch=1,
            grid=(chips, 2),
            in_specs=[spec, spec],
            out_specs=pl.BlockSpec(
                (2, 1, 1, planes * rows, both // 2), lambda c, k, core: (0, c, (core[0] + k) % 2, 0, 0)
            ),
        ),
        out_shape=jax.ShapeDtypeStruct((2, chips, 2, planes * rows, both // 2), BF),
        compiler_params=pltpu.CompilerParams(vmem_limit_bytes=32 * 2**20),
        cost_estimate=SHORT,
        name="join",
    )(core.reshape(1), mine, theirs)
    return out.reshape(2, 2 * chips * planes * rows, both // 2)


def ffn_kernel(*refs, cuts):
    b_hbm, dy_hbm, wgu_hbm, wd_hbm, hid_hbm, dg_hbm, du_hbm, db_hbm, y_hbm = refs[:9]
    b_ref, dy_ref, wg_ref, wu_ref, wd_ref, hid_ref, dg_ref, du_ref, db_ref, y_ref, sems = refs[9:]
    count = len(cuts) - 1

    def move(source, target, index):
        copy = pltpu.make_async_copy(source, target, sems.at[index])
        copy.start()
        return copy

    b_copy = move(b_hbm, b_ref, 3 * count)
    weights = []
    for c in range(count):
        span = slice(cuts[c], cuts[c + 1])
        gate_copy = move(wgu_hbm.at[0, :, span], wg_ref.at[:, span], 3 * c)
        up_copy = move(wgu_hbm.at[1, :, span], wu_ref.at[:, span], 3 * c + 1)
        weights.append([gate_copy, up_copy])
        if c == 0:
            dy_copy = move(dy_hbm, dy_ref, 3 * count + 1)
        weights[-1].append(move(wd_hbm.at[span, :], wd_ref.at[span, :], 3 * c + 2))
    b_copy.wait()
    for c in range(count):
        span = slice(cuts[c], cuts[c + 1])
        for copy in weights[c][:2]:
            copy.wait()
        gate = jnp.dot(b_ref[...], wg_ref[:, span], preferred_element_type=F32)
        up = jnp.dot(b_ref[...], wu_ref[:, span], preferred_element_type=F32)
        if c == 0:
            dy_copy.wait()
        weights[c][2].wait()
        d_hidden = lax.dot_general(dy_ref[...], wd_ref[span, :], NT, preferred_element_type=F32)
        sigmoid_g = jax.nn.sigmoid(gate)
        silu_gate = gate * sigmoid_g
        hid_ref[:, span] = (silu_gate * up).astype(BF)
        dg_ref[:, span] = (d_hidden * up * (sigmoid_g * (1.0 + gate * (1.0 - sigmoid_g)))).astype(BF)
        du_ref[:, span] = (d_hidden * silu_gate).astype(BF)
    base = 3 * count + 2
    outs = [move(hid_ref, hid_hbm, base), move(dg_ref, dg_hbm, base + 1), move(du_ref, du_hbm, base + 2)]
    y_ref[...] = jnp.dot(hid_ref[...], wd_ref[...], preferred_element_type=F32).astype(BF)
    outs.append(move(y_ref, y_hbm, base + 3))
    d_in = lax.dot_general(dg_ref[...], wg_ref[...], NT, preferred_element_type=F32)
    db_ref[...] = (d_in + lax.dot_general(du_ref[...], wu_ref[...], NT, preferred_element_type=F32)).astype(BF)
    outs.append(move(db_ref, db_hbm, base + 4))
    for copy in outs:
        copy.wait()


def ffn(b_rows, dy_rows, w_gu, w_dn):
    rows, width = b_rows.shape
    hidden = w_dn.shape[0]
    pieces = 3
    cuts = tuple(round(hidden * c / pieces / 128) * 128 for c in range(pieces)) + (hidden,)
    hbm = pl.BlockSpec(memory_space=pl.ANY)
    return pl.pallas_call(
        functools.partial(ffn_kernel, cuts=cuts),
        in_specs=[hbm] * 4,
        out_specs=[hbm] * 5,
        out_shape=[jax.ShapeDtypeStruct((rows, hidden), BF)] * 3 + [jax.ShapeDtypeStruct((rows, width), BF)] * 2,
        scratch_shapes=[pltpu.VMEM((rows, width), BF)] * 2
        + [pltpu.VMEM((width, hidden), BF)] * 2
        + [pltpu.VMEM((hidden, width), BF)]
        + [pltpu.VMEM((rows, hidden), BF)] * 3
        + [pltpu.VMEM((rows, width), BF)] * 2
        + [pltpu.SemaphoreType.DMA((3 * pieces + 7,))],
        compiler_params=pltpu.CompilerParams(vmem_limit_bytes=58 * 2**20),
        cost_estimate=SHORT,
        name="ffn",
    )(b_rows, dy_rows, w_gu, w_dn)


def grad_gu_kernel(core_ref, *refs, count):
    left, right = refs[: 2 * count], refs[2 * count : 4 * count]
    half = right[0].shape[1]
    for side in range(2):
        for kind in range(2):
            total = None
            for r in range(count):
                a_rows = left[side * count + r][...]
                part = lax.dot_general(a_rows, right[kind * count + r][...], TN, preferred_element_type=F32)
                total = part if total is None else total + part
            out_ref = refs[4 * count + side]
            planes, _, rows, _ = out_ref.shape
            out_ref[:, 0, :, kind * half : (kind + 1) * half] = total.astype(BF).reshape(planes, rows, half)


def grad_gu(core, b_rows, dg_rows, du_rows, share, planes):
    count = len(b_rows)
    tokens, width = b_rows[0].shape
    hidden = dg_rows[0].shape[1]
    keep = pl.BlockSpec((tokens, share), lambda c, core: (0, 2 * c + core[0]))
    give = pl.BlockSpec((tokens, share), lambda c, core: (0, 2 * c + 1 - core[0]))
    whole = pl.BlockSpec((tokens, hidden), lambda c, core: (0, 0))
    rows = share // planes
    out = pl.BlockSpec((planes, 1, rows, 2 * hidden), lambda c, core: (0, c, 0, 0))
    return pl.pallas_call(
        functools.partial(grad_gu_kernel, count=count),
        grid_spec=pltpu.PrefetchScalarGridSpec(
            num_scalar_prefetch=1,
            grid=(width // (2 * share),),
            in_specs=[keep] * count + [give] * count + [whole] * (2 * count),
            out_specs=[out, out],
        ),
        out_shape=[jax.ShapeDtypeStruct((planes, width // (2 * share), rows, 2 * hidden), BF)] * 2,
        compiler_params=pltpu.CompilerParams(vmem_limit_bytes=58 * 2**20),
        cost_estimate=SHORT,
        name="grad_gu",
    )(core.reshape(1), *b_rows, *b_rows, *dg_rows, *du_rows)


def grad_qkv_kernel(place_ref, *refs, count):
    dp_ref, out_ref = refs[-2:]
    total = None
    for r in range(count):
        part = lax.dot_general(refs[r][...], dp_ref[place_ref[r]], TN, preferred_element_type=F32)
        total = part if total is None else total + part
    planes, rows, wide = out_ref.shape
    columns = total.shape[1]
    for k in range(wide // columns):
        block = total[k * planes * rows : (k + 1) * planes * rows].astype(BF)
        out_ref[:, :, k * columns : (k + 1) * columns] = block.reshape(planes, rows, columns)


def grad_qkv(places, a_rows, dp_heads, planes):
    count = len(a_rows)
    tokens, width = a_rows[0].shape
    columns = dp_heads.shape[2]
    share = width // count
    depth = 2 * share
    return pl.pallas_call(
        functools.partial(grad_qkv_kernel, count=count),
        grid_spec=pltpu.PrefetchScalarGridSpec(
            num_scalar_prefetch=1,
            grid=(width // depth,),
            in_specs=[pl.BlockSpec((tokens, depth), lambda i, p: (0, i))] * count
            + [pl.BlockSpec(dp_heads.shape, lambda i, p: (0, 0, 0))],
            out_specs=pl.BlockSpec((planes, share // planes, 2 * columns), lambda i, p: (0, 0, i)),
        ),
        out_shape=jax.ShapeDtypeStruct((planes, share // planes, count * columns), BF),
        compiler_params=pltpu.CompilerParams(vmem_limit_bytes=48 * 2**20),
        cost_estimate=SHORT,
        name="grad_qkv",
    )(places, *a_rows, dp_heads)


def swap_halves(values):
    width = values.shape[-1]
    lane = lax.broadcasted_iota(jnp.int32, values.shape, 1)
    ahead = pltpu.roll(values, width - HD // 2, 1)
    behind = pltpu.roll(values, HD // 2, 1)
    return jnp.where(lane % HD < HD // 2, ahead, behind)


def project_kernel(place_ref, x_ref, gain_ref, cos_ref, sin_ref, *refs, count):
    wq_refs, wkv_refs = refs[:count], refs[count : 2 * count]
    send_ref, normed_ref, inv_ref, normed_scr = refs[2 * count :]
    share = normed_scr.shape[2]

    @pl.when(pl.program_id(0) == 0)
    def _():
        x = x_ref[...].astype(F32)
        inv = lax.rsqrt(jnp.mean(x * x, axis=-1, keepdims=True) + EPSILON)
        normed = (x * inv * gain_ref[...]).astype(BF)
        normed_ref[...] = normed
        inv_ref[...] = inv
        for part in range(count):
            normed_scr[part] = normed[:, part * share : (part + 1) * share]

    pq = pkv = None
    for r in range(count):
        a_rows = normed_scr[place_ref[r]]
        q_part = jnp.dot(a_rows, wq_refs[r][...], preferred_element_type=F32)
        kv_part = jnp.dot(a_rows, wkv_refs[r][...], preferred_element_type=F32)
        pq = q_part if pq is None else pq + q_part
        pkv = kv_part if pkv is None else pkv + kv_part
    cos = cos_ref[...]
    sin = sin_ref[...]
    heads = pq.shape[1]
    q_scale = LOG2E * HD**-0.5
    turned = pq * jnp.tile(cos, (1, heads // 128)) + swap_halves(pq) * jnp.tile(sin, (1, heads // 128))
    send_ref[0, :, :heads] = (turned * q_scale).astype(BF)
    lane = lax.broadcasted_iota(jnp.int32, pkv.shape, 1)
    turned_kv = jnp.where(lane < HD, pkv * cos + swap_halves(pkv) * sin, pkv)
    send_ref[0, :, heads:] = turned_kv.astype(BF)


def project(places, x, gain, cos, sin, parts):
    rows, width = x.shape
    count = len(parts)
    heads = width // count
    out_width = heads + 2 * HD
    depth = parts[0].shape[0]
    first_kv = width // (2 * HD)
    return pl.pallas_call(
        functools.partial(project_kernel, count=count),
        grid_spec=pltpu.PrefetchScalarGridSpec(
            num_scalar_prefetch=1,
            grid=(count,),
            in_specs=[
                pl.BlockSpec((rows, width), lambda d, p: (0, 0)),
                pl.BlockSpec((1, width), lambda d, p: (0, 0)),
                pl.BlockSpec((rows, 128), lambda d, p: (0, 0)),
                pl.BlockSpec((rows, 128), lambda d, p: (0, 0)),
            ]
            + [pl.BlockSpec((depth, heads), lambda d, p: (0, d))] * count
            + [pl.BlockSpec((depth, 2 * HD), lambda d, p: (0, first_kv + d // 2))] * count,
            out_specs=[
                pl.BlockSpec((1, rows, out_width), lambda d, p: (d, 0, 0)),
                pl.BlockSpec((rows, width), lambda d, p: (0, 0)),
                pl.BlockSpec((rows, 1), lambda d, p: (0, 0)),
            ],
            scratch_shapes=[pltpu.VMEM((count, rows, width // count), BF)],
        ),
        out_shape=[
            jax.ShapeDtypeStruct((count, rows, out_width), BF),
            jax.ShapeDtypeStruct((rows, width), BF),
            jax.ShapeDtypeStruct((rows, 1), F32),
        ],
        compiler_params=pltpu.CompilerParams(vmem_limit_bytes=48 * 2**20),
        cost_estimate=SHORT,
        name="project",
    )(places, x, gain, cos, sin, *parts, *parts)


def out_proj_kernel(place_ref, attn_ref, x_ref, gain_ref, *refs, count):
    parts, (resid_ref, inv_ref, inner_ref) = refs[:count], refs[count:]
    width = x_ref.shape[1]
    tile = 512
    square = None
    for begin in range(0, width, tile):
        cols = slice(begin, begin + tile)
        total = x_ref[:, cols].astype(F32)
        for r in range(count):
            total = total + jnp.dot(attn_ref[place_ref[r]], parts[r][:, cols], preferred_element_type=F32)
        resid_ref[:, cols] = total
        part = jnp.sum(total * total, axis=-1, keepdims=True)
        square = part if square is None else square + part
    inv = lax.rsqrt(square / width + EPSILON)
    inv_ref[...] = inv
    inner_ref[...] = (resid_ref[...] * inv * gain_ref[...]).astype(BF)


def out_proj(places, attn, x, gain, parts):
    count, rows, share = attn.shape
    width = x.shape[1]
    step = rows // 2
    line = pl.BlockSpec((step, width), lambda i, p: (i, 0))
    return pl.pallas_call(
        functools.partial(out_proj_kernel, count=count),
        grid_spec=pltpu.PrefetchScalarGridSpec(
            num_scalar_prefetch=1,
            grid=(rows // step,),
            in_specs=[
                pl.BlockSpec((count, step, share), lambda i, p: (0, i, 0)),
                line,
                pl.BlockSpec((1, width), lambda i, p: (0, 0)),
            ]
            + [pl.BlockSpec((share, width), lambda i, p: (0, 0))] * count,
            out_specs=[line, pl.BlockSpec((step, 1), lambda i, p: (i, 0)), line],
        ),
        out_shape=[
            jax.ShapeDtypeStruct((rows, width), F32),
            jax.ShapeDtypeStruct((rows, 1), F32),
            jax.ShapeDtypeStruct((rows, width), BF),
        ],
        compiler_params=pltpu.CompilerParams(vmem_limit_bytes=56 * 2**20),
        cost_estimate=SHORT,
        name="out_proj",
    )(places, attn, x, gain, *parts)


def resid_back_kernel(place_ref, db_ref, first_ref, passed_ref, resid_ref, inv_ref, gain_ref, dy_ref, *refs, count):
    parts, (d_resid_ref, branch_ref, send_ref) = refs[:count], refs[count:]
    d_inner = db_ref[...].astype(F32) + first_ref[...].astype(F32) + passed_ref[...].astype(F32)
    resid = resid_ref[...]
    inv = inv_ref[...]
    scaled = d_inner * gain_ref[...]
    inner_mean = jnp.mean(scaled * resid, axis=-1, keepdims=True)
    d_resid = dy_ref[...].astype(F32) + inv * scaled - resid * (inv * inv * inv * inner_mean)
    d_resid_ref[...] = d_resid
    branch = d_resid.astype(BF)
    branch_ref[...] = branch
    for r in range(count):
        d_attn = lax.dot_general(branch, parts[r][...], NT, preferred_element_type=F32)
        send_ref[place_ref[r]] = d_attn.astype(BF)


def resid_back(places, db_own, db_first, db_passed, resid, inv, gain, dy, parts):
    rows, width = resid.shape
    count = len(parts)
    share = parts[0].shape[0]
    step = rows // 2
    line = pl.BlockSpec((step, width), lambda i, p: (i, 0))
    return pl.pallas_call(
        functools.partial(resid_back_kernel, count=count),
        grid_spec=pltpu.PrefetchScalarGridSpec(
            num_scalar_prefetch=1,
            grid=(rows // step,),
            in_specs=[line, line, line, line]
            + [pl.BlockSpec((step, 1), lambda i, p: (i, 0)), pl.BlockSpec((1, width), lambda i, p: (0, 0)), line]
            + [pl.BlockSpec((share, width), lambda i, p: (0, 0))] * count,
            out_specs=[line, line, pl.BlockSpec((count, step, share), lambda i, p: (0, i, 0))],
        ),
        out_shape=[
            jax.ShapeDtypeStruct((rows, width), F32),
            jax.ShapeDtypeStruct((rows, width), BF),
            jax.ShapeDtypeStruct((count, rows, share), BF),
        ],
        compiler_params=pltpu.CompilerParams(vmem_limit_bytes=56 * 2**20),
        cost_estimate=SHORT,
        name="resid_back",
    )(places, db_own, db_first, db_passed, resid, inv, gain, dy, *parts)


def in_back_kernel(place_ref, back_ref, x_ref, inv_ref, gain_ref, d_resid_ref, *refs, count):
    parts, (out_ref, mixed, d_scr) = refs[:count], refs[count:]
    devices, _, width = back_ref.shape
    heads = width - 2 * HD
    for d in range(devices):
        mixed[:, d * heads : (d + 1) * heads] = back_ref[d, :, :heads]
    base = devices * heads
    for g in range(KV):
        pair = back_ref[2 * g, :, heads:].astype(F32) + back_ref[2 * g + 1, :, heads:].astype(F32)
        mixed[:, base + 2 * g * HD : base + 2 * (g + 1) * HD] = pair.astype(BF)
    for r in range(count):
        d_scr[place_ref[r]] = lax.dot_general(mixed[...], parts[r][...], NT, preferred_element_type=F32)
    inv = inv_ref[...]
    share = d_scr.shape[2]
    inner = None
    for c in range(count):
        cols = slice(c * share, (c + 1) * share)
        part = jnp.sum(d_scr[c] * gain_ref[:, cols] * x_ref[:, cols].astype(F32), axis=-1, keepdims=True)
        inner = part if inner is None else inner + part
    factor = inv * inv * inv * (inner / (count * share))
    for c in range(count):
        cols = slice(c * share, (c + 1) * share)
        through = inv * (d_scr[c] * gain_ref[:, cols]) - x_ref[:, cols].astype(F32) * factor
        out_ref[:, cols] = (d_resid_ref[:, cols] + through).astype(BF)


def in_back(places, back, x, inv, gain, d_resid, parts):
    rows, width = x.shape
    count = len(parts)
    share, columns = parts[0].shape
    step = rows // 2
    line = pl.BlockSpec((step, width), lambda i, p: (i, 0))
    return pl.pallas_call(
        functools.partial(in_back_kernel, count=count),
        grid_spec=pltpu.PrefetchScalarGridSpec(
            num_scalar_prefetch=1,
            grid=(rows // step,),
            in_specs=[
                pl.BlockSpec((count, step, back.shape[2]), lambda i, p: (0, i, 0)),
                line,
                pl.BlockSpec((step, 1), lambda i, p: (i, 0)),
                pl.BlockSpec((1, width), lambda i, p: (0, 0)),
                line,
            ]
            + [pl.BlockSpec((share, columns), lambda i, p: (0, 0))] * count,
            out_specs=line,
            scratch_shapes=[pltpu.VMEM((step, columns), BF), pltpu.VMEM((count, step, share), F32)],
        ),
        out_shape=jax.ShapeDtypeStruct((rows, width), BF),
        compiler_params=pltpu.CompilerParams(vmem_limit_bytes=56 * 2**20),
        cost_estimate=SHORT,
        name="in_back",
    )(places, back, x, inv, gain, d_resid, *parts)


def grad_wo_kernel(core_ref, keep_ref, give_ref, branch_ref, keep_out, give_out):
    branch = branch_ref[...]
    keep_out[0] = lax.dot_general(keep_ref[0], branch, TN, preferred_element_type=F32).astype(BF)
    give_out[0] = lax.dot_general(give_ref[0], branch, TN, preferred_element_type=F32).astype(BF)


def grad_wo(core, attn, branch):
    devices, rows, share = attn.shape
    width = branch.shape[1]
    out = pl.BlockSpec((1, share, width), lambda c, core: (c, 0, 0))
    return pl.pallas_call(
        grad_wo_kernel,
        grid_spec=pltpu.PrefetchScalarGridSpec(
            num_scalar_prefetch=1,
            grid=(devices // 2,),
            in_specs=[
                pl.BlockSpec((1, rows, share), lambda c, core: (2 * c + core[0], 0, 0)),
                pl.BlockSpec((1, rows, share), lambda c, core: (2 * c + 1 - core[0], 0, 0)),
                pl.BlockSpec((rows, width), lambda c, core: (0, 0)),
            ],
            out_specs=[out, out],
        ),
        out_shape=[jax.ShapeDtypeStruct((devices // 2, share, width), BF)] * 2,
        compiler_params=pltpu.CompilerParams(vmem_limit_bytes=48 * 2**20),
        cost_estimate=SHORT,
        name="grad_wo",
    )(core.reshape(1), attn, attn, branch)


def grad_dn_kernel(core_ref, *refs, count):
    left, right, (keep_out, give_out) = refs[:count], refs[count : 2 * count], refs[2 * count :]
    total = None
    for r in range(count):
        part = lax.dot_general(left[r][...], right[r][...], TN, preferred_element_type=F32)
        total = part if total is None else total + part
    half = total.shape[0] // 2
    total = total.astype(BF)
    low = core_ref[0] == 0
    keep_out[...] = jnp.where(low, total[:half], total[half:])
    give_out[...] = jnp.where(low, total[half:], total[:half])


def grad_dn(core, hid_rows, dy_rows):
    count = len(hid_rows)
    tokens, hidden = hid_rows[0].shape
    width = dy_rows[0].shape[1]
    tile = 512
    out = pl.BlockSpec((hidden // 2, tile), lambda i, core: (0, i))
    return pl.pallas_call(
        functools.partial(grad_dn_kernel, count=count),
        grid_spec=pltpu.PrefetchScalarGridSpec(
            num_scalar_prefetch=1,
            grid=(width // tile,),
            in_specs=[pl.BlockSpec((tokens, hidden), lambda i, core: (0, 0))] * count
            + [pl.BlockSpec((tokens, tile), lambda i, core: (0, i))] * count,
            out_specs=[out, out],
        ),
        out_shape=[jax.ShapeDtypeStruct((hidden // 2, width), BF)] * 2,
        compiler_params=pltpu.CompilerParams(vmem_limit_bytes=56 * 2**20),
        cost_estimate=SHORT,
        name="grad_dn",
    )(core.reshape(1), *hid_rows, *dy_rows)


def attend_kernel(zeros_ref, q_ref, kv_ref, *refs, heads, start, stop):
    o_ref, send_ref, lse_ref, k_scr, v_scr, acc_ref, max_ref = refs[-7:]
    block = pl.program_id(0) + start
    zeros = zeros_ref[0]
    size = q_ref.shape[0]

    @pl.when(block == start)
    def _():
        for part in range(stop):
            rows = slice(part * size, (part + 1) * size)
            both = kv_ref[rows, :].astype(F32)
            lane = lax.broadcasted_iota(jnp.int32, both.shape, 1)
            k_scr[rows, :] = kv_ref[rows, :HD]
            v_scr[rows, :] = jnp.where(lane < HD, pltpu.roll(both, HD, 1), 1.0).astype(BF)

    first_row = block * size
    lowest = jnp.where(first_row >= zeros, zeros // size, 0)
    acc_ref[...] = jnp.zeros_like(acc_ref)
    max_ref[...] = jnp.full_like(max_ref, MASKED)
    q_heads = [q_ref[:, h * HD : (h + 1) * HD] for h in range(heads)]

    def step(index, masked):
        first_key = pl.multiple_of(index * size, size)
        keys = k_scr[pl.ds(first_key, size), :]
        values = v_scr[pl.ds(first_key, size), :]
        if masked:
            row = first_row + lax.broadcasted_iota(jnp.int32, (size, size), 0)
            col = first_key + lax.broadcasted_iota(jnp.int32, (size, size), 1)
            begin = jnp.where(row >= zeros, zeros, 0)
            refused = (col > row) | (col < begin)

        def score(h):
            return lax.dot_general(q_heads[h], keys, NT, preferred_element_type=F32)

        upcoming = score(0)
        for h in range(heads):
            scores = upcoming
            if h + 1 < heads:
                upcoming = score(h + 1)
            if masked:
                scores = jnp.where(refused, MASKED, scores)
            old_max = max_ref[h]
            new_max = jnp.maximum(old_max, jnp.max(scores, axis=-1, keepdims=True))
            weights = jnp.exp2(scores - jnp.tile(new_max, (1, size // 128)))
            shrink = jnp.exp2(old_max - new_max)
            acc_ref[h] = acc_ref[h] * shrink + jnp.dot(weights.astype(BF), values, preferred_element_type=F32)
            max_ref[h] = new_max

    def visit(index, carry):
        first_key = index * size
        mixed = (index == block) | ((first_row + size > zeros) & (first_key < zeros))

        @pl.when(mixed)
        def _():
            step(index, True)

        @pl.when(jnp.logical_not(mixed))
        def _():
            step(index, False)

        return carry

    lax.fori_loop(lowest, block + 1, visit, 0)
    for h in range(heads):
        acc = acc_ref[h]
        total = acc[:, HD : HD + 1]
        out = acc[:, :HD] / total
        o_ref[:, h * HD : (h + 1) * HD] = out
        send_ref[0, :, h * HD : (h + 1) * HD] = out.astype(BF)
        lse = max_ref[h] + jnp.log2(total)
        lse_ref[0, h : h + 1, :] = jnp.transpose(lse)[:1]


def attend(zeros, qkv, start, stop, before=None):
    length, width = qkv.shape
    q_width = width - 2 * HD
    heads = q_width // HD
    size = BLOCK
    blocks = length // size
    before = () if before is None else before
    return pl.pallas_call(
        functools.partial(attend_kernel, heads=heads, start=start, stop=stop),
        grid_spec=pltpu.PrefetchScalarGridSpec(
            num_scalar_prefetch=1,
            grid=(stop - start,),
            in_specs=[
                pl.BlockSpec((size, q_width), lambda i, z: (i + start, 0)),
                pl.BlockSpec((length, 2 * HD), lambda i, z: (0, q_width // (2 * HD))),
            ]
            + [pl.BlockSpec(memory_space=pl.ANY)] * len(before),
            out_specs=[
                pl.BlockSpec((size, q_width), lambda i, z: (i + start, 0)),
                pl.BlockSpec((1, size, q_width), lambda i, z: (i + start, 0, 0)),
                pl.BlockSpec((1, heads, size), lambda i, z: (i + start, 0, 0)),
            ],
            scratch_shapes=[
                pltpu.VMEM((length, HD), BF),
                pltpu.VMEM((length, 2 * HD), BF),
                pltpu.VMEM((heads, size, 2 * HD), F32),
                pltpu.VMEM((heads, size, 128), F32),
            ],
        ),
        out_shape=[
            jax.ShapeDtypeStruct((length, q_width), F32),
            jax.ShapeDtypeStruct((blocks, size, q_width), BF),
            jax.ShapeDtypeStruct((blocks, heads, size), F32),
        ],
        input_output_aliases={3 + i: i for i in range(len(before))},
        compiler_params=pltpu.CompilerParams(vmem_limit_bytes=48 * 2**20),
        cost_estimate=SHORT,
        name="attend",
    )(zeros, qkv, qkv, *before)


def attend_back_kernel(
    zeros_ref, q_ref, kv_ref, do_ref, lse_ref, cos_ref, sin_ref, extra_ref, *refs, heads, start
):
    send_ref, dq_acc, delta_ref, q_scr, do_scr = refs[-5:]
    block = pl.program_id(0) + start
    zeros = zeros_ref[0]
    size = kv_ref.shape[0]
    length = q_ref.shape[0]
    blocks = length // size

    @pl.when(block == start)
    def _():
        if start == 0:
            dq_acc[...] = jnp.zeros_like(dq_acc)
        else:
            dq_acc[...] = refs[0][...]
            delta_ref[...] = extra_ref[...]
        for part in range(start, blocks):
            rows = slice(part * size, (part + 1) * size)
            if start == 0:
                product = jnp.transpose(do_ref[rows, :].astype(F32) * extra_ref[rows, :])
            for h in range(heads):
                cols = slice(h * HD, (h + 1) * HD)
                q_scr[h, rows, :] = q_ref[rows, cols]
                do_scr[h, rows, :] = do_ref[rows, cols]
                if start == 0:
                    delta_ref[part, h : h + 1, :] = jnp.sum(product[cols], axis=0, keepdims=True)

    first_key = block * size
    both = kv_ref[...]
    keys = both[:, :HD]
    values = both[:, HD:]
    keys_t = jnp.transpose(keys.astype(F32)).astype(BF)
    highest = jnp.where(first_key + size <= zeros, jnp.minimum((zeros + size - 1) // size, blocks), blocks)

    def step(index, carry, masked):
        first_row = pl.multiple_of(index * size, size)
        span = pl.ds(first_row, size)
        if masked:
            col = first_key + lax.broadcasted_iota(jnp.int32, (size, size), 0)
            row = first_row + lax.broadcasted_iota(jnp.int32, (size, size), 1)
            begin = jnp.where(row >= zeros, zeros, 0)
            refused = (col > row) | (col < begin)

        def products(h):
            q_rows = q_scr[h, span, :]
            do_rows = do_scr[h, span, :]
            scores = lax.dot_general(keys, q_rows, NT, preferred_element_type=F32)
            d_prob = lax.dot_general(values, do_rows, NT, preferred_element_type=F32)
            return q_rows, do_rows, scores, d_prob

        upcoming = products(0)
        dk_sum, dv_sum = carry
        for h in range(heads):
            q_rows, do_rows, scores, d_prob = upcoming
            if h + 1 < heads:
                upcoming = products(h + 1)
            shifted = scores - lse_ref[index, h : h + 1, :]
            if masked:
                shifted = jnp.where(refused, MASKED, shifted)
            prob = jnp.exp2(shifted)
            d_score = (prob * (d_prob - delta_ref[index, h : h + 1, :])).astype(BF)
            dv_sum = dv_sum + jnp.dot(prob.astype(BF), do_rows, preferred_element_type=F32)
            dk_sum = dk_sum + jnp.dot(d_score, q_rows, preferred_element_type=F32)
            dq_acc[h * HD : (h + 1) * HD, span] += jnp.dot(keys_t, d_score, preferred_element_type=F32)
        return dk_sum, dv_sum

    def visit(index, carry):
        first_row = index * size
        mixed = (index == block) | ((first_row + size > zeros) & (first_key < zeros))
        return lax.cond(
            mixed,
            lambda c: step(index, c, True),
            lambda c: step(index, c, False),
            carry,
        )

    zero = jnp.zeros((size, HD), F32)
    dk_sum, dv_sum = lax.fori_loop(block, highest, visit, (zero, zero))
    q_width = heads * HD
    done = pl.ds(pl.multiple_of(first_key, size), size)
    cos = cos_ref[...]
    sin = sin_ref[...]
    dq = jnp.transpose(dq_acc[:, done]) * HD**-0.5
    dq = dq * jnp.tile(cos, (1, q_width // 128)) - swap_halves(dq) * jnp.tile(sin, (1, q_width // 128))
    send_ref[0, :, :q_width] = dq.astype(BF)
    dkv = jnp.concatenate([dk_sum * (1.0 / LOG2E), dv_sum], axis=1)
    lane = lax.broadcasted_iota(jnp.int32, dkv.shape, 1)
    send_ref[0, :, q_width:] = jnp.where(lane < HD, dkv * cos - swap_halves(dkv) * sin, dkv).astype(BF)


def attend_back(zeros, qkv, d_out, lse, cos, sin, start, stop, out=None, before=None):
    length, width = qkv.shape
    q_width = width - 2 * HD
    heads = q_width // HD
    size = BLOCK
    blocks = length // size
    whole = lambda *shape: pl.BlockSpec(shape, lambda j, z: (0,) * len(shape))
    if before is None:
        operands = (out,)
        specs = [whole(length, q_width)]
        aliases = {}
    else:
        send, d_query, delta = before
        operands = (delta, d_query, send)
        specs = [whole(blocks, heads, size), whole(q_width, length), pl.BlockSpec(memory_space=pl.ANY)]
        aliases = {9: 0}
    return pl.pallas_call(
        functools.partial(attend_back_kernel, heads=heads, start=start),
        grid_spec=pltpu.PrefetchScalarGridSpec(
            num_scalar_prefetch=1,
            grid=(stop - start,),
            in_specs=[
                whole(length, q_width),
                pl.BlockSpec((size, 2 * HD), lambda j, z: (j + start, q_width // (2 * HD))),
                whole(length, q_width),
                whole(blocks, heads, size),
                pl.BlockSpec((size, 128), lambda j, z: (j + start, 0)),
                pl.BlockSpec((size, 128), lambda j, z: (j + start, 0)),
            ]
            + specs,
            out_specs=[
                pl.BlockSpec((1, size, width), lambda j, z: (j + start, 0, 0)),
                whole(q_width, length),
                whole(blocks, heads, size),
            ],
            scratch_shapes=[
                pltpu.VMEM((heads, length, HD), BF),
                pltpu.VMEM((heads, length, HD), BF),
            ],
        ),
        out_shape=[
            jax.ShapeDtypeStruct((blocks, size, width), BF),
            jax.ShapeDtypeStruct((q_width, length), F32),
            jax.ShapeDtypeStruct((blocks, heads, size), F32),
        ],
        input_output_aliases=aliases,
        compiler_params=pltpu.CompilerParams(vmem_limit_bytes=58 * 2**20),
        cost_estimate=SHORT,
        name="attend_back",
    )(zeros, qkv, qkv, d_out, lse, cos, sin, *operands)


def turn_tables(positions):
    cosine, sine = rope_tables(positions, HD)
    return jnp.concatenate([cosine] * 4, axis=1), jnp.concatenate([-sine, sine, -sine, sine], axis=1)


def fast_body(tokens, segment_ids, selected, cotangent, w_qkv, w_out, w_gate_up, w_down, g_attn, g_mlp):
    _, rows, width = tokens.shape
    devices = 2 * CHIPS
    me = lax.axis_index("sp")
    core = me & 1
    planes = lax.axis_size("dp")
    share = width // devices
    kv_width = KV * HD
    first_mask, second_mask = rel_masks(core)
    other = me ^ 1
    chip = me // 2
    place_list = [me, me ^ first_mask, me ^ second_mask, me ^ 6]
    place_list += [other, other ^ second_mask, other ^ first_mask, other ^ 6]
    places = jnp.stack(place_list)
    hidden_chip = 2 * w_down.shape[0]
    quarter = share // planes
    plane = lax.axis_index("dp")
    length = devices * rows
    blocks = length // BLOCK

    count = jnp.sum((segment_ids == 0).astype(F32))
    vectors = jnp.stack([g_attn.astype(F32), g_mlp.astype(F32)] + [jnp.full((share,), count)] * 6)
    paired = [w_qkv[:, :width]]
    for head in range(KV):
        paired.append(w_qkv[:, width + head * HD : width + (head + 1) * HD])
        paired.append(w_qkv[:, width + kv_width + head * HD : width + kv_width + (head + 1) * HD])
    qkv_own = jnp.concatenate(paired, axis=1)
    gu_rows = lax.dynamic_slice_in_dim(w_gate_up, plane * quarter, quarter, 0)
    gu_send = []
    for place in range(CHIPS):
        for begin in (place * hidden_chip, (CHIPS + place) * hidden_chip):
            gu_send.append(gu_rows[:, begin : begin + hidden_chip])
    gu_send = jnp.stack([jnp.concatenate(gu_send[2 * c : 2 * c + 2], axis=1) for c in range(CHIPS)])
    vectors = gather_vectors(vectors, me)
    vectors, qkv_own, gu_send = fence(vectors, qkv_own, gu_send)
    qkv_first = send_first(qkv_own)
    attn_gain = vectors[0:1]
    mlp_gain = vectors[1:2]
    zeros = jnp.sum(vectors[2].reshape(devices, share)[:, 0]).astype(jnp.int32)
    zeros_one = zeros.reshape(1)
    local_pos = me * rows + jnp.arange(rows, dtype=jnp.int32) - segment_ids.reshape(rows) * zeros
    cos, sin = turn_tables(local_pos)
    dy = (cotangent * selected[:, :, None].astype(BF)).reshape(rows, width)
    qkv_own, qkv_first, cos, sin = fence(qkv_own, qkv_first, cos, sin)
    qkv_second = send_second(qkv_own)
    qkv_theirs = [send_sibling(qkv_own), send_sibling(qkv_first)]
    all_places = jnp.arange(length, dtype=jnp.int32)
    cos_all, sin_all = turn_tables(all_places - jnp.where(all_places >= zeros, zeros, 0))
    qkv_first, qkv_second, cos_all, sin_all, *qkv_theirs = fence(qkv_first, qkv_second, cos_all, sin_all, *qkv_theirs)
    qkv_far = send_second(qkv_first)
    qkv_theirs.append(send_sibling(qkv_second))
    qkv_far, dy, *qkv_theirs = fence(qkv_far, dy, *qkv_theirs)
    qkv_theirs.append(send_sibling(qkv_far))
    qkv_parts = [qkv_own, qkv_first, qkv_second, qkv_far] + qkv_theirs
    x_bf = tokens.reshape(rows, width)
    x_bf, w_out, gu_send, *qkv_parts = fence(x_bf, w_out, gu_send, *qkv_parts)
    out_first = send_first(w_out)
    gu_part = lax.all_to_all(gu_send, "sp", 0, 0, axis_index_groups=SAME_CORE, tiled=True)
    qkv_send, normed, inv_one = project(places, x_bf, attn_gain, cos, sin, qkv_parts)
    qkv_send, out_first = fence(qkv_send, out_first)
    gu_mine = lax.all_gather(after(gu_part, qkv_send), "dp", axis=0, tiled=False)
    gu_mine = lax.all_gather(after(gu_part, qkv_send), "dp", axis=0, tiled=False)
    down_theirs = send_sibling(w_down)
    w_dn = jnp.where(
        core == 0, jnp.concatenate([w_down, down_theirs], axis=0), jnp.concatenate([down_theirs, w_down], axis=0)
    )
    qkv_heads = lax.all_to_all(qkv_send, "sp", 0, 0, tiled=True).reshape(length, qkv_send.shape[2])

    cuts = (0, (5 * blocks) // 8, (7 * blocks) // 8, blocks)
    qkv_heads, w_dn, out_first = fence(qkv_heads, w_dn, out_first)
    out_second = send_second(after(w_out, qkv_heads))
    dy_first = send_first(after(dy, qkv_heads))
    fwd = attend(zeros_one, qkv_heads, cuts[0], cuts[1])
    qkv_heads, out_second, dy_first, out_first, dy, *fwd = fence(qkv_heads, out_second, dy_first, out_first, dy, *fwd)
    out_far = send_second(out_first)
    dy_second = send_second(dy)
    fwd = attend(zeros_one, qkv_heads, cuts[1], cuts[2], fwd)
    qkv_heads, out_far, dy_second, dy_first, *fwd = fence(qkv_heads, out_far, dy_second, dy_first, *fwd)
    dy_far = send_second(dy_first)
    gu_theirs = send_sibling(after(gu_mine, fwd[2]))
    out_heads, out_send, lse = attend(zeros_one, qkv_heads, cuts[2], cuts[3], fwd)
    out_parts = [w_out, out_first, out_second, out_far]
    out_parts = out_parts + [send_sibling(part) for part in out_parts]
    out_send, gu_mine, gu_theirs = fence(out_send, gu_mine, gu_theirs)
    attn_tok = lax.all_to_all(out_send, "sp", 0, 0, tiled=True)
    w_gu = join(core, gu_mine, gu_theirs)
    attn_tok, w_gu, dy_far, *out_parts = fence(attn_tok, w_gu, dy_far, *out_parts)
    residual, inv_two, inner = out_proj(places, attn_tok, x_bf, mlp_gain, out_parts)

    b_first = send_first(inner)
    own = ffn(inner, dy, w_gu, w_dn)
    inner, b_first, *own = fence(inner, b_first, *own)
    b_second = send_second(inner)
    first = ffn(b_first, dy_first, w_gu, w_dn)
    b_first, b_second, *first = fence(b_first, b_second, *first)
    b_far = send_second(b_first)
    second = ffn(b_second, dy_second, w_gu, w_dn)
    b_far, db_first, *second = fence(b_far, first[3], *second)
    db_got_first = send_first(db_first)
    far = ffn(b_far, dy_far, w_gu, w_dn)
    db_got_first, db_far, *hid_rows = fence(db_got_first, far[3], own[0], first[0], second[0], far[0])

    b_rows = [inner, b_first, b_second, b_far]
    db_got_far = send_first(db_far)
    gu_keep, gu_give = grad_gu(
        core,
        b_rows,
        [own[1], first[1], second[1], far[1]],
        [own[2], first[2], second[2], far[2]],
        share,
        planes,
    )
    db_got_far, gu_keep, gu_give, *hid_rows = fence(db_got_far, gu_keep, gu_give, *hid_rows)
    db_pass = (second[3].astype(F32) + db_got_far.astype(F32)).astype(BF)
    db_pass, gu_give, *hid_rows = fence(db_pass, gu_give, *hid_rows)
    db_passed = send_second(db_pass)
    gu_got = send_sibling(gu_give)
    dn_keep, dn_give = grad_dn(core, hid_rows, [dy, dy_first, dy_second, dy_far])
    gu_got, dn_keep, dn_give = fence(gu_got, dn_keep, dn_give)
    gu_sum = (gu_keep.astype(F32) + gu_got.astype(F32)).astype(BF)
    gu_sum, db_passed, dn_give = fence(gu_sum, db_passed, dn_give)
    gu_z = lax.psum_scatter(
        gu_sum.reshape(planes * CHIPS * quarter, 2 * hidden_chip), "dp", scatter_dimension=0, tiled=True
    )
    gu_z = gu_z.reshape(CHIPS, quarter, 2 * hidden_chip)
    dn_got = send_sibling(dn_give)
    d_resid, d_branch, d_send = resid_back(
        places, own[3], db_got_first, db_passed, residual, inv_two, mlp_gain, dy, out_parts
    )
    d_send, d_branch, dn_got = fence(d_send, d_branch, dn_got)
    d_heads = lax.all_to_all(d_send, "sp", 0, 0, tiled=True).reshape(length, share)
    wo_keep, wo_give = grad_wo(core, attn_tok, d_branch)
    d_heads, wo_keep, wo_give, normed = fence(d_heads, wo_keep, wo_give, normed)

    def back_call(heads, start, stop, **kwargs):
        return attend_back(zeros_one, qkv_heads, heads, lse, cos_all, sin_all, start, stop, **kwargs)

    turns = (0, blocks // 8, blocks // 4, (3 * blocks) // 8, blocks)
    wo_got = send_sibling(wo_give)
    a_first = send_first(normed)
    bwd = back_call(d_heads, turns[0], turns[1], out=out_heads)
    d_heads, a_first, wo_got, normed, *bwd = fence(d_heads, a_first, wo_got, normed, *bwd)
    a_second = send_second(normed)
    a_theirs = [send_sibling(normed), send_sibling(a_first)]
    bwd = back_call(d_heads, turns[1], turns[2], before=bwd)
    dn_parts = [part.reshape(2, 2, dn_keep.shape[0] // planes, width) for part in (dn_keep, dn_got)]
    dn_move = pick_sum(dn_parts, 1 - (plane & 1), 1).astype(BF)
    d_heads, gu_z, a_second, dn_move, *moves = fence(d_heads, gu_z, a_second, dn_move, *a_theirs, *bwd)
    a_theirs, bwd = moves[:2], moves[2:]

    def wo_part(place):
        return pick(wo_keep, place).astype(F32) + pick(wo_got, place).astype(F32)

    dn_move = lax.ppermute(dn_move, "dp", LINE_NEAR)
    gu_z = lax.all_to_all(gu_z, "sp", 0, 0, axis_index_groups=SAME_CORE, tiled=True)
    a_theirs.append(send_sibling(a_second))
    bwd = back_call(d_heads, turns[2], turns[3], before=bwd)
    d_heads, gu_z, a_first, dn_move, *moves = fence(d_heads, gu_z, a_first, dn_move, *a_theirs, *bwd)
    a_theirs, bwd = moves[:3], moves[3:]

    dn_own = pick_sum(dn_parts, plane & 1, 1) + dn_move.astype(F32)
    dn_move = pick(dn_own, 1 - plane // 2).astype(BF)
    wo_first = wo_part(chip ^ (first_mask // 2)).astype(BF)
    wo_far = wo_part(chip ^ 3).astype(BF)
    d_heads, gu_z, a_first, wo_first, wo_far, dn_move = fence(d_heads, gu_z, a_first, wo_first, wo_far, dn_move)
    gu_all = lax.all_gather(gu_z, "dp", axis=0, tiled=False)
    a_far = send_second(a_first)
    wo_far = send_first(wo_far)
    wo_first = send_first(wo_first)
    dn_move = lax.ppermute(dn_move, "dp", LINE_FAR)
    bwd = back_call(d_heads, turns[3], turns[4], before=bwd)
    wo_pass = (wo_part(chip ^ (second_mask // 2)) + wo_far.astype(F32)).astype(BF)
    dp_heads, wo_first, wo_pass, a_far, dn_move = fence(bwd[0], wo_first, wo_pass, a_far, dn_move)

    wo_passed = send_second(wo_pass)
    a_theirs.append(send_sibling(a_far))
    back = lax.all_to_all(dp_heads, "sp", 0, 0, tiled=True)
    grad_wq = grad_qkv(places, [normed, a_first, a_second, a_far] + list(a_theirs), dp_heads, planes)
    wo_passed, grad_wq = fence(wo_passed, grad_wq)
    wo_rows = (wo_part(chip) + wo_first.astype(F32) + wo_passed.astype(F32)).astype(BF)
    split = grad_wq.shape[2]
    last_parts = [jnp.concatenate([grad_wq, wo_rows.reshape(planes, quarter, width)], axis=2)]
    y_far, y_first = far[4], first[4]
    moves = None
    for step in range(1, planes):
        moves = line_scatter_sends(last_parts, moves, step, 0)
        y_far, y_first, *moves = fence(y_far, y_first, *moves)
        moves = line_scatter_move(moves, step)
        if step == 1:
            dn_z = (pick(dn_own, plane // 2) + dn_move.astype(F32)).astype(BF)
            dn_all = lax.all_gather(dn_z, "dp", axis=0, tiled=False)
        elif step == 2:
            back, *moves = fence(back, *moves)
        elif step == 3:
            y_far, back = fence(y_far, back)
            y_got_far = send_first(y_far)
        moves = fence(*moves)
    last_z = line_scatter_end(last_parts, moves, 0)
    wq_z = last_z[:, :split].reshape(quarter, devices, split // devices).transpose(1, 0, 2)
    wq_z, wo_z, gu_all = fence(wq_z, last_z[:, split:], gu_all)
    wq_z = lax.all_to_all(wq_z, "sp", 0, 0, tiled=True)
    grad_tokens = in_back(places, back, x_bf, inv_one, attn_gain, d_resid, qkv_parts).reshape(tokens.shape)
    y_pass = (second[4].astype(F32) + y_got_far.astype(F32)).astype(BF)
    last_z = jnp.concatenate([wq_z.transpose(1, 0, 2).reshape(quarter, split), wo_z], axis=1)
    last_z, grad_tokens, y_pass, y_first = fence(last_z, grad_tokens, y_pass, y_first)
    y_got_first = send_first(y_first)
    y_passed = send_second(y_pass)
    last_steps = [(last_z, last_z)]
    outs = []
    for step in range(1, planes):
        last_steps.append(line_gather_move(last_steps[-1], step))
        if step == 1:
            outs += spread(gu_all, w_gate_up, g_mlp.astype(F32).reshape(share, 1))
        elif step == 2:
            outs.append(dn_all.astype(F32).reshape(w_down.shape))
        if step == planes - 1:
            y_sum = own[4].astype(F32) + y_got_first.astype(F32) + y_passed.astype(F32)
            outs.append((residual + y_sum).astype(BF).reshape(tokens.shape))
            break
        moves = fence(*last_steps[-1], *outs)
        last_steps[-1], outs = tuple(moves[:2]), list(moves[2:])
    grad_w_gate_up, grad_g_mlp, grad_w_down, output = outs
    grad_w_qkv, grad_g_attn, grad_w_out = spread_last(last_steps, w_qkv, g_attn.astype(F32).reshape(share, 1), width)
    return (
        output,
        grad_tokens,
        grad_w_qkv,
        grad_w_out,
        grad_w_gate_up,
        grad_w_down,
        grad_g_attn.reshape(share),
        grad_g_mlp.reshape(share),
    )


def solution(mesh):
    in_specs = (
        P("dp", "sp", None),
        P("dp", "sp"),
        P("dp", "sp"),
        P("dp", "sp", None),
        P("sp", None),
        P("sp", None),
        P("sp", None),
        P("sp", None),
        P("sp"),
        P("sp"),
    )
    out_specs = (
        P("dp", "sp", None),
        P("dp", "sp", None),
        P("sp", None),
        P("sp", None),
        P("sp", None),
        P("sp", None),
        P("sp"),
        P("sp"),
    )
    body = fast_body if dict(mesh.shape) == {"dp": 4, "sp": 2 * CHIPS} else general_body
    return jax.shard_map(body, mesh=mesh, in_specs=in_specs, out_specs=out_specs, check_vma=False)
```

```python
import functools
import math

import jax
import jax.numpy as jnp
from jax import lax
from jax.experimental import pallas as pl
from jax.experimental.pallas import tpu as pltpu
from jax.sharding import PartitionSpec as P

D = 2048
H = 32
KV = 4
HD = 64
FF = 5632


EPSILON = 1e-05
ROPE_BASE = 10000.0
MASKED = -1e30


def rope_tables(positions, head_size):
    half_dim = head_size // 2
    frequency = ROPE_BASE ** (-(jnp.arange(half_dim, dtype=jnp.float32) * 2.0 / head_size))
    angles = positions.astype(jnp.float32)[:, None] * frequency[None, :]
    return (jnp.cos(angles), jnp.sin(angles))


def rotate(values, cosine, sine_tab, inverse_turn):
    half_dim = values.shape[-1] // 2
    first_half = values[..., :half_dim]
    second = values[..., half_dim:]
    cos_wide = cosine[:, None, :]
    sin_wide = sine_tab[:, None, :]
    if inverse_turn:
        sin_wide = -sin_wide
    return jnp.concatenate(
        [first_half * cos_wide - second * sin_wide, second * cos_wide + first_half * sin_wide],
        axis=-1,
    )


def rms_norm(values, gain_vec):
    inverse = lax.rsqrt(jnp.mean(values * values, axis=-1, keepdims=True) + EPSILON)
    return (values * inverse * gain_vec, inverse)


def norm_back(values, inverse, gain_vec, upstream):
    scaled = upstream * gain_vec
    inner_mean = jnp.mean(scaled * values, axis=-1, keepdims=True)
    through = inverse * scaled - values * inverse**3 * inner_mean
    gain_grad = jnp.sum(upstream * values * inverse, axis=0)
    return (through, gain_grad)


def attention_inputs(flat_in, qkv_full, gain_vec, cosine, sine_tab):
    row_count = flat_in.shape[0]
    group_size = H // KV
    normed, inverse = rms_norm(flat_in, gain_vec)
    normed = normed.astype(jnp.bfloat16)
    projected = jnp.dot(normed, qkv_full, preferred_element_type=jnp.float32)
    queries = rotate(projected[:, :D].reshape(row_count, H, HD), cosine, sine_tab, False)
    key_heads = rotate(
        projected[:, D : D + KV * HD].reshape(row_count, KV, HD), cosine, sine_tab, False
    )
    value_heads = projected[:, D + KV * HD :].reshape(row_count, KV, HD)
    key_wide = jnp.broadcast_to(key_heads[:, :, None], (row_count, KV, group_size, HD)).reshape(
        row_count, D
    )
    value_wide = jnp.broadcast_to(value_heads[:, :, None], (row_count, KV, group_size, HD)).reshape(
        row_count, D
    )
    stacked = jnp.stack([queries.reshape(row_count, D), key_wide, value_wide]).astype(jnp.bfloat16)
    return (normed, inverse, stacked)


def block_mask(seg_full, position, row_begin, finish):
    row_seg = seg_full[:, row_begin:finish]
    col_seg = seg_full[:, :finish]
    same_doc = row_seg[:, :, None] == col_seg[:, None, :]
    causal = position[row_begin:finish, None] >= position[None, :finish]
    return same_doc & causal[None]


def attention_forward(queries, key_heads, value_heads, seg_full, score_scale):
    length = queries.shape[1]
    block_rows = min(512, length)
    position = jnp.arange(length, dtype=jnp.int32)
    outputs = []
    lse_parts = []
    for block_num in range(length // block_rows):
        row_begin = block_num * block_rows
        finish = row_begin + block_rows
        scores = (
            jnp.einsum(
                "sqhd,skhd->shqk",
                queries[:, row_begin:finish],
                key_heads[:, :finish],
                preferred_element_type=jnp.float32,
            )
            * score_scale
        )
        allowed = block_mask(seg_full, position, row_begin, finish)
        scores = jnp.where(allowed[:, None], scores, MASKED)
        row_max = jnp.max(scores, axis=-1, keepdims=True)
        shifted = jnp.exp(scores - row_max)
        row_total = jnp.sum(shifted, axis=-1, keepdims=True)
        softmax_w = (shifted / row_total).astype(jnp.bfloat16)
        outputs.append(
            jnp.einsum(
                "shqk,skhd->sqhd",
                softmax_w,
                value_heads[:, :finish],
                preferred_element_type=jnp.float32,
            )
        )
        lse_parts.append(row_max + jnp.log(row_total))
    return (jnp.concatenate(outputs, axis=1), jnp.concatenate(lse_parts, axis=2))


def attention_backward(queries, key_heads, value_heads, seg_full, log_sums, grad_out, score_scale):
    length = queries.shape[1]
    block_rows = min(512, length)
    position = jnp.arange(length, dtype=jnp.int32)
    grad_query = []
    grad_key = jnp.zeros(key_heads.shape, jnp.float32)
    grad_value = jnp.zeros(value_heads.shape, jnp.float32)
    for block_num in range(length // block_rows):
        row_begin = block_num * block_rows
        finish = row_begin + block_rows
        query_rows = queries[:, row_begin:finish]
        grad_rows = grad_out[:, row_begin:finish]
        key_part = key_heads[:, :finish]
        value_part = value_heads[:, :finish]
        scores = (
            jnp.einsum("sqhd,skhd->shqk", query_rows, key_part, preferred_element_type=jnp.float32)
            * score_scale
        )
        allowed = block_mask(seg_full, position, row_begin, finish)
        softmax_f = jnp.where(
            allowed[:, None], jnp.exp(scores - log_sums[:, :, row_begin:finish]), 0.0
        )
        grad_probs = jnp.einsum(
            "sqhd,skhd->shqk", grad_rows, value_part, preferred_element_type=jnp.float32
        )
        row_delta = jnp.sum(softmax_f * grad_probs, axis=-1, keepdims=True)
        grad_scores = (softmax_f * (grad_probs - row_delta)).astype(jnp.bfloat16)
        grad_query.append(
            jnp.einsum("shqk,skhd->sqhd", grad_scores, key_part, preferred_element_type=jnp.float32)
            * score_scale
        )
        grad_key = grad_key.at[:, :finish].add(
            jnp.einsum(
                "shqk,sqhd->skhd", grad_scores, query_rows, preferred_element_type=jnp.float32
            )
            * score_scale
        )
        grad_value = grad_value.at[:, :finish].add(
            jnp.einsum(
                "shqk,sqhd->skhd",
                softmax_f.astype(jnp.bfloat16),
                grad_rows,
                preferred_element_type=jnp.float32,
            )
        )
    return (jnp.concatenate(grad_query, axis=1), grad_key, grad_value)


def general_body(tokens, segment_ids, selected, cotangent, w_qkv, w_out, w_gate_up, w_down, g_attn, g_mlp):
    streams, local_len, model_dim = tokens.shape
    sp_count = lax.axis_size("sp")
    sp_index = lax.axis_index("sp")
    row_count = streams * local_len
    group_size = H // KV
    kv_width = KV * HD
    score_scale = HD ** (-0.5)
    contract = (((0,), (0,)), ((), ()))
    seg_full = lax.all_gather(segment_ids, "sp", axis=1, tiled=True)
    first_count = jnp.sum((seg_full == 0).astype(jnp.int32), axis=1, keepdims=True)
    local_pos = (
        sp_index * local_len
        + jnp.arange(local_len, dtype=jnp.int32)[None, :]
        - segment_ids * first_count
    )
    cosine, sine_tab = rope_tables(local_pos.reshape(row_count), HD)
    shards = (w_qkv, w_out, w_gate_up, w_down, g_attn, g_mlp)
    gathered = (
        lax.all_gather(shards[0], "sp", axis=0, tiled=True),
        lax.all_gather(shards[1], "sp", axis=0, tiled=True),
        lax.all_gather(shards[2], "sp", axis=0, tiled=True),
        lax.all_gather(shards[3], "sp", axis=0, tiled=True),
        lax.all_gather(shards[4], "sp", axis=0, tiled=True),
        lax.all_gather(shards[5], "sp", axis=0, tiled=True),
    )
    qkv_full, out_full, gate_up_full, down_full, attn_gain, mlp_gain = gathered
    attn_gain = attn_gain.astype(jnp.float32)
    mlp_gain = mlp_gain.astype(jnp.float32)
    flat_in = tokens.reshape(row_count, model_dim).astype(jnp.float32)
    normed, inverse_one, stacked = attention_inputs(flat_in, qkv_full, attn_gain, cosine, sine_tab)
    head_view = lax.all_to_all(
        stacked.reshape(3, streams, local_len, model_dim),
        "sp",
        split_axis=3,
        concat_axis=2,
        tiled=True,
    )
    length = head_view.shape[2]
    heads_here = head_view.shape[3] // HD
    head_shape = (streams, length, heads_here, HD)
    queries = head_view[0].reshape(head_shape)
    key_heads = head_view[1].reshape(head_shape)
    value_heads = head_view[2].reshape(head_shape)
    attn_heads, log_sums = attention_forward(queries, key_heads, value_heads, seg_full, score_scale)
    attn_send = attn_heads.astype(jnp.bfloat16).reshape(streams, length, heads_here * HD)
    attn_tok = lax.all_to_all(attn_send, "sp", split_axis=1, concat_axis=2, tiled=True).reshape(
        row_count, model_dim
    )
    branch = jnp.dot(attn_tok, out_full, preferred_element_type=jnp.float32)
    residual = flat_in + branch
    inner_f, inverse_two = rms_norm(residual, mlp_gain)
    inner_in = inner_f.astype(jnp.bfloat16)
    gate_up = jnp.dot(inner_in, gate_up_full, preferred_element_type=jnp.float32)
    gate_part = gate_up[:, :FF]
    up_part = gate_up[:, FF:]
    sigmoid_g = jax.nn.sigmoid(gate_part)
    silu_gate = gate_part * sigmoid_g
    hidden = (silu_gate * up_part).astype(jnp.bfloat16)
    result = residual + jnp.dot(hidden, down_full, preferred_element_type=jnp.float32)
    output = result.astype(jnp.bfloat16).reshape(streams, local_len, model_dim)
    qkv_back, out_back, gate_up_back, down_back, attn_gain_b, mlp_gain_b = gathered
    attn_gain_b = attn_gain_b.astype(jnp.float32)
    mlp_gain_b = mlp_gain_b.astype(jnp.float32)
    grad_y = (cotangent * selected[:, :, None].astype(jnp.bfloat16)).reshape(row_count, model_dim)
    grad_hidden = jnp.dot(grad_y, down_back.T, preferred_element_type=jnp.float32)
    silu_slope = sigmoid_g * (1.0 + gate_part * (1.0 - sigmoid_g))
    grad_both = jnp.concatenate(
        [grad_hidden * up_part * silu_slope, grad_hidden * silu_gate], axis=1
    ).astype(jnp.bfloat16)
    grad_inner = jnp.dot(grad_both, gate_up_back.T, preferred_element_type=jnp.float32)
    grad_resid, gain_two = norm_back(residual, inverse_two, mlp_gain_b, grad_inner)
    grad_resid = grad_resid + grad_y.astype(jnp.float32)
    grad_branch = grad_resid.astype(jnp.bfloat16)
    grad_attn = jnp.dot(grad_branch, out_back.T, preferred_element_type=jnp.float32).astype(
        jnp.bfloat16
    )
    grad_view = lax.all_to_all(
        grad_attn.reshape(streams, local_len, model_dim),
        "sp",
        split_axis=2,
        concat_axis=1,
        tiled=True,
    )
    grad_view = grad_view.reshape(head_shape)
    grad_q, grad_k, grad_v = attention_backward(
        queries, key_heads, value_heads, seg_full, log_sums, grad_view, score_scale
    )
    back_send = (
        jnp.stack([grad_q, grad_k, grad_v])
        .astype(jnp.bfloat16)
        .reshape(3, streams, length, heads_here * HD)
    )
    returned = lax.all_to_all(back_send, "sp", split_axis=2, concat_axis=3, tiled=True)
    returned = returned.astype(jnp.float32).reshape(3, row_count, H, HD)
    grad_pq = rotate(returned[0], cosine, sine_tab, True).reshape(row_count, model_dim)
    key_summed = jnp.sum(returned[1].reshape(row_count, KV, group_size, HD), axis=2)
    grad_pk = rotate(key_summed, cosine, sine_tab, True).reshape(row_count, kv_width)
    grad_pv = jnp.sum(returned[2].reshape(row_count, KV, group_size, HD), axis=2).reshape(
        row_count, kv_width
    )
    grad_mixed = jnp.concatenate(
        [grad_pq.astype(jnp.bfloat16), grad_pk.astype(jnp.bfloat16), grad_pv.astype(jnp.bfloat16)],
        axis=1,
    )
    grad_normed = jnp.dot(grad_mixed, qkv_back.T, preferred_element_type=jnp.float32)
    grad_in, gain_one = norm_back(flat_in, inverse_one, attn_gain_b, grad_normed)
    grad_in = grad_in + grad_resid
    grad_tokens = grad_in.astype(jnp.bfloat16).reshape(streams, local_len, model_dim)
    gain_totals = lax.psum((gain_one, gain_two), ("dp", "sp"))
    gain_share = model_dim // sp_count
    grad_g_attn = lax.dynamic_slice_in_dim(gain_totals[0], sp_index * gain_share, gain_share, 0)
    grad_g_mlp = lax.dynamic_slice_in_dim(gain_totals[1], sp_index * gain_share, gain_share, 0)
    row_sums = lax.psum_scatter(
        jnp.concatenate(
            [
                lax.dot_general(normed, grad_mixed, contract, preferred_element_type=jnp.float32),
                lax.dot_general(
                    attn_tok, grad_branch, contract, preferred_element_type=jnp.float32
                ),
                lax.dot_general(inner_in, grad_both, contract, preferred_element_type=jnp.float32),
            ],
            axis=1,
        ).astype(jnp.bfloat16),
        "sp",
        scatter_dimension=0,
        tiled=True,
    )
    down_sums = lax.psum_scatter(
        lax.dot_general(hidden, grad_y, contract, preferred_element_type=jnp.float32).astype(
            jnp.bfloat16
        ),
        "sp",
        scatter_dimension=0,
        tiled=True,
    )
    weight_rows, down_rows = (
        lax.psum(row_sums, "dp").astype(jnp.float32),
        lax.psum(down_sums, "dp").astype(jnp.float32),
    )
    qkv_cols = model_dim + 2 * kv_width
    grad_w_qkv = weight_rows[:, :qkv_cols]
    grad_w_out = weight_rows[:, qkv_cols : qkv_cols + model_dim]
    grad_w_gate_up = weight_rows[:, qkv_cols + model_dim :]
    return (
        output,
        grad_tokens,
        grad_w_qkv,
        grad_w_out,
        grad_w_gate_up,
        down_rows,
        grad_g_attn,
        grad_g_mlp,
    )


CHIPS = 4
BLOCK = 512
SHORT = pl.CostEstimate(flops=1, bytes_accessed=1, transcendentals=0)
LOG2E = math.log2(math.e)
BF = jnp.bfloat16
F32 = jnp.float32
NT = (((1,), (1,)), ((), ()))
TN = (((0,), (0,)), ((), ()))


def swap_pairs(even_mask, odd_mask):
    return [(i, i ^ (odd_mask if i & 1 else even_mask)) for i in range(2 * CHIPS)]


FIRST = swap_pairs(2, 4)
SECOND = swap_pairs(4, 2)
SIBLING = swap_pairs(1, 1)
SAME_CORE = [[0, 2, 4, 6], [1, 3, 5, 7]]


def send_first(x):
    return lax.ppermute(x, "sp", FIRST)


def send_second(x):
    return lax.ppermute(x, "sp", SECOND)


def send_sibling(x):
    return lax.ppermute(x, "sp", SIBLING)


def after(value, *others):
    return lax.optimization_barrier((value,) + others)[0]


def gather_chips(own):
    first = send_first(own)
    second = send_second(after(own, first))
    far = send_second(after(first, second))
    return [own, first, second, far]


def rel_masks(core):
    first = jnp.where(core == 0, 2, 4)
    return first, 6 - first


def fence(*values):
    return lax.optimization_barrier(values)


def gather_vectors(own, me):
    for bit in (1, 2, 4):
        got = lax.ppermute(own, "sp", swap_pairs(bit, bit))
        high = (me & bit) != 0
        own = jnp.concatenate([jnp.where(high, got, own), jnp.where(high, own, got)], axis=1)
    return own


def pick(parts, index):
    return lax.dynamic_index_in_dim(parts, index, 0, keepdims=False)


def pick_sum(parts, index, axis):
    return sum(lax.dynamic_index_in_dim(p, index, axis, keepdims=False).astype(F32) for p in parts)


def line_scatter_sends(parts, got, step, axis):
    planes = parts[0].shape[axis]
    z = lax.axis_index("dp")
    ahead = pick_sum(parts, jnp.clip(planes - step + z, 0, planes - 1), axis)
    back = pick_sum(parts, jnp.clip(z - planes + step, 0, planes - 1), axis)
    if got is not None:
        ahead = ahead + got[0].astype(F32)
        back = back + got[1].astype(F32)
    return ahead.astype(BF), back.astype(BF)


def line_scatter_move(sends, step):
    planes = lax.axis_size("dp")
    right = lax.ppermute(sends[0], "dp", [(i, i + 1) for i in range(step)])
    left = lax.ppermute(sends[1], "dp", [(planes - 1 - i, planes - 2 - i) for i in range(step)])
    return right, left


def line_scatter_end(parts, got, axis):
    own = pick_sum(parts, lax.axis_index("dp"), axis)
    return (own + got[0].astype(F32) + got[1].astype(F32)).astype(BF)


def line_gather_move(got, step):
    planes = lax.axis_size("dp")
    right = lax.ppermute(got[0], "dp", [(i, i + 1) for i in range(step - 1, planes - 1)])
    left = lax.ppermute(got[1], "dp", [(i + 1, i) for i in range(planes - step)])
    return right, left


def line_values(refs, planes, z):
    for step in range(planes):
        place = lax.rem(z - step + planes, planes)
        if step == 0:
            yield place, lambda index: refs[0][index]
        else:
            right, left = refs[step], refs[2 * planes - 1 - step]
            yield place, lambda index, right=right, left=left, step=step: jnp.where(z >= step, right[index], left[index])


def spread_kernel(in_ref, w_ref, g_ref, out_ref, gain_ref):
    planes, _, rows, width = in_ref.shape
    out = in_ref[...].reshape(planes * rows, width).astype(F32)
    out_ref[...] = out
    part = jnp.sum(out * w_ref[...].astype(F32), axis=-1, keepdims=True) / g_ref[...]

    @pl.when(pl.program_id(0) == 0)
    def _():
        gain_ref[...] = part

    @pl.when(pl.program_id(0) > 0)
    def _():
        gain_ref[...] += part


def spread(parts, weight, gain):
    planes, chips, rows, both = parts.shape
    half = both // 2
    total = planes * rows
    line = pl.BlockSpec((total, half), lambda i: (0, i))
    column = pl.BlockSpec((total, 1), lambda i: (0, 0))
    return pl.pallas_call(
        spread_kernel,
        grid=(2 * chips,),
        in_specs=[pl.BlockSpec((planes, 1, rows, half), lambda i: (0, i % chips, 0, i // chips)), line, column],
        out_specs=[line, column],
        out_shape=[jax.ShapeDtypeStruct(weight.shape, F32), jax.ShapeDtypeStruct((total, 1), F32)],
        compiler_params=pltpu.CompilerParams(vmem_limit_bytes=32 * 2**20),
        cost_estimate=SHORT,
        name="spread",
    )(parts, weight, gain)


def spread_last_kernel(z_ref, *refs, planes):
    blocks, (w_ref, g_ref, out_ref, gain_ref, wo_ref) = refs[:-5], refs[-5:]
    rows = blocks[0].shape[0]
    devices = 2 * CHIPS
    width = wo_ref.shape[1]
    heads = width // devices
    each = heads + 2 * HD
    for place, load in line_values(blocks, planes, z_ref[0]):
        span = pl.ds(pl.multiple_of(place * rows, rows), rows)
        pairs = []
        for d in range(devices):
            begin = d * each
            cols = slice(begin, begin + heads)
            out_ref[span, d * heads : (d + 1) * heads] = load((slice(None), cols)).astype(F32)
            pairs.append(load((slice(None), slice(begin + heads, begin + each))).astype(F32))
        for g in range(0, KV, 2):
            low = pairs[2 * g] + pairs[2 * g + 1]
            high = pairs[2 * g + 2] + pairs[2 * g + 3]
            lane = lax.broadcasted_iota(jnp.int32, low.shape, 1)
            begin = width + g * HD
            out_ref[span, begin : begin + 2 * HD] = jnp.where(lane < HD, low, pltpu.roll(high, HD, 1))
            begin = width + (KV + g) * HD
            out_ref[span, begin : begin + 2 * HD] = jnp.where(lane < HD, pltpu.roll(low, HD, 1), high)
        wo_ref[span, :] = load((slice(None), slice(devices * each, devices * each + width))).astype(F32)
    gain_ref[...] = jnp.sum(out_ref[...] * w_ref[...].astype(F32), axis=-1, keepdims=True) / g_ref[...]


def spread_last(steps, weight, gain, width):
    planes = len(steps)
    blocks = [steps[0][0]] + [s[0] for s in steps[1:]] + [s[1] for s in steps[1:]]
    vmem = pl.BlockSpec(memory_space=pltpu.VMEM)
    total = weight.shape[0]
    return pl.pallas_call(
        functools.partial(spread_last_kernel, planes=planes),
        in_specs=[pl.BlockSpec(memory_space=pltpu.SMEM)] + [vmem] * (len(blocks) + 2),
        out_specs=[vmem] * 3,
        out_shape=[
            jax.ShapeDtypeStruct(weight.shape, F32),
            jax.ShapeDtypeStruct((total, 1), F32),
            jax.ShapeDtypeStruct((total, width), F32),
        ],
        compiler_params=pltpu.CompilerParams(vmem_limit_bytes=32 * 2**20),
        cost_estimate=SHORT,
        name="spread_last",
    )(lax.axis_index("dp").reshape(1), *blocks, weight, gain)


def join_kernel(core_ref, mine_ref, theirs_ref, out_ref):
    planes, _, rows, both = mine_ref.shape
    block = jnp.where(pl.program_id(1) == 0, mine_ref[...], theirs_ref[...]).reshape(planes * rows, both)
    out_ref[0, 0, 0] = block[:, : both // 2]
    out_ref[1, 0, 0] = block[:, both // 2 :]


def join(core, mine, theirs):
    planes, chips, rows, both = mine.shape
    spec = pl.BlockSpec((planes, 1, rows, both), lambda c, k, core: (0, c, 0, 0))
    out = pl.pallas_call(
        join_kernel,
        grid_spec=pltpu.PrefetchScalarGridSpec(
            num_scalar_prefetch=1,
            grid=(chips, 2),
            in_specs=[spec, spec],
            out_specs=pl.BlockSpec(
                (2, 1, 1, planes * rows, both // 2), lambda c, k, core: (0, c, (core[0] + k) % 2, 0, 0)
            ),
        ),
        out_shape=jax.ShapeDtypeStruct((2, chips, 2, planes * rows, both // 2), BF),
        compiler_params=pltpu.CompilerParams(vmem_limit_bytes=32 * 2**20),
        cost_estimate=SHORT,
        name="join",
    )(core.reshape(1), mine, theirs)
    return out.reshape(2, 2 * chips * planes * rows, both // 2)


def ffn_kernel(*refs, cuts):
    b_hbm, dy_hbm, wgu_hbm, wd_hbm, hid_hbm, dg_hbm, du_hbm, db_hbm, y_hbm = refs[:9]
    b_ref, dy_ref, wg_ref, wu_ref, wd_ref, hid_ref, dg_ref, du_ref, db_ref, y_ref, sems = refs[9:]
    count = len(cuts) - 1

    def move(source, target, index):
        copy = pltpu.make_async_copy(source, target, sems.at[index])
        copy.start()
        return copy

    b_copy = move(b_hbm, b_ref, 3 * count)
    weights = []
    for c in range(count):
        span = slice(cuts[c], cuts[c + 1])
        gate_copy = move(wgu_hbm.at[0, :, span], wg_ref.at[:, span], 3 * c)
        up_copy = move(wgu_hbm.at[1, :, span], wu_ref.at[:, span], 3 * c + 1)
        weights.append([gate_copy, up_copy])
        if c == 0:
            dy_copy = move(dy_hbm, dy_ref, 3 * count + 1)
        weights[-1].append(move(wd_hbm.at[span, :], wd_ref.at[span, :], 3 * c + 2))
    b_copy.wait()
    for c in range(count):
        span = slice(cuts[c], cuts[c + 1])
        for copy in weights[c][:2]:
            copy.wait()
        gate = jnp.dot(b_ref[...], wg_ref[:, span], preferred_element_type=F32)
        up = jnp.dot(b_ref[...], wu_ref[:, span], preferred_element_type=F32)
        if c == 0:
            dy_copy.wait()
        weights[c][2].wait()
        d_hidden = lax.dot_general(dy_ref[...], wd_ref[span, :], NT, preferred_element_type=F32)
        sigmoid_g = jax.nn.sigmoid(gate)
        silu_gate = gate * sigmoid_g
        hid_ref[:, span] = (silu_gate * up).astype(BF)
        dg_ref[:, span] = (d_hidden * up * (sigmoid_g * (1.0 + gate * (1.0 - sigmoid_g)))).astype(BF)
        du_ref[:, span] = (d_hidden * silu_gate).astype(BF)
    base = 3 * count + 2
    outs = [move(hid_ref, hid_hbm, base), move(dg_ref, dg_hbm, base + 1), move(du_ref, du_hbm, base + 2)]
    y_ref[...] = jnp.dot(hid_ref[...], wd_ref[...], preferred_element_type=F32).astype(BF)
    outs.append(move(y_ref, y_hbm, base + 3))
    d_in = lax.dot_general(dg_ref[...], wg_ref[...], NT, preferred_element_type=F32)
    db_ref[...] = (d_in + lax.dot_general(du_ref[...], wu_ref[...], NT, preferred_element_type=F32)).astype(BF)
    outs.append(move(db_ref, db_hbm, base + 4))
    for copy in outs:
        copy.wait()


def ffn(b_rows, dy_rows, w_gu, w_dn):
    rows, width = b_rows.shape
    hidden = w_dn.shape[0]
    pieces = 3
    cuts = tuple(round(hidden * c / pieces / 128) * 128 for c in range(pieces)) + (hidden,)
    hbm = pl.BlockSpec(memory_space=pl.ANY)
    return pl.pallas_call(
        functools.partial(ffn_kernel, cuts=cuts),
        in_specs=[hbm] * 4,
        out_specs=[hbm] * 5,
        out_shape=[jax.ShapeDtypeStruct((rows, hidden), BF)] * 3 + [jax.ShapeDtypeStruct((rows, width), BF)] * 2,
        scratch_shapes=[pltpu.VMEM((rows, width), BF)] * 2
        + [pltpu.VMEM((width, hidden), BF)] * 2
        + [pltpu.VMEM((hidden, width), BF)]
        + [pltpu.VMEM((rows, hidden), BF)] * 3
        + [pltpu.VMEM((rows, width), BF)] * 2
        + [pltpu.SemaphoreType.DMA((3 * pieces + 7,))],
        compiler_params=pltpu.CompilerParams(vmem_limit_bytes=58 * 2**20),
        cost_estimate=SHORT,
        name="ffn",
    )(b_rows, dy_rows, w_gu, w_dn)


def grad_gu_kernel(core_ref, *refs, count):
    left, right = refs[: 2 * count], refs[2 * count : 4 * count]
    half = right[0].shape[1]
    for side in range(2):
        for kind in range(2):
            total = None
            for r in range(count):
                a_rows = left[side * count + r][...]
                part = lax.dot_general(a_rows, right[kind * count + r][...], TN, preferred_element_type=F32)
                total = part if total is None else total + part
            out_ref = refs[4 * count + side]
            planes, _, rows, _ = out_ref.shape
            out_ref[:, 0, :, kind * half : (kind + 1) * half] = total.astype(BF).reshape(planes, rows, half)


def grad_gu(core, b_rows, dg_rows, du_rows, share, planes):
    count = len(b_rows)
    tokens, width = b_rows[0].shape
    hidden = dg_rows[0].shape[1]
    keep = pl.BlockSpec((tokens, share), lambda c, core: (0, 2 * c + core[0]))
    give = pl.BlockSpec((tokens, share), lambda c, core: (0, 2 * c + 1 - core[0]))
    whole = pl.BlockSpec((tokens, hidden), lambda c, core: (0, 0))
    rows = share // planes
    out = pl.BlockSpec((planes, 1, rows, 2 * hidden), lambda c, core: (0, c, 0, 0))
    return pl.pallas_call(
        functools.partial(grad_gu_kernel, count=count),
        grid_spec=pltpu.PrefetchScalarGridSpec(
            num_scalar_prefetch=1,
            grid=(width // (2 * share),),
            in_specs=[keep] * count + [give] * count + [whole] * (2 * count),
            out_specs=[out, out],
        ),
        out_shape=[jax.ShapeDtypeStruct((planes, width // (2 * share), rows, 2 * hidden), BF)] * 2,
        compiler_params=pltpu.CompilerParams(vmem_limit_bytes=58 * 2**20),
        cost_estimate=SHORT,
        name="grad_gu",
    )(core.reshape(1), *b_rows, *b_rows, *dg_rows, *du_rows)


def grad_qkv_kernel(place_ref, *refs, count):
    dp_ref, out_ref = refs[-2:]
    total = None
    for r in range(count):
        part = lax.dot_general(refs[r][...], dp_ref[place_ref[r]], TN, preferred_element_type=F32)
        total = part if total is None else total + part
    planes, rows, wide = out_ref.shape
    columns = total.shape[1]
    for k in range(wide // columns):
        block = total[k * planes * rows : (k + 1) * planes * rows].astype(BF)
        out_ref[:, :, k * columns : (k + 1) * columns] = block.reshape(planes, rows, columns)


def grad_qkv(places, a_rows, dp_heads, planes):
    count = len(a_rows)
    tokens, width = a_rows[0].shape
    columns = dp_heads.shape[2]
    share = width // count
    depth = 2 * share
    return pl.pallas_call(
        functools.partial(grad_qkv_kernel, count=count),
        grid_spec=pltpu.PrefetchScalarGridSpec(
            num_scalar_prefetch=1,
            grid=(width // depth,),
            in_specs=[pl.BlockSpec((tokens, depth), lambda i, p: (0, i))] * count
            + [pl.BlockSpec(dp_heads.shape, lambda i, p: (0, 0, 0))],
            out_specs=pl.BlockSpec((planes, share // planes, 2 * columns), lambda i, p: (0, 0, i)),
        ),
        out_shape=jax.ShapeDtypeStruct((planes, share // planes, count * columns), BF),
        compiler_params=pltpu.CompilerParams(vmem_limit_bytes=48 * 2**20),
        cost_estimate=SHORT,
        name="grad_qkv",
    )(places, *a_rows, dp_heads)


def swap_halves(values):
    width = values.shape[-1]
    lane = lax.broadcasted_iota(jnp.int32, values.shape, 1)
    ahead = pltpu.roll(values, width - HD // 2, 1)
    behind = pltpu.roll(values, HD // 2, 1)
    return jnp.where(lane % HD < HD // 2, ahead, behind)


def project_kernel(place_ref, x_ref, gain_ref, cos_ref, sin_ref, *refs, count):
    wq_refs, wkv_refs = refs[:count], refs[count : 2 * count]
    send_ref, normed_ref, inv_ref, normed_scr = refs[2 * count :]
    share = normed_scr.shape[2]

    @pl.when(pl.program_id(0) == 0)
    def _():
        x = x_ref[...].astype(F32)
        inv = lax.rsqrt(jnp.mean(x * x, axis=-1, keepdims=True) + EPSILON)
        normed = (x * inv * gain_ref[...]).astype(BF)
        normed_ref[...] = normed
        inv_ref[...] = inv
        for part in range(count):
            normed_scr[part] = normed[:, part * share : (part + 1) * share]

    pq = pkv = None
    for r in range(count):
        a_rows = normed_scr[place_ref[r]]
        q_part = jnp.dot(a_rows, wq_refs[r][...], preferred_element_type=F32)
        kv_part = jnp.dot(a_rows, wkv_refs[r][...], preferred_element_type=F32)
        pq = q_part if pq is None else pq + q_part
        pkv = kv_part if pkv is None else pkv + kv_part
    cos = cos_ref[...]
    sin = sin_ref[...]
    heads = pq.shape[1]
    q_scale = LOG2E * HD**-0.5
    turned = pq * jnp.tile(cos, (1, heads // 128)) + swap_halves(pq) * jnp.tile(sin, (1, heads // 128))
    send_ref[0, :, :heads] = (turned * q_scale).astype(BF)
    lane = lax.broadcasted_iota(jnp.int32, pkv.shape, 1)
    turned_kv = jnp.where(lane < HD, pkv * cos + swap_halves(pkv) * sin, pkv)
    send_ref[0, :, heads:] = turned_kv.astype(BF)


def project(places, x, gain, cos, sin, parts):
    rows, width = x.shape
    count = len(parts)
    heads = width // count
    out_width = heads + 2 * HD
    depth = parts[0].shape[0]
    first_kv = width // (2 * HD)
    return pl.pallas_call(
        functools.partial(project_kernel, count=count),
        grid_spec=pltpu.PrefetchScalarGridSpec(
            num_scalar_prefetch=1,
            grid=(count,),
            in_specs=[
                pl.BlockSpec((rows, width), lambda d, p: (0, 0)),
                pl.BlockSpec((1, width), lambda d, p: (0, 0)),
                pl.BlockSpec((rows, 128), lambda d, p: (0, 0)),
                pl.BlockSpec((rows, 128), lambda d, p: (0, 0)),
            ]
            + [pl.BlockSpec((depth, heads), lambda d, p: (0, d))] * count
            + [pl.BlockSpec((depth, 2 * HD), lambda d, p: (0, first_kv + d // 2))] * count,
            out_specs=[
                pl.BlockSpec((1, rows, out_width), lambda d, p: (d, 0, 0)),
                pl.BlockSpec((rows, width), lambda d, p: (0, 0)),
                pl.BlockSpec((rows, 1), lambda d, p: (0, 0)),
            ],
            scratch_shapes=[pltpu.VMEM((count, rows, width // count), BF)],
        ),
        out_shape=[
            jax.ShapeDtypeStruct((count, rows, out_width), BF),
            jax.ShapeDtypeStruct((rows, width), BF),
            jax.ShapeDtypeStruct((rows, 1), F32),
        ],
        compiler_params=pltpu.CompilerParams(vmem_limit_bytes=48 * 2**20),
        cost_estimate=SHORT,
        name="project",
    )(places, x, gain, cos, sin, *parts, *parts)


def out_proj_kernel(place_ref, attn_ref, x_ref, gain_ref, *refs, count):
    parts, (resid_ref, inv_ref, inner_ref) = refs[:count], refs[count:]
    width = x_ref.shape[1]
    tile = 512
    square = None
    for begin in range(0, width, tile):
        cols = slice(begin, begin + tile)
        total = x_ref[:, cols].astype(F32)
        for r in range(count):
            total = total + jnp.dot(attn_ref[place_ref[r]], parts[r][:, cols], preferred_element_type=F32)
        resid_ref[:, cols] = total
        part = jnp.sum(total * total, axis=-1, keepdims=True)
        square = part if square is None else square + part
    inv = lax.rsqrt(square / width + EPSILON)
    inv_ref[...] = inv
    inner_ref[...] = (resid_ref[...] * inv * gain_ref[...]).astype(BF)


def out_proj(places, attn, x, gain, parts):
    count, rows, share = attn.shape
    width = x.shape[1]
    step = rows // 2
    line = pl.BlockSpec((step, width), lambda i, p: (i, 0))
    return pl.pallas_call(
        functools.partial(out_proj_kernel, count=count),
        grid_spec=pltpu.PrefetchScalarGridSpec(
            num_scalar_prefetch=1,
            grid=(rows // step,),
            in_specs=[
                pl.BlockSpec((count, step, share), lambda i, p: (0, i, 0)),
                line,
                pl.BlockSpec((1, width), lambda i, p: (0, 0)),
            ]
            + [pl.BlockSpec((share, width), lambda i, p: (0, 0))] * count,
            out_specs=[line, pl.BlockSpec((step, 1), lambda i, p: (i, 0)), line],
        ),
        out_shape=[
            jax.ShapeDtypeStruct((rows, width), F32),
            jax.ShapeDtypeStruct((rows, 1), F32),
            jax.ShapeDtypeStruct((rows, width), BF),
        ],
        compiler_params=pltpu.CompilerParams(vmem_limit_bytes=56 * 2**20),
        cost_estimate=SHORT,
        name="out_proj",
    )(places, attn, x, gain, *parts)


def resid_back_kernel(place_ref, db_ref, first_ref, passed_ref, resid_ref, inv_ref, gain_ref, dy_ref, *refs, count):
    parts, (d_resid_ref, branch_ref, send_ref) = refs[:count], refs[count:]
    d_inner = db_ref[...].astype(F32) + first_ref[...].astype(F32) + passed_ref[...].astype(F32)
    resid = resid_ref[...]
    inv = inv_ref[...]
    scaled = d_inner * gain_ref[...]
    inner_mean = jnp.mean(scaled * resid, axis=-1, keepdims=True)
    d_resid = dy_ref[...].astype(F32) + inv * scaled - resid * (inv * inv * inv * inner_mean)
    d_resid_ref[...] = d_resid
    branch = d_resid.astype(BF)
    branch_ref[...] = branch
    for r in range(count):
        d_attn = lax.dot_general(branch, parts[r][...], NT, preferred_element_type=F32)
        send_ref[place_ref[r]] = d_attn.astype(BF)


def resid_back(places, db_own, db_first, db_passed, resid, inv, gain, dy, parts):
    rows, width = resid.shape
    count = len(parts)
    share = parts[0].shape[0]
    step = rows // 2
    line = pl.BlockSpec((step, width), lambda i, p: (i, 0))
    return pl.pallas_call(
        functools.partial(resid_back_kernel, count=count),
        grid_spec=pltpu.PrefetchScalarGridSpec(
            num_scalar_prefetch=1,
            grid=(rows // step,),
            in_specs=[line, line, line, line]
            + [pl.BlockSpec((step, 1), lambda i, p: (i, 0)), pl.BlockSpec((1, width), lambda i, p: (0, 0)), line]
            + [pl.BlockSpec((share, width), lambda i, p: (0, 0))] * count,
            out_specs=[line, line, pl.BlockSpec((count, step, share), lambda i, p: (0, i, 0))],
        ),
        out_shape=[
            jax.ShapeDtypeStruct((rows, width), F32),
            jax.ShapeDtypeStruct((rows, width), BF),
            jax.ShapeDtypeStruct((count, rows, share), BF),
        ],
        compiler_params=pltpu.CompilerParams(vmem_limit_bytes=56 * 2**20),
        cost_estimate=SHORT,
        name="resid_back",
    )(places, db_own, db_first, db_passed, resid, inv, gain, dy, *parts)


def in_back_kernel(place_ref, back_ref, x_ref, inv_ref, gain_ref, d_resid_ref, *refs, count):
    parts, (out_ref, mixed, d_scr) = refs[:count], refs[count:]
    devices, _, width = back_ref.shape
    heads = width - 2 * HD
    for d in range(devices):
        mixed[:, d * heads : (d + 1) * heads] = back_ref[d, :, :heads]
    base = devices * heads
    for g in range(KV):
        pair = back_ref[2 * g, :, heads:].astype(F32) + back_ref[2 * g + 1, :, heads:].astype(F32)
        mixed[:, base + 2 * g * HD : base + 2 * (g + 1) * HD] = pair.astype(BF)
    for r in range(count):
        d_scr[place_ref[r]] = lax.dot_general(mixed[...], parts[r][...], NT, preferred_element_type=F32)
    inv = inv_ref[...]
    share = d_scr.shape[2]
    inner = None
    for c in range(count):
        cols = slice(c * share, (c + 1) * share)
        part = jnp.sum(d_scr[c] * gain_ref[:, cols] * x_ref[:, cols].astype(F32), axis=-1, keepdims=True)
        inner = part if inner is None else inner + part
    factor = inv * inv * inv * (inner / (count * share))
    for c in range(count):
        cols = slice(c * share, (c + 1) * share)
        through = inv * (d_scr[c] * gain_ref[:, cols]) - x_ref[:, cols].astype(F32) * factor
        out_ref[:, cols] = (d_resid_ref[:, cols] + through).astype(BF)


def in_back(places, back, x, inv, gain, d_resid, parts):
    rows, width = x.shape
    count = len(parts)
    share, columns = parts[0].shape
    step = rows // 2
    line = pl.BlockSpec((step, width), lambda i, p: (i, 0))
    return pl.pallas_call(
        functools.partial(in_back_kernel, count=count),
        grid_spec=pltpu.PrefetchScalarGridSpec(
            num_scalar_prefetch=1,
            grid=(rows // step,),
            in_specs=[
                pl.BlockSpec((count, step, back.shape[2]), lambda i, p: (0, i, 0)),
                line,
                pl.BlockSpec((step, 1), lambda i, p: (i, 0)),
                pl.BlockSpec((1, width), lambda i, p: (0, 0)),
                line,
            ]
            + [pl.BlockSpec((share, columns), lambda i, p: (0, 0))] * count,
            out_specs=line,
            scratch_shapes=[pltpu.VMEM((step, columns), BF), pltpu.VMEM((count, step, share), F32)],
        ),
        out_shape=jax.ShapeDtypeStruct((rows, width), BF),
        compiler_params=pltpu.CompilerParams(vmem_limit_bytes=56 * 2**20),
        cost_estimate=SHORT,
        name="in_back",
    )(places, back, x, inv, gain, d_resid, *parts)


def grad_wo_kernel(core_ref, keep_ref, give_ref, branch_ref, keep_out, give_out):
    branch = branch_ref[...]
    keep_out[0] = lax.dot_general(keep_ref[0], branch, TN, preferred_element_type=F32).astype(BF)
    give_out[0] = lax.dot_general(give_ref[0], branch, TN, preferred_element_type=F32).astype(BF)


def grad_wo(core, attn, branch):
    devices, rows, share = attn.shape
    width = branch.shape[1]
    out = pl.BlockSpec((1, share, width), lambda c, core: (c, 0, 0))
    return pl.pallas_call(
        grad_wo_kernel,
        grid_spec=pltpu.PrefetchScalarGridSpec(
            num_scalar_prefetch=1,
            grid=(devices // 2,),
            in_specs=[
                pl.BlockSpec((1, rows, share), lambda c, core: (2 * c + core[0], 0, 0)),
                pl.BlockSpec((1, rows, share), lambda c, core: (2 * c + 1 - core[0], 0, 0)),
                pl.BlockSpec((rows, width), lambda c, core: (0, 0)),
            ],
            out_specs=[out, out],
        ),
        out_shape=[jax.ShapeDtypeStruct((devices // 2, share, width), BF)] * 2,
        compiler_params=pltpu.CompilerParams(vmem_limit_bytes=48 * 2**20),
        cost_estimate=SHORT,
        name="grad_wo",
    )(core.reshape(1), attn, attn, branch)


def grad_dn_kernel(core_ref, *refs, count):
    left, right, (keep_out, give_out) = refs[:count], refs[count : 2 * count], refs[2 * count :]
    total = None
    for r in range(count):
        part = lax.dot_general(left[r][...], right[r][...], TN, preferred_element_type=F32)
        total = part if total is None else total + part
    half = total.shape[0] // 2
    total = total.astype(BF)
    low = core_ref[0] == 0
    keep_out[...] = jnp.where(low, total[:half], total[half:])
    give_out[...] = jnp.where(low, total[half:], total[:half])


def grad_dn(core, hid_rows, dy_rows):
    count = len(hid_rows)
    tokens, hidden = hid_rows[0].shape
    width = dy_rows[0].shape[1]
    tile = 512
    out = pl.BlockSpec((hidden // 2, tile), lambda i, core: (0, i))
    return pl.pallas_call(
        functools.partial(grad_dn_kernel, count=count),
        grid_spec=pltpu.PrefetchScalarGridSpec(
            num_scalar_prefetch=1,
            grid=(width // tile,),
            in_specs=[pl.BlockSpec((tokens, hidden), lambda i, core: (0, 0))] * count
            + [pl.BlockSpec((tokens, tile), lambda i, core: (0, i))] * count,
            out_specs=[out, out],
        ),
        out_shape=[jax.ShapeDtypeStruct((hidden // 2, width), BF)] * 2,
        compiler_params=pltpu.CompilerParams(vmem_limit_bytes=56 * 2**20),
        cost_estimate=SHORT,
        name="grad_dn",
    )(core.reshape(1), *hid_rows, *dy_rows)


def attend_kernel(zeros_ref, q_ref, kv_ref, *refs, heads, start, stop):
    o_ref, send_ref, lse_ref, k_scr, v_scr, acc_ref, max_ref = refs[-7:]
    block = pl.program_id(0) + start
    zeros = zeros_ref[0]
    size = q_ref.shape[0]

    @pl.when(block == start)
    def _():
        for part in range(stop):
            rows = slice(part * size, (part + 1) * size)
            both = kv_ref[rows, :].astype(F32)
            lane = lax.broadcasted_iota(jnp.int32, both.shape, 1)
            k_scr[rows, :] = kv_ref[rows, :HD]
            v_scr[rows, :] = jnp.where(lane < HD, pltpu.roll(both, HD, 1), 1.0).astype(BF)

    first_row = block * size
    lowest = jnp.where(first_row >= zeros, zeros // size, 0)
    acc_ref[...] = jnp.zeros_like(acc_ref)
    max_ref[...] = jnp.full_like(max_ref, MASKED)
    q_heads = [q_ref[:, h * HD : (h + 1) * HD] for h in range(heads)]

    def step(index, masked):
        first_key = pl.multiple_of(index * size, size)
        keys = k_scr[pl.ds(first_key, size), :]
        values = v_scr[pl.ds(first_key, size), :]
        if masked:
            row = first_row + lax.broadcasted_iota(jnp.int32, (size, size), 0)
            col = first_key + lax.broadcasted_iota(jnp.int32, (size, size), 1)
            begin = jnp.where(row >= zeros, zeros, 0)
            refused = (col > row) | (col < begin)

        def score(h):
            return lax.dot_general(q_heads[h], keys, NT, preferred_element_type=F32)

        upcoming = score(0)
        for h in range(heads):
            scores = upcoming
            if h + 1 < heads:
                upcoming = score(h + 1)
            if masked:
                scores = jnp.where(refused, MASKED, scores)
            old_max = max_ref[h]
            new_max = jnp.maximum(old_max, jnp.max(scores, axis=-1, keepdims=True))
            weights = jnp.exp2(scores - jnp.tile(new_max, (1, size // 128)))
            shrink = jnp.exp2(old_max - new_max)
            acc_ref[h] = acc_ref[h] * shrink + jnp.dot(weights.astype(BF), values, preferred_element_type=F32)
            max_ref[h] = new_max

    def visit(index, carry):
        first_key = index * size
        mixed = (index == block) | ((first_row + size > zeros) & (first_key < zeros))

        @pl.when(mixed)
        def _():
            step(index, True)

        @pl.when(jnp.logical_not(mixed))
        def _():
            step(index, False)

        return carry

    lax.fori_loop(lowest, block + 1, visit, 0)
    for h in range(heads):
        acc = acc_ref[h]
        total = acc[:, HD : HD + 1]
        out = acc[:, :HD] / total
        o_ref[:, h * HD : (h + 1) * HD] = out
        send_ref[0, :, h * HD : (h + 1) * HD] = out.astype(BF)
        lse = max_ref[h] + jnp.log2(total)
        lse_ref[0, h : h + 1, :] = jnp.transpose(lse)[:1]


def attend(zeros, qkv, start, stop, before=None):
    length, width = qkv.shape
    q_width = width - 2 * HD
    heads = q_width // HD
    size = BLOCK
    blocks = length // size
    before = () if before is None else before
    return pl.pallas_call(
        functools.partial(attend_kernel, heads=heads, start=start, stop=stop),
        grid_spec=pltpu.PrefetchScalarGridSpec(
            num_scalar_prefetch=1,
            grid=(stop - start,),
            in_specs=[
                pl.BlockSpec((size, q_width), lambda i, z: (i + start, 0)),
                pl.BlockSpec((length, 2 * HD), lambda i, z: (0, q_width // (2 * HD))),
            ]
            + [pl.BlockSpec(memory_space=pl.ANY)] * len(before),
            out_specs=[
                pl.BlockSpec((size, q_width), lambda i, z: (i + start, 0)),
                pl.BlockSpec((1, size, q_width), lambda i, z: (i + start, 0, 0)),
                pl.BlockSpec((1, heads, size), lambda i, z: (i + start, 0, 0)),
            ],
            scratch_shapes=[
                pltpu.VMEM((length, HD), BF),
                pltpu.VMEM((length, 2 * HD), BF),
                pltpu.VMEM((heads, size, 2 * HD), F32),
                pltpu.VMEM((heads, size, 128), F32),
            ],
        ),
        out_shape=[
            jax.ShapeDtypeStruct((length, q_width), F32),
            jax.ShapeDtypeStruct((blocks, size, q_width), BF),
            jax.ShapeDtypeStruct((blocks, heads, size), F32),
        ],
        input_output_aliases={3 + i: i for i in range(len(before))},
        compiler_params=pltpu.CompilerParams(vmem_limit_bytes=48 * 2**20),
        cost_estimate=SHORT,
        name="attend",
    )(zeros, qkv, qkv, *before)


def attend_back_kernel(
    zeros_ref, q_ref, kv_ref, do_ref, lse_ref, cos_ref, sin_ref, extra_ref, *refs, heads, start
):
    send_ref, dq_acc, delta_ref, q_scr, do_scr = refs[-5:]
    block = pl.program_id(0) + start
    zeros = zeros_ref[0]
    size = kv_ref.shape[0]
    length = q_ref.shape[0]
    blocks = length // size

    @pl.when(block == start)
    def _():
        if start == 0:
            dq_acc[...] = jnp.zeros_like(dq_acc)
        else:
            dq_acc[...] = refs[0][...]
            delta_ref[...] = extra_ref[...]
        for part in range(start, blocks):
            rows = slice(part * size, (part + 1) * size)
            if start == 0:
                product = jnp.transpose(do_ref[rows, :].astype(F32) * extra_ref[rows, :])
            for h in range(heads):
                cols = slice(h * HD, (h + 1) * HD)
                q_scr[h, rows, :] = q_ref[rows, cols]
                do_scr[h, rows, :] = do_ref[rows, cols]
                if start == 0:
                    delta_ref[part, h : h + 1, :] = jnp.sum(product[cols], axis=0, keepdims=True)

    first_key = block * size
    both = kv_ref[...]
    keys = both[:, :HD]
    values = both[:, HD:]
    keys_t = jnp.transpose(keys.astype(F32)).astype(BF)
    highest = jnp.where(first_key + size <= zeros, jnp.minimum((zeros + size - 1) // size, blocks), blocks)

    def step(index, carry, masked):
        first_row = pl.multiple_of(index * size, size)
        span = pl.ds(first_row, size)
        if masked:
            col = first_key + lax.broadcasted_iota(jnp.int32, (size, size), 0)
            row = first_row + lax.broadcasted_iota(jnp.int32, (size, size), 1)
            begin = jnp.where(row >= zeros, zeros, 0)
            refused = (col > row) | (col < begin)

        def products(h):
            q_rows = q_scr[h, span, :]
            do_rows = do_scr[h, span, :]
            scores = lax.dot_general(keys, q_rows, NT, preferred_element_type=F32)
            d_prob = lax.dot_general(values, do_rows, NT, preferred_element_type=F32)
            return q_rows, do_rows, scores, d_prob

        upcoming = products(0)
        dk_sum, dv_sum = carry
        for h in range(heads):
            q_rows, do_rows, scores, d_prob = upcoming
            if h + 1 < heads:
                upcoming = products(h + 1)
            shifted = scores - lse_ref[index, h : h + 1, :]
            if masked:
                shifted = jnp.where(refused, MASKED, shifted)
            prob = jnp.exp2(shifted)
            d_score = (prob * (d_prob - delta_ref[index, h : h + 1, :])).astype(BF)
            dv_sum = dv_sum + jnp.dot(prob.astype(BF), do_rows, preferred_element_type=F32)
            dk_sum = dk_sum + jnp.dot(d_score, q_rows, preferred_element_type=F32)
            dq_acc[h * HD : (h + 1) * HD, span] += jnp.dot(keys_t, d_score, preferred_element_type=F32)
        return dk_sum, dv_sum

    def visit(index, carry):
        first_row = index * size
        mixed = (index == block) | ((first_row + size > zeros) & (first_key < zeros))
        return lax.cond(
            mixed,
            lambda c: step(index, c, True),
            lambda c: step(index, c, False),
            carry,
        )

    zero = jnp.zeros((size, HD), F32)
    dk_sum, dv_sum = lax.fori_loop(block, highest, visit, (zero, zero))
    q_width = heads * HD
    done = pl.ds(pl.multiple_of(first_key, size), size)
    cos = cos_ref[...]
    sin = sin_ref[...]
    dq = jnp.transpose(dq_acc[:, done]) * HD**-0.5
    dq = dq * jnp.tile(cos, (1, q_width // 128)) - swap_halves(dq) * jnp.tile(sin, (1, q_width // 128))
    send_ref[0, :, :q_width] = dq.astype(BF)
    dkv = jnp.concatenate([dk_sum * (1.0 / LOG2E), dv_sum], axis=1)
    lane = lax.broadcasted_iota(jnp.int32, dkv.shape, 1)
    send_ref[0, :, q_width:] = jnp.where(lane < HD, dkv * cos - swap_halves(dkv) * sin, dkv).astype(BF)


def attend_back(zeros, qkv, d_out, lse, cos, sin, start, stop, out=None, before=None):
    length, width = qkv.shape
    q_width = width - 2 * HD
    heads = q_width // HD
    size = BLOCK
    blocks = length // size
    whole = lambda *shape: pl.BlockSpec(shape, lambda j, z: (0,) * len(shape))
    if before is None:
        operands = (out,)
        specs = [whole(length, q_width)]
        aliases = {}
    else:
        send, d_query, delta = before
        operands = (delta, d_query, send)
        specs = [whole(blocks, heads, size), whole(q_width, length), pl.BlockSpec(memory_space=pl.ANY)]
        aliases = {9: 0}
    return pl.pallas_call(
        functools.partial(attend_back_kernel, heads=heads, start=start),
        grid_spec=pltpu.PrefetchScalarGridSpec(
            num_scalar_prefetch=1,
            grid=(stop - start,),
            in_specs=[
                whole(length, q_width),
                pl.BlockSpec((size, 2 * HD), lambda j, z: (j + start, q_width // (2 * HD))),
                whole(length, q_width),
                whole(blocks, heads, size),
                pl.BlockSpec((size, 128), lambda j, z: (j + start, 0)),
                pl.BlockSpec((size, 128), lambda j, z: (j + start, 0)),
            ]
            + specs,
            out_specs=[
                pl.BlockSpec((1, size, width), lambda j, z: (j + start, 0, 0)),
                whole(q_width, length),
                whole(blocks, heads, size),
            ],
            scratch_shapes=[
                pltpu.VMEM((heads, length, HD), BF),
                pltpu.VMEM((heads, length, HD), BF),
            ],
        ),
        out_shape=[
            jax.ShapeDtypeStruct((blocks, size, width), BF),
            jax.ShapeDtypeStruct((q_width, length), F32),
            jax.ShapeDtypeStruct((blocks, heads, size), F32),
        ],
        input_output_aliases=aliases,
        compiler_params=pltpu.CompilerParams(vmem_limit_bytes=58 * 2**20),
        cost_estimate=SHORT,
        name="attend_back",
    )(zeros, qkv, qkv, d_out, lse, cos, sin, *operands)


def turn_tables(positions):
    cosine, sine = rope_tables(positions, HD)
    return jnp.concatenate([cosine] * 4, axis=1), jnp.concatenate([-sine, sine, -sine, sine], axis=1)


def fast_body(tokens, segment_ids, selected, cotangent, w_qkv, w_out, w_gate_up, w_down, g_attn, g_mlp):
    _, rows, width = tokens.shape
    devices = 2 * CHIPS
    me = lax.axis_index("sp")
    core = me & 1
    planes = lax.axis_size("dp")
    share = width // devices
    kv_width = KV * HD
    first_mask, second_mask = rel_masks(core)
    other = me ^ 1
    chip = me // 2
    place_list = [me, me ^ first_mask, me ^ second_mask, me ^ 6]
    place_list += [other, other ^ second_mask, other ^ first_mask, other ^ 6]
    places = jnp.stack(place_list)
    hidden_chip = 2 * w_down.shape[0]
    quarter = share // planes
    plane = lax.axis_index("dp")
    length = devices * rows
    blocks = length // BLOCK

    count = jnp.sum((segment_ids == 0).astype(F32))
    vectors = jnp.stack([g_attn.astype(F32), g_mlp.astype(F32)] + [jnp.full((share,), count)] * 6)
    paired = [w_qkv[:, :width]]
    for head in range(KV):
        paired.append(w_qkv[:, width + head * HD : width + (head + 1) * HD])
        paired.append(w_qkv[:, width + kv_width + head * HD : width + kv_width + (head + 1) * HD])
    qkv_own = jnp.concatenate(paired, axis=1)
    gu_rows = lax.dynamic_slice_in_dim(w_gate_up, plane * quarter, quarter, 0)
    gu_send = []
    for place in range(CHIPS):
        for begin in (place * hidden_chip, (CHIPS + place) * hidden_chip):
            gu_send.append(gu_rows[:, begin : begin + hidden_chip])
    gu_send = jnp.stack([jnp.concatenate(gu_send[2 * c : 2 * c + 2], axis=1) for c in range(CHIPS)])
    vectors = gather_vectors(vectors, me)
    vectors, qkv_own, gu_send = fence(vectors, qkv_own, gu_send)
    qkv_first = send_first(qkv_own)
    attn_gain = vectors[0:1]
    mlp_gain = vectors[1:2]
    zeros = jnp.sum(vectors[2].reshape(devices, share)[:, 0]).astype(jnp.int32)
    zeros_one = zeros.reshape(1)
    local_pos = me * rows + jnp.arange(rows, dtype=jnp.int32) - segment_ids.reshape(rows) * zeros
    cos, sin = turn_tables(local_pos)
    dy = (cotangent * selected[:, :, None].astype(BF)).reshape(rows, width)
    qkv_own, qkv_first, cos, sin = fence(qkv_own, qkv_first, cos, sin)
    qkv_second = send_second(qkv_own)
    qkv_theirs = [send_sibling(qkv_own), send_sibling(qkv_first)]
    all_places = jnp.arange(length, dtype=jnp.int32)
    cos_all, sin_all = turn_tables(all_places - jnp.where(all_places >= zeros, zeros, 0))
    qkv_first, qkv_second, cos_all, sin_all, *qkv_theirs = fence(qkv_first, qkv_second, cos_all, sin_all, *qkv_theirs)
    qkv_far = send_second(qkv_first)
    qkv_theirs.append(send_sibling(qkv_second))
    qkv_far, dy, *qkv_theirs = fence(qkv_far, dy, *qkv_theirs)
    qkv_theirs.append(send_sibling(qkv_far))
    qkv_parts = [qkv_own, qkv_first, qkv_second, qkv_far] + qkv_theirs
    x_bf = tokens.reshape(rows, width)
    x_bf, w_out, gu_send, *qkv_parts = fence(x_bf, w_out, gu_send, *qkv_parts)
    out_first = send_first(w_out)
    gu_part = lax.all_to_all(gu_send, "sp", 0, 0, axis_index_groups=SAME_CORE, tiled=True)
    qkv_send, normed, inv_one = project(places, x_bf, attn_gain, cos, sin, qkv_parts)
    qkv_send, out_first = fence(qkv_send, out_first)
    gu_mine = lax.all_gather(after(gu_part, qkv_send), "dp", axis=0, tiled=False)
    gu_mine = lax.all_gather(after(gu_part, qkv_send), "dp", axis=0, tiled=False)
    down_theirs = send_sibling(w_down)
    w_dn = jnp.where(
        core == 0, jnp.concatenate([w_down, down_theirs], axis=0), jnp.concatenate([down_theirs, w_down], axis=0)
    )
    qkv_heads = lax.all_to_all(qkv_send, "sp", 0, 0, tiled=True).reshape(length, qkv_send.shape[2])

    cuts = (0, (5 * blocks) // 8, (7 * blocks) // 8, blocks)
    qkv_heads, w_dn, out_first = fence(qkv_heads, w_dn, out_first)
    out_second = send_second(after(w_out, qkv_heads))
    dy_first = send_first(after(dy, qkv_heads))
    fwd = attend(zeros_one, qkv_heads, cuts[0], cuts[1])
    qkv_heads, out_second, dy_first, out_first, dy, *fwd = fence(qkv_heads, out_second, dy_first, out_first, dy, *fwd)
    out_far = send_second(out_first)
    dy_second = send_second(dy)
    fwd = attend(zeros_one, qkv_heads, cuts[1], cuts[2], fwd)
    qkv_heads, out_far, dy_second, dy_first, *fwd = fence(qkv_heads, out_far, dy_second, dy_first, *fwd)
    dy_far = send_second(dy_first)
    gu_theirs = send_sibling(after(gu_mine, fwd[2]))
    out_heads, out_send, lse = attend(zeros_one, qkv_heads, cuts[2], cuts[3], fwd)
    out_parts = [w_out, out_first, out_second, out_far]
    out_parts = out_parts + [send_sibling(part) for part in out_parts]
    out_send, gu_mine, gu_theirs = fence(out_send, gu_mine, gu_theirs)
    attn_tok = lax.all_to_all(out_send, "sp", 0, 0, tiled=True)
    w_gu = join(core, gu_mine, gu_theirs)
    attn_tok, w_gu, dy_far, *out_parts = fence(attn_tok, w_gu, dy_far, *out_parts)
    residual, inv_two, inner = out_proj(places, attn_tok, x_bf, mlp_gain, out_parts)

    b_first = send_first(inner)
    own = ffn(inner, dy, w_gu, w_dn)
    inner, b_first, *own = fence(inner, b_first, *own)
    b_second = send_second(inner)
    first = ffn(b_first, dy_first, w_gu, w_dn)
    b_first, b_second, *first = fence(b_first, b_second, *first)
    b_far = send_second(b_first)
    second = ffn(b_second, dy_second, w_gu, w_dn)
    b_far, db_first, *second = fence(b_far, first[3], *second)
    db_got_first = send_first(db_first)
    far = ffn(b_far, dy_far, w_gu, w_dn)
    db_got_first, db_far, *hid_rows = fence(db_got_first, far[3], own[0], first[0], second[0], far[0])

    b_rows = [inner, b_first, b_second, b_far]
    db_got_far = send_first(db_far)
    gu_keep, gu_give = grad_gu(
        core,
        b_rows,
        [own[1], first[1], second[1], far[1]],
        [own[2], first[2], second[2], far[2]],
        share,
        planes,
    )
    db_got_far, gu_keep, gu_give, *hid_rows = fence(db_got_far, gu_keep, gu_give, *hid_rows)
    db_pass = (second[3].astype(F32) + db_got_far.astype(F32)).astype(BF)
    db_pass, gu_give, *hid_rows = fence(db_pass, gu_give, *hid_rows)
    db_passed = send_second(db_pass)
    gu_got = send_sibling(gu_give)
    dn_keep, dn_give = grad_dn(core, hid_rows, [dy, dy_first, dy_second, dy_far])
    gu_got, dn_keep, dn_give = fence(gu_got, dn_keep, dn_give)
    gu_sum = (gu_keep.astype(F32) + gu_got.astype(F32)).astype(BF)
    gu_sum, db_passed, dn_give = fence(gu_sum, db_passed, dn_give)
    gu_z = lax.psum_scatter(
        gu_sum.reshape(planes * CHIPS * quarter, 2 * hidden_chip), "dp", scatter_dimension=0, tiled=True
    )
    gu_z = gu_z.reshape(CHIPS, quarter, 2 * hidden_chip)
    dn_got = send_sibling(dn_give)
    d_resid, d_branch, d_send = resid_back(
        places, own[3], db_got_first, db_passed, residual, inv_two, mlp_gain, dy, out_parts
    )
    d_send, d_branch, dn_got = fence(d_send, d_branch, dn_got)
    d_heads = lax.all_to_all(d_send, "sp", 0, 0, tiled=True).reshape(length, share)
    wo_keep, wo_give = grad_wo(core, attn_tok, d_branch)
    d_heads, wo_keep, wo_give, normed = fence(d_heads, wo_keep, wo_give, normed)

    def back_call(heads, start, stop, **kwargs):
        return attend_back(zeros_one, qkv_heads, heads, lse, cos_all, sin_all, start, stop, **kwargs)

    turns = (0, blocks // 4, (3 * blocks) // 8, blocks)
    wo_got = send_sibling(wo_give)
    a_first = send_first(normed)
    a_second = send_second(normed)
    a_theirs = [send_sibling(normed)]
    dn_sum = (dn_keep.astype(F32) + dn_got.astype(F32)).astype(BF)
    bwd = back_call(d_heads, turns[0], turns[1], out=out_heads)
    d_heads, a_first, a_second, wo_got, gu_z, dn_sum, *moves = fence(
        d_heads, a_first, a_second, wo_got, gu_z, dn_sum, *a_theirs, *bwd
    )
    a_theirs, bwd = moves[:1], moves[1:]

    def wo_part(place):
        return pick(wo_keep, place).astype(F32) + pick(wo_got, place).astype(F32)

    dn_z = lax.psum_scatter(dn_sum, "dp", scatter_dimension=0, tiled=True)
    gu_z = lax.all_to_all(gu_z, "sp", 0, 0, axis_index_groups=SAME_CORE, tiled=True)
    a_theirs += [send_sibling(a_first), send_sibling(a_second)]
    bwd = back_call(d_heads, turns[1], turns[2], before=bwd)
    d_heads, gu_z, a_first, *moves = fence(d_heads, gu_z, a_first, *a_theirs, *bwd)
    a_theirs, bwd = moves[:3], moves[3:]

    wo_first = wo_part(chip ^ (first_mask // 2)).astype(BF)
    wo_far = wo_part(chip ^ 3).astype(BF)
    d_heads, gu_z, a_first, wo_first, wo_far = fence(d_heads, gu_z, a_first, wo_first, wo_far)
    gu_all = lax.all_gather(gu_z, "dp", axis=0, tiled=False)
    a_far = send_second(a_first)
    wo_far = send_first(wo_far)
    wo_first = send_first(wo_first)
    bwd = back_call(d_heads, turns[2], turns[3], before=bwd)
    wo_pass = (wo_part(chip ^ (second_mask // 2)) + wo_far.astype(F32)).astype(BF)
    dp_heads, wo_first, wo_pass, a_far = fence(bwd[0], wo_first, wo_pass, a_far)

    wo_passed = send_second(wo_pass)
    a_theirs.append(send_sibling(a_far))
    back = lax.all_to_all(dp_heads, "sp", 0, 0, tiled=True)
    grad_wq = grad_qkv(places, [normed, a_first, a_second, a_far] + list(a_theirs), dp_heads, planes)
    wo_passed, grad_wq = fence(wo_passed, grad_wq)
    wo_rows = (wo_part(chip) + wo_first.astype(F32) + wo_passed.astype(F32)).astype(BF)
    split = grad_wq.shape[2]
    last_parts = [jnp.concatenate([grad_wq, wo_rows.reshape(planes, quarter, width)], axis=2)]
    y_far, y_first = far[4], first[4]
    moves = None
    for step in range(1, planes):
        moves = line_scatter_sends(last_parts, moves, step, 0)
        y_far, y_first, *moves = fence(y_far, y_first, *moves)
        moves = line_scatter_move(moves, step)
        if step == 1:
            dn_all = lax.all_gather(dn_z, "dp", axis=0, tiled=False)
        elif step == 2:
            back, *moves = fence(back, *moves)
        elif step == 3:
            y_far, back = fence(y_far, back)
            y_got_far = send_first(y_far)
        moves = fence(*moves)
    last_z = line_scatter_end(last_parts, moves, 0)
    wq_z = last_z[:, :split].reshape(quarter, devices, split // devices).transpose(1, 0, 2)
    wq_z, wo_z, gu_all = fence(wq_z, last_z[:, split:], gu_all)
    wq_z = lax.all_to_all(wq_z, "sp", 0, 0, tiled=True)
    grad_tokens = in_back(places, back, x_bf, inv_one, attn_gain, d_resid, qkv_parts).reshape(tokens.shape)
    y_pass = (second[4].astype(F32) + y_got_far.astype(F32)).astype(BF)
    last_z = jnp.concatenate([wq_z.transpose(1, 0, 2).reshape(quarter, split), wo_z], axis=1)
    last_z, grad_tokens, y_pass, y_first = fence(last_z, grad_tokens, y_pass, y_first)
    y_got_first = send_first(y_first)
    y_passed = send_second(y_pass)
    last_steps = [(last_z, last_z)]
    outs = []
    for step in range(1, planes):
        if step == planes - 1:
            y_got_first, y_passed, *moves = fence(y_got_first, y_passed, *last_steps[-1])
            last_steps[-1] = tuple(moves)
        last_steps.append(line_gather_move(last_steps[-1], step))
        if step == 1:
            outs += spread(gu_all, w_gate_up, g_mlp.astype(F32).reshape(share, 1))
        elif step == 2:
            outs.append(dn_all.astype(F32).reshape(w_down.shape))
        if step == planes - 1:
            y_sum = own[4].astype(F32) + y_got_first.astype(F32) + y_passed.astype(F32)
            outs.append((residual + y_sum).astype(BF).reshape(tokens.shape))
        moves = fence(*last_steps[-1], *outs)
        last_steps[-1], outs = tuple(moves[:2]), list(moves[2:])
    grad_w_gate_up, grad_g_mlp, grad_w_down, output = outs
    grad_w_qkv, grad_g_attn, grad_w_out = spread_last(last_steps, w_qkv, g_attn.astype(F32).reshape(share, 1), width)
    return (
        output,
        grad_tokens,
        grad_w_qkv,
        grad_w_out,
        grad_w_gate_up,
        grad_w_down,
        grad_g_attn.reshape(share),
        grad_g_mlp.reshape(share),
    )


def solution(mesh):
    in_specs = (
        P("dp", "sp", None),
        P("dp", "sp"),
        P("dp", "sp"),
        P("dp", "sp", None),
        P("sp", None),
        P("sp", None),
        P("sp", None),
        P("sp", None),
        P("sp"),
        P("sp"),
    )
    out_specs = (
        P("dp", "sp", None),
        P("dp", "sp", None),
        P("sp", None),
        P("sp", None),
        P("sp", None),
        P("sp", None),
        P("sp"),
        P("sp"),
    )
    body = fast_body if dict(mesh.shape) == {"dp": 4, "sp": 2 * CHIPS} else general_body
    return jax.shard_map(body, mesh=mesh, in_specs=in_specs, out_specs=out_specs, check_vma=False)
```

```python
import functools
import math

import jax
import jax.numpy as jnp
from jax import lax
from jax.experimental import pallas as pl
from jax.experimental.pallas import tpu as pltpu
from jax.sharding import PartitionSpec as P

D = 2048
H = 32
KV = 4
HD = 64
FF = 5632


EPSILON = 1e-05
ROPE_BASE = 10000.0
MASKED = -1e30


def rope_tables(positions, head_size):
    half_dim = head_size // 2
    frequency = ROPE_BASE ** (-(jnp.arange(half_dim, dtype=jnp.float32) * 2.0 / head_size))
    angles = positions.astype(jnp.float32)[:, None] * frequency[None, :]
    return (jnp.cos(angles), jnp.sin(angles))


def rotate(values, cosine, sine_tab, inverse_turn):
    half_dim = values.shape[-1] // 2
    first_half = values[..., :half_dim]
    second = values[..., half_dim:]
    cos_wide = cosine[:, None, :]
    sin_wide = sine_tab[:, None, :]
    if inverse_turn:
        sin_wide = -sin_wide
    return jnp.concatenate(
        [first_half * cos_wide - second * sin_wide, second * cos_wide + first_half * sin_wide],
        axis=-1,
    )


def rms_norm(values, gain_vec):
    inverse = lax.rsqrt(jnp.mean(values * values, axis=-1, keepdims=True) + EPSILON)
    return (values * inverse * gain_vec, inverse)


def norm_back(values, inverse, gain_vec, upstream):
    scaled = upstream * gain_vec
    inner_mean = jnp.mean(scaled * values, axis=-1, keepdims=True)
    through = inverse * scaled - values * inverse**3 * inner_mean
    gain_grad = jnp.sum(upstream * values * inverse, axis=0)
    return (through, gain_grad)


def attention_inputs(flat_in, qkv_full, gain_vec, cosine, sine_tab):
    row_count = flat_in.shape[0]
    group_size = H // KV
    normed, inverse = rms_norm(flat_in, gain_vec)
    normed = normed.astype(jnp.bfloat16)
    projected = jnp.dot(normed, qkv_full, preferred_element_type=jnp.float32)
    queries = rotate(projected[:, :D].reshape(row_count, H, HD), cosine, sine_tab, False)
    key_heads = rotate(
        projected[:, D : D + KV * HD].reshape(row_count, KV, HD), cosine, sine_tab, False
    )
    value_heads = projected[:, D + KV * HD :].reshape(row_count, KV, HD)
    key_wide = jnp.broadcast_to(key_heads[:, :, None], (row_count, KV, group_size, HD)).reshape(
        row_count, D
    )
    value_wide = jnp.broadcast_to(value_heads[:, :, None], (row_count, KV, group_size, HD)).reshape(
        row_count, D
    )
    stacked = jnp.stack([queries.reshape(row_count, D), key_wide, value_wide]).astype(jnp.bfloat16)
    return (normed, inverse, stacked)


def block_mask(seg_full, position, row_begin, finish):
    row_seg = seg_full[:, row_begin:finish]
    col_seg = seg_full[:, :finish]
    same_doc = row_seg[:, :, None] == col_seg[:, None, :]
    causal = position[row_begin:finish, None] >= position[None, :finish]
    return same_doc & causal[None]


def attention_forward(queries, key_heads, value_heads, seg_full, score_scale):
    length = queries.shape[1]
    block_rows = min(512, length)
    position = jnp.arange(length, dtype=jnp.int32)
    outputs = []
    lse_parts = []
    for block_num in range(length // block_rows):
        row_begin = block_num * block_rows
        finish = row_begin + block_rows
        scores = (
            jnp.einsum(
                "sqhd,skhd->shqk",
                queries[:, row_begin:finish],
                key_heads[:, :finish],
                preferred_element_type=jnp.float32,
            )
            * score_scale
        )
        allowed = block_mask(seg_full, position, row_begin, finish)
        scores = jnp.where(allowed[:, None], scores, MASKED)
        row_max = jnp.max(scores, axis=-1, keepdims=True)
        shifted = jnp.exp(scores - row_max)
        row_total = jnp.sum(shifted, axis=-1, keepdims=True)
        softmax_w = (shifted / row_total).astype(jnp.bfloat16)
        outputs.append(
            jnp.einsum(
                "shqk,skhd->sqhd",
                softmax_w,
                value_heads[:, :finish],
                preferred_element_type=jnp.float32,
            )
        )
        lse_parts.append(row_max + jnp.log(row_total))
    return (jnp.concatenate(outputs, axis=1), jnp.concatenate(lse_parts, axis=2))


def attention_backward(queries, key_heads, value_heads, seg_full, log_sums, grad_out, score_scale):
    length = queries.shape[1]
    block_rows = min(512, length)
    position = jnp.arange(length, dtype=jnp.int32)
    grad_query = []
    grad_key = jnp.zeros(key_heads.shape, jnp.float32)
    grad_value = jnp.zeros(value_heads.shape, jnp.float32)
    for block_num in range(length // block_rows):
        row_begin = block_num * block_rows
        finish = row_begin + block_rows
        query_rows = queries[:, row_begin:finish]
        grad_rows = grad_out[:, row_begin:finish]
        key_part = key_heads[:, :finish]
        value_part = value_heads[:, :finish]
        scores = (
            jnp.einsum("sqhd,skhd->shqk", query_rows, key_part, preferred_element_type=jnp.float32)
            * score_scale
        )
        allowed = block_mask(seg_full, position, row_begin, finish)
        softmax_f = jnp.where(
            allowed[:, None], jnp.exp(scores - log_sums[:, :, row_begin:finish]), 0.0
        )
        grad_probs = jnp.einsum(
            "sqhd,skhd->shqk", grad_rows, value_part, preferred_element_type=jnp.float32
        )
        row_delta = jnp.sum(softmax_f * grad_probs, axis=-1, keepdims=True)
        grad_scores = (softmax_f * (grad_probs - row_delta)).astype(jnp.bfloat16)
        grad_query.append(
            jnp.einsum("shqk,skhd->sqhd", grad_scores, key_part, preferred_element_type=jnp.float32)
            * score_scale
        )
        grad_key = grad_key.at[:, :finish].add(
            jnp.einsum(
                "shqk,sqhd->skhd", grad_scores, query_rows, preferred_element_type=jnp.float32
            )
            * score_scale
        )
        grad_value = grad_value.at[:, :finish].add(
            jnp.einsum(
                "shqk,sqhd->skhd",
                softmax_f.astype(jnp.bfloat16),
                grad_rows,
                preferred_element_type=jnp.float32,
            )
        )
    return (jnp.concatenate(grad_query, axis=1), grad_key, grad_value)


def general_body(tokens, segment_ids, selected, cotangent, w_qkv, w_out, w_gate_up, w_down, g_attn, g_mlp):
    streams, local_len, model_dim = tokens.shape
    sp_count = lax.axis_size("sp")
    sp_index = lax.axis_index("sp")
    row_count = streams * local_len
    group_size = H // KV
    kv_width = KV * HD
    score_scale = HD ** (-0.5)
    contract = (((0,), (0,)), ((), ()))
    seg_full = lax.all_gather(segment_ids, "sp", axis=1, tiled=True)
    first_count = jnp.sum((seg_full == 0).astype(jnp.int32), axis=1, keepdims=True)
    local_pos = (
        sp_index * local_len
        + jnp.arange(local_len, dtype=jnp.int32)[None, :]
        - segment_ids * first_count
    )
    cosine, sine_tab = rope_tables(local_pos.reshape(row_count), HD)
    shards = (w_qkv, w_out, w_gate_up, w_down, g_attn, g_mlp)
    gathered = (
        lax.all_gather(shards[0], "sp", axis=0, tiled=True),
        lax.all_gather(shards[1], "sp", axis=0, tiled=True),
        lax.all_gather(shards[2], "sp", axis=0, tiled=True),
        lax.all_gather(shards[3], "sp", axis=0, tiled=True),
        lax.all_gather(shards[4], "sp", axis=0, tiled=True),
        lax.all_gather(shards[5], "sp", axis=0, tiled=True),
    )
    qkv_full, out_full, gate_up_full, down_full, attn_gain, mlp_gain = gathered
    attn_gain = attn_gain.astype(jnp.float32)
    mlp_gain = mlp_gain.astype(jnp.float32)
    flat_in = tokens.reshape(row_count, model_dim).astype(jnp.float32)
    normed, inverse_one, stacked = attention_inputs(flat_in, qkv_full, attn_gain, cosine, sine_tab)
    head_view = lax.all_to_all(
        stacked.reshape(3, streams, local_len, model_dim),
        "sp",
        split_axis=3,
        concat_axis=2,
        tiled=True,
    )
    length = head_view.shape[2]
    heads_here = head_view.shape[3] // HD
    head_shape = (streams, length, heads_here, HD)
    queries = head_view[0].reshape(head_shape)
    key_heads = head_view[1].reshape(head_shape)
    value_heads = head_view[2].reshape(head_shape)
    attn_heads, log_sums = attention_forward(queries, key_heads, value_heads, seg_full, score_scale)
    attn_send = attn_heads.astype(jnp.bfloat16).reshape(streams, length, heads_here * HD)
    attn_tok = lax.all_to_all(attn_send, "sp", split_axis=1, concat_axis=2, tiled=True).reshape(
        row_count, model_dim
    )
    branch = jnp.dot(attn_tok, out_full, preferred_element_type=jnp.float32)
    residual = flat_in + branch
    inner_f, inverse_two = rms_norm(residual, mlp_gain)
    inner_in = inner_f.astype(jnp.bfloat16)
    gate_up = jnp.dot(inner_in, gate_up_full, preferred_element_type=jnp.float32)
    gate_part = gate_up[:, :FF]
    up_part = gate_up[:, FF:]
    sigmoid_g = jax.nn.sigmoid(gate_part)
    silu_gate = gate_part * sigmoid_g
    hidden = (silu_gate * up_part).astype(jnp.bfloat16)
    result = residual + jnp.dot(hidden, down_full, preferred_element_type=jnp.float32)
    output = result.astype(jnp.bfloat16).reshape(streams, local_len, model_dim)
    qkv_back, out_back, gate_up_back, down_back, attn_gain_b, mlp_gain_b = gathered
    attn_gain_b = attn_gain_b.astype(jnp.float32)
    mlp_gain_b = mlp_gain_b.astype(jnp.float32)
    grad_y = (cotangent * selected[:, :, None].astype(jnp.bfloat16)).reshape(row_count, model_dim)
    grad_hidden = jnp.dot(grad_y, down_back.T, preferred_element_type=jnp.float32)
    silu_slope = sigmoid_g * (1.0 + gate_part * (1.0 - sigmoid_g))
    grad_both = jnp.concatenate(
        [grad_hidden * up_part * silu_slope, grad_hidden * silu_gate], axis=1
    ).astype(jnp.bfloat16)
    grad_inner = jnp.dot(grad_both, gate_up_back.T, preferred_element_type=jnp.float32)
    grad_resid, gain_two = norm_back(residual, inverse_two, mlp_gain_b, grad_inner)
    grad_resid = grad_resid + grad_y.astype(jnp.float32)
    grad_branch = grad_resid.astype(jnp.bfloat16)
    grad_attn = jnp.dot(grad_branch, out_back.T, preferred_element_type=jnp.float32).astype(
        jnp.bfloat16
    )
    grad_view = lax.all_to_all(
        grad_attn.reshape(streams, local_len, model_dim),
        "sp",
        split_axis=2,
        concat_axis=1,
        tiled=True,
    )
    grad_view = grad_view.reshape(head_shape)
    grad_q, grad_k, grad_v = attention_backward(
        queries, key_heads, value_heads, seg_full, log_sums, grad_view, score_scale
    )
    back_send = (
        jnp.stack([grad_q, grad_k, grad_v])
        .astype(jnp.bfloat16)
        .reshape(3, streams, length, heads_here * HD)
    )
    returned = lax.all_to_all(back_send, "sp", split_axis=2, concat_axis=3, tiled=True)
    returned = returned.astype(jnp.float32).reshape(3, row_count, H, HD)
    grad_pq = rotate(returned[0], cosine, sine_tab, True).reshape(row_count, model_dim)
    key_summed = jnp.sum(returned[1].reshape(row_count, KV, group_size, HD), axis=2)
    grad_pk = rotate(key_summed, cosine, sine_tab, True).reshape(row_count, kv_width)
    grad_pv = jnp.sum(returned[2].reshape(row_count, KV, group_size, HD), axis=2).reshape(
        row_count, kv_width
    )
    grad_mixed = jnp.concatenate(
        [grad_pq.astype(jnp.bfloat16), grad_pk.astype(jnp.bfloat16), grad_pv.astype(jnp.bfloat16)],
        axis=1,
    )
    grad_normed = jnp.dot(grad_mixed, qkv_back.T, preferred_element_type=jnp.float32)
    grad_in, gain_one = norm_back(flat_in, inverse_one, attn_gain_b, grad_normed)
    grad_in = grad_in + grad_resid
    grad_tokens = grad_in.astype(jnp.bfloat16).reshape(streams, local_len, model_dim)
    gain_totals = lax.psum((gain_one, gain_two), ("dp", "sp"))
    gain_share = model_dim // sp_count
    grad_g_attn = lax.dynamic_slice_in_dim(gain_totals[0], sp_index * gain_share, gain_share, 0)
    grad_g_mlp = lax.dynamic_slice_in_dim(gain_totals[1], sp_index * gain_share, gain_share, 0)
    row_sums = lax.psum_scatter(
        jnp.concatenate(
            [
                lax.dot_general(normed, grad_mixed, contract, preferred_element_type=jnp.float32),
                lax.dot_general(
                    attn_tok, grad_branch, contract, preferred_element_type=jnp.float32
                ),
                lax.dot_general(inner_in, grad_both, contract, preferred_element_type=jnp.float32),
            ],
            axis=1,
        ).astype(jnp.bfloat16),
        "sp",
        scatter_dimension=0,
        tiled=True,
    )
    down_sums = lax.psum_scatter(
        lax.dot_general(hidden, grad_y, contract, preferred_element_type=jnp.float32).astype(
            jnp.bfloat16
        ),
        "sp",
        scatter_dimension=0,
        tiled=True,
    )
    weight_rows, down_rows = (
        lax.psum(row_sums, "dp").astype(jnp.float32),
        lax.psum(down_sums, "dp").astype(jnp.float32),
    )
    qkv_cols = model_dim + 2 * kv_width
    grad_w_qkv = weight_rows[:, :qkv_cols]
    grad_w_out = weight_rows[:, qkv_cols : qkv_cols + model_dim]
    grad_w_gate_up = weight_rows[:, qkv_cols + model_dim :]
    return (
        output,
        grad_tokens,
        grad_w_qkv,
        grad_w_out,
        grad_w_gate_up,
        down_rows,
        grad_g_attn,
        grad_g_mlp,
    )


CHIPS = 4
BLOCK = 512
SHORT = pl.CostEstimate(flops=1, bytes_accessed=1, transcendentals=0)
LOG2E = math.log2(math.e)
BF = jnp.bfloat16
F32 = jnp.float32
NT = (((1,), (1,)), ((), ()))
TN = (((0,), (0,)), ((), ()))


def swap_pairs(even_mask, odd_mask):
    return [(i, i ^ (odd_mask if i & 1 else even_mask)) for i in range(2 * CHIPS)]


FIRST = swap_pairs(2, 4)
SECOND = swap_pairs(4, 2)
SIBLING = swap_pairs(1, 1)
SAME_CORE = [[0, 2, 4, 6], [1, 3, 5, 7]]


def send_first(x):
    return lax.ppermute(x, "sp", FIRST)


def send_second(x):
    return lax.ppermute(x, "sp", SECOND)


def send_sibling(x):
    return lax.ppermute(x, "sp", SIBLING)


def after(value, *others):
    return lax.optimization_barrier((value,) + others)[0]


def gather_chips(own):
    first = send_first(own)
    second = send_second(after(own, first))
    far = send_second(after(first, second))
    return [own, first, second, far]


def rel_masks(core):
    first = jnp.where(core == 0, 2, 4)
    return first, 6 - first


def fence(*values):
    return lax.optimization_barrier(values)


def gather_vectors(own, me):
    for bit in (1, 2, 4):
        got = lax.ppermute(own, "sp", swap_pairs(bit, bit))
        high = (me & bit) != 0
        own = jnp.concatenate([jnp.where(high, got, own), jnp.where(high, own, got)], axis=1)
    return own


def pick(parts, index):
    return lax.dynamic_index_in_dim(parts, index, 0, keepdims=False)


def pick_sum(parts, index, axis):
    return sum(lax.dynamic_index_in_dim(p, index, axis, keepdims=False).astype(F32) for p in parts)


def line_scatter_sends(parts, got, step, axis):
    planes = parts[0].shape[axis]
    z = lax.axis_index("dp")
    ahead = pick_sum(parts, jnp.clip(planes - step + z, 0, planes - 1), axis)
    back = pick_sum(parts, jnp.clip(z - planes + step, 0, planes - 1), axis)
    if got is not None:
        ahead = ahead + got[0].astype(F32)
        back = back + got[1].astype(F32)
    return ahead.astype(BF), back.astype(BF)


def line_scatter_move(sends, step):
    planes = lax.axis_size("dp")
    right = lax.ppermute(sends[0], "dp", [(i, i + 1) for i in range(step)])
    left = lax.ppermute(sends[1], "dp", [(planes - 1 - i, planes - 2 - i) for i in range(step)])
    return right, left


def line_scatter_end(parts, got, axis):
    own = pick_sum(parts, lax.axis_index("dp"), axis)
    return (own + got[0].astype(F32) + got[1].astype(F32)).astype(BF)


def line_gather_move(got, step):
    planes = lax.axis_size("dp")
    right = lax.ppermute(got[0], "dp", [(i, i + 1) for i in range(step - 1, planes - 1)])
    left = lax.ppermute(got[1], "dp", [(i + 1, i) for i in range(planes - step)])
    return right, left


def line_values(refs, planes, z):
    for step in range(planes):
        place = lax.rem(z - step + planes, planes)
        if step == 0:
            yield place, lambda index: refs[0][index]
        else:
            right, left = refs[step], refs[2 * planes - 1 - step]
            yield place, lambda index, right=right, left=left, step=step: jnp.where(z >= step, right[index], left[index])


def spread_kernel(in_ref, w_ref, g_ref, out_ref, gain_ref):
    planes, _, rows, width = in_ref.shape
    out = in_ref[...].reshape(planes * rows, width).astype(F32)
    out_ref[...] = out
    part = jnp.sum(out * w_ref[...].astype(F32), axis=-1, keepdims=True) / g_ref[...]

    @pl.when(pl.program_id(0) == 0)
    def _():
        gain_ref[...] = part

    @pl.when(pl.program_id(0) > 0)
    def _():
        gain_ref[...] += part


def spread(parts, weight, gain):
    planes, chips, rows, both = parts.shape
    half = both // 2
    total = planes * rows
    line = pl.BlockSpec((total, half), lambda i: (0, i))
    column = pl.BlockSpec((total, 1), lambda i: (0, 0))
    return pl.pallas_call(
        spread_kernel,
        grid=(2 * chips,),
        in_specs=[pl.BlockSpec((planes, 1, rows, half), lambda i: (0, i % chips, 0, i // chips)), line, column],
        out_specs=[line, column],
        out_shape=[jax.ShapeDtypeStruct(weight.shape, F32), jax.ShapeDtypeStruct((total, 1), F32)],
        compiler_params=pltpu.CompilerParams(vmem_limit_bytes=32 * 2**20),
        cost_estimate=SHORT,
        name="spread",
    )(parts, weight, gain)


def spread_last_kernel(z_ref, *refs, planes):
    blocks, (w_ref, g_ref, out_ref, gain_ref, wo_ref) = refs[:-5], refs[-5:]
    rows = blocks[0].shape[0]
    devices = 2 * CHIPS
    width = wo_ref.shape[1]
    heads = width // devices
    each = heads + 2 * HD
    for place, load in line_values(blocks, planes, z_ref[0]):
        span = pl.ds(pl.multiple_of(place * rows, rows), rows)
        pairs = []
        for d in range(devices):
            begin = d * each
            cols = slice(begin, begin + heads)
            out_ref[span, d * heads : (d + 1) * heads] = load((slice(None), cols)).astype(F32)
            pairs.append(load((slice(None), slice(begin + heads, begin + each))).astype(F32))
        for g in range(0, KV, 2):
            low = pairs[2 * g] + pairs[2 * g + 1]
            high = pairs[2 * g + 2] + pairs[2 * g + 3]
            lane = lax.broadcasted_iota(jnp.int32, low.shape, 1)
            begin = width + g * HD
            out_ref[span, begin : begin + 2 * HD] = jnp.where(lane < HD, low, pltpu.roll(high, HD, 1))
            begin = width + (KV + g) * HD
            out_ref[span, begin : begin + 2 * HD] = jnp.where(lane < HD, pltpu.roll(low, HD, 1), high)
        wo_ref[span, :] = load((slice(None), slice(devices * each, devices * each + width))).astype(F32)
    gain_ref[...] = jnp.sum(out_ref[...] * w_ref[...].astype(F32), axis=-1, keepdims=True) / g_ref[...]


def spread_last(steps, weight, gain, width):
    planes = len(steps)
    blocks = [steps[0][0]] + [s[0] for s in steps[1:]] + [s[1] for s in steps[1:]]
    vmem = pl.BlockSpec(memory_space=pltpu.VMEM)
    total = weight.shape[0]
    return pl.pallas_call(
        functools.partial(spread_last_kernel, planes=planes),
        in_specs=[pl.BlockSpec(memory_space=pltpu.SMEM)] + [vmem] * (len(blocks) + 2),
        out_specs=[vmem] * 3,
        out_shape=[
            jax.ShapeDtypeStruct(weight.shape, F32),
            jax.ShapeDtypeStruct((total, 1), F32),
            jax.ShapeDtypeStruct((total, width), F32),
        ],
        compiler_params=pltpu.CompilerParams(vmem_limit_bytes=32 * 2**20),
        cost_estimate=SHORT,
        name="spread_last",
    )(lax.axis_index("dp").reshape(1), *blocks, weight, gain)


def join_kernel(core_ref, mine_ref, theirs_ref, out_ref):
    planes, _, rows, both = mine_ref.shape
    block = jnp.where(pl.program_id(1) == 0, mine_ref[...], theirs_ref[...]).reshape(planes * rows, both)
    out_ref[0, 0, 0] = block[:, : both // 2]
    out_ref[1, 0, 0] = block[:, both // 2 :]


def join(core, mine, theirs):
    planes, chips, rows, both = mine.shape
    spec = pl.BlockSpec((planes, 1, rows, both), lambda c, k, core: (0, c, 0, 0))
    out = pl.pallas_call(
        join_kernel,
        grid_spec=pltpu.PrefetchScalarGridSpec(
            num_scalar_prefetch=1,
            grid=(chips, 2),
            in_specs=[spec, spec],
            out_specs=pl.BlockSpec(
                (2, 1, 1, planes * rows, both // 2), lambda c, k, core: (0, c, (core[0] + k) % 2, 0, 0)
            ),
        ),
        out_shape=jax.ShapeDtypeStruct((2, chips, 2, planes * rows, both // 2), BF),
        compiler_params=pltpu.CompilerParams(vmem_limit_bytes=32 * 2**20),
        cost_estimate=SHORT,
        name="join",
    )(core.reshape(1), mine, theirs)
    return out.reshape(2, 2 * chips * planes * rows, both // 2)


def ffn_kernel(*refs, cuts):
    b_hbm, dy_hbm, wgu_hbm, wd_hbm, hid_hbm, dg_hbm, du_hbm, db_hbm, y_hbm = refs[:9]
    b_ref, dy_ref, wg_ref, wu_ref, wd_ref, hid_ref, dg_ref, du_ref, db_ref, y_ref, sems = refs[9:]
    count = len(cuts) - 1

    def move(source, target, index):
        copy = pltpu.make_async_copy(source, target, sems.at[index])
        copy.start()
        return copy

    b_copy = move(b_hbm, b_ref, 3 * count)
    weights = []
    for c in range(count):
        span = slice(cuts[c], cuts[c + 1])
        gate_copy = move(wgu_hbm.at[0, :, span], wg_ref.at[:, span], 3 * c)
        up_copy = move(wgu_hbm.at[1, :, span], wu_ref.at[:, span], 3 * c + 1)
        weights.append([gate_copy, up_copy])
        if c == 0:
            dy_copy = move(dy_hbm, dy_ref, 3 * count + 1)
        weights[-1].append(move(wd_hbm.at[span, :], wd_ref.at[span, :], 3 * c + 2))
    b_copy.wait()
    for c in range(count):
        span = slice(cuts[c], cuts[c + 1])
        for copy in weights[c][:2]:
            copy.wait()
        gate = jnp.dot(b_ref[...], wg_ref[:, span], preferred_element_type=F32)
        up = jnp.dot(b_ref[...], wu_ref[:, span], preferred_element_type=F32)
        if c == 0:
            dy_copy.wait()
        weights[c][2].wait()
        d_hidden = lax.dot_general(dy_ref[...], wd_ref[span, :], NT, preferred_element_type=F32)
        sigmoid_g = jax.nn.sigmoid(gate)
        silu_gate = gate * sigmoid_g
        hid_ref[:, span] = (silu_gate * up).astype(BF)
        dg_ref[:, span] = (d_hidden * up * (sigmoid_g * (1.0 + gate * (1.0 - sigmoid_g)))).astype(BF)
        du_ref[:, span] = (d_hidden * silu_gate).astype(BF)
    base = 3 * count + 2
    outs = [move(hid_ref, hid_hbm, base), move(dg_ref, dg_hbm, base + 1), move(du_ref, du_hbm, base + 2)]
    y_ref[...] = jnp.dot(hid_ref[...], wd_ref[...], preferred_element_type=F32).astype(BF)
    outs.append(move(y_ref, y_hbm, base + 3))
    d_in = lax.dot_general(dg_ref[...], wg_ref[...], NT, preferred_element_type=F32)
    db_ref[...] = (d_in + lax.dot_general(du_ref[...], wu_ref[...], NT, preferred_element_type=F32)).astype(BF)
    outs.append(move(db_ref, db_hbm, base + 4))
    for copy in outs:
        copy.wait()


def ffn(b_rows, dy_rows, w_gu, w_dn):
    rows, width = b_rows.shape
    hidden = w_dn.shape[0]
    pieces = 3
    cuts = tuple(round(hidden * c / pieces / 128) * 128 for c in range(pieces)) + (hidden,)
    hbm = pl.BlockSpec(memory_space=pl.ANY)
    return pl.pallas_call(
        functools.partial(ffn_kernel, cuts=cuts),
        in_specs=[hbm] * 4,
        out_specs=[hbm] * 5,
        out_shape=[jax.ShapeDtypeStruct((rows, hidden), BF)] * 3 + [jax.ShapeDtypeStruct((rows, width), BF)] * 2,
        scratch_shapes=[pltpu.VMEM((rows, width), BF)] * 2
        + [pltpu.VMEM((width, hidden), BF)] * 2
        + [pltpu.VMEM((hidden, width), BF)]
        + [pltpu.VMEM((rows, hidden), BF)] * 3
        + [pltpu.VMEM((rows, width), BF)] * 2
        + [pltpu.SemaphoreType.DMA((3 * pieces + 7,))],
        compiler_params=pltpu.CompilerParams(vmem_limit_bytes=58 * 2**20),
        cost_estimate=SHORT,
        name="ffn",
    )(b_rows, dy_rows, w_gu, w_dn)


def grad_gu_kernel(core_ref, *refs, count):
    left, right = refs[: 2 * count], refs[2 * count : 4 * count]
    half = right[0].shape[1]
    for side in range(2):
        for kind in range(2):
            total = None
            for r in range(count):
                a_rows = left[side * count + r][...]
                part = lax.dot_general(a_rows, right[kind * count + r][...], TN, preferred_element_type=F32)
                total = part if total is None else total + part
            out_ref = refs[4 * count + side]
            planes, _, rows, _ = out_ref.shape
            out_ref[:, 0, :, kind * half : (kind + 1) * half] = total.astype(BF).reshape(planes, rows, half)


def grad_gu(core, b_rows, dg_rows, du_rows, share, planes):
    count = len(b_rows)
    tokens, width = b_rows[0].shape
    hidden = dg_rows[0].shape[1]
    keep = pl.BlockSpec((tokens, share), lambda c, core: (0, 2 * c + core[0]))
    give = pl.BlockSpec((tokens, share), lambda c, core: (0, 2 * c + 1 - core[0]))
    whole = pl.BlockSpec((tokens, hidden), lambda c, core: (0, 0))
    rows = share // planes
    out = pl.BlockSpec((planes, 1, rows, 2 * hidden), lambda c, core: (0, c, 0, 0))
    return pl.pallas_call(
        functools.partial(grad_gu_kernel, count=count),
        grid_spec=pltpu.PrefetchScalarGridSpec(
            num_scalar_prefetch=1,
            grid=(width // (2 * share),),
            in_specs=[keep] * count + [give] * count + [whole] * (2 * count),
            out_specs=[out, out],
        ),
        out_shape=[jax.ShapeDtypeStruct((planes, width // (2 * share), rows, 2 * hidden), BF)] * 2,
        compiler_params=pltpu.CompilerParams(vmem_limit_bytes=58 * 2**20),
        cost_estimate=SHORT,
        name="grad_gu",
    )(core.reshape(1), *b_rows, *b_rows, *dg_rows, *du_rows)


def grad_qkv_kernel(place_ref, *refs, count):
    dp_ref, out_ref = refs[-2:]
    total = None
    for r in range(count):
        part = lax.dot_general(refs[r][...], dp_ref[place_ref[r]], TN, preferred_element_type=F32)
        total = part if total is None else total + part
    planes, rows, wide = out_ref.shape
    columns = total.shape[1]
    for k in range(wide // columns):
        block = total[k * planes * rows : (k + 1) * planes * rows].astype(BF)
        out_ref[:, :, k * columns : (k + 1) * columns] = block.reshape(planes, rows, columns)


def grad_qkv(places, a_rows, dp_heads, planes):
    count = len(a_rows)
    tokens, width = a_rows[0].shape
    columns = dp_heads.shape[2]
    share = width // count
    depth = 2 * share
    return pl.pallas_call(
        functools.partial(grad_qkv_kernel, count=count),
        grid_spec=pltpu.PrefetchScalarGridSpec(
            num_scalar_prefetch=1,
            grid=(width // depth,),
            in_specs=[pl.BlockSpec((tokens, depth), lambda i, p: (0, i))] * count
            + [pl.BlockSpec(dp_heads.shape, lambda i, p: (0, 0, 0))],
            out_specs=pl.BlockSpec((planes, share // planes, 2 * columns), lambda i, p: (0, 0, i)),
        ),
        out_shape=jax.ShapeDtypeStruct((planes, share // planes, count * columns), BF),
        compiler_params=pltpu.CompilerParams(vmem_limit_bytes=48 * 2**20),
        cost_estimate=SHORT,
        name="grad_qkv",
    )(places, *a_rows, dp_heads)


def swap_halves(values):
    width = values.shape[-1]
    lane = lax.broadcasted_iota(jnp.int32, values.shape, 1)
    ahead = pltpu.roll(values, width - HD // 2, 1)
    behind = pltpu.roll(values, HD // 2, 1)
    return jnp.where(lane % HD < HD // 2, ahead, behind)


def project_kernel(place_ref, x_ref, gain_ref, cos_ref, sin_ref, *refs, count):
    wq_refs, wkv_refs = refs[:count], refs[count : 2 * count]
    send_ref, normed_ref, inv_ref, normed_scr = refs[2 * count :]
    share = normed_scr.shape[2]

    @pl.when(pl.program_id(0) == 0)
    def _():
        x = x_ref[...].astype(F32)
        inv = lax.rsqrt(jnp.mean(x * x, axis=-1, keepdims=True) + EPSILON)
        normed = (x * inv * gain_ref[...]).astype(BF)
        normed_ref[...] = normed
        inv_ref[...] = inv
        for part in range(count):
            normed_scr[part] = normed[:, part * share : (part + 1) * share]

    pq = pkv = None
    for r in range(count):
        a_rows = normed_scr[place_ref[r]]
        q_part = jnp.dot(a_rows, wq_refs[r][...], preferred_element_type=F32)
        kv_part = jnp.dot(a_rows, wkv_refs[r][...], preferred_element_type=F32)
        pq = q_part if pq is None else pq + q_part
        pkv = kv_part if pkv is None else pkv + kv_part
    cos = cos_ref[...]
    sin = sin_ref[...]
    heads = pq.shape[1]
    q_scale = LOG2E * HD**-0.5
    turned = pq * jnp.tile(cos, (1, heads // 128)) + swap_halves(pq) * jnp.tile(sin, (1, heads // 128))
    send_ref[0, :, :heads] = (turned * q_scale).astype(BF)
    lane = lax.broadcasted_iota(jnp.int32, pkv.shape, 1)
    turned_kv = jnp.where(lane < HD, pkv * cos + swap_halves(pkv) * sin, pkv)
    send_ref[0, :, heads:] = turned_kv.astype(BF)


def project(places, x, gain, cos, sin, parts):
    rows, width = x.shape
    count = len(parts)
    heads = width // count
    out_width = heads + 2 * HD
    depth = parts[0].shape[0]
    first_kv = width // (2 * HD)
    return pl.pallas_call(
        functools.partial(project_kernel, count=count),
        grid_spec=pltpu.PrefetchScalarGridSpec(
            num_scalar_prefetch=1,
            grid=(count,),
            in_specs=[
                pl.BlockSpec((rows, width), lambda d, p: (0, 0)),
                pl.BlockSpec((1, width), lambda d, p: (0, 0)),
                pl.BlockSpec((rows, 128), lambda d, p: (0, 0)),
                pl.BlockSpec((rows, 128), lambda d, p: (0, 0)),
            ]
            + [pl.BlockSpec((depth, heads), lambda d, p: (0, d))] * count
            + [pl.BlockSpec((depth, 2 * HD), lambda d, p: (0, first_kv + d // 2))] * count,
            out_specs=[
                pl.BlockSpec((1, rows, out_width), lambda d, p: (d, 0, 0)),
                pl.BlockSpec((rows, width), lambda d, p: (0, 0)),
                pl.BlockSpec((rows, 1), lambda d, p: (0, 0)),
            ],
            scratch_shapes=[pltpu.VMEM((count, rows, width // count), BF)],
        ),
        out_shape=[
            jax.ShapeDtypeStruct((count, rows, out_width), BF),
            jax.ShapeDtypeStruct((rows, width), BF),
            jax.ShapeDtypeStruct((rows, 1), F32),
        ],
        compiler_params=pltpu.CompilerParams(vmem_limit_bytes=48 * 2**20),
        cost_estimate=SHORT,
        name="project",
    )(places, x, gain, cos, sin, *parts, *parts)


def out_proj_kernel(place_ref, attn_ref, x_ref, gain_ref, *refs, count):
    parts, (resid_ref, inv_ref, inner_ref) = refs[:count], refs[count:]
    width = x_ref.shape[1]
    tile = 512
    square = None
    for begin in range(0, width, tile):
        cols = slice(begin, begin + tile)
        total = x_ref[:, cols].astype(F32)
        for r in range(count):
            total = total + jnp.dot(attn_ref[place_ref[r]], parts[r][:, cols], preferred_element_type=F32)
        resid_ref[:, cols] = total
        part = jnp.sum(total * total, axis=-1, keepdims=True)
        square = part if square is None else square + part
    inv = lax.rsqrt(square / width + EPSILON)
    inv_ref[...] = inv
    inner_ref[...] = (resid_ref[...] * inv * gain_ref[...]).astype(BF)


def out_proj(places, attn, x, gain, parts):
    count, rows, share = attn.shape
    width = x.shape[1]
    step = rows // 2
    line = pl.BlockSpec((step, width), lambda i, p: (i, 0))
    return pl.pallas_call(
        functools.partial(out_proj_kernel, count=count),
        grid_spec=pltpu.PrefetchScalarGridSpec(
            num_scalar_prefetch=1,
            grid=(rows // step,),
            in_specs=[
                pl.BlockSpec((count, step, share), lambda i, p: (0, i, 0)),
                line,
                pl.BlockSpec((1, width), lambda i, p: (0, 0)),
            ]
            + [pl.BlockSpec((share, width), lambda i, p: (0, 0))] * count,
            out_specs=[line, pl.BlockSpec((step, 1), lambda i, p: (i, 0)), line],
        ),
        out_shape=[
            jax.ShapeDtypeStruct((rows, width), F32),
            jax.ShapeDtypeStruct((rows, 1), F32),
            jax.ShapeDtypeStruct((rows, width), BF),
        ],
        compiler_params=pltpu.CompilerParams(vmem_limit_bytes=56 * 2**20),
        cost_estimate=SHORT,
        name="out_proj",
    )(places, attn, x, gain, *parts)


def resid_back_kernel(place_ref, db_ref, first_ref, passed_ref, resid_ref, inv_ref, gain_ref, dy_ref, *refs, count):
    parts, (d_resid_ref, branch_ref, send_ref) = refs[:count], refs[count:]
    d_inner = db_ref[...].astype(F32) + first_ref[...].astype(F32) + passed_ref[...].astype(F32)
    resid = resid_ref[...]
    inv = inv_ref[...]
    scaled = d_inner * gain_ref[...]
    inner_mean = jnp.mean(scaled * resid, axis=-1, keepdims=True)
    d_resid = dy_ref[...].astype(F32) + inv * scaled - resid * (inv * inv * inv * inner_mean)
    d_resid_ref[...] = d_resid
    branch = d_resid.astype(BF)
    branch_ref[...] = branch
    for r in range(count):
        d_attn = lax.dot_general(branch, parts[r][...], NT, preferred_element_type=F32)
        send_ref[place_ref[r]] = d_attn.astype(BF)


def resid_back(places, db_own, db_first, db_passed, resid, inv, gain, dy, parts):
    rows, width = resid.shape
    count = len(parts)
    share = parts[0].shape[0]
    step = rows // 2
    line = pl.BlockSpec((step, width), lambda i, p: (i, 0))
    return pl.pallas_call(
        functools.partial(resid_back_kernel, count=count),
        grid_spec=pltpu.PrefetchScalarGridSpec(
            num_scalar_prefetch=1,
            grid=(rows // step,),
            in_specs=[line, line, line, line]
            + [pl.BlockSpec((step, 1), lambda i, p: (i, 0)), pl.BlockSpec((1, width), lambda i, p: (0, 0)), line]
            + [pl.BlockSpec((share, width), lambda i, p: (0, 0))] * count,
            out_specs=[line, line, pl.BlockSpec((count, step, share), lambda i, p: (0, i, 0))],
        ),
        out_shape=[
            jax.ShapeDtypeStruct((rows, width), F32),
            jax.ShapeDtypeStruct((rows, width), BF),
            jax.ShapeDtypeStruct((count, rows, share), BF),
        ],
        compiler_params=pltpu.CompilerParams(vmem_limit_bytes=56 * 2**20),
        cost_estimate=SHORT,
        name="resid_back",
    )(places, db_own, db_first, db_passed, resid, inv, gain, dy, *parts)


def in_back_kernel(place_ref, back_ref, x_ref, inv_ref, gain_ref, d_resid_ref, *refs, count):
    parts, (out_ref, mixed, d_scr) = refs[:count], refs[count:]
    devices, _, width = back_ref.shape
    heads = width - 2 * HD
    for d in range(devices):
        mixed[:, d * heads : (d + 1) * heads] = back_ref[d, :, :heads]
    base = devices * heads
    for g in range(KV):
        pair = back_ref[2 * g, :, heads:].astype(F32) + back_ref[2 * g + 1, :, heads:].astype(F32)
        mixed[:, base + 2 * g * HD : base + 2 * (g + 1) * HD] = pair.astype(BF)
    for r in range(count):
        d_scr[place_ref[r]] = lax.dot_general(mixed[...], parts[r][...], NT, preferred_element_type=F32)
    inv = inv_ref[...]
    share = d_scr.shape[2]
    inner = None
    for c in range(count):
        cols = slice(c * share, (c + 1) * share)
        part = jnp.sum(d_scr[c] * gain_ref[:, cols] * x_ref[:, cols].astype(F32), axis=-1, keepdims=True)
        inner = part if inner is None else inner + part
    factor = inv * inv * inv * (inner / (count * share))
    for c in range(count):
        cols = slice(c * share, (c + 1) * share)
        through = inv * (d_scr[c] * gain_ref[:, cols]) - x_ref[:, cols].astype(F32) * factor
        out_ref[:, cols] = (d_resid_ref[:, cols] + through).astype(BF)


def in_back(places, back, x, inv, gain, d_resid, parts):
    rows, width = x.shape
    count = len(parts)
    share, columns = parts[0].shape
    step = rows // 2
    line = pl.BlockSpec((step, width), lambda i, p: (i, 0))
    return pl.pallas_call(
        functools.partial(in_back_kernel, count=count),
        grid_spec=pltpu.PrefetchScalarGridSpec(
            num_scalar_prefetch=1,
            grid=(rows // step,),
            in_specs=[
                pl.BlockSpec((count, step, back.shape[2]), lambda i, p: (0, i, 0)),
                line,
                pl.BlockSpec((step, 1), lambda i, p: (i, 0)),
                pl.BlockSpec((1, width), lambda i, p: (0, 0)),
                line,
            ]
            + [pl.BlockSpec((share, columns), lambda i, p: (0, 0))] * count,
            out_specs=line,
            scratch_shapes=[pltpu.VMEM((step, columns), BF), pltpu.VMEM((count, step, share), F32)],
        ),
        out_shape=jax.ShapeDtypeStruct((rows, width), BF),
        compiler_params=pltpu.CompilerParams(vmem_limit_bytes=56 * 2**20),
        cost_estimate=SHORT,
        name="in_back",
    )(places, back, x, inv, gain, d_resid, *parts)


def grad_wo_kernel(core_ref, keep_ref, give_ref, branch_ref, keep_out, give_out):
    branch = branch_ref[...]
    keep_out[0] = lax.dot_general(keep_ref[0], branch, TN, preferred_element_type=F32).astype(BF)
    give_out[0] = lax.dot_general(give_ref[0], branch, TN, preferred_element_type=F32).astype(BF)


def grad_wo(core, attn, branch):
    devices, rows, share = attn.shape
    width = branch.shape[1]
    out = pl.BlockSpec((1, share, width), lambda c, core: (c, 0, 0))
    return pl.pallas_call(
        grad_wo_kernel,
        grid_spec=pltpu.PrefetchScalarGridSpec(
            num_scalar_prefetch=1,
            grid=(devices // 2,),
            in_specs=[
                pl.BlockSpec((1, rows, share), lambda c, core: (2 * c + core[0], 0, 0)),
                pl.BlockSpec((1, rows, share), lambda c, core: (2 * c + 1 - core[0], 0, 0)),
                pl.BlockSpec((rows, width), lambda c, core: (0, 0)),
            ],
            out_specs=[out, out],
        ),
        out_shape=[jax.ShapeDtypeStruct((devices // 2, share, width), BF)] * 2,
        compiler_params=pltpu.CompilerParams(vmem_limit_bytes=48 * 2**20),
        cost_estimate=SHORT,
        name="grad_wo",
    )(core.reshape(1), attn, attn, branch)


def grad_dn_kernel(core_ref, *refs, count):
    left, right, (keep_out, give_out) = refs[:count], refs[count : 2 * count], refs[2 * count :]
    total = None
    for r in range(count):
        part = lax.dot_general(left[r][...], right[r][...], TN, preferred_element_type=F32)
        total = part if total is None else total + part
    half = total.shape[0] // 2
    total = total.astype(BF)
    low = core_ref[0] == 0
    keep_out[...] = jnp.where(low, total[:half], total[half:])
    give_out[...] = jnp.where(low, total[half:], total[:half])


def grad_dn(core, hid_rows, dy_rows):
    count = len(hid_rows)
    tokens, hidden = hid_rows[0].shape
    width = dy_rows[0].shape[1]
    tile = 512
    out = pl.BlockSpec((hidden // 2, tile), lambda i, core: (0, i))
    return pl.pallas_call(
        functools.partial(grad_dn_kernel, count=count),
        grid_spec=pltpu.PrefetchScalarGridSpec(
            num_scalar_prefetch=1,
            grid=(width // tile,),
            in_specs=[pl.BlockSpec((tokens, hidden), lambda i, core: (0, 0))] * count
            + [pl.BlockSpec((tokens, tile), lambda i, core: (0, i))] * count,
            out_specs=[out, out],
        ),
        out_shape=[jax.ShapeDtypeStruct((hidden // 2, width), BF)] * 2,
        compiler_params=pltpu.CompilerParams(vmem_limit_bytes=56 * 2**20),
        cost_estimate=SHORT,
        name="grad_dn",
    )(core.reshape(1), *hid_rows, *dy_rows)


def attend_kernel(zeros_ref, q_ref, kv_ref, *refs, heads, start, stop):
    o_ref, send_ref, lse_ref, k_scr, v_scr, acc_ref, max_ref = refs[-7:]
    block = pl.program_id(0) + start
    zeros = zeros_ref[0]
    size = q_ref.shape[0]

    @pl.when(block == start)
    def _():
        for part in range(stop):
            rows = slice(part * size, (part + 1) * size)
            both = kv_ref[rows, :].astype(F32)
            lane = lax.broadcasted_iota(jnp.int32, both.shape, 1)
            k_scr[rows, :] = kv_ref[rows, :HD]
            v_scr[rows, :] = jnp.where(lane < HD, pltpu.roll(both, HD, 1), 1.0).astype(BF)

    first_row = block * size
    lowest = jnp.where(first_row >= zeros, zeros // size, 0)
    acc_ref[...] = jnp.zeros_like(acc_ref)
    max_ref[...] = jnp.full_like(max_ref, MASKED)
    q_heads = [q_ref[:, h * HD : (h + 1) * HD] for h in range(heads)]

    def step(index, masked):
        first_key = pl.multiple_of(index * size, size)
        keys = k_scr[pl.ds(first_key, size), :]
        values = v_scr[pl.ds(first_key, size), :]
        if masked:
            row = first_row + lax.broadcasted_iota(jnp.int32, (size, size), 0)
            col = first_key + lax.broadcasted_iota(jnp.int32, (size, size), 1)
            begin = jnp.where(row >= zeros, zeros, 0)
            refused = (col > row) | (col < begin)

        def score(h):
            return lax.dot_general(q_heads[h], keys, NT, preferred_element_type=F32)

        upcoming = score(0)
        for h in range(heads):
            scores = upcoming
            if h + 1 < heads:
                upcoming = score(h + 1)
            if masked:
                scores = jnp.where(refused, MASKED, scores)
            old_max = max_ref[h]
            new_max = jnp.maximum(old_max, jnp.max(scores, axis=-1, keepdims=True))
            weights = jnp.exp2(scores - jnp.tile(new_max, (1, size // 128)))
            shrink = jnp.exp2(old_max - new_max)
            acc_ref[h] = acc_ref[h] * shrink + jnp.dot(weights.astype(BF), values, preferred_element_type=F32)
            max_ref[h] = new_max

    def visit(index, carry):
        first_key = index * size
        mixed = (index == block) | ((first_row + size > zeros) & (first_key < zeros))

        @pl.when(mixed)
        def _():
            step(index, True)

        @pl.when(jnp.logical_not(mixed))
        def _():
            step(index, False)

        return carry

    lax.fori_loop(lowest, block + 1, visit, 0)
    for h in range(heads):
        acc = acc_ref[h]
        total = acc[:, HD : HD + 1]
        out = acc[:, :HD] / total
        o_ref[:, h * HD : (h + 1) * HD] = out
        send_ref[0, :, h * HD : (h + 1) * HD] = out.astype(BF)
        lse = max_ref[h] + jnp.log2(total)
        lse_ref[0, h : h + 1, :] = jnp.transpose(lse)[:1]


def attend(zeros, qkv, start, stop, before=None):
    length, width = qkv.shape
    q_width = width - 2 * HD
    heads = q_width // HD
    size = BLOCK
    blocks = length // size
    before = () if before is None else before
    return pl.pallas_call(
        functools.partial(attend_kernel, heads=heads, start=start, stop=stop),
        grid_spec=pltpu.PrefetchScalarGridSpec(
            num_scalar_prefetch=1,
            grid=(stop - start,),
            in_specs=[
                pl.BlockSpec((size, q_width), lambda i, z: (i + start, 0)),
                pl.BlockSpec((length, 2 * HD), lambda i, z: (0, q_width // (2 * HD))),
            ]
            + [pl.BlockSpec(memory_space=pl.ANY)] * len(before),
            out_specs=[
                pl.BlockSpec((size, q_width), lambda i, z: (i + start, 0)),
                pl.BlockSpec((1, size, q_width), lambda i, z: (i + start, 0, 0)),
                pl.BlockSpec((1, heads, size), lambda i, z: (i + start, 0, 0)),
            ],
            scratch_shapes=[
                pltpu.VMEM((length, HD), BF),
                pltpu.VMEM((length, 2 * HD), BF),
                pltpu.VMEM((heads, size, 2 * HD), F32),
                pltpu.VMEM((heads, size, 128), F32),
            ],
        ),
        out_shape=[
            jax.ShapeDtypeStruct((length, q_width), F32),
            jax.ShapeDtypeStruct((blocks, size, q_width), BF),
            jax.ShapeDtypeStruct((blocks, heads, size), F32),
        ],
        input_output_aliases={3 + i: i for i in range(len(before))},
        compiler_params=pltpu.CompilerParams(vmem_limit_bytes=48 * 2**20),
        cost_estimate=SHORT,
        name="attend",
    )(zeros, qkv, qkv, *before)


def attend_back_kernel(
    zeros_ref, q_ref, kv_ref, do_ref, lse_ref, cos_ref, sin_ref, extra_ref, *refs, heads, start
):
    send_ref, dq_acc, delta_ref, q_scr, do_scr = refs[-5:]
    block = pl.program_id(0) + start
    zeros = zeros_ref[0]
    size = kv_ref.shape[0]
    length = q_ref.shape[0]
    blocks = length // size

    @pl.when(block == start)
    def _():
        if start == 0:
            dq_acc[...] = jnp.zeros_like(dq_acc)
        else:
            dq_acc[...] = refs[0][...]
            delta_ref[...] = extra_ref[...]
        for part in range(start, blocks):
            rows = slice(part * size, (part + 1) * size)
            if start == 0:
                product = jnp.transpose(do_ref[rows, :].astype(F32) * extra_ref[rows, :])
            for h in range(heads):
                cols = slice(h * HD, (h + 1) * HD)
                q_scr[h, rows, :] = q_ref[rows, cols]
                do_scr[h, rows, :] = do_ref[rows, cols]
                if start == 0:
                    delta_ref[part, h : h + 1, :] = jnp.sum(product[cols], axis=0, keepdims=True)

    first_key = block * size
    both = kv_ref[...]
    keys = both[:, :HD]
    values = both[:, HD:]
    keys_t = jnp.transpose(keys.astype(F32)).astype(BF)
    highest = jnp.where(first_key + size <= zeros, jnp.minimum((zeros + size - 1) // size, blocks), blocks)

    def step(index, carry, masked):
        first_row = pl.multiple_of(index * size, size)
        span = pl.ds(first_row, size)
        if masked:
            col = first_key + lax.broadcasted_iota(jnp.int32, (size, size), 0)
            row = first_row + lax.broadcasted_iota(jnp.int32, (size, size), 1)
            begin = jnp.where(row >= zeros, zeros, 0)
            refused = (col > row) | (col < begin)

        def products(h):
            q_rows = q_scr[h, span, :]
            do_rows = do_scr[h, span, :]
            scores = lax.dot_general(keys, q_rows, NT, preferred_element_type=F32)
            d_prob = lax.dot_general(values, do_rows, NT, preferred_element_type=F32)
            return q_rows, do_rows, scores, d_prob

        upcoming = products(0)
        dk_sum, dv_sum = carry
        for h in range(heads):
            q_rows, do_rows, scores, d_prob = upcoming
            if h + 1 < heads:
                upcoming = products(h + 1)
            shifted = scores - lse_ref[index, h : h + 1, :]
            if masked:
                shifted = jnp.where(refused, MASKED, shifted)
            prob = jnp.exp2(shifted)
            d_score = (prob * (d_prob - delta_ref[index, h : h + 1, :])).astype(BF)
            dv_sum = dv_sum + jnp.dot(prob.astype(BF), do_rows, preferred_element_type=F32)
            dk_sum = dk_sum + jnp.dot(d_score, q_rows, preferred_element_type=F32)
            dq_acc[h * HD : (h + 1) * HD, span] += jnp.dot(keys_t, d_score, preferred_element_type=F32)
        return dk_sum, dv_sum

    def visit(index, carry):
        first_row = index * size
        mixed = (index == block) | ((first_row + size > zeros) & (first_key < zeros))
        return lax.cond(
            mixed,
            lambda c: step(index, c, True),
            lambda c: step(index, c, False),
            carry,
        )

    zero = jnp.zeros((size, HD), F32)
    dk_sum, dv_sum = lax.fori_loop(block, highest, visit, (zero, zero))
    q_width = heads * HD
    done = pl.ds(pl.multiple_of(first_key, size), size)
    cos = cos_ref[...]
    sin = sin_ref[...]
    dq = jnp.transpose(dq_acc[:, done]) * HD**-0.5
    dq = dq * jnp.tile(cos, (1, q_width // 128)) - swap_halves(dq) * jnp.tile(sin, (1, q_width // 128))
    send_ref[0, :, :q_width] = dq.astype(BF)
    dkv = jnp.concatenate([dk_sum * (1.0 / LOG2E), dv_sum], axis=1)
    lane = lax.broadcasted_iota(jnp.int32, dkv.shape, 1)
    send_ref[0, :, q_width:] = jnp.where(lane < HD, dkv * cos - swap_halves(dkv) * sin, dkv).astype(BF)


def attend_back(zeros, qkv, d_out, lse, cos, sin, start, stop, out=None, before=None):
    length, width = qkv.shape
    q_width = width - 2 * HD
    heads = q_width // HD
    size = BLOCK
    blocks = length // size
    whole = lambda *shape: pl.BlockSpec(shape, lambda j, z: (0,) * len(shape))
    if before is None:
        operands = (out,)
        specs = [whole(length, q_width)]
        aliases = {}
    else:
        send, d_query, delta = before
        operands = (delta, d_query, send)
        specs = [whole(blocks, heads, size), whole(q_width, length), pl.BlockSpec(memory_space=pl.ANY)]
        aliases = {9: 0}
    return pl.pallas_call(
        functools.partial(attend_back_kernel, heads=heads, start=start),
        grid_spec=pltpu.PrefetchScalarGridSpec(
            num_scalar_prefetch=1,
            grid=(stop - start,),
            in_specs=[
                whole(length, q_width),
                pl.BlockSpec((size, 2 * HD), lambda j, z: (j + start, q_width // (2 * HD))),
                whole(length, q_width),
                whole(blocks, heads, size),
                pl.BlockSpec((size, 128), lambda j, z: (j + start, 0)),
                pl.BlockSpec((size, 128), lambda j, z: (j + start, 0)),
            ]
            + specs,
            out_specs=[
                pl.BlockSpec((1, size, width), lambda j, z: (j + start, 0, 0)),
                whole(q_width, length),
                whole(blocks, heads, size),
            ],
            scratch_shapes=[
                pltpu.VMEM((heads, length, HD), BF),
                pltpu.VMEM((heads, length, HD), BF),
            ],
        ),
        out_shape=[
            jax.ShapeDtypeStruct((blocks, size, width), BF),
            jax.ShapeDtypeStruct((q_width, length), F32),
            jax.ShapeDtypeStruct((blocks, heads, size), F32),
        ],
        input_output_aliases=aliases,
        compiler_params=pltpu.CompilerParams(vmem_limit_bytes=58 * 2**20),
        cost_estimate=SHORT,
        name="attend_back",
    )(zeros, qkv, qkv, d_out, lse, cos, sin, *operands)


def turn_tables(positions):
    cosine, sine = rope_tables(positions, HD)
    return jnp.concatenate([cosine] * 4, axis=1), jnp.concatenate([-sine, sine, -sine, sine], axis=1)


def fast_body(tokens, segment_ids, selected, cotangent, w_qkv, w_out, w_gate_up, w_down, g_attn, g_mlp):
    _, rows, width = tokens.shape
    devices = 2 * CHIPS
    me = lax.axis_index("sp")
    core = me & 1
    planes = lax.axis_size("dp")
    share = width // devices
    kv_width = KV * HD
    first_mask, second_mask = rel_masks(core)
    other = me ^ 1
    chip = me // 2
    place_list = [me, me ^ first_mask, me ^ second_mask, me ^ 6]
    place_list += [other, other ^ second_mask, other ^ first_mask, other ^ 6]
    places = jnp.stack(place_list)
    hidden_chip = 2 * w_down.shape[0]
    quarter = share // planes
    plane = lax.axis_index("dp")
    length = devices * rows
    blocks = length // BLOCK

    count = jnp.sum((segment_ids == 0).astype(F32))
    vectors = jnp.stack([g_attn.astype(F32), g_mlp.astype(F32)] + [jnp.full((share,), count)] * 6)
    paired = [w_qkv[:, :width]]
    for head in range(KV):
        paired.append(w_qkv[:, width + head * HD : width + (head + 1) * HD])
        paired.append(w_qkv[:, width + kv_width + head * HD : width + kv_width + (head + 1) * HD])
    qkv_own = jnp.concatenate(paired, axis=1)
    gu_rows = lax.dynamic_slice_in_dim(w_gate_up, plane * quarter, quarter, 0)
    gu_send = []
    for place in range(CHIPS):
        for begin in (place * hidden_chip, (CHIPS + place) * hidden_chip):
            gu_send.append(gu_rows[:, begin : begin + hidden_chip])
    gu_send = jnp.stack([jnp.concatenate(gu_send[2 * c : 2 * c + 2], axis=1) for c in range(CHIPS)])
    vectors = gather_vectors(vectors, me)
    vectors, qkv_own, gu_send = fence(vectors, qkv_own, gu_send)
    qkv_first = send_first(qkv_own)
    attn_gain = vectors[0:1]
    mlp_gain = vectors[1:2]
    zeros = jnp.sum(vectors[2].reshape(devices, share)[:, 0]).astype(jnp.int32)
    zeros_one = zeros.reshape(1)
    local_pos = me * rows + jnp.arange(rows, dtype=jnp.int32) - segment_ids.reshape(rows) * zeros
    cos, sin = turn_tables(local_pos)
    dy = (cotangent * selected[:, :, None].astype(BF)).reshape(rows, width)
    qkv_own, qkv_first, cos, sin = fence(qkv_own, qkv_first, cos, sin)
    qkv_second = send_second(qkv_own)
    qkv_theirs = [send_sibling(qkv_own), send_sibling(qkv_first)]
    all_places = jnp.arange(length, dtype=jnp.int32)
    cos_all, sin_all = turn_tables(all_places - jnp.where(all_places >= zeros, zeros, 0))
    qkv_first, qkv_second, cos_all, sin_all, *qkv_theirs = fence(qkv_first, qkv_second, cos_all, sin_all, *qkv_theirs)
    qkv_far = send_second(qkv_first)
    qkv_theirs.append(send_sibling(qkv_second))
    qkv_far, dy, *qkv_theirs = fence(qkv_far, dy, *qkv_theirs)
    qkv_theirs.append(send_sibling(qkv_far))
    qkv_parts = [qkv_own, qkv_first, qkv_second, qkv_far] + qkv_theirs
    x_bf = tokens.reshape(rows, width)
    x_bf, w_out, gu_send, *qkv_parts = fence(x_bf, w_out, gu_send, *qkv_parts)
    out_first = send_first(w_out)
    gu_part = lax.all_to_all(gu_send, "sp", 0, 0, axis_index_groups=SAME_CORE, tiled=True)
    qkv_send, normed, inv_one = project(places, x_bf, attn_gain, cos, sin, qkv_parts)
    qkv_send, out_first = fence(qkv_send, out_first)
    gu_mine = lax.all_gather(after(gu_part, qkv_send), "dp", axis=0, tiled=False)
    gu_mine = lax.all_gather(after(gu_part, qkv_send), "dp", axis=0, tiled=False)
    down_theirs = send_sibling(w_down)
    w_dn = jnp.where(
        core == 0, jnp.concatenate([w_down, down_theirs], axis=0), jnp.concatenate([down_theirs, w_down], axis=0)
    )
    qkv_heads = lax.all_to_all(qkv_send, "sp", 0, 0, tiled=True).reshape(length, qkv_send.shape[2])

    cuts = (0, (5 * blocks) // 8, (7 * blocks) // 8, blocks)
    qkv_heads, w_dn, out_first = fence(qkv_heads, w_dn, out_first)
    out_second = send_second(after(w_out, qkv_heads))
    dy_first = send_first(after(dy, qkv_heads))
    fwd = attend(zeros_one, qkv_heads, cuts[0], cuts[1])
    qkv_heads, out_second, dy_first, out_first, dy, *fwd = fence(qkv_heads, out_second, dy_first, out_first, dy, *fwd)
    out_far = send_second(out_first)
    dy_second = send_second(dy)
    fwd = attend(zeros_one, qkv_heads, cuts[1], cuts[2], fwd)
    qkv_heads, out_far, dy_second, dy_first, *fwd = fence(qkv_heads, out_far, dy_second, dy_first, *fwd)
    dy_far = send_second(dy_first)
    gu_theirs = send_sibling(after(gu_mine, fwd[2]))
    out_heads, out_send, lse = attend(zeros_one, qkv_heads, cuts[2], cuts[3], fwd)
    out_parts = [w_out, out_first, out_second, out_far]
    out_parts = out_parts + [send_sibling(part) for part in out_parts]
    out_send, gu_mine, gu_theirs = fence(out_send, gu_mine, gu_theirs)
    attn_tok = lax.all_to_all(out_send, "sp", 0, 0, tiled=True)
    w_gu = join(core, gu_mine, gu_theirs)
    attn_tok, w_gu, dy_far, *out_parts = fence(attn_tok, w_gu, dy_far, *out_parts)
    residual, inv_two, inner = out_proj(places, attn_tok, x_bf, mlp_gain, out_parts)

    b_first = send_first(inner)
    own = ffn(inner, dy, w_gu, w_dn)
    inner, b_first, *own = fence(inner, b_first, *own)
    b_second = send_second(inner)
    first = ffn(b_first, dy_first, w_gu, w_dn)
    b_first, b_second, *first = fence(b_first, b_second, *first)
    b_far = send_second(b_first)
    second = ffn(b_second, dy_second, w_gu, w_dn)
    b_far, db_first, *second = fence(b_far, first[3], *second)
    db_got_first = send_first(db_first)
    far = ffn(b_far, dy_far, w_gu, w_dn)
    db_got_first, db_far, *hid_rows = fence(db_got_first, far[3], own[0], first[0], second[0], far[0])

    b_rows = [inner, b_first, b_second, b_far]
    db_got_far = send_first(db_far)
    gu_keep, gu_give = grad_gu(
        core,
        b_rows,
        [own[1], first[1], second[1], far[1]],
        [own[2], first[2], second[2], far[2]],
        share,
        planes,
    )
    db_got_far, gu_keep, gu_give, *hid_rows = fence(db_got_far, gu_keep, gu_give, *hid_rows)
    db_pass = (second[3].astype(F32) + db_got_far.astype(F32)).astype(BF)
    db_pass, gu_give, *hid_rows = fence(db_pass, gu_give, *hid_rows)
    db_passed = send_second(db_pass)
    gu_got = send_sibling(gu_give)
    dn_keep, dn_give = grad_dn(core, hid_rows, [dy, dy_first, dy_second, dy_far])
    gu_got, dn_keep, dn_give = fence(gu_got, dn_keep, dn_give)
    gu_sum = (gu_keep.astype(F32) + gu_got.astype(F32)).astype(BF)
    gu_sum, db_passed, dn_give = fence(gu_sum, db_passed, dn_give)
    gu_z = lax.psum_scatter(
        gu_sum.reshape(planes * CHIPS * quarter, 2 * hidden_chip), "dp", scatter_dimension=0, tiled=True
    )
    gu_z = gu_z.reshape(CHIPS, quarter, 2 * hidden_chip)
    dn_got = send_sibling(dn_give)
    d_resid, d_branch, d_send = resid_back(
        places, own[3], db_got_first, db_passed, residual, inv_two, mlp_gain, dy, out_parts
    )
    d_send, d_branch, dn_got = fence(d_send, d_branch, dn_got)
    d_heads = lax.all_to_all(d_send, "sp", 0, 0, tiled=True).reshape(length, share)
    wo_keep, wo_give = grad_wo(core, attn_tok, d_branch)
    dn_sum = (dn_keep.astype(F32) + dn_got.astype(F32)).astype(BF)
    d_heads, wo_keep, wo_give, normed, dn_sum = fence(d_heads, wo_keep, wo_give, normed, dn_sum)

    def back_call(heads, start, stop, **kwargs):
        return attend_back(zeros_one, qkv_heads, heads, lse, cos_all, sin_all, start, stop, **kwargs)

    turns = (0, blocks // 4, (3 * blocks) // 8, blocks)
    wo_got = send_sibling(wo_give)
    a_first = send_first(normed)
    a_second = send_second(normed)
    a_theirs = [send_sibling(normed)]
    bwd = back_call(d_heads, turns[0], turns[1], out=out_heads)
    d_heads, a_first, a_second, wo_got, gu_z, dn_sum, *moves = fence(
        d_heads, a_first, a_second, wo_got, gu_z, dn_sum, *a_theirs, *bwd
    )
    a_theirs, bwd = moves[:1], moves[1:]

    def wo_part(place):
        return pick(wo_keep, place).astype(F32) + pick(wo_got, place).astype(F32)

    dn_z = lax.psum_scatter(dn_sum, "dp", scatter_dimension=0, tiled=True)
    gu_z = lax.all_to_all(gu_z, "sp", 0, 0, axis_index_groups=SAME_CORE, tiled=True)
    a_theirs += [send_sibling(a_first), send_sibling(a_second)]
    bwd = back_call(d_heads, turns[1], turns[2], before=bwd)
    d_heads, gu_z, a_first, *moves = fence(d_heads, gu_z, a_first, *a_theirs, *bwd)
    a_theirs, bwd = moves[:3], moves[3:]

    wo_first = wo_part(chip ^ (first_mask // 2)).astype(BF)
    wo_far = wo_part(chip ^ 3).astype(BF)
    d_heads, gu_z, a_first, wo_first, wo_far = fence(d_heads, gu_z, a_first, wo_first, wo_far)
    gu_all = lax.all_gather(gu_z, "dp", axis=0, tiled=False)
    a_far = send_second(a_first)
    wo_far = send_first(wo_far)
    wo_first = send_first(wo_first)
    bwd = back_call(d_heads, turns[2], turns[3], before=bwd)
    wo_pass = (wo_part(chip ^ (second_mask // 2)) + wo_far.astype(F32)).astype(BF)
    dp_heads, wo_first, wo_pass, a_far, dn_z = fence(bwd[0], wo_first, wo_pass, a_far, dn_z)

    wo_passed = send_second(wo_pass)
    a_theirs.append(send_sibling(a_far))
    back = lax.all_to_all(dp_heads, "sp", 0, 0, tiled=True)
    grad_wq = grad_qkv(places, [normed, a_first, a_second, a_far] + list(a_theirs), dp_heads, planes)
    wo_passed, grad_wq = fence(wo_passed, grad_wq)
    wo_rows = (wo_part(chip) + wo_first.astype(F32) + wo_passed.astype(F32)).astype(BF)
    split = grad_wq.shape[2]
    last_parts = [jnp.concatenate([grad_wq, wo_rows.reshape(planes, quarter, width)], axis=2)]
    y_far, y_first = far[4], first[4]
    moves = None
    for step in range(1, planes):
        moves = line_scatter_sends(last_parts, moves, step, 0)
        y_far, y_first, *moves = fence(y_far, y_first, *moves)
        moves = line_scatter_move(moves, step)
        if step == 1:
            dn_all = lax.all_gather(dn_z, "dp", axis=0, tiled=False)
            back, *moves = fence(back, *moves)
        elif step == 2:
            y_got_far = send_first(y_far)
            y_got_far, gu_all, *moves = fence(y_got_far, gu_all, *moves)
        moves = fence(*moves)
    last_z = line_scatter_end(last_parts, moves, 0)
    wq_z = last_z[:, :split].reshape(quarter, devices, split // devices).transpose(1, 0, 2)
    wq_z, wo_z, gu_all = fence(wq_z, last_z[:, split:], gu_all)
    wq_z = lax.all_to_all(wq_z, "sp", 0, 0, tiled=True)
    grad_tokens = in_back(places, back, x_bf, inv_one, attn_gain, d_resid, qkv_parts).reshape(tokens.shape)
    y_pass = (second[4].astype(F32) + y_got_far.astype(F32)).astype(BF)
    last_z = jnp.concatenate([wq_z.transpose(1, 0, 2).reshape(quarter, split), wo_z], axis=1)
    last_z, grad_tokens, y_pass, y_first = fence(last_z, grad_tokens, y_pass, y_first)
    y_got_first = send_first(y_first)
    y_passed = send_second(y_pass)
    last_steps = [(last_z, last_z)]
    outs = []
    for step in range(1, planes):
        if step == planes - 1:
            y_got_first, y_passed, *moves = fence(y_got_first, y_passed, *last_steps[-1])
            last_steps[-1] = tuple(moves)
        last_steps.append(line_gather_move(last_steps[-1], step))
        if step == 1:
            outs += spread(gu_all, w_gate_up, g_mlp.astype(F32).reshape(share, 1))
        elif step == 2:
            outs.append(dn_all.astype(F32).reshape(w_down.shape))
        if step == planes - 1:
            y_sum = own[4].astype(F32) + y_got_first.astype(F32) + y_passed.astype(F32)
            outs.append((residual + y_sum).astype(BF).reshape(tokens.shape))
        moves = fence(*last_steps[-1], *outs)
        last_steps[-1], outs = tuple(moves[:2]), list(moves[2:])
    grad_w_gate_up, grad_g_mlp, grad_w_down, output = outs
    grad_w_qkv, grad_g_attn, grad_w_out = spread_last(last_steps, w_qkv, g_attn.astype(F32).reshape(share, 1), width)
    return (
        output,
        grad_tokens,
        grad_w_qkv,
        grad_w_out,
        grad_w_gate_up,
        grad_w_down,
        grad_g_attn.reshape(share),
        grad_g_mlp.reshape(share),
    )


def solution(mesh):
    in_specs = (
        P("dp", "sp", None),
        P("dp", "sp"),
        P("dp", "sp"),
        P("dp", "sp", None),
        P("sp", None),
        P("sp", None),
        P("sp", None),
        P("sp", None),
        P("sp"),
        P("sp"),
    )
    out_specs = (
        P("dp", "sp", None),
        P("dp", "sp", None),
        P("sp", None),
        P("sp", None),
        P("sp", None),
        P("sp", None),
        P("sp"),
        P("sp"),
    )
    body = fast_body if dict(mesh.shape) == {"dp": 4, "sp": 2 * CHIPS} else general_body
    return jax.shard_map(body, mesh=mesh, in_specs=in_specs, out_specs=out_specs, check_vma=False)
```

```python
import functools
import math

import jax
import jax.numpy as jnp
from jax import lax
from jax.experimental import pallas as pl
from jax.experimental.pallas import tpu as pltpu
from jax.sharding import PartitionSpec as P

D = 2048
H = 32
KV = 4
HD = 64
FF = 5632


EPSILON = 1e-05
ROPE_BASE = 10000.0
MASKED = -1e30


def rope_tables(positions, head_size):
    half_dim = head_size // 2
    frequency = ROPE_BASE ** (-(jnp.arange(half_dim, dtype=jnp.float32) * 2.0 / head_size))
    angles = positions.astype(jnp.float32)[:, None] * frequency[None, :]
    return (jnp.cos(angles), jnp.sin(angles))


def rotate(values, cosine, sine_tab, inverse_turn):
    half_dim = values.shape[-1] // 2
    first_half = values[..., :half_dim]
    second = values[..., half_dim:]
    cos_wide = cosine[:, None, :]
    sin_wide = sine_tab[:, None, :]
    if inverse_turn:
        sin_wide = -sin_wide
    return jnp.concatenate(
        [first_half * cos_wide - second * sin_wide, second * cos_wide + first_half * sin_wide],
        axis=-1,
    )


def rms_norm(values, gain_vec):
    inverse = lax.rsqrt(jnp.mean(values * values, axis=-1, keepdims=True) + EPSILON)
    return (values * inverse * gain_vec, inverse)


def norm_back(values, inverse, gain_vec, upstream):
    scaled = upstream * gain_vec
    inner_mean = jnp.mean(scaled * values, axis=-1, keepdims=True)
    through = inverse * scaled - values * inverse**3 * inner_mean
    gain_grad = jnp.sum(upstream * values * inverse, axis=0)
    return (through, gain_grad)


def attention_inputs(flat_in, qkv_full, gain_vec, cosine, sine_tab):
    row_count = flat_in.shape[0]
    group_size = H // KV
    normed, inverse = rms_norm(flat_in, gain_vec)
    normed = normed.astype(jnp.bfloat16)
    projected = jnp.dot(normed, qkv_full, preferred_element_type=jnp.float32)
    queries = rotate(projected[:, :D].reshape(row_count, H, HD), cosine, sine_tab, False)
    key_heads = rotate(
        projected[:, D : D + KV * HD].reshape(row_count, KV, HD), cosine, sine_tab, False
    )
    value_heads = projected[:, D + KV * HD :].reshape(row_count, KV, HD)
    key_wide = jnp.broadcast_to(key_heads[:, :, None], (row_count, KV, group_size, HD)).reshape(
        row_count, D
    )
    value_wide = jnp.broadcast_to(value_heads[:, :, None], (row_count, KV, group_size, HD)).reshape(
        row_count, D
    )
    stacked = jnp.stack([queries.reshape(row_count, D), key_wide, value_wide]).astype(jnp.bfloat16)
    return (normed, inverse, stacked)


def block_mask(seg_full, position, row_begin, finish):
    row_seg = seg_full[:, row_begin:finish]
    col_seg = seg_full[:, :finish]
    same_doc = row_seg[:, :, None] == col_seg[:, None, :]
    causal = position[row_begin:finish, None] >= position[None, :finish]
    return same_doc & causal[None]


def attention_forward(queries, key_heads, value_heads, seg_full, score_scale):
    length = queries.shape[1]
    block_rows = min(512, length)
    position = jnp.arange(length, dtype=jnp.int32)
    outputs = []
    lse_parts = []
    for block_num in range(length // block_rows):
        row_begin = block_num * block_rows
        finish = row_begin + block_rows
        scores = (
            jnp.einsum(
                "sqhd,skhd->shqk",
                queries[:, row_begin:finish],
                key_heads[:, :finish],
                preferred_element_type=jnp.float32,
            )
            * score_scale
        )
        allowed = block_mask(seg_full, position, row_begin, finish)
        scores = jnp.where(allowed[:, None], scores, MASKED)
        row_max = jnp.max(scores, axis=-1, keepdims=True)
        shifted = jnp.exp(scores - row_max)
        row_total = jnp.sum(shifted, axis=-1, keepdims=True)
        softmax_w = (shifted / row_total).astype(jnp.bfloat16)
        outputs.append(
            jnp.einsum(
                "shqk,skhd->sqhd",
                softmax_w,
                value_heads[:, :finish],
                preferred_element_type=jnp.float32,
            )
        )
        lse_parts.append(row_max + jnp.log(row_total))
    return (jnp.concatenate(outputs, axis=1), jnp.concatenate(lse_parts, axis=2))


def attention_backward(queries, key_heads, value_heads, seg_full, log_sums, grad_out, score_scale):
    length = queries.shape[1]
    block_rows = min(512, length)
    position = jnp.arange(length, dtype=jnp.int32)
    grad_query = []
    grad_key = jnp.zeros(key_heads.shape, jnp.float32)
    grad_value = jnp.zeros(value_heads.shape, jnp.float32)
    for block_num in range(length // block_rows):
        row_begin = block_num * block_rows
        finish = row_begin + block_rows
        query_rows = queries[:, row_begin:finish]
        grad_rows = grad_out[:, row_begin:finish]
        key_part = key_heads[:, :finish]
        value_part = value_heads[:, :finish]
        scores = (
            jnp.einsum("sqhd,skhd->shqk", query_rows, key_part, preferred_element_type=jnp.float32)
            * score_scale
        )
        allowed = block_mask(seg_full, position, row_begin, finish)
        softmax_f = jnp.where(
            allowed[:, None], jnp.exp(scores - log_sums[:, :, row_begin:finish]), 0.0
        )
        grad_probs = jnp.einsum(
            "sqhd,skhd->shqk", grad_rows, value_part, preferred_element_type=jnp.float32
        )
        row_delta = jnp.sum(softmax_f * grad_probs, axis=-1, keepdims=True)
        grad_scores = (softmax_f * (grad_probs - row_delta)).astype(jnp.bfloat16)
        grad_query.append(
            jnp.einsum("shqk,skhd->sqhd", grad_scores, key_part, preferred_element_type=jnp.float32)
            * score_scale
        )
        grad_key = grad_key.at[:, :finish].add(
            jnp.einsum(
                "shqk,sqhd->skhd", grad_scores, query_rows, preferred_element_type=jnp.float32
            )
            * score_scale
        )
        grad_value = grad_value.at[:, :finish].add(
            jnp.einsum(
                "shqk,sqhd->skhd",
                softmax_f.astype(jnp.bfloat16),
                grad_rows,
                preferred_element_type=jnp.float32,
            )
        )
    return (jnp.concatenate(grad_query, axis=1), grad_key, grad_value)


def general_body(tokens, segment_ids, selected, cotangent, w_qkv, w_out, w_gate_up, w_down, g_attn, g_mlp):
    streams, local_len, model_dim = tokens.shape
    sp_count = lax.axis_size("sp")
    sp_index = lax.axis_index("sp")
    row_count = streams * local_len
    group_size = H // KV
    kv_width = KV * HD
    score_scale = HD ** (-0.5)
    contract = (((0,), (0,)), ((), ()))
    seg_full = lax.all_gather(segment_ids, "sp", axis=1, tiled=True)
    first_count = jnp.sum((seg_full == 0).astype(jnp.int32), axis=1, keepdims=True)
    local_pos = (
        sp_index * local_len
        + jnp.arange(local_len, dtype=jnp.int32)[None, :]
        - segment_ids * first_count
    )
    cosine, sine_tab = rope_tables(local_pos.reshape(row_count), HD)
    shards = (w_qkv, w_out, w_gate_up, w_down, g_attn, g_mlp)
    gathered = (
        lax.all_gather(shards[0], "sp", axis=0, tiled=True),
        lax.all_gather(shards[1], "sp", axis=0, tiled=True),
        lax.all_gather(shards[2], "sp", axis=0, tiled=True),
        lax.all_gather(shards[3], "sp", axis=0, tiled=True),
        lax.all_gather(shards[4], "sp", axis=0, tiled=True),
        lax.all_gather(shards[5], "sp", axis=0, tiled=True),
    )
    qkv_full, out_full, gate_up_full, down_full, attn_gain, mlp_gain = gathered
    attn_gain = attn_gain.astype(jnp.float32)
    mlp_gain = mlp_gain.astype(jnp.float32)
    flat_in = tokens.reshape(row_count, model_dim).astype(jnp.float32)
    normed, inverse_one, stacked = attention_inputs(flat_in, qkv_full, attn_gain, cosine, sine_tab)
    head_view = lax.all_to_all(
        stacked.reshape(3, streams, local_len, model_dim),
        "sp",
        split_axis=3,
        concat_axis=2,
        tiled=True,
    )
    length = head_view.shape[2]
    heads_here = head_view.shape[3] // HD
    head_shape = (streams, length, heads_here, HD)
    queries = head_view[0].reshape(head_shape)
    key_heads = head_view[1].reshape(head_shape)
    value_heads = head_view[2].reshape(head_shape)
    attn_heads, log_sums = attention_forward(queries, key_heads, value_heads, seg_full, score_scale)
    attn_send = attn_heads.astype(jnp.bfloat16).reshape(streams, length, heads_here * HD)
    attn_tok = lax.all_to_all(attn_send, "sp", split_axis=1, concat_axis=2, tiled=True).reshape(
        row_count, model_dim
    )
    branch = jnp.dot(attn_tok, out_full, preferred_element_type=jnp.float32)
    residual = flat_in + branch
    inner_f, inverse_two = rms_norm(residual, mlp_gain)
    inner_in = inner_f.astype(jnp.bfloat16)
    gate_up = jnp.dot(inner_in, gate_up_full, preferred_element_type=jnp.float32)
    gate_part = gate_up[:, :FF]
    up_part = gate_up[:, FF:]
    sigmoid_g = jax.nn.sigmoid(gate_part)
    silu_gate = gate_part * sigmoid_g
    hidden = (silu_gate * up_part).astype(jnp.bfloat16)
    result = residual + jnp.dot(hidden, down_full, preferred_element_type=jnp.float32)
    output = result.astype(jnp.bfloat16).reshape(streams, local_len, model_dim)
    qkv_back, out_back, gate_up_back, down_back, attn_gain_b, mlp_gain_b = gathered
    attn_gain_b = attn_gain_b.astype(jnp.float32)
    mlp_gain_b = mlp_gain_b.astype(jnp.float32)
    grad_y = (cotangent * selected[:, :, None].astype(jnp.bfloat16)).reshape(row_count, model_dim)
    grad_hidden = jnp.dot(grad_y, down_back.T, preferred_element_type=jnp.float32)
    silu_slope = sigmoid_g * (1.0 + gate_part * (1.0 - sigmoid_g))
    grad_both = jnp.concatenate(
        [grad_hidden * up_part * silu_slope, grad_hidden * silu_gate], axis=1
    ).astype(jnp.bfloat16)
    grad_inner = jnp.dot(grad_both, gate_up_back.T, preferred_element_type=jnp.float32)
    grad_resid, gain_two = norm_back(residual, inverse_two, mlp_gain_b, grad_inner)
    grad_resid = grad_resid + grad_y.astype(jnp.float32)
    grad_branch = grad_resid.astype(jnp.bfloat16)
    grad_attn = jnp.dot(grad_branch, out_back.T, preferred_element_type=jnp.float32).astype(
        jnp.bfloat16
    )
    grad_view = lax.all_to_all(
        grad_attn.reshape(streams, local_len, model_dim),
        "sp",
        split_axis=2,
        concat_axis=1,
        tiled=True,
    )
    grad_view = grad_view.reshape(head_shape)
    grad_q, grad_k, grad_v = attention_backward(
        queries, key_heads, value_heads, seg_full, log_sums, grad_view, score_scale
    )
    back_send = (
        jnp.stack([grad_q, grad_k, grad_v])
        .astype(jnp.bfloat16)
        .reshape(3, streams, length, heads_here * HD)
    )
    returned = lax.all_to_all(back_send, "sp", split_axis=2, concat_axis=3, tiled=True)
    returned = returned.astype(jnp.float32).reshape(3, row_count, H, HD)
    grad_pq = rotate(returned[0], cosine, sine_tab, True).reshape(row_count, model_dim)
    key_summed = jnp.sum(returned[1].reshape(row_count, KV, group_size, HD), axis=2)
    grad_pk = rotate(key_summed, cosine, sine_tab, True).reshape(row_count, kv_width)
    grad_pv = jnp.sum(returned[2].reshape(row_count, KV, group_size, HD), axis=2).reshape(
        row_count, kv_width
    )
    grad_mixed = jnp.concatenate(
        [grad_pq.astype(jnp.bfloat16), grad_pk.astype(jnp.bfloat16), grad_pv.astype(jnp.bfloat16)],
        axis=1,
    )
    grad_normed = jnp.dot(grad_mixed, qkv_back.T, preferred_element_type=jnp.float32)
    grad_in, gain_one = norm_back(flat_in, inverse_one, attn_gain_b, grad_normed)
    grad_in = grad_in + grad_resid
    grad_tokens = grad_in.astype(jnp.bfloat16).reshape(streams, local_len, model_dim)
    gain_totals = lax.psum((gain_one, gain_two), ("dp", "sp"))
    gain_share = model_dim // sp_count
    grad_g_attn = lax.dynamic_slice_in_dim(gain_totals[0], sp_index * gain_share, gain_share, 0)
    grad_g_mlp = lax.dynamic_slice_in_dim(gain_totals[1], sp_index * gain_share, gain_share, 0)
    row_sums = lax.psum_scatter(
        jnp.concatenate(
            [
                lax.dot_general(normed, grad_mixed, contract, preferred_element_type=jnp.float32),
                lax.dot_general(
                    attn_tok, grad_branch, contract, preferred_element_type=jnp.float32
                ),
                lax.dot_general(inner_in, grad_both, contract, preferred_element_type=jnp.float32),
            ],
            axis=1,
        ).astype(jnp.bfloat16),
        "sp",
        scatter_dimension=0,
        tiled=True,
    )
    down_sums = lax.psum_scatter(
        lax.dot_general(hidden, grad_y, contract, preferred_element_type=jnp.float32).astype(
            jnp.bfloat16
        ),
        "sp",
        scatter_dimension=0,
        tiled=True,
    )
    weight_rows, down_rows = (
        lax.psum(row_sums, "dp").astype(jnp.float32),
        lax.psum(down_sums, "dp").astype(jnp.float32),
    )
    qkv_cols = model_dim + 2 * kv_width
    grad_w_qkv = weight_rows[:, :qkv_cols]
    grad_w_out = weight_rows[:, qkv_cols : qkv_cols + model_dim]
    grad_w_gate_up = weight_rows[:, qkv_cols + model_dim :]
    return (
        output,
        grad_tokens,
        grad_w_qkv,
        grad_w_out,
        grad_w_gate_up,
        down_rows,
        grad_g_attn,
        grad_g_mlp,
    )


CHIPS = 4
BLOCK = 512
SHORT = pl.CostEstimate(flops=1, bytes_accessed=1, transcendentals=0)
LOG2E = math.log2(math.e)
BF = jnp.bfloat16
F32 = jnp.float32
NT = (((1,), (1,)), ((), ()))
TN = (((0,), (0,)), ((), ()))


def swap_pairs(even_mask, odd_mask):
    return [(i, i ^ (odd_mask if i & 1 else even_mask)) for i in range(2 * CHIPS)]


FIRST = swap_pairs(2, 4)
SECOND = swap_pairs(4, 2)
SIBLING = swap_pairs(1, 1)
SAME_CORE = [[0, 2, 4, 6], [1, 3, 5, 7]]
LINE_NEAR = [(z, z ^ 1) for z in range(4)]
LINE_FAR = [(z, z ^ 2) for z in range(4)]


def send_first(x):
    return lax.ppermute(x, "sp", FIRST)


def send_second(x):
    return lax.ppermute(x, "sp", SECOND)


def send_sibling(x):
    return lax.ppermute(x, "sp", SIBLING)


def after(value, *others):
    return lax.optimization_barrier((value,) + others)[0]


def gather_chips(own):
    first = send_first(own)
    second = send_second(after(own, first))
    far = send_second(after(first, second))
    return [own, first, second, far]


def rel_masks(core):
    first = jnp.where(core == 0, 2, 4)
    return first, 6 - first


def fence(*values):
    return lax.optimization_barrier(values)


def gather_vectors(own, me):
    for bit in (1, 2, 4):
        got = lax.ppermute(own, "sp", swap_pairs(bit, bit))
        high = (me & bit) != 0
        own = jnp.concatenate([jnp.where(high, got, own), jnp.where(high, own, got)], axis=1)
    return own


def pick(parts, index):
    return lax.dynamic_index_in_dim(parts, index, 0, keepdims=False)


def pick_sum(parts, index, axis):
    return sum(lax.dynamic_index_in_dim(p, index, axis, keepdims=False).astype(F32) for p in parts)


def line_scatter_sends(parts, got, step, axis):
    planes = parts[0].shape[axis]
    z = lax.axis_index("dp")
    ahead = pick_sum(parts, jnp.clip(planes - step + z, 0, planes - 1), axis)
    back = pick_sum(parts, jnp.clip(z - planes + step, 0, planes - 1), axis)
    if got is not None:
        ahead = ahead + got[0].astype(F32)
        back = back + got[1].astype(F32)
    return ahead.astype(BF), back.astype(BF)


def line_scatter_move(sends, step):
    planes = lax.axis_size("dp")
    right = lax.ppermute(sends[0], "dp", [(i, i + 1) for i in range(step)])
    left = lax.ppermute(sends[1], "dp", [(planes - 1 - i, planes - 2 - i) for i in range(step)])
    return right, left


def line_scatter_end(parts, got, axis):
    own = pick_sum(parts, lax.axis_index("dp"), axis)
    return (own + got[0].astype(F32) + got[1].astype(F32)).astype(BF)


def line_gather_move(got, step):
    planes = lax.axis_size("dp")
    right = lax.ppermute(got[0], "dp", [(i, i + 1) for i in range(step - 1, planes - 1)])
    left = lax.ppermute(got[1], "dp", [(i + 1, i) for i in range(planes - step)])
    return right, left


def line_values(refs, planes, z):
    for step in range(planes):
        place = lax.rem(z - step + planes, planes)
        if step == 0:
            yield place, lambda index: refs[0][index]
        else:
            right, left = refs[step], refs[2 * planes - 1 - step]
            yield place, lambda index, right=right, left=left, step=step: jnp.where(z >= step, right[index], left[index])


def spread_kernel(in_ref, w_ref, g_ref, out_ref, gain_ref):
    planes, _, rows, width = in_ref.shape
    out = in_ref[...].reshape(planes * rows, width).astype(F32)
    out_ref[...] = out
    part = jnp.sum(out * w_ref[...].astype(F32), axis=-1, keepdims=True) / g_ref[...]

    @pl.when(pl.program_id(0) == 0)
    def _():
        gain_ref[...] = part

    @pl.when(pl.program_id(0) > 0)
    def _():
        gain_ref[...] += part


def spread(parts, weight, gain):
    planes, chips, rows, both = parts.shape
    half = both // 2
    total = planes * rows
    line = pl.BlockSpec((total, half), lambda i: (0, i))
    column = pl.BlockSpec((total, 1), lambda i: (0, 0))
    return pl.pallas_call(
        spread_kernel,
        grid=(2 * chips,),
        in_specs=[pl.BlockSpec((planes, 1, rows, half), lambda i: (0, i % chips, 0, i // chips)), line, column],
        out_specs=[line, column],
        out_shape=[jax.ShapeDtypeStruct(weight.shape, F32), jax.ShapeDtypeStruct((total, 1), F32)],
        compiler_params=pltpu.CompilerParams(vmem_limit_bytes=32 * 2**20),
        cost_estimate=SHORT,
        name="spread",
    )(parts, weight, gain)


def spread_last_kernel(z_ref, *refs, planes):
    blocks, (w_ref, g_ref, out_ref, gain_ref, wo_ref) = refs[:-5], refs[-5:]
    rows = blocks[0].shape[0]
    devices = 2 * CHIPS
    width = wo_ref.shape[1]
    heads = width // devices
    each = heads + 2 * HD
    for place, load in line_values(blocks, planes, z_ref[0]):
        span = pl.ds(pl.multiple_of(place * rows, rows), rows)
        pairs = []
        for d in range(devices):
            begin = d * each
            cols = slice(begin, begin + heads)
            out_ref[span, d * heads : (d + 1) * heads] = load((slice(None), cols)).astype(F32)
            pairs.append(load((slice(None), slice(begin + heads, begin + each))).astype(F32))
        for g in range(0, KV, 2):
            low = pairs[2 * g] + pairs[2 * g + 1]
            high = pairs[2 * g + 2] + pairs[2 * g + 3]
            lane = lax.broadcasted_iota(jnp.int32, low.shape, 1)
            begin = width + g * HD
            out_ref[span, begin : begin + 2 * HD] = jnp.where(lane < HD, low, pltpu.roll(high, HD, 1))
            begin = width + (KV + g) * HD
            out_ref[span, begin : begin + 2 * HD] = jnp.where(lane < HD, pltpu.roll(low, HD, 1), high)
        wo_ref[span, :] = load((slice(None), slice(devices * each, devices * each + width))).astype(F32)
    gain_ref[...] = jnp.sum(out_ref[...] * w_ref[...].astype(F32), axis=-1, keepdims=True) / g_ref[...]


def spread_last(steps, weight, gain, width):
    planes = len(steps)
    blocks = [steps[0][0]] + [s[0] for s in steps[1:]] + [s[1] for s in steps[1:]]
    vmem = pl.BlockSpec(memory_space=pltpu.VMEM)
    total = weight.shape[0]
    return pl.pallas_call(
        functools.partial(spread_last_kernel, planes=planes),
        in_specs=[pl.BlockSpec(memory_space=pltpu.SMEM)] + [vmem] * (len(blocks) + 2),
        out_specs=[vmem] * 3,
        out_shape=[
            jax.ShapeDtypeStruct(weight.shape, F32),
            jax.ShapeDtypeStruct((total, 1), F32),
            jax.ShapeDtypeStruct((total, width), F32),
        ],
        compiler_params=pltpu.CompilerParams(vmem_limit_bytes=32 * 2**20),
        cost_estimate=SHORT,
        name="spread_last",
    )(lax.axis_index("dp").reshape(1), *blocks, weight, gain)


def join_kernel(core_ref, mine_ref, theirs_ref, out_ref):
    planes, _, rows, both = mine_ref.shape
    block = jnp.where(pl.program_id(1) == 0, mine_ref[...], theirs_ref[...]).reshape(planes * rows, both)
    out_ref[0, 0, 0] = block[:, : both // 2]
    out_ref[1, 0, 0] = block[:, both // 2 :]


def join(core, mine, theirs):
    planes, chips, rows, both = mine.shape
    spec = pl.BlockSpec((planes, 1, rows, both), lambda c, k, core: (0, c, 0, 0))
    out = pl.pallas_call(
        join_kernel,
        grid_spec=pltpu.PrefetchScalarGridSpec(
            num_scalar_prefetch=1,
            grid=(chips, 2),
            in_specs=[spec, spec],
            out_specs=pl.BlockSpec(
                (2, 1, 1, planes * rows, both // 2), lambda c, k, core: (0, c, (core[0] + k) % 2, 0, 0)
            ),
        ),
        out_shape=jax.ShapeDtypeStruct((2, chips, 2, planes * rows, both // 2), BF),
        compiler_params=pltpu.CompilerParams(vmem_limit_bytes=32 * 2**20),
        cost_estimate=SHORT,
        name="join",
    )(core.reshape(1), mine, theirs)
    return out.reshape(2, 2 * chips * planes * rows, both // 2)


def ffn_kernel(*refs, cuts):
    b_hbm, dy_hbm, wgu_hbm, wd_hbm, hid_hbm, dg_hbm, du_hbm, db_hbm, y_hbm = refs[:9]
    b_ref, dy_ref, wg_ref, wu_ref, wd_ref, hid_ref, dg_ref, du_ref, db_ref, y_ref, sems = refs[9:]
    count = len(cuts) - 1

    def move(source, target, index):
        copy = pltpu.make_async_copy(source, target, sems.at[index])
        copy.start()
        return copy

    b_copy = move(b_hbm, b_ref, 3 * count)
    weights = []
    for c in range(count):
        span = slice(cuts[c], cuts[c + 1])
        gate_copy = move(wgu_hbm.at[0, :, span], wg_ref.at[:, span], 3 * c)
        up_copy = move(wgu_hbm.at[1, :, span], wu_ref.at[:, span], 3 * c + 1)
        weights.append([gate_copy, up_copy])
        if c == 0:
            dy_copy = move(dy_hbm, dy_ref, 3 * count + 1)
        weights[-1].append(move(wd_hbm.at[span, :], wd_ref.at[span, :], 3 * c + 2))
    b_copy.wait()
    for c in range(count):
        span = slice(cuts[c], cuts[c + 1])
        for copy in weights[c][:2]:
            copy.wait()
        gate = jnp.dot(b_ref[...], wg_ref[:, span], preferred_element_type=F32)
        up = jnp.dot(b_ref[...], wu_ref[:, span], preferred_element_type=F32)
        if c == 0:
            dy_copy.wait()
        weights[c][2].wait()
        d_hidden = lax.dot_general(dy_ref[...], wd_ref[span, :], NT, preferred_element_type=F32)
        sigmoid_g = jax.nn.sigmoid(gate)
        silu_gate = gate * sigmoid_g
        hid_ref[:, span] = (silu_gate * up).astype(BF)
        dg_ref[:, span] = (d_hidden * up * (sigmoid_g * (1.0 + gate * (1.0 - sigmoid_g)))).astype(BF)
        du_ref[:, span] = (d_hidden * silu_gate).astype(BF)
    base = 3 * count + 2
    outs = [move(hid_ref, hid_hbm, base), move(dg_ref, dg_hbm, base + 1), move(du_ref, du_hbm, base + 2)]
    y_ref[...] = jnp.dot(hid_ref[...], wd_ref[...], preferred_element_type=F32).astype(BF)
    outs.append(move(y_ref, y_hbm, base + 3))
    d_in = lax.dot_general(dg_ref[...], wg_ref[...], NT, preferred_element_type=F32)
    db_ref[...] = (d_in + lax.dot_general(du_ref[...], wu_ref[...], NT, preferred_element_type=F32)).astype(BF)
    outs.append(move(db_ref, db_hbm, base + 4))
    for copy in outs:
        copy.wait()


def ffn(b_rows, dy_rows, w_gu, w_dn):
    rows, width = b_rows.shape
    hidden = w_dn.shape[0]
    pieces = 3
    cuts = tuple(round(hidden * c / pieces / 128) * 128 for c in range(pieces)) + (hidden,)
    hbm = pl.BlockSpec(memory_space=pl.ANY)
    return pl.pallas_call(
        functools.partial(ffn_kernel, cuts=cuts),
        in_specs=[hbm] * 4,
        out_specs=[hbm] * 5,
        out_shape=[jax.ShapeDtypeStruct((rows, hidden), BF)] * 3 + [jax.ShapeDtypeStruct((rows, width), BF)] * 2,
        scratch_shapes=[pltpu.VMEM((rows, width), BF)] * 2
        + [pltpu.VMEM((width, hidden), BF)] * 2
        + [pltpu.VMEM((hidden, width), BF)]
        + [pltpu.VMEM((rows, hidden), BF)] * 3
        + [pltpu.VMEM((rows, width), BF)] * 2
        + [pltpu.SemaphoreType.DMA((3 * pieces + 7,))],
        compiler_params=pltpu.CompilerParams(vmem_limit_bytes=58 * 2**20),
        cost_estimate=SHORT,
        name="ffn",
    )(b_rows, dy_rows, w_gu, w_dn)


def grad_gu_kernel(core_ref, *refs, count):
    left, right = refs[: 2 * count], refs[2 * count : 4 * count]
    half = right[0].shape[1]
    for side in range(2):
        for kind in range(2):
            total = None
            for r in range(count):
                a_rows = left[side * count + r][...]
                part = lax.dot_general(a_rows, right[kind * count + r][...], TN, preferred_element_type=F32)
                total = part if total is None else total + part
            out_ref = refs[4 * count + side]
            planes, _, rows, _ = out_ref.shape
            out_ref[:, 0, :, kind * half : (kind + 1) * half] = total.astype(BF).reshape(planes, rows, half)


def grad_gu(core, b_rows, dg_rows, du_rows, share, planes):
    count = len(b_rows)
    tokens, width = b_rows[0].shape
    hidden = dg_rows[0].shape[1]
    keep = pl.BlockSpec((tokens, share), lambda c, core: (0, 2 * c + core[0]))
    give = pl.BlockSpec((tokens, share), lambda c, core: (0, 2 * c + 1 - core[0]))
    whole = pl.BlockSpec((tokens, hidden), lambda c, core: (0, 0))
    rows = share // planes
    out = pl.BlockSpec((planes, 1, rows, 2 * hidden), lambda c, core: (0, c, 0, 0))
    return pl.pallas_call(
        functools.partial(grad_gu_kernel, count=count),
        grid_spec=pltpu.PrefetchScalarGridSpec(
            num_scalar_prefetch=1,
            grid=(width // (2 * share),),
            in_specs=[keep] * count + [give] * count + [whole] * (2 * count),
            out_specs=[out, out],
        ),
        out_shape=[jax.ShapeDtypeStruct((planes, width // (2 * share), rows, 2 * hidden), BF)] * 2,
        compiler_params=pltpu.CompilerParams(vmem_limit_bytes=58 * 2**20),
        cost_estimate=SHORT,
        name="grad_gu",
    )(core.reshape(1), *b_rows, *b_rows, *dg_rows, *du_rows)


def grad_qkv_kernel(place_ref, *refs, count):
    dp_ref, out_ref = refs[-2:]
    total = None
    for r in range(count):
        part = lax.dot_general(refs[r][...], dp_ref[place_ref[r]], TN, preferred_element_type=F32)
        total = part if total is None else total + part
    planes, rows, wide = out_ref.shape
    columns = total.shape[1]
    for k in range(wide // columns):
        block = total[k * planes * rows : (k + 1) * planes * rows].astype(BF)
        out_ref[:, :, k * columns : (k + 1) * columns] = block.reshape(planes, rows, columns)


def grad_qkv(places, a_rows, dp_heads, planes):
    count = len(a_rows)
    tokens, width = a_rows[0].shape
    columns = dp_heads.shape[2]
    share = width // count
    depth = 2 * share
    return pl.pallas_call(
        functools.partial(grad_qkv_kernel, count=count),
        grid_spec=pltpu.PrefetchScalarGridSpec(
            num_scalar_prefetch=1,
            grid=(width // depth,),
            in_specs=[pl.BlockSpec((tokens, depth), lambda i, p: (0, i))] * count
            + [pl.BlockSpec(dp_heads.shape, lambda i, p: (0, 0, 0))],
            out_specs=pl.BlockSpec((planes, share // planes, 2 * columns), lambda i, p: (0, 0, i)),
        ),
        out_shape=jax.ShapeDtypeStruct((planes, share // planes, count * columns), BF),
        compiler_params=pltpu.CompilerParams(vmem_limit_bytes=48 * 2**20),
        cost_estimate=SHORT,
        name="grad_qkv",
    )(places, *a_rows, dp_heads)


def swap_halves(values):
    width = values.shape[-1]
    lane = lax.broadcasted_iota(jnp.int32, values.shape, 1)
    ahead = pltpu.roll(values, width - HD // 2, 1)
    behind = pltpu.roll(values, HD // 2, 1)
    return jnp.where(lane % HD < HD // 2, ahead, behind)


def project_kernel(place_ref, x_ref, gain_ref, cos_ref, sin_ref, *refs, count):
    wq_refs, wkv_refs = refs[:count], refs[count : 2 * count]
    send_ref, normed_ref, inv_ref, normed_scr = refs[2 * count :]
    share = normed_scr.shape[2]

    @pl.when(pl.program_id(0) == 0)
    def _():
        x = x_ref[...].astype(F32)
        inv = lax.rsqrt(jnp.mean(x * x, axis=-1, keepdims=True) + EPSILON)
        normed = (x * inv * gain_ref[...]).astype(BF)
        normed_ref[...] = normed
        inv_ref[...] = inv
        for part in range(count):
            normed_scr[part] = normed[:, part * share : (part + 1) * share]

    pq = pkv = None
    for r in range(count):
        a_rows = normed_scr[place_ref[r]]
        q_part = jnp.dot(a_rows, wq_refs[r][...], preferred_element_type=F32)
        kv_part = jnp.dot(a_rows, wkv_refs[r][...], preferred_element_type=F32)
        pq = q_part if pq is None else pq + q_part
        pkv = kv_part if pkv is None else pkv + kv_part
    cos = cos_ref[...]
    sin = sin_ref[...]
    heads = pq.shape[1]
    q_scale = LOG2E * HD**-0.5
    turned = pq * jnp.tile(cos, (1, heads // 128)) + swap_halves(pq) * jnp.tile(sin, (1, heads // 128))
    send_ref[0, :, :heads] = (turned * q_scale).astype(BF)
    lane = lax.broadcasted_iota(jnp.int32, pkv.shape, 1)
    turned_kv = jnp.where(lane < HD, pkv * cos + swap_halves(pkv) * sin, pkv)
    send_ref[0, :, heads:] = turned_kv.astype(BF)


def project(places, x, gain, cos, sin, parts):
    rows, width = x.shape
    count = len(parts)
    heads = width // count
    out_width = heads + 2 * HD
    depth = parts[0].shape[0]
    first_kv = width // (2 * HD)
    return pl.pallas_call(
        functools.partial(project_kernel, count=count),
        grid_spec=pltpu.PrefetchScalarGridSpec(
            num_scalar_prefetch=1,
            grid=(count,),
            in_specs=[
                pl.BlockSpec((rows, width), lambda d, p: (0, 0)),
                pl.BlockSpec((1, width), lambda d, p: (0, 0)),
                pl.BlockSpec((rows, 128), lambda d, p: (0, 0)),
                pl.BlockSpec((rows, 128), lambda d, p: (0, 0)),
            ]
            + [pl.BlockSpec((depth, heads), lambda d, p: (0, d))] * count
            + [pl.BlockSpec((depth, 2 * HD), lambda d, p: (0, first_kv + d // 2))] * count,
            out_specs=[
                pl.BlockSpec((1, rows, out_width), lambda d, p: (d, 0, 0)),
                pl.BlockSpec((rows, width), lambda d, p: (0, 0)),
                pl.BlockSpec((rows, 1), lambda d, p: (0, 0)),
            ],
            scratch_shapes=[pltpu.VMEM((count, rows, width // count), BF)],
        ),
        out_shape=[
            jax.ShapeDtypeStruct((count, rows, out_width), BF),
            jax.ShapeDtypeStruct((rows, width), BF),
            jax.ShapeDtypeStruct((rows, 1), F32),
        ],
        compiler_params=pltpu.CompilerParams(vmem_limit_bytes=48 * 2**20),
        cost_estimate=SHORT,
        name="project",
    )(places, x, gain, cos, sin, *parts, *parts)


def out_proj_kernel(place_ref, attn_ref, x_ref, gain_ref, *refs, count):
    parts, (resid_ref, inv_ref, inner_ref) = refs[:count], refs[count:]
    width = x_ref.shape[1]
    tile = 512
    square = None
    for begin in range(0, width, tile):
        cols = slice(begin, begin + tile)
        total = x_ref[:, cols].astype(F32)
        for r in range(count):
            total = total + jnp.dot(attn_ref[place_ref[r]], parts[r][:, cols], preferred_element_type=F32)
        resid_ref[:, cols] = total
        part = jnp.sum(total * total, axis=-1, keepdims=True)
        square = part if square is None else square + part
    inv = lax.rsqrt(square / width + EPSILON)
    inv_ref[...] = inv
    inner_ref[...] = (resid_ref[...] * inv * gain_ref[...]).astype(BF)


def out_proj(places, attn, x, gain, parts):
    count, rows, share = attn.shape
    width = x.shape[1]
    step = rows // 2
    line = pl.BlockSpec((step, width), lambda i, p: (i, 0))
    return pl.pallas_call(
        functools.partial(out_proj_kernel, count=count),
        grid_spec=pltpu.PrefetchScalarGridSpec(
            num_scalar_prefetch=1,
            grid=(rows // step,),
            in_specs=[
                pl.BlockSpec((count, step, share), lambda i, p: (0, i, 0)),
                line,
                pl.BlockSpec((1, width), lambda i, p: (0, 0)),
            ]
            + [pl.BlockSpec((share, width), lambda i, p: (0, 0))] * count,
            out_specs=[line, pl.BlockSpec((step, 1), lambda i, p: (i, 0)), line],
        ),
        out_shape=[
            jax.ShapeDtypeStruct((rows, width), F32),
            jax.ShapeDtypeStruct((rows, 1), F32),
            jax.ShapeDtypeStruct((rows, width), BF),
        ],
        compiler_params=pltpu.CompilerParams(vmem_limit_bytes=56 * 2**20),
        cost_estimate=SHORT,
        name="out_proj",
    )(places, attn, x, gain, *parts)


def resid_back_kernel(place_ref, db_ref, first_ref, passed_ref, resid_ref, inv_ref, gain_ref, dy_ref, *refs, count):
    parts, (d_resid_ref, branch_ref, send_ref) = refs[:count], refs[count:]
    d_inner = db_ref[...].astype(F32) + first_ref[...].astype(F32) + passed_ref[...].astype(F32)
    resid = resid_ref[...]
    inv = inv_ref[...]
    scaled = d_inner * gain_ref[...]
    inner_mean = jnp.mean(scaled * resid, axis=-1, keepdims=True)
    d_resid = dy_ref[...].astype(F32) + inv * scaled - resid * (inv * inv * inv * inner_mean)
    d_resid_ref[...] = d_resid
    branch = d_resid.astype(BF)
    branch_ref[...] = branch
    for r in range(count):
        d_attn = lax.dot_general(branch, parts[r][...], NT, preferred_element_type=F32)
        send_ref[place_ref[r]] = d_attn.astype(BF)


def resid_back(places, db_own, db_first, db_passed, resid, inv, gain, dy, parts):
    rows, width = resid.shape
    count = len(parts)
    share = parts[0].shape[0]
    step = rows // 2
    line = pl.BlockSpec((step, width), lambda i, p: (i, 0))
    return pl.pallas_call(
        functools.partial(resid_back_kernel, count=count),
        grid_spec=pltpu.PrefetchScalarGridSpec(
            num_scalar_prefetch=1,
            grid=(rows // step,),
            in_specs=[line, line, line, line]
            + [pl.BlockSpec((step, 1), lambda i, p: (i, 0)), pl.BlockSpec((1, width), lambda i, p: (0, 0)), line]
            + [pl.BlockSpec((share, width), lambda i, p: (0, 0))] * count,
            out_specs=[line, line, pl.BlockSpec((count, step, share), lambda i, p: (0, i, 0))],
        ),
        out_shape=[
            jax.ShapeDtypeStruct((rows, width), F32),
            jax.ShapeDtypeStruct((rows, width), BF),
            jax.ShapeDtypeStruct((count, rows, share), BF),
        ],
        compiler_params=pltpu.CompilerParams(vmem_limit_bytes=56 * 2**20),
        cost_estimate=SHORT,
        name="resid_back",
    )(places, db_own, db_first, db_passed, resid, inv, gain, dy, *parts)


def in_back_kernel(place_ref, back_ref, x_ref, inv_ref, gain_ref, d_resid_ref, *refs, count):
    parts, (out_ref, mixed, d_scr) = refs[:count], refs[count:]
    devices, _, width = back_ref.shape
    heads = width - 2 * HD
    for d in range(devices):
        mixed[:, d * heads : (d + 1) * heads] = back_ref[d, :, :heads]
    base = devices * heads
    for g in range(KV):
        pair = back_ref[2 * g, :, heads:].astype(F32) + back_ref[2 * g + 1, :, heads:].astype(F32)
        mixed[:, base + 2 * g * HD : base + 2 * (g + 1) * HD] = pair.astype(BF)
    for r in range(count):
        d_scr[place_ref[r]] = lax.dot_general(mixed[...], parts[r][...], NT, preferred_element_type=F32)
    inv = inv_ref[...]
    share = d_scr.shape[2]
    inner = None
    for c in range(count):
        cols = slice(c * share, (c + 1) * share)
        part = jnp.sum(d_scr[c] * gain_ref[:, cols] * x_ref[:, cols].astype(F32), axis=-1, keepdims=True)
        inner = part if inner is None else inner + part
    factor = inv * inv * inv * (inner / (count * share))
    for c in range(count):
        cols = slice(c * share, (c + 1) * share)
        through = inv * (d_scr[c] * gain_ref[:, cols]) - x_ref[:, cols].astype(F32) * factor
        out_ref[:, cols] = (d_resid_ref[:, cols] + through).astype(BF)


def in_back(places, back, x, inv, gain, d_resid, parts):
    rows, width = x.shape
    count = len(parts)
    share, columns = parts[0].shape
    step = rows // 2
    line = pl.BlockSpec((step, width), lambda i, p: (i, 0))
    return pl.pallas_call(
        functools.partial(in_back_kernel, count=count),
        grid_spec=pltpu.PrefetchScalarGridSpec(
            num_scalar_prefetch=1,
            grid=(rows // step,),
            in_specs=[
                pl.BlockSpec((count, step, back.shape[2]), lambda i, p: (0, i, 0)),
                line,
                pl.BlockSpec((step, 1), lambda i, p: (i, 0)),
                pl.BlockSpec((1, width), lambda i, p: (0, 0)),
                line,
            ]
            + [pl.BlockSpec((share, columns), lambda i, p: (0, 0))] * count,
            out_specs=line,
            scratch_shapes=[pltpu.VMEM((step, columns), BF), pltpu.VMEM((count, step, share), F32)],
        ),
        out_shape=jax.ShapeDtypeStruct((rows, width), BF),
        compiler_params=pltpu.CompilerParams(vmem_limit_bytes=56 * 2**20),
        cost_estimate=SHORT,
        name="in_back",
    )(places, back, x, inv, gain, d_resid, *parts)


def grad_wo_kernel(core_ref, keep_ref, give_ref, branch_ref, keep_out, give_out):
    branch = branch_ref[...]
    keep_out[0] = lax.dot_general(keep_ref[0], branch, TN, preferred_element_type=F32).astype(BF)
    give_out[0] = lax.dot_general(give_ref[0], branch, TN, preferred_element_type=F32).astype(BF)


def grad_wo(core, attn, branch):
    devices, rows, share = attn.shape
    width = branch.shape[1]
    out = pl.BlockSpec((1, share, width), lambda c, core: (c, 0, 0))
    return pl.pallas_call(
        grad_wo_kernel,
        grid_spec=pltpu.PrefetchScalarGridSpec(
            num_scalar_prefetch=1,
            grid=(devices // 2,),
            in_specs=[
                pl.BlockSpec((1, rows, share), lambda c, core: (2 * c + core[0], 0, 0)),
                pl.BlockSpec((1, rows, share), lambda c, core: (2 * c + 1 - core[0], 0, 0)),
                pl.BlockSpec((rows, width), lambda c, core: (0, 0)),
            ],
            out_specs=[out, out],
        ),
        out_shape=[jax.ShapeDtypeStruct((devices // 2, share, width), BF)] * 2,
        compiler_params=pltpu.CompilerParams(vmem_limit_bytes=48 * 2**20),
        cost_estimate=SHORT,
        name="grad_wo",
    )(core.reshape(1), attn, attn, branch)


def grad_dn_kernel(core_ref, *refs, count):
    left, right, (keep_out, give_out) = refs[:count], refs[count : 2 * count], refs[2 * count :]
    total = None
    for r in range(count):
        part = lax.dot_general(left[r][...], right[r][...], TN, preferred_element_type=F32)
        total = part if total is None else total + part
    half = total.shape[0] // 2
    total = total.astype(BF)
    low = core_ref[0] == 0
    keep_out[...] = jnp.where(low, total[:half], total[half:])
    give_out[...] = jnp.where(low, total[half:], total[:half])


def grad_dn(core, hid_rows, dy_rows):
    count = len(hid_rows)
    tokens, hidden = hid_rows[0].shape
    width = dy_rows[0].shape[1]
    tile = 512
    out = pl.BlockSpec((hidden // 2, tile), lambda i, core: (0, i))
    return pl.pallas_call(
        functools.partial(grad_dn_kernel, count=count),
        grid_spec=pltpu.PrefetchScalarGridSpec(
            num_scalar_prefetch=1,
            grid=(width // tile,),
            in_specs=[pl.BlockSpec((tokens, hidden), lambda i, core: (0, 0))] * count
            + [pl.BlockSpec((tokens, tile), lambda i, core: (0, i))] * count,
            out_specs=[out, out],
        ),
        out_shape=[jax.ShapeDtypeStruct((hidden // 2, width), BF)] * 2,
        compiler_params=pltpu.CompilerParams(vmem_limit_bytes=56 * 2**20),
        cost_estimate=SHORT,
        name="grad_dn",
    )(core.reshape(1), *hid_rows, *dy_rows)


def attend_kernel(zeros_ref, q_ref, kv_ref, *refs, heads, start, stop):
    o_ref, send_ref, lse_ref, k_scr, v_scr, acc_ref, max_ref = refs[-7:]
    block = pl.program_id(0) + start
    zeros = zeros_ref[0]
    size = q_ref.shape[0]

    @pl.when(block == start)
    def _():
        for part in range(stop):
            rows = slice(part * size, (part + 1) * size)
            both = kv_ref[rows, :].astype(F32)
            lane = lax.broadcasted_iota(jnp.int32, both.shape, 1)
            k_scr[rows, :] = kv_ref[rows, :HD]
            v_scr[rows, :] = jnp.where(lane < HD, pltpu.roll(both, HD, 1), 1.0).astype(BF)

    first_row = block * size
    lowest = jnp.where(first_row >= zeros, zeros // size, 0)
    acc_ref[...] = jnp.zeros_like(acc_ref)
    max_ref[...] = jnp.full_like(max_ref, MASKED)
    q_heads = [q_ref[:, h * HD : (h + 1) * HD] for h in range(heads)]

    def step(index, masked):
        first_key = pl.multiple_of(index * size, size)
        keys = k_scr[pl.ds(first_key, size), :]
        values = v_scr[pl.ds(first_key, size), :]
        if masked:
            row = first_row + lax.broadcasted_iota(jnp.int32, (size, size), 0)
            col = first_key + lax.broadcasted_iota(jnp.int32, (size, size), 1)
            begin = jnp.where(row >= zeros, zeros, 0)
            refused = (col > row) | (col < begin)

        def score(h):
            return lax.dot_general(q_heads[h], keys, NT, preferred_element_type=F32)

        upcoming = score(0)
        for h in range(heads):
            scores = upcoming
            if h + 1 < heads:
                upcoming = score(h + 1)
            if masked:
                scores = jnp.where(refused, MASKED, scores)
            old_max = max_ref[h]
            new_max = jnp.maximum(old_max, jnp.max(scores, axis=-1, keepdims=True))
            weights = jnp.exp2(scores - jnp.tile(new_max, (1, size // 128)))
            shrink = jnp.exp2(old_max - new_max)
            acc_ref[h] = acc_ref[h] * shrink + jnp.dot(weights.astype(BF), values, preferred_element_type=F32)
            max_ref[h] = new_max

    def visit(index, carry):
        first_key = index * size
        mixed = (index == block) | ((first_row + size > zeros) & (first_key < zeros))

        @pl.when(mixed)
        def _():
            step(index, True)

        @pl.when(jnp.logical_not(mixed))
        def _():
            step(index, False)

        return carry

    lax.fori_loop(lowest, block + 1, visit, 0)
    for h in range(heads):
        acc = acc_ref[h]
        total = acc[:, HD : HD + 1]
        out = acc[:, :HD] / total
        o_ref[:, h * HD : (h + 1) * HD] = out
        send_ref[0, :, h * HD : (h + 1) * HD] = out.astype(BF)
        lse = max_ref[h] + jnp.log2(total)
        lse_ref[0, h : h + 1, :] = jnp.transpose(lse)[:1]


def attend(zeros, qkv, start, stop, before=None):
    length, width = qkv.shape
    q_width = width - 2 * HD
    heads = q_width // HD
    size = BLOCK
    blocks = length // size
    before = () if before is None else before
    return pl.pallas_call(
        functools.partial(attend_kernel, heads=heads, start=start, stop=stop),
        grid_spec=pltpu.PrefetchScalarGridSpec(
            num_scalar_prefetch=1,
            grid=(stop - start,),
            in_specs=[
                pl.BlockSpec((size, q_width), lambda i, z: (i + start, 0)),
                pl.BlockSpec((length, 2 * HD), lambda i, z: (0, q_width // (2 * HD))),
            ]
            + [pl.BlockSpec(memory_space=pl.ANY)] * len(before),
            out_specs=[
                pl.BlockSpec((size, q_width), lambda i, z: (i + start, 0)),
                pl.BlockSpec((1, size, q_width), lambda i, z: (i + start, 0, 0)),
                pl.BlockSpec((1, heads, size), lambda i, z: (i + start, 0, 0)),
            ],
            scratch_shapes=[
                pltpu.VMEM((length, HD), BF),
                pltpu.VMEM((length, 2 * HD), BF),
                pltpu.VMEM((heads, size, 2 * HD), F32),
                pltpu.VMEM((heads, size, 128), F32),
            ],
        ),
        out_shape=[
            jax.ShapeDtypeStruct((length, q_width), F32),
            jax.ShapeDtypeStruct((blocks, size, q_width), BF),
            jax.ShapeDtypeStruct((blocks, heads, size), F32),
        ],
        input_output_aliases={3 + i: i for i in range(len(before))},
        compiler_params=pltpu.CompilerParams(vmem_limit_bytes=48 * 2**20),
        cost_estimate=SHORT,
        name="attend",
    )(zeros, qkv, qkv, *before)


def attend_back_kernel(
    zeros_ref, q_ref, kv_ref, do_ref, lse_ref, cos_ref, sin_ref, extra_ref, *refs, heads, start
):
    send_ref, dq_acc, delta_ref, q_scr, do_scr = refs[-5:]
    block = pl.program_id(0) + start
    zeros = zeros_ref[0]
    size = kv_ref.shape[0]
    length = q_ref.shape[0]
    blocks = length // size

    @pl.when(block == start)
    def _():
        if start == 0:
            dq_acc[...] = jnp.zeros_like(dq_acc)
        else:
            dq_acc[...] = refs[0][...]
            delta_ref[...] = extra_ref[...]
        for part in range(start, blocks):
            rows = slice(part * size, (part + 1) * size)
            if start == 0:
                product = jnp.transpose(do_ref[rows, :].astype(F32) * extra_ref[rows, :])
            for h in range(heads):
                cols = slice(h * HD, (h + 1) * HD)
                q_scr[h, rows, :] = q_ref[rows, cols]
                do_scr[h, rows, :] = do_ref[rows, cols]
                if start == 0:
                    delta_ref[part, h : h + 1, :] = jnp.sum(product[cols], axis=0, keepdims=True)

    first_key = block * size
    both = kv_ref[...]
    keys = both[:, :HD]
    values = both[:, HD:]
    keys_t = jnp.transpose(keys.astype(F32)).astype(BF)
    highest = jnp.where(first_key + size <= zeros, jnp.minimum((zeros + size - 1) // size, blocks), blocks)

    def step(index, carry, masked):
        first_row = pl.multiple_of(index * size, size)
        span = pl.ds(first_row, size)
        if masked:
            col = first_key + lax.broadcasted_iota(jnp.int32, (size, size), 0)
            row = first_row + lax.broadcasted_iota(jnp.int32, (size, size), 1)
            begin = jnp.where(row >= zeros, zeros, 0)
            refused = (col > row) | (col < begin)

        def products(h):
            q_rows = q_scr[h, span, :]
            do_rows = do_scr[h, span, :]
            scores = lax.dot_general(keys, q_rows, NT, preferred_element_type=F32)
            d_prob = lax.dot_general(values, do_rows, NT, preferred_element_type=F32)
            return q_rows, do_rows, scores, d_prob

        upcoming = products(0)
        dk_sum, dv_sum = carry
        for h in range(heads):
            q_rows, do_rows, scores, d_prob = upcoming
            if h + 1 < heads:
                upcoming = products(h + 1)
            shifted = scores - lse_ref[index, h : h + 1, :]
            if masked:
                shifted = jnp.where(refused, MASKED, shifted)
            prob = jnp.exp2(shifted)
            d_score = (prob * (d_prob - delta_ref[index, h : h + 1, :])).astype(BF)
            dv_sum = dv_sum + jnp.dot(prob.astype(BF), do_rows, preferred_element_type=F32)
            dk_sum = dk_sum + jnp.dot(d_score, q_rows, preferred_element_type=F32)
            dq_acc[h * HD : (h + 1) * HD, span] += jnp.dot(keys_t, d_score, preferred_element_type=F32)
        return dk_sum, dv_sum

    def visit(index, carry):
        first_row = index * size
        mixed = (index == block) | ((first_row + size > zeros) & (first_key < zeros))
        return lax.cond(
            mixed,
            lambda c: step(index, c, True),
            lambda c: step(index, c, False),
            carry,
        )

    zero = jnp.zeros((size, HD), F32)
    dk_sum, dv_sum = lax.fori_loop(block, highest, visit, (zero, zero))
    q_width = heads * HD
    done = pl.ds(pl.multiple_of(first_key, size), size)
    cos = cos_ref[...]
    sin = sin_ref[...]
    dq = jnp.transpose(dq_acc[:, done]) * HD**-0.5
    dq = dq * jnp.tile(cos, (1, q_width // 128)) - swap_halves(dq) * jnp.tile(sin, (1, q_width // 128))
    send_ref[0, :, :q_width] = dq.astype(BF)
    dkv = jnp.concatenate([dk_sum * (1.0 / LOG2E), dv_sum], axis=1)
    lane = lax.broadcasted_iota(jnp.int32, dkv.shape, 1)
    send_ref[0, :, q_width:] = jnp.where(lane < HD, dkv * cos - swap_halves(dkv) * sin, dkv).astype(BF)


def attend_back(zeros, qkv, d_out, lse, cos, sin, start, stop, out=None, before=None):
    length, width = qkv.shape
    q_width = width - 2 * HD
    heads = q_width // HD
    size = BLOCK
    blocks = length // size
    whole = lambda *shape: pl.BlockSpec(shape, lambda j, z: (0,) * len(shape))
    if before is None:
        operands = (out,)
        specs = [whole(length, q_width)]
        aliases = {}
    else:
        send, d_query, delta = before
        operands = (delta, d_query, send)
        specs = [whole(blocks, heads, size), whole(q_width, length), pl.BlockSpec(memory_space=pl.ANY)]
        aliases = {9: 0}
    return pl.pallas_call(
        functools.partial(attend_back_kernel, heads=heads, start=start),
        grid_spec=pltpu.PrefetchScalarGridSpec(
            num_scalar_prefetch=1,
            grid=(stop - start,),
            in_specs=[
                whole(length, q_width),
                pl.BlockSpec((size, 2 * HD), lambda j, z: (j + start, q_width // (2 * HD))),
                whole(length, q_width),
                whole(blocks, heads, size),
                pl.BlockSpec((size, 128), lambda j, z: (j + start, 0)),
                pl.BlockSpec((size, 128), lambda j, z: (j + start, 0)),
            ]
            + specs,
            out_specs=[
                pl.BlockSpec((1, size, width), lambda j, z: (j + start, 0, 0)),
                whole(q_width, length),
                whole(blocks, heads, size),
            ],
            scratch_shapes=[
                pltpu.VMEM((heads, length, HD), BF),
                pltpu.VMEM((heads, length, HD), BF),
            ],
        ),
        out_shape=[
            jax.ShapeDtypeStruct((blocks, size, width), BF),
            jax.ShapeDtypeStruct((q_width, length), F32),
            jax.ShapeDtypeStruct((blocks, heads, size), F32),
        ],
        input_output_aliases=aliases,
        compiler_params=pltpu.CompilerParams(vmem_limit_bytes=58 * 2**20),
        cost_estimate=SHORT,
        name="attend_back",
    )(zeros, qkv, qkv, d_out, lse, cos, sin, *operands)


def turn_tables(positions):
    cosine, sine = rope_tables(positions, HD)
    return jnp.concatenate([cosine] * 4, axis=1), jnp.concatenate([-sine, sine, -sine, sine], axis=1)


def fast_body(tokens, segment_ids, selected, cotangent, w_qkv, w_out, w_gate_up, w_down, g_attn, g_mlp):
    _, rows, width = tokens.shape
    devices = 2 * CHIPS
    me = lax.axis_index("sp")
    core = me & 1
    planes = lax.axis_size("dp")
    share = width // devices
    kv_width = KV * HD
    first_mask, second_mask = rel_masks(core)
    other = me ^ 1
    chip = me // 2
    place_list = [me, me ^ first_mask, me ^ second_mask, me ^ 6]
    place_list += [other, other ^ second_mask, other ^ first_mask, other ^ 6]
    places = jnp.stack(place_list)
    hidden_chip = 2 * w_down.shape[0]
    quarter = share // planes
    plane = lax.axis_index("dp")
    length = devices * rows
    blocks = length // BLOCK

    count = jnp.sum((segment_ids == 0).astype(F32))
    vectors = jnp.stack([g_attn.astype(F32), g_mlp.astype(F32)] + [jnp.full((share,), count)] * 6)
    paired = [w_qkv[:, :width]]
    for head in range(KV):
        paired.append(w_qkv[:, width + head * HD : width + (head + 1) * HD])
        paired.append(w_qkv[:, width + kv_width + head * HD : width + kv_width + (head + 1) * HD])
    qkv_own = jnp.concatenate(paired, axis=1)
    gu_rows = lax.dynamic_slice_in_dim(w_gate_up, plane * quarter, quarter, 0)
    gu_send = []
    for place in range(CHIPS):
        for begin in (place * hidden_chip, (CHIPS + place) * hidden_chip):
            gu_send.append(gu_rows[:, begin : begin + hidden_chip])
    gu_send = jnp.stack([jnp.concatenate(gu_send[2 * c : 2 * c + 2], axis=1) for c in range(CHIPS)])
    vectors = gather_vectors(vectors, me)
    vectors, qkv_own, gu_send = fence(vectors, qkv_own, gu_send)
    qkv_first = send_first(qkv_own)
    attn_gain = vectors[0:1]
    mlp_gain = vectors[1:2]
    zeros = jnp.sum(vectors[2].reshape(devices, share)[:, 0]).astype(jnp.int32)
    zeros_one = zeros.reshape(1)
    local_pos = me * rows + jnp.arange(rows, dtype=jnp.int32) - segment_ids.reshape(rows) * zeros
    cos, sin = turn_tables(local_pos)
    dy = (cotangent * selected[:, :, None].astype(BF)).reshape(rows, width)
    qkv_own, qkv_first, cos, sin = fence(qkv_own, qkv_first, cos, sin)
    qkv_second = send_second(qkv_own)
    qkv_theirs = [send_sibling(qkv_own), send_sibling(qkv_first)]
    all_places = jnp.arange(length, dtype=jnp.int32)
    cos_all, sin_all = turn_tables(all_places - jnp.where(all_places >= zeros, zeros, 0))
    qkv_first, qkv_second, cos_all, sin_all, *qkv_theirs = fence(qkv_first, qkv_second, cos_all, sin_all, *qkv_theirs)
    qkv_far = send_second(qkv_first)
    qkv_theirs.append(send_sibling(qkv_second))
    qkv_far, dy, *qkv_theirs = fence(qkv_far, dy, *qkv_theirs)
    qkv_theirs.append(send_sibling(qkv_far))
    qkv_parts = [qkv_own, qkv_first, qkv_second, qkv_far] + qkv_theirs
    x_bf = tokens.reshape(rows, width)
    x_bf, w_out, gu_send, *qkv_parts = fence(x_bf, w_out, gu_send, *qkv_parts)
    out_first = send_first(w_out)
    gu_part = lax.all_to_all(gu_send, "sp", 0, 0, axis_index_groups=SAME_CORE, tiled=True)
    qkv_send, normed, inv_one = project(places, x_bf, attn_gain, cos, sin, qkv_parts)
    qkv_send, out_first = fence(qkv_send, out_first)
    gu_mine = lax.all_gather(after(gu_part, qkv_send), "dp", axis=0, tiled=False)
    gu_mine = lax.all_gather(after(gu_part, qkv_send), "dp", axis=0, tiled=False)
    down_theirs = send_sibling(w_down)
    w_dn = jnp.where(
        core == 0, jnp.concatenate([w_down, down_theirs], axis=0), jnp.concatenate([down_theirs, w_down], axis=0)
    )
    qkv_heads = lax.all_to_all(qkv_send, "sp", 0, 0, tiled=True).reshape(length, qkv_send.shape[2])

    cuts = (0, (5 * blocks) // 8, (7 * blocks) // 8, blocks)
    qkv_heads, w_dn, out_first = fence(qkv_heads, w_dn, out_first)
    out_second = send_second(after(w_out, qkv_heads))
    dy_first = send_first(after(dy, qkv_heads))
    fwd = attend(zeros_one, qkv_heads, cuts[0], cuts[1])
    qkv_heads, out_second, dy_first, out_first, dy, *fwd = fence(qkv_heads, out_second, dy_first, out_first, dy, *fwd)
    out_far = send_second(out_first)
    dy_second = send_second(dy)
    fwd = attend(zeros_one, qkv_heads, cuts[1], cuts[2], fwd)
    qkv_heads, out_far, dy_second, dy_first, *fwd = fence(qkv_heads, out_far, dy_second, dy_first, *fwd)
    dy_far = send_second(dy_first)
    gu_theirs = send_sibling(after(gu_mine, fwd[2]))
    out_heads, out_send, lse = attend(zeros_one, qkv_heads, cuts[2], cuts[3], fwd)
    out_parts = [w_out, out_first, out_second, out_far]
    out_parts = out_parts + [send_sibling(part) for part in out_parts]
    out_send, gu_mine, gu_theirs = fence(out_send, gu_mine, gu_theirs)
    attn_tok = lax.all_to_all(out_send, "sp", 0, 0, tiled=True)
    w_gu = join(core, gu_mine, gu_theirs)
    attn_tok, w_gu, dy_far, *out_parts = fence(attn_tok, w_gu, dy_far, *out_parts)
    residual, inv_two, inner = out_proj(places, attn_tok, x_bf, mlp_gain, out_parts)

    b_first = send_first(inner)
    own = ffn(inner, dy, w_gu, w_dn)
    inner, b_first, *own = fence(inner, b_first, *own)
    b_second = send_second(inner)
    first = ffn(b_first, dy_first, w_gu, w_dn)
    b_first, b_second, *first = fence(b_first, b_second, *first)
    b_far = send_second(b_first)
    second = ffn(b_second, dy_second, w_gu, w_dn)
    b_far, db_first, *second = fence(b_far, first[3], *second)
    db_got_first = send_first(db_first)
    far = ffn(b_far, dy_far, w_gu, w_dn)
    db_got_first, db_far, *hid_rows = fence(db_got_first, far[3], own[0], first[0], second[0], far[0])

    b_rows = [inner, b_first, b_second, b_far]
    db_got_far = send_first(db_far)
    dn_keep, dn_give = grad_dn(core, hid_rows, [dy, dy_first, dy_second, dy_far])
    dn_got = send_sibling(dn_give)
    db_got_far, dn_keep, dn_got = fence(db_got_far, dn_keep, dn_got)
    db_pass = (second[3].astype(F32) + db_got_far.astype(F32)).astype(BF)
    dn_parts = [part.reshape(2, 2, dn_keep.shape[0] // planes, width) for part in (dn_keep, dn_got)]
    dn_move = pick_sum(dn_parts, 1 - (plane & 1), 1).astype(BF)
    db_pass, dn_move, *b_rows = fence(db_pass, dn_move, *b_rows)
    db_passed = send_second(db_pass)
    dn_move = lax.ppermute(dn_move, "dp", LINE_NEAR)
    gu_keep, gu_give = grad_gu(
        core,
        b_rows,
        [own[1], first[1], second[1], far[1]],
        [own[2], first[2], second[2], far[2]],
        share,
        planes,
    )
    db_passed, gu_keep, gu_give, dn_move = fence(db_passed, gu_keep, gu_give, dn_move)
    dn_own = pick_sum(dn_parts, plane & 1, 1) + dn_move.astype(F32)
    dn_move = pick(dn_own, 1 - plane // 2).astype(BF)
    db_passed, gu_give, dn_move = fence(db_passed, gu_give, dn_move)
    gu_got = send_sibling(gu_give)
    dn_move = lax.ppermute(dn_move, "dp", LINE_FAR)
    d_resid, d_branch, d_send = resid_back(
        places, own[3], db_got_first, db_passed, residual, inv_two, mlp_gain, dy, out_parts
    )
    d_send, d_branch, gu_got = fence(d_send, d_branch, gu_got)
    d_heads = lax.all_to_all(d_send, "sp", 0, 0, tiled=True).reshape(length, share)
    gu_sum = (gu_keep.astype(F32) + gu_got.astype(F32)).astype(BF)
    gu_z = lax.psum_scatter(
        gu_sum.reshape(planes * CHIPS * quarter, 2 * hidden_chip), "dp", scatter_dimension=0, tiled=True
    )
    gu_z = gu_z.reshape(CHIPS, quarter, 2 * hidden_chip)
    wo_keep, wo_give = grad_wo(core, attn_tok, d_branch)
    d_heads, wo_keep, wo_give, normed, gu_sum = fence(d_heads, wo_keep, wo_give, normed, gu_sum)

    def back_call(heads, start, stop, **kwargs):
        return attend_back(zeros_one, qkv_heads, heads, lse, cos_all, sin_all, start, stop, **kwargs)

    def wo_part(place):
        return pick(wo_keep, place).astype(F32) + pick(wo_got, place).astype(F32)

    turns = (0, (3 * blocks) // 8, blocks // 2, blocks)
    wo_got = send_sibling(wo_give)
    a_first = send_first(normed)
    a_second = send_second(normed)
    bwd = back_call(d_heads, turns[0], turns[1], out=out_heads)
    d_heads, a_first, a_second, wo_got, dn_move, gu_z, normed, *bwd = fence(
        d_heads, a_first, a_second, wo_got, dn_move, gu_z, normed, *bwd
    )
    dn_z = (pick(dn_own, plane // 2) + dn_move.astype(F32)).astype(BF)
    dn_all = lax.all_gather(dn_z, "dp", axis=0, tiled=False)

    gu_z = lax.all_to_all(gu_z, "sp", 0, 0, axis_index_groups=SAME_CORE, tiled=True)
    a_theirs = [send_sibling(normed), send_sibling(a_first), send_sibling(a_second)]
    bwd = back_call(d_heads, turns[1], turns[2], before=bwd)
    wo_first = wo_part(chip ^ (first_mask // 2)).astype(BF)
    wo_far = wo_part(chip ^ 3).astype(BF)
    d_heads, gu_z, a_first, wo_first, wo_far, *moves = fence(d_heads, gu_z, a_first, wo_first, wo_far, *a_theirs, *bwd)
    a_theirs, bwd = moves[:3], moves[3:]

    gu_all = lax.all_gather(gu_z, "dp", axis=0, tiled=False)
    a_far = send_second(a_first)
    wo_far = send_first(wo_far)
    wo_first = send_first(wo_first)
    bwd = back_call(d_heads, turns[2], turns[3], before=bwd)
    wo_pass = (wo_part(chip ^ (second_mask // 2)) + wo_far.astype(F32)).astype(BF)
    dp_heads, wo_first, wo_pass, a_far, dn_all = fence(bwd[0], wo_first, wo_pass, a_far, dn_all)

    wo_passed = send_second(wo_pass)
    a_theirs.append(send_sibling(a_far))
    back = lax.all_to_all(dp_heads, "sp", 0, 0, tiled=True)
    grad_wq = grad_qkv(places, [normed, a_first, a_second, a_far] + list(a_theirs), dp_heads, planes)
    wo_passed, grad_wq = fence(wo_passed, grad_wq)
    wo_rows = (wo_part(chip) + wo_first.astype(F32) + wo_passed.astype(F32)).astype(BF)
    split = grad_wq.shape[2]
    last_parts = [jnp.concatenate([grad_wq, wo_rows.reshape(planes, quarter, width)], axis=2)]
    y_far, y_first = far[4], first[4]
    moves = None
    for step in range(1, planes):
        moves = line_scatter_sends(last_parts, moves, step, 0)
        y_far, y_first, *moves = fence(y_far, y_first, *moves)
        moves = line_scatter_move(moves, step)
        if step == 1:
            back, *moves = fence(back, *moves)
        elif step == 2:
            y_got_far = send_first(y_far)
            y_got_far, *moves = fence(y_got_far, *moves)
        moves = fence(*moves)
    last_z = line_scatter_end(last_parts, moves, 0)
    wq_z = last_z[:, :split].reshape(quarter, devices, split // devices).transpose(1, 0, 2)
    wq_z, wo_z, gu_all = fence(wq_z, last_z[:, split:], gu_all)
    wq_z = lax.all_to_all(wq_z, "sp", 0, 0, tiled=True)
    grad_tokens = in_back(places, back, x_bf, inv_one, attn_gain, d_resid, qkv_parts).reshape(tokens.shape)
    y_pass = (second[4].astype(F32) + y_got_far.astype(F32)).astype(BF)
    last_z = jnp.concatenate([wq_z.transpose(1, 0, 2).reshape(quarter, split), wo_z], axis=1)
    last_z, grad_tokens, y_pass, y_first = fence(last_z, grad_tokens, y_pass, y_first)
    y_got_first = send_first(y_first)
    y_passed = send_second(y_pass)
    last_steps = [(last_z, last_z)]
    outs = []
    for step in range(1, planes):
        if step == planes - 1:
            y_got_first, y_passed, *moves = fence(y_got_first, y_passed, *last_steps[-1])
            last_steps[-1] = tuple(moves)
        last_steps.append(line_gather_move(last_steps[-1], step))
        if step == 1:
            outs += spread(gu_all, w_gate_up, g_mlp.astype(F32).reshape(share, 1))
        elif step == 2:
            outs.append(dn_all.astype(F32).reshape(w_down.shape))
        if step == planes - 1:
            y_sum = own[4].astype(F32) + y_got_first.astype(F32) + y_passed.astype(F32)
            outs.append((residual + y_sum).astype(BF).reshape(tokens.shape))
        moves = fence(*last_steps[-1], *outs)
        last_steps[-1], outs = tuple(moves[:2]), list(moves[2:])
    grad_w_gate_up, grad_g_mlp, grad_w_down, output = outs
    grad_w_qkv, grad_g_attn, grad_w_out = spread_last(last_steps, w_qkv, g_attn.astype(F32).reshape(share, 1), width)
    return (
        output,
        grad_tokens,
        grad_w_qkv,
        grad_w_out,
        grad_w_gate_up,
        grad_w_down,
        grad_g_attn.reshape(share),
        grad_g_mlp.reshape(share),
    )


def solution(mesh):
    in_specs = (
        P("dp", "sp", None),
        P("dp", "sp"),
        P("dp", "sp"),
        P("dp", "sp", None),
        P("sp", None),
        P("sp", None),
        P("sp", None),
        P("sp", None),
        P("sp"),
        P("sp"),
    )
    out_specs = (
        P("dp", "sp", None),
        P("dp", "sp", None),
        P("sp", None),
        P("sp", None),
        P("sp", None),
        P("sp", None),
        P("sp"),
        P("sp"),
    )
    body = fast_body if dict(mesh.shape) == {"dp": 4, "sp": 2 * CHIPS} else general_body
    return jax.shard_map(body, mesh=mesh, in_specs=in_specs, out_specs=out_specs, check_vma=False)
```

```python
import functools
import math

import jax
import jax.numpy as jnp
from jax import lax
from jax.experimental import pallas as pl
from jax.experimental.pallas import tpu as pltpu
from jax.sharding import PartitionSpec as P

D = 2048
H = 32
KV = 4
HD = 64
FF = 5632


EPSILON = 1e-05
ROPE_BASE = 10000.0
MASKED = -1e30


def rope_tables(positions, head_size):
    half_dim = head_size // 2
    frequency = ROPE_BASE ** (-(jnp.arange(half_dim, dtype=jnp.float32) * 2.0 / head_size))
    angles = positions.astype(jnp.float32)[:, None] * frequency[None, :]
    return (jnp.cos(angles), jnp.sin(angles))


def rotate(values, cosine, sine_tab, inverse_turn):
    half_dim = values.shape[-1] // 2
    first_half = values[..., :half_dim]
    second = values[..., half_dim:]
    cos_wide = cosine[:, None, :]
    sin_wide = sine_tab[:, None, :]
    if inverse_turn:
        sin_wide = -sin_wide
    return jnp.concatenate(
        [first_half * cos_wide - second * sin_wide, second * cos_wide + first_half * sin_wide],
        axis=-1,
    )


def rms_norm(values, gain_vec):
    inverse = lax.rsqrt(jnp.mean(values * values, axis=-1, keepdims=True) + EPSILON)
    return (values * inverse * gain_vec, inverse)


def norm_back(values, inverse, gain_vec, upstream):
    scaled = upstream * gain_vec
    inner_mean = jnp.mean(scaled * values, axis=-1, keepdims=True)
    through = inverse * scaled - values * inverse**3 * inner_mean
    gain_grad = jnp.sum(upstream * values * inverse, axis=0)
    return (through, gain_grad)


def attention_inputs(flat_in, qkv_full, gain_vec, cosine, sine_tab):
    row_count = flat_in.shape[0]
    group_size = H // KV
    normed, inverse = rms_norm(flat_in, gain_vec)
    normed = normed.astype(jnp.bfloat16)
    projected = jnp.dot(normed, qkv_full, preferred_element_type=jnp.float32)
    queries = rotate(projected[:, :D].reshape(row_count, H, HD), cosine, sine_tab, False)
    key_heads = rotate(
        projected[:, D : D + KV * HD].reshape(row_count, KV, HD), cosine, sine_tab, False
    )
    value_heads = projected[:, D + KV * HD :].reshape(row_count, KV, HD)
    key_wide = jnp.broadcast_to(key_heads[:, :, None], (row_count, KV, group_size, HD)).reshape(
        row_count, D
    )
    value_wide = jnp.broadcast_to(value_heads[:, :, None], (row_count, KV, group_size, HD)).reshape(
        row_count, D
    )
    stacked = jnp.stack([queries.reshape(row_count, D), key_wide, value_wide]).astype(jnp.bfloat16)
    return (normed, inverse, stacked)


def block_mask(seg_full, position, row_begin, finish):
    row_seg = seg_full[:, row_begin:finish]
    col_seg = seg_full[:, :finish]
    same_doc = row_seg[:, :, None] == col_seg[:, None, :]
    causal = position[row_begin:finish, None] >= position[None, :finish]
    return same_doc & causal[None]


def attention_forward(queries, key_heads, value_heads, seg_full, score_scale):
    length = queries.shape[1]
    block_rows = min(512, length)
    position = jnp.arange(length, dtype=jnp.int32)
    outputs = []
    lse_parts = []
    for block_num in range(length // block_rows):
        row_begin = block_num * block_rows
        finish = row_begin + block_rows
        scores = (
            jnp.einsum(
                "sqhd,skhd->shqk",
                queries[:, row_begin:finish],
                key_heads[:, :finish],
                preferred_element_type=jnp.float32,
            )
            * score_scale
        )
        allowed = block_mask(seg_full, position, row_begin, finish)
        scores = jnp.where(allowed[:, None], scores, MASKED)
        row_max = jnp.max(scores, axis=-1, keepdims=True)
        shifted = jnp.exp(scores - row_max)
        row_total = jnp.sum(shifted, axis=-1, keepdims=True)
        softmax_w = (shifted / row_total).astype(jnp.bfloat16)
        outputs.append(
            jnp.einsum(
                "shqk,skhd->sqhd",
                softmax_w,
                value_heads[:, :finish],
                preferred_element_type=jnp.float32,
            )
        )
        lse_parts.append(row_max + jnp.log(row_total))
    return (jnp.concatenate(outputs, axis=1), jnp.concatenate(lse_parts, axis=2))


def attention_backward(queries, key_heads, value_heads, seg_full, log_sums, grad_out, score_scale):
    length = queries.shape[1]
    block_rows = min(512, length)
    position = jnp.arange(length, dtype=jnp.int32)
    grad_query = []
    grad_key = jnp.zeros(key_heads.shape, jnp.float32)
    grad_value = jnp.zeros(value_heads.shape, jnp.float32)
    for block_num in range(length // block_rows):
        row_begin = block_num * block_rows
        finish = row_begin + block_rows
        query_rows = queries[:, row_begin:finish]
        grad_rows = grad_out[:, row_begin:finish]
        key_part = key_heads[:, :finish]
        value_part = value_heads[:, :finish]
        scores = (
            jnp.einsum("sqhd,skhd->shqk", query_rows, key_part, preferred_element_type=jnp.float32)
            * score_scale
        )
        allowed = block_mask(seg_full, position, row_begin, finish)
        softmax_f = jnp.where(
            allowed[:, None], jnp.exp(scores - log_sums[:, :, row_begin:finish]), 0.0
        )
        grad_probs = jnp.einsum(
            "sqhd,skhd->shqk", grad_rows, value_part, preferred_element_type=jnp.float32
        )
        row_delta = jnp.sum(softmax_f * grad_probs, axis=-1, keepdims=True)
        grad_scores = (softmax_f * (grad_probs - row_delta)).astype(jnp.bfloat16)
        grad_query.append(
            jnp.einsum("shqk,skhd->sqhd", grad_scores, key_part, preferred_element_type=jnp.float32)
            * score_scale
        )
        grad_key = grad_key.at[:, :finish].add(
            jnp.einsum(
                "shqk,sqhd->skhd", grad_scores, query_rows, preferred_element_type=jnp.float32
            )
            * score_scale
        )
        grad_value = grad_value.at[:, :finish].add(
            jnp.einsum(
                "shqk,sqhd->skhd",
                softmax_f.astype(jnp.bfloat16),
                grad_rows,
                preferred_element_type=jnp.float32,
            )
        )
    return (jnp.concatenate(grad_query, axis=1), grad_key, grad_value)


def general_body(tokens, segment_ids, selected, cotangent, w_qkv, w_out, w_gate_up, w_down, g_attn, g_mlp):
    streams, local_len, model_dim = tokens.shape
    sp_count = lax.axis_size("sp")
    sp_index = lax.axis_index("sp")
    row_count = streams * local_len
    group_size = H // KV
    kv_width = KV * HD
    score_scale = HD ** (-0.5)
    contract = (((0,), (0,)), ((), ()))
    seg_full = lax.all_gather(segment_ids, "sp", axis=1, tiled=True)
    first_count = jnp.sum((seg_full == 0).astype(jnp.int32), axis=1, keepdims=True)
    local_pos = (
        sp_index * local_len
        + jnp.arange(local_len, dtype=jnp.int32)[None, :]
        - segment_ids * first_count
    )
    cosine, sine_tab = rope_tables(local_pos.reshape(row_count), HD)
    shards = (w_qkv, w_out, w_gate_up, w_down, g_attn, g_mlp)
    gathered = (
        lax.all_gather(shards[0], "sp", axis=0, tiled=True),
        lax.all_gather(shards[1], "sp", axis=0, tiled=True),
        lax.all_gather(shards[2], "sp", axis=0, tiled=True),
        lax.all_gather(shards[3], "sp", axis=0, tiled=True),
        lax.all_gather(shards[4], "sp", axis=0, tiled=True),
        lax.all_gather(shards[5], "sp", axis=0, tiled=True),
    )
    qkv_full, out_full, gate_up_full, down_full, attn_gain, mlp_gain = gathered
    attn_gain = attn_gain.astype(jnp.float32)
    mlp_gain = mlp_gain.astype(jnp.float32)
    flat_in = tokens.reshape(row_count, model_dim).astype(jnp.float32)
    normed, inverse_one, stacked = attention_inputs(flat_in, qkv_full, attn_gain, cosine, sine_tab)
    head_view = lax.all_to_all(
        stacked.reshape(3, streams, local_len, model_dim),
        "sp",
        split_axis=3,
        concat_axis=2,
        tiled=True,
    )
    length = head_view.shape[2]
    heads_here = head_view.shape[3] // HD
    head_shape = (streams, length, heads_here, HD)
    queries = head_view[0].reshape(head_shape)
    key_heads = head_view[1].reshape(head_shape)
    value_heads = head_view[2].reshape(head_shape)
    attn_heads, log_sums = attention_forward(queries, key_heads, value_heads, seg_full, score_scale)
    attn_send = attn_heads.astype(jnp.bfloat16).reshape(streams, length, heads_here * HD)
    attn_tok = lax.all_to_all(attn_send, "sp", split_axis=1, concat_axis=2, tiled=True).reshape(
        row_count, model_dim
    )
    branch = jnp.dot(attn_tok, out_full, preferred_element_type=jnp.float32)
    residual = flat_in + branch
    inner_f, inverse_two = rms_norm(residual, mlp_gain)
    inner_in = inner_f.astype(jnp.bfloat16)
    gate_up = jnp.dot(inner_in, gate_up_full, preferred_element_type=jnp.float32)
    gate_part = gate_up[:, :FF]
    up_part = gate_up[:, FF:]
    sigmoid_g = jax.nn.sigmoid(gate_part)
    silu_gate = gate_part * sigmoid_g
    hidden = (silu_gate * up_part).astype(jnp.bfloat16)
    result = residual + jnp.dot(hidden, down_full, preferred_element_type=jnp.float32)
    output = result.astype(jnp.bfloat16).reshape(streams, local_len, model_dim)
    qkv_back, out_back, gate_up_back, down_back, attn_gain_b, mlp_gain_b = gathered
    attn_gain_b = attn_gain_b.astype(jnp.float32)
    mlp_gain_b = mlp_gain_b.astype(jnp.float32)
    grad_y = (cotangent * selected[:, :, None].astype(jnp.bfloat16)).reshape(row_count, model_dim)
    grad_hidden = jnp.dot(grad_y, down_back.T, preferred_element_type=jnp.float32)
    silu_slope = sigmoid_g * (1.0 + gate_part * (1.0 - sigmoid_g))
    grad_both = jnp.concatenate(
        [grad_hidden * up_part * silu_slope, grad_hidden * silu_gate], axis=1
    ).astype(jnp.bfloat16)
    grad_inner = jnp.dot(grad_both, gate_up_back.T, preferred_element_type=jnp.float32)
    grad_resid, gain_two = norm_back(residual, inverse_two, mlp_gain_b, grad_inner)
    grad_resid = grad_resid + grad_y.astype(jnp.float32)
    grad_branch = grad_resid.astype(jnp.bfloat16)
    grad_attn = jnp.dot(grad_branch, out_back.T, preferred_element_type=jnp.float32).astype(
        jnp.bfloat16
    )
    grad_view = lax.all_to_all(
        grad_attn.reshape(streams, local_len, model_dim),
        "sp",
        split_axis=2,
        concat_axis=1,
        tiled=True,
    )
    grad_view = grad_view.reshape(head_shape)
    grad_q, grad_k, grad_v = attention_backward(
        queries, key_heads, value_heads, seg_full, log_sums, grad_view, score_scale
    )
    back_send = (
        jnp.stack([grad_q, grad_k, grad_v])
        .astype(jnp.bfloat16)
        .reshape(3, streams, length, heads_here * HD)
    )
    returned = lax.all_to_all(back_send, "sp", split_axis=2, concat_axis=3, tiled=True)
    returned = returned.astype(jnp.float32).reshape(3, row_count, H, HD)
    grad_pq = rotate(returned[0], cosine, sine_tab, True).reshape(row_count, model_dim)
    key_summed = jnp.sum(returned[1].reshape(row_count, KV, group_size, HD), axis=2)
    grad_pk = rotate(key_summed, cosine, sine_tab, True).reshape(row_count, kv_width)
    grad_pv = jnp.sum(returned[2].reshape(row_count, KV, group_size, HD), axis=2).reshape(
        row_count, kv_width
    )
    grad_mixed = jnp.concatenate(
        [grad_pq.astype(jnp.bfloat16), grad_pk.astype(jnp.bfloat16), grad_pv.astype(jnp.bfloat16)],
        axis=1,
    )
    grad_normed = jnp.dot(grad_mixed, qkv_back.T, preferred_element_type=jnp.float32)
    grad_in, gain_one = norm_back(flat_in, inverse_one, attn_gain_b, grad_normed)
    grad_in = grad_in + grad_resid
    grad_tokens = grad_in.astype(jnp.bfloat16).reshape(streams, local_len, model_dim)
    gain_totals = lax.psum((gain_one, gain_two), ("dp", "sp"))
    gain_share = model_dim // sp_count
    grad_g_attn = lax.dynamic_slice_in_dim(gain_totals[0], sp_index * gain_share, gain_share, 0)
    grad_g_mlp = lax.dynamic_slice_in_dim(gain_totals[1], sp_index * gain_share, gain_share, 0)
    row_sums = lax.psum_scatter(
        jnp.concatenate(
            [
                lax.dot_general(normed, grad_mixed, contract, preferred_element_type=jnp.float32),
                lax.dot_general(
                    attn_tok, grad_branch, contract, preferred_element_type=jnp.float32
                ),
                lax.dot_general(inner_in, grad_both, contract, preferred_element_type=jnp.float32),
            ],
            axis=1,
        ).astype(jnp.bfloat16),
        "sp",
        scatter_dimension=0,
        tiled=True,
    )
    down_sums = lax.psum_scatter(
        lax.dot_general(hidden, grad_y, contract, preferred_element_type=jnp.float32).astype(
            jnp.bfloat16
        ),
        "sp",
        scatter_dimension=0,
        tiled=True,
    )
    weight_rows, down_rows = (
        lax.psum(row_sums, "dp").astype(jnp.float32),
        lax.psum(down_sums, "dp").astype(jnp.float32),
    )
    qkv_cols = model_dim + 2 * kv_width
    grad_w_qkv = weight_rows[:, :qkv_cols]
    grad_w_out = weight_rows[:, qkv_cols : qkv_cols + model_dim]
    grad_w_gate_up = weight_rows[:, qkv_cols + model_dim :]
    return (
        output,
        grad_tokens,
        grad_w_qkv,
        grad_w_out,
        grad_w_gate_up,
        down_rows,
        grad_g_attn,
        grad_g_mlp,
    )


CHIPS = 4
BLOCK = 512
SHORT = pl.CostEstimate(flops=1, bytes_accessed=1, transcendentals=0)
LOG2E = math.log2(math.e)
BF = jnp.bfloat16
F32 = jnp.float32
NT = (((1,), (1,)), ((), ()))
TN = (((0,), (0,)), ((), ()))


def swap_pairs(even_mask, odd_mask):
    return [(i, i ^ (odd_mask if i & 1 else even_mask)) for i in range(2 * CHIPS)]


FIRST = swap_pairs(2, 4)
SECOND = swap_pairs(4, 2)
SIBLING = swap_pairs(1, 1)
SAME_CORE = [[0, 2, 4, 6], [1, 3, 5, 7]]


def send_first(x):
    return lax.ppermute(x, "sp", FIRST)


def send_second(x):
    return lax.ppermute(x, "sp", SECOND)


def send_sibling(x):
    return lax.ppermute(x, "sp", SIBLING)


def after(value, *others):
    return lax.optimization_barrier((value,) + others)[0]


def gather_chips(own):
    first = send_first(own)
    second = send_second(after(own, first))
    far = send_second(after(first, second))
    return [own, first, second, far]


def rel_masks(core):
    first = jnp.where(core == 0, 2, 4)
    return first, 6 - first


def fence(*values):
    return lax.optimization_barrier(values)


def gather_vectors(own, me):
    for bit in (1, 2, 4):
        got = lax.ppermute(own, "sp", swap_pairs(bit, bit))
        high = (me & bit) != 0
        own = jnp.concatenate([jnp.where(high, got, own), jnp.where(high, own, got)], axis=1)
    return own


def pick(parts, index):
    return lax.dynamic_index_in_dim(parts, index, 0, keepdims=False)


def pick_sum(parts, index, axis):
    return sum(lax.dynamic_index_in_dim(p, index, axis, keepdims=False).astype(F32) for p in parts)


def line_scatter_sends(parts, got, step, axis):
    planes = parts[0].shape[axis]
    z = lax.axis_index("dp")
    ahead = pick_sum(parts, jnp.clip(planes - step + z, 0, planes - 1), axis)
    back = pick_sum(parts, jnp.clip(z - planes + step, 0, planes - 1), axis)
    if got is not None:
        ahead = ahead + got[0].astype(F32)
        back = back + got[1].astype(F32)
    return ahead.astype(BF), back.astype(BF)


def line_scatter_move(sends, step):
    planes = lax.axis_size("dp")
    right = lax.ppermute(sends[0], "dp", [(i, i + 1) for i in range(step)])
    left = lax.ppermute(sends[1], "dp", [(planes - 1 - i, planes - 2 - i) for i in range(step)])
    return right, left


def line_scatter_end(parts, got, axis):
    own = pick_sum(parts, lax.axis_index("dp"), axis)
    return (own + got[0].astype(F32) + got[1].astype(F32)).astype(BF)


def line_gather_move(got, step):
    planes = lax.axis_size("dp")
    right = lax.ppermute(got[0], "dp", [(i, i + 1) for i in range(step - 1, planes - 1)])
    left = lax.ppermute(got[1], "dp", [(i + 1, i) for i in range(planes - step)])
    return right, left


def line_values(refs, planes, z):
    for step in range(planes):
        place = lax.rem(z - step + planes, planes)
        if step == 0:
            yield place, lambda index: refs[0][index]
        else:
            right, left = refs[step], refs[2 * planes - 1 - step]
            yield place, lambda index, right=right, left=left, step=step: jnp.where(z >= step, right[index], left[index])


def spread_kernel(in_ref, w_ref, g_ref, out_ref, gain_ref):
    planes, _, rows, width = in_ref.shape
    out = in_ref[...].reshape(planes * rows, width).astype(F32)
    out_ref[...] = out
    part = jnp.sum(out * w_ref[...].astype(F32), axis=-1, keepdims=True) / g_ref[...]

    @pl.when(pl.program_id(0) == 0)
    def _():
        gain_ref[...] = part

    @pl.when(pl.program_id(0) > 0)
    def _():
        gain_ref[...] += part


def spread(parts, weight, gain):
    planes, chips, rows, both = parts.shape
    half = both // 2
    total = planes * rows
    line = pl.BlockSpec((total, half), lambda i: (0, i))
    column = pl.BlockSpec((total, 1), lambda i: (0, 0))
    return pl.pallas_call(
        spread_kernel,
        grid=(2 * chips,),
        in_specs=[pl.BlockSpec((planes, 1, rows, half), lambda i: (0, i % chips, 0, i // chips)), line, column],
        out_specs=[line, column],
        out_shape=[jax.ShapeDtypeStruct(weight.shape, F32), jax.ShapeDtypeStruct((total, 1), F32)],
        compiler_params=pltpu.CompilerParams(vmem_limit_bytes=32 * 2**20),
        cost_estimate=SHORT,
        name="spread",
    )(parts, weight, gain)


def spread_last_kernel(z_ref, *refs, planes):
    blocks, (w_ref, g_ref, out_ref, gain_ref, wo_ref) = refs[:-5], refs[-5:]
    rows = blocks[0].shape[0]
    devices = 2 * CHIPS
    width = wo_ref.shape[1]
    heads = width // devices
    each = heads + 2 * HD
    for place, load in line_values(blocks, planes, z_ref[0]):
        span = pl.ds(pl.multiple_of(place * rows, rows), rows)
        pairs = []
        for d in range(devices):
            begin = d * each
            cols = slice(begin, begin + heads)
            out_ref[span, d * heads : (d + 1) * heads] = load((slice(None), cols)).astype(F32)
            pairs.append(load((slice(None), slice(begin + heads, begin + each))).astype(F32))
        for g in range(0, KV, 2):
            low = pairs[2 * g] + pairs[2 * g + 1]
            high = pairs[2 * g + 2] + pairs[2 * g + 3]
            lane = lax.broadcasted_iota(jnp.int32, low.shape, 1)
            begin = width + g * HD
            out_ref[span, begin : begin + 2 * HD] = jnp.where(lane < HD, low, pltpu.roll(high, HD, 1))
            begin = width + (KV + g) * HD
            out_ref[span, begin : begin + 2 * HD] = jnp.where(lane < HD, pltpu.roll(low, HD, 1), high)
        wo_ref[span, :] = load((slice(None), slice(devices * each, devices * each + width))).astype(F32)
    gain_ref[...] = jnp.sum(out_ref[...] * w_ref[...].astype(F32), axis=-1, keepdims=True) / g_ref[...]


def spread_last(steps, weight, gain, width):
    planes = len(steps)
    blocks = [steps[0][0]] + [s[0] for s in steps[1:]] + [s[1] for s in steps[1:]]
    vmem = pl.BlockSpec(memory_space=pltpu.VMEM)
    total = weight.shape[0]
    return pl.pallas_call(
        functools.partial(spread_last_kernel, planes=planes),
        in_specs=[pl.BlockSpec(memory_space=pltpu.SMEM)] + [vmem] * (len(blocks) + 2),
        out_specs=[vmem] * 3,
        out_shape=[
            jax.ShapeDtypeStruct(weight.shape, F32),
            jax.ShapeDtypeStruct((total, 1), F32),
            jax.ShapeDtypeStruct((total, width), F32),
        ],
        compiler_params=pltpu.CompilerParams(vmem_limit_bytes=32 * 2**20),
        cost_estimate=SHORT,
        name="spread_last",
    )(lax.axis_index("dp").reshape(1), *blocks, weight, gain)


def join_kernel(core_ref, mine_ref, theirs_ref, out_ref):
    planes, _, rows, both = mine_ref.shape
    block = jnp.where(pl.program_id(1) == 0, mine_ref[...], theirs_ref[...]).reshape(planes * rows, both)
    out_ref[0, 0, 0] = block[:, : both // 2]
    out_ref[1, 0, 0] = block[:, both // 2 :]


def join(core, mine, theirs):
    planes, chips, rows, both = mine.shape
    spec = pl.BlockSpec((planes, 1, rows, both), lambda c, k, core: (0, c, 0, 0))
    out = pl.pallas_call(
        join_kernel,
        grid_spec=pltpu.PrefetchScalarGridSpec(
            num_scalar_prefetch=1,
            grid=(chips, 2),
            in_specs=[spec, spec],
            out_specs=pl.BlockSpec(
                (2, 1, 1, planes * rows, both // 2), lambda c, k, core: (0, c, (core[0] + k) % 2, 0, 0)
            ),
        ),
        out_shape=jax.ShapeDtypeStruct((2, chips, 2, planes * rows, both // 2), BF),
        compiler_params=pltpu.CompilerParams(vmem_limit_bytes=32 * 2**20),
        cost_estimate=SHORT,
        name="join",
    )(core.reshape(1), mine, theirs)
    return out.reshape(2, 2 * chips * planes * rows, both // 2)


def ffn_kernel(*refs, cuts):
    b_hbm, dy_hbm, wgu_hbm, wd_hbm, hid_hbm, dg_hbm, du_hbm, db_hbm, y_hbm = refs[:9]
    b_ref, dy_ref, wg_ref, wu_ref, wd_ref, hid_ref, dg_ref, du_ref, db_ref, y_ref, sems = refs[9:]
    count = len(cuts) - 1

    def move(source, target, index):
        copy = pltpu.make_async_copy(source, target, sems.at[index])
        copy.start()
        return copy

    b_copy = move(b_hbm, b_ref, 3 * count)
    weights = []
    for c in range(count):
        span = slice(cuts[c], cuts[c + 1])
        gate_copy = move(wgu_hbm.at[0, :, span], wg_ref.at[:, span], 3 * c)
        up_copy = move(wgu_hbm.at[1, :, span], wu_ref.at[:, span], 3 * c + 1)
        weights.append([gate_copy, up_copy])
        if c == 0:
            dy_copy = move(dy_hbm, dy_ref, 3 * count + 1)
        weights[-1].append(move(wd_hbm.at[span, :], wd_ref.at[span, :], 3 * c + 2))
    b_copy.wait()
    for c in range(count):
        span = slice(cuts[c], cuts[c + 1])
        for copy in weights[c][:2]:
            copy.wait()
        gate = jnp.dot(b_ref[...], wg_ref[:, span], preferred_element_type=F32)
        up = jnp.dot(b_ref[...], wu_ref[:, span], preferred_element_type=F32)
        if c == 0:
            dy_copy.wait()
        weights[c][2].wait()
        d_hidden = lax.dot_general(dy_ref[...], wd_ref[span, :], NT, preferred_element_type=F32)
        sigmoid_g = jax.nn.sigmoid(gate)
        silu_gate = gate * sigmoid_g
        hid_ref[:, span] = (silu_gate * up).astype(BF)
        dg_ref[:, span] = (d_hidden * up * (sigmoid_g * (1.0 + gate * (1.0 - sigmoid_g)))).astype(BF)
        du_ref[:, span] = (d_hidden * silu_gate).astype(BF)
    base = 3 * count + 2
    outs = [move(hid_ref, hid_hbm, base), move(dg_ref, dg_hbm, base + 1), move(du_ref, du_hbm, base + 2)]
    y_ref[...] = jnp.dot(hid_ref[...], wd_ref[...], preferred_element_type=F32).astype(BF)
    outs.append(move(y_ref, y_hbm, base + 3))
    d_in = lax.dot_general(dg_ref[...], wg_ref[...], NT, preferred_element_type=F32)
    db_ref[...] = (d_in + lax.dot_general(du_ref[...], wu_ref[...], NT, preferred_element_type=F32)).astype(BF)
    outs.append(move(db_ref, db_hbm, base + 4))
    for copy in outs:
        copy.wait()


def ffn(b_rows, dy_rows, w_gu, w_dn):
    rows, width = b_rows.shape
    hidden = w_dn.shape[0]
    pieces = 3
    cuts = tuple(round(hidden * c / pieces / 128) * 128 for c in range(pieces)) + (hidden,)
    hbm = pl.BlockSpec(memory_space=pl.ANY)
    return pl.pallas_call(
        functools.partial(ffn_kernel, cuts=cuts),
        in_specs=[hbm] * 4,
        out_specs=[hbm] * 5,
        out_shape=[jax.ShapeDtypeStruct((rows, hidden), BF)] * 3 + [jax.ShapeDtypeStruct((rows, width), BF)] * 2,
        scratch_shapes=[pltpu.VMEM((rows, width), BF)] * 2
        + [pltpu.VMEM((width, hidden), BF)] * 2
        + [pltpu.VMEM((hidden, width), BF)]
        + [pltpu.VMEM((rows, hidden), BF)] * 3
        + [pltpu.VMEM((rows, width), BF)] * 2
        + [pltpu.SemaphoreType.DMA((3 * pieces + 7,))],
        compiler_params=pltpu.CompilerParams(vmem_limit_bytes=58 * 2**20),
        cost_estimate=SHORT,
        name="ffn",
    )(b_rows, dy_rows, w_gu, w_dn)


def grad_gu_kernel(core_ref, *refs, count):
    left, right = refs[: 2 * count], refs[2 * count : 4 * count]
    half = right[0].shape[1]
    for side in range(2):
        for kind in range(2):
            total = None
            for r in range(count):
                a_rows = left[side * count + r][...]
                part = lax.dot_general(a_rows, right[kind * count + r][...], TN, preferred_element_type=F32)
                total = part if total is None else total + part
            out_ref = refs[4 * count + side]
            planes, _, rows, _ = out_ref.shape
            out_ref[:, 0, :, kind * half : (kind + 1) * half] = total.astype(BF).reshape(planes, rows, half)


def grad_gu(core, b_rows, dg_rows, du_rows, share, planes):
    count = len(b_rows)
    tokens, width = b_rows[0].shape
    hidden = dg_rows[0].shape[1]
    keep = pl.BlockSpec((tokens, share), lambda c, core: (0, 2 * c + core[0]))
    give = pl.BlockSpec((tokens, share), lambda c, core: (0, 2 * c + 1 - core[0]))
    whole = pl.BlockSpec((tokens, hidden), lambda c, core: (0, 0))
    rows = share // planes
    out = pl.BlockSpec((planes, 1, rows, 2 * hidden), lambda c, core: (0, c, 0, 0))
    return pl.pallas_call(
        functools.partial(grad_gu_kernel, count=count),
        grid_spec=pltpu.PrefetchScalarGridSpec(
            num_scalar_prefetch=1,
            grid=(width // (2 * share),),
            in_specs=[keep] * count + [give] * count + [whole] * (2 * count),
            out_specs=[out, out],
        ),
        out_shape=[jax.ShapeDtypeStruct((planes, width // (2 * share), rows, 2 * hidden), BF)] * 2,
        compiler_params=pltpu.CompilerParams(vmem_limit_bytes=58 * 2**20),
        cost_estimate=SHORT,
        name="grad_gu",
    )(core.reshape(1), *b_rows, *b_rows, *dg_rows, *du_rows)


def grad_qkv_kernel(place_ref, *refs, count):
    dp_ref, out_ref = refs[-2:]
    total = None
    for r in range(count):
        part = lax.dot_general(refs[r][...], dp_ref[place_ref[r]], TN, preferred_element_type=F32)
        total = part if total is None else total + part
    planes, rows, wide = out_ref.shape
    columns = total.shape[1]
    for k in range(wide // columns):
        block = total[k * planes * rows : (k + 1) * planes * rows].astype(BF)
        out_ref[:, :, k * columns : (k + 1) * columns] = block.reshape(planes, rows, columns)


def grad_qkv(places, a_rows, dp_heads, planes):
    count = len(a_rows)
    tokens, width = a_rows[0].shape
    columns = dp_heads.shape[2]
    share = width // count
    depth = 2 * share
    return pl.pallas_call(
        functools.partial(grad_qkv_kernel, count=count),
        grid_spec=pltpu.PrefetchScalarGridSpec(
            num_scalar_prefetch=1,
            grid=(width // depth,),
            in_specs=[pl.BlockSpec((tokens, depth), lambda i, p: (0, i))] * count
            + [pl.BlockSpec(dp_heads.shape, lambda i, p: (0, 0, 0))],
            out_specs=pl.BlockSpec((planes, share // planes, 2 * columns), lambda i, p: (0, 0, i)),
        ),
        out_shape=jax.ShapeDtypeStruct((planes, share // planes, count * columns), BF),
        compiler_params=pltpu.CompilerParams(vmem_limit_bytes=48 * 2**20),
        cost_estimate=SHORT,
        name="grad_qkv",
    )(places, *a_rows, dp_heads)


def swap_halves(values):
    width = values.shape[-1]
    lane = lax.broadcasted_iota(jnp.int32, values.shape, 1)
    ahead = pltpu.roll(values, width - HD // 2, 1)
    behind = pltpu.roll(values, HD // 2, 1)
    return jnp.where(lane % HD < HD // 2, ahead, behind)


def project_kernel(place_ref, x_ref, gain_ref, cos_ref, sin_ref, *refs, count):
    wq_refs, wkv_refs = refs[:count], refs[count : 2 * count]
    send_ref, normed_ref, inv_ref, normed_scr = refs[2 * count :]
    share = normed_scr.shape[2]

    @pl.when(pl.program_id(0) == 0)
    def _():
        x = x_ref[...].astype(F32)
        inv = lax.rsqrt(jnp.mean(x * x, axis=-1, keepdims=True) + EPSILON)
        normed = (x * inv * gain_ref[...]).astype(BF)
        normed_ref[...] = normed
        inv_ref[...] = inv
        for part in range(count):
            normed_scr[part] = normed[:, part * share : (part + 1) * share]

    pq = pkv = None
    for r in range(count):
        a_rows = normed_scr[place_ref[r]]
        q_part = jnp.dot(a_rows, wq_refs[r][...], preferred_element_type=F32)
        kv_part = jnp.dot(a_rows, wkv_refs[r][...], preferred_element_type=F32)
        pq = q_part if pq is None else pq + q_part
        pkv = kv_part if pkv is None else pkv + kv_part
    cos = cos_ref[...]
    sin = sin_ref[...]
    heads = pq.shape[1]
    q_scale = LOG2E * HD**-0.5
    turned = pq * jnp.tile(cos, (1, heads // 128)) + swap_halves(pq) * jnp.tile(sin, (1, heads // 128))
    send_ref[0, :, :heads] = (turned * q_scale).astype(BF)
    lane = lax.broadcasted_iota(jnp.int32, pkv.shape, 1)
    turned_kv = jnp.where(lane < HD, pkv * cos + swap_halves(pkv) * sin, pkv)
    send_ref[0, :, heads:] = turned_kv.astype(BF)


def project(places, x, gain, cos, sin, parts):
    rows, width = x.shape
    count = len(parts)
    heads = width // count
    out_width = heads + 2 * HD
    depth = parts[0].shape[0]
    first_kv = width // (2 * HD)
    return pl.pallas_call(
        functools.partial(project_kernel, count=count),
        grid_spec=pltpu.PrefetchScalarGridSpec(
            num_scalar_prefetch=1,
            grid=(count,),
            in_specs=[
                pl.BlockSpec((rows, width), lambda d, p: (0, 0)),
                pl.BlockSpec((1, width), lambda d, p: (0, 0)),
                pl.BlockSpec((rows, 128), lambda d, p: (0, 0)),
                pl.BlockSpec((rows, 128), lambda d, p: (0, 0)),
            ]
            + [pl.BlockSpec((depth, heads), lambda d, p: (0, d))] * count
            + [pl.BlockSpec((depth, 2 * HD), lambda d, p: (0, first_kv + d // 2))] * count,
            out_specs=[
                pl.BlockSpec((1, rows, out_width), lambda d, p: (d, 0, 0)),
                pl.BlockSpec((rows, width), lambda d, p: (0, 0)),
                pl.BlockSpec((rows, 1), lambda d, p: (0, 0)),
            ],
            scratch_shapes=[pltpu.VMEM((count, rows, width // count), BF)],
        ),
        out_shape=[
            jax.ShapeDtypeStruct((count, rows, out_width), BF),
            jax.ShapeDtypeStruct((rows, width), BF),
            jax.ShapeDtypeStruct((rows, 1), F32),
        ],
        compiler_params=pltpu.CompilerParams(vmem_limit_bytes=48 * 2**20),
        cost_estimate=SHORT,
        name="project",
    )(places, x, gain, cos, sin, *parts, *parts)


def out_proj_kernel(place_ref, attn_ref, x_ref, gain_ref, *refs, count):
    parts, (resid_ref, inv_ref, inner_ref) = refs[:count], refs[count:]
    width = x_ref.shape[1]
    tile = 512
    square = None
    for begin in range(0, width, tile):
        cols = slice(begin, begin + tile)
        total = x_ref[:, cols].astype(F32)
        for r in range(count):
            total = total + jnp.dot(attn_ref[place_ref[r]], parts[r][:, cols], preferred_element_type=F32)
        resid_ref[:, cols] = total
        part = jnp.sum(total * total, axis=-1, keepdims=True)
        square = part if square is None else square + part
    inv = lax.rsqrt(square / width + EPSILON)
    inv_ref[...] = inv
    inner_ref[...] = (resid_ref[...] * inv * gain_ref[...]).astype(BF)


def out_proj(places, attn, x, gain, parts):
    count, rows, share = attn.shape
    width = x.shape[1]
    step = rows // 2
    line = pl.BlockSpec((step, width), lambda i, p: (i, 0))
    return pl.pallas_call(
        functools.partial(out_proj_kernel, count=count),
        grid_spec=pltpu.PrefetchScalarGridSpec(
            num_scalar_prefetch=1,
            grid=(rows // step,),
            in_specs=[
                pl.BlockSpec((count, step, share), lambda i, p: (0, i, 0)),
                line,
                pl.BlockSpec((1, width), lambda i, p: (0, 0)),
            ]
            + [pl.BlockSpec((share, width), lambda i, p: (0, 0))] * count,
            out_specs=[line, pl.BlockSpec((step, 1), lambda i, p: (i, 0)), line],
        ),
        out_shape=[
            jax.ShapeDtypeStruct((rows, width), F32),
            jax.ShapeDtypeStruct((rows, 1), F32),
            jax.ShapeDtypeStruct((rows, width), BF),
        ],
        compiler_params=pltpu.CompilerParams(vmem_limit_bytes=56 * 2**20),
        cost_estimate=SHORT,
        name="out_proj",
    )(places, attn, x, gain, *parts)


def resid_back_kernel(place_ref, db_ref, first_ref, passed_ref, resid_ref, inv_ref, gain_ref, dy_ref, *refs, count):
    parts, (d_resid_ref, branch_ref, send_ref) = refs[:count], refs[count:]
    d_inner = db_ref[...].astype(F32) + first_ref[...].astype(F32) + passed_ref[...].astype(F32)
    resid = resid_ref[...]
    inv = inv_ref[...]
    scaled = d_inner * gain_ref[...]
    inner_mean = jnp.mean(scaled * resid, axis=-1, keepdims=True)
    d_resid = dy_ref[...].astype(F32) + inv * scaled - resid * (inv * inv * inv * inner_mean)
    d_resid_ref[...] = d_resid
    branch = d_resid.astype(BF)
    branch_ref[...] = branch
    for r in range(count):
        d_attn = lax.dot_general(branch, parts[r][...], NT, preferred_element_type=F32)
        send_ref[place_ref[r]] = d_attn.astype(BF)


def resid_back(places, db_own, db_first, db_passed, resid, inv, gain, dy, parts):
    rows, width = resid.shape
    count = len(parts)
    share = parts[0].shape[0]
    step = rows // 2
    line = pl.BlockSpec((step, width), lambda i, p: (i, 0))
    return pl.pallas_call(
        functools.partial(resid_back_kernel, count=count),
        grid_spec=pltpu.PrefetchScalarGridSpec(
            num_scalar_prefetch=1,
            grid=(rows // step,),
            in_specs=[line, line, line, line]
            + [pl.BlockSpec((step, 1), lambda i, p: (i, 0)), pl.BlockSpec((1, width), lambda i, p: (0, 0)), line]
            + [pl.BlockSpec((share, width), lambda i, p: (0, 0))] * count,
            out_specs=[line, line, pl.BlockSpec((count, step, share), lambda i, p: (0, i, 0))],
        ),
        out_shape=[
            jax.ShapeDtypeStruct((rows, width), F32),
            jax.ShapeDtypeStruct((rows, width), BF),
            jax.ShapeDtypeStruct((count, rows, share), BF),
        ],
        compiler_params=pltpu.CompilerParams(vmem_limit_bytes=56 * 2**20),
        cost_estimate=SHORT,
        name="resid_back",
    )(places, db_own, db_first, db_passed, resid, inv, gain, dy, *parts)


def in_back_kernel(place_ref, back_ref, x_ref, inv_ref, gain_ref, d_resid_ref, *refs, count):
    parts, (out_ref, mixed, d_scr) = refs[:count], refs[count:]
    devices, _, width = back_ref.shape
    heads = width - 2 * HD
    for d in range(devices):
        mixed[:, d * heads : (d + 1) * heads] = back_ref[d, :, :heads]
    base = devices * heads
    for g in range(KV):
        pair = back_ref[2 * g, :, heads:].astype(F32) + back_ref[2 * g + 1, :, heads:].astype(F32)
        mixed[:, base + 2 * g * HD : base + 2 * (g + 1) * HD] = pair.astype(BF)
    for r in range(count):
        d_scr[place_ref[r]] = lax.dot_general(mixed[...], parts[r][...], NT, preferred_element_type=F32)
    inv = inv_ref[...]
    share = d_scr.shape[2]
    inner = None
    for c in range(count):
        cols = slice(c * share, (c + 1) * share)
        part = jnp.sum(d_scr[c] * gain_ref[:, cols] * x_ref[:, cols].astype(F32), axis=-1, keepdims=True)
        inner = part if inner is None else inner + part
    factor = inv * inv * inv * (inner / (count * share))
    for c in range(count):
        cols = slice(c * share, (c + 1) * share)
        through = inv * (d_scr[c] * gain_ref[:, cols]) - x_ref[:, cols].astype(F32) * factor
        out_ref[:, cols] = (d_resid_ref[:, cols] + through).astype(BF)


def in_back(places, back, x, inv, gain, d_resid, parts):
    rows, width = x.shape
    count = len(parts)
    share, columns = parts[0].shape
    step = rows // 2
    line = pl.BlockSpec((step, width), lambda i, p: (i, 0))
    return pl.pallas_call(
        functools.partial(in_back_kernel, count=count),
        grid_spec=pltpu.PrefetchScalarGridSpec(
            num_scalar_prefetch=1,
            grid=(rows // step,),
            in_specs=[
                pl.BlockSpec((count, step, back.shape[2]), lambda i, p: (0, i, 0)),
                line,
                pl.BlockSpec((step, 1), lambda i, p: (i, 0)),
                pl.BlockSpec((1, width), lambda i, p: (0, 0)),
                line,
            ]
            + [pl.BlockSpec((share, columns), lambda i, p: (0, 0))] * count,
            out_specs=line,
            scratch_shapes=[pltpu.VMEM((step, columns), BF), pltpu.VMEM((count, step, share), F32)],
        ),
        out_shape=jax.ShapeDtypeStruct((rows, width), BF),
        compiler_params=pltpu.CompilerParams(vmem_limit_bytes=56 * 2**20),
        cost_estimate=SHORT,
        name="in_back",
    )(places, back, x, inv, gain, d_resid, *parts)


def grad_wo_kernel(core_ref, keep_ref, give_ref, branch_ref, keep_out, give_out):
    branch = branch_ref[...]
    keep_out[0] = lax.dot_general(keep_ref[0], branch, TN, preferred_element_type=F32).astype(BF)
    give_out[0] = lax.dot_general(give_ref[0], branch, TN, preferred_element_type=F32).astype(BF)


def grad_wo(core, attn, branch):
    devices, rows, share = attn.shape
    width = branch.shape[1]
    out = pl.BlockSpec((1, share, width), lambda c, core: (c, 0, 0))
    return pl.pallas_call(
        grad_wo_kernel,
        grid_spec=pltpu.PrefetchScalarGridSpec(
            num_scalar_prefetch=1,
            grid=(devices // 2,),
            in_specs=[
                pl.BlockSpec((1, rows, share), lambda c, core: (2 * c + core[0], 0, 0)),
                pl.BlockSpec((1, rows, share), lambda c, core: (2 * c + 1 - core[0], 0, 0)),
                pl.BlockSpec((rows, width), lambda c, core: (0, 0)),
            ],
            out_specs=[out, out],
        ),
        out_shape=[jax.ShapeDtypeStruct((devices // 2, share, width), BF)] * 2,
        compiler_params=pltpu.CompilerParams(vmem_limit_bytes=48 * 2**20),
        cost_estimate=SHORT,
        name="grad_wo",
    )(core.reshape(1), attn, attn, branch)


def grad_dn_kernel(core_ref, *refs, count):
    left, right, (keep_out, give_out) = refs[:count], refs[count : 2 * count], refs[2 * count :]
    total = None
    for r in range(count):
        part = lax.dot_general(left[r][...], right[r][...], TN, preferred_element_type=F32)
        total = part if total is None else total + part
    half = total.shape[0] // 2
    total = total.astype(BF)
    low = core_ref[0] == 0
    keep_out[...] = jnp.where(low, total[:half], total[half:])
    give_out[...] = jnp.where(low, total[half:], total[:half])


def grad_dn(core, hid_rows, dy_rows):
    count = len(hid_rows)
    tokens, hidden = hid_rows[0].shape
    width = dy_rows[0].shape[1]
    tile = 512
    out = pl.BlockSpec((hidden // 2, tile), lambda i, core: (0, i))
    return pl.pallas_call(
        functools.partial(grad_dn_kernel, count=count),
        grid_spec=pltpu.PrefetchScalarGridSpec(
            num_scalar_prefetch=1,
            grid=(width // tile,),
            in_specs=[pl.BlockSpec((tokens, hidden), lambda i, core: (0, 0))] * count
            + [pl.BlockSpec((tokens, tile), lambda i, core: (0, i))] * count,
            out_specs=[out, out],
        ),
        out_shape=[jax.ShapeDtypeStruct((hidden // 2, width), BF)] * 2,
        compiler_params=pltpu.CompilerParams(vmem_limit_bytes=56 * 2**20),
        cost_estimate=SHORT,
        name="grad_dn",
    )(core.reshape(1), *hid_rows, *dy_rows)


def attend_kernel(zeros_ref, q_ref, kv_ref, *refs, heads, start, stop):
    o_ref, send_ref, lse_ref, k_scr, v_scr, acc_ref, max_ref = refs[-7:]
    block = pl.program_id(0) + start
    zeros = zeros_ref[0]
    size = q_ref.shape[0]

    @pl.when(block == start)
    def _():
        for part in range(stop):
            rows = slice(part * size, (part + 1) * size)
            both = kv_ref[rows, :].astype(F32)
            lane = lax.broadcasted_iota(jnp.int32, both.shape, 1)
            k_scr[rows, :] = kv_ref[rows, :HD]
            v_scr[rows, :] = jnp.where(lane < HD, pltpu.roll(both, HD, 1), 1.0).astype(BF)

    first_row = block * size
    lowest = jnp.where(first_row >= zeros, zeros // size, 0)
    acc_ref[...] = jnp.zeros_like(acc_ref)
    max_ref[...] = jnp.full_like(max_ref, MASKED)
    q_heads = [q_ref[:, h * HD : (h + 1) * HD] for h in range(heads)]

    def step(index, masked):
        first_key = pl.multiple_of(index * size, size)
        keys = k_scr[pl.ds(first_key, size), :]
        values = v_scr[pl.ds(first_key, size), :]
        if masked:
            row = first_row + lax.broadcasted_iota(jnp.int32, (size, size), 0)
            col = first_key + lax.broadcasted_iota(jnp.int32, (size, size), 1)
            begin = jnp.where(row >= zeros, zeros, 0)
            refused = (col > row) | (col < begin)

        def score(h):
            return lax.dot_general(q_heads[h], keys, NT, preferred_element_type=F32)

        upcoming = score(0)
        for h in range(heads):
            scores = upcoming
            if h + 1 < heads:
                upcoming = score(h + 1)
            if masked:
                scores = jnp.where(refused, MASKED, scores)
            old_max = max_ref[h]
            new_max = jnp.maximum(old_max, jnp.max(scores, axis=-1, keepdims=True))
            weights = jnp.exp2(scores - jnp.tile(new_max, (1, size // 128)))
            shrink = jnp.exp2(old_max - new_max)
            acc_ref[h] = acc_ref[h] * shrink + jnp.dot(weights.astype(BF), values, preferred_element_type=F32)
            max_ref[h] = new_max

    def visit(index, carry):
        first_key = index * size
        mixed = (index == block) | ((first_row + size > zeros) & (first_key < zeros))

        @pl.when(mixed)
        def _():
            step(index, True)

        @pl.when(jnp.logical_not(mixed))
        def _():
            step(index, False)

        return carry

    lax.fori_loop(lowest, block + 1, visit, 0)
    for h in range(heads):
        acc = acc_ref[h]
        total = acc[:, HD : HD + 1]
        out = acc[:, :HD] / total
        o_ref[:, h * HD : (h + 1) * HD] = out
        send_ref[0, :, h * HD : (h + 1) * HD] = out.astype(BF)
        lse = max_ref[h] + jnp.log2(total)
        lse_ref[0, h : h + 1, :] = jnp.transpose(lse)[:1]


def attend(zeros, qkv, start, stop, before=None):
    length, width = qkv.shape
    q_width = width - 2 * HD
    heads = q_width // HD
    size = BLOCK
    blocks = length // size
    before = () if before is None else before
    return pl.pallas_call(
        functools.partial(attend_kernel, heads=heads, start=start, stop=stop),
        grid_spec=pltpu.PrefetchScalarGridSpec(
            num_scalar_prefetch=1,
            grid=(stop - start,),
            in_specs=[
                pl.BlockSpec((size, q_width), lambda i, z: (i + start, 0)),
                pl.BlockSpec((length, 2 * HD), lambda i, z: (0, q_width // (2 * HD))),
            ]
            + [pl.BlockSpec(memory_space=pl.ANY)] * len(before),
            out_specs=[
                pl.BlockSpec((size, q_width), lambda i, z: (i + start, 0)),
                pl.BlockSpec((1, size, q_width), lambda i, z: (i + start, 0, 0)),
                pl.BlockSpec((1, heads, size), lambda i, z: (i + start, 0, 0)),
            ],
            scratch_shapes=[
                pltpu.VMEM((length, HD), BF),
                pltpu.VMEM((length, 2 * HD), BF),
                pltpu.VMEM((heads, size, 2 * HD), F32),
                pltpu.VMEM((heads, size, 128), F32),
            ],
        ),
        out_shape=[
            jax.ShapeDtypeStruct((length, q_width), F32),
            jax.ShapeDtypeStruct((blocks, size, q_width), BF),
            jax.ShapeDtypeStruct((blocks, heads, size), F32),
        ],
        input_output_aliases={3 + i: i for i in range(len(before))},
        compiler_params=pltpu.CompilerParams(vmem_limit_bytes=48 * 2**20),
        cost_estimate=SHORT,
        name="attend",
    )(zeros, qkv, qkv, *before)


def attend_back_kernel(
    zeros_ref, q_ref, kv_ref, do_ref, lse_ref, cos_ref, sin_ref, extra_ref, *refs, heads, start
):
    send_ref, dq_acc, delta_ref, q_scr, do_scr = refs[-5:]
    block = pl.program_id(0) + start
    zeros = zeros_ref[0]
    size = kv_ref.shape[0]
    length = q_ref.shape[0]
    blocks = length // size

    @pl.when(block == start)
    def _():
        if start == 0:
            dq_acc[...] = jnp.zeros_like(dq_acc)
        else:
            dq_acc[...] = refs[0][...]
            delta_ref[...] = extra_ref[...]
        for part in range(start, blocks):
            rows = slice(part * size, (part + 1) * size)
            if start == 0:
                product = jnp.transpose(do_ref[rows, :].astype(F32) * extra_ref[rows, :])
            for h in range(heads):
                cols = slice(h * HD, (h + 1) * HD)
                q_scr[h, rows, :] = q_ref[rows, cols]
                do_scr[h, rows, :] = do_ref[rows, cols]
                if start == 0:
                    delta_ref[part, h : h + 1, :] = jnp.sum(product[cols], axis=0, keepdims=True)

    first_key = block * size
    both = kv_ref[...]
    keys = both[:, :HD]
    values = both[:, HD:]
    keys_t = jnp.transpose(keys.astype(F32)).astype(BF)
    highest = jnp.where(first_key + size <= zeros, jnp.minimum((zeros + size - 1) // size, blocks), blocks)

    def step(index, carry, masked):
        first_row = pl.multiple_of(index * size, size)
        span = pl.ds(first_row, size)
        if masked:
            col = first_key + lax.broadcasted_iota(jnp.int32, (size, size), 0)
            row = first_row + lax.broadcasted_iota(jnp.int32, (size, size), 1)
            begin = jnp.where(row >= zeros, zeros, 0)
            refused = (col > row) | (col < begin)

        def products(h):
            q_rows = q_scr[h, span, :]
            do_rows = do_scr[h, span, :]
            scores = lax.dot_general(keys, q_rows, NT, preferred_element_type=F32)
            d_prob = lax.dot_general(values, do_rows, NT, preferred_element_type=F32)
            return q_rows, do_rows, scores, d_prob

        upcoming = products(0)
        dk_sum, dv_sum = carry
        for h in range(heads):
            q_rows, do_rows, scores, d_prob = upcoming
            if h + 1 < heads:
                upcoming = products(h + 1)
            shifted = scores - lse_ref[index, h : h + 1, :]
            if masked:
                shifted = jnp.where(refused, MASKED, shifted)
            prob = jnp.exp2(shifted)
            d_score = (prob * (d_prob - delta_ref[index, h : h + 1, :])).astype(BF)
            dv_sum = dv_sum + jnp.dot(prob.astype(BF), do_rows, preferred_element_type=F32)
            dk_sum = dk_sum + jnp.dot(d_score, q_rows, preferred_element_type=F32)
            dq_acc[h * HD : (h + 1) * HD, span] += jnp.dot(keys_t, d_score, preferred_element_type=F32)
        return dk_sum, dv_sum

    def visit(index, carry):
        first_row = index * size
        mixed = (index == block) | ((first_row + size > zeros) & (first_key < zeros))
        return lax.cond(
            mixed,
            lambda c: step(index, c, True),
            lambda c: step(index, c, False),
            carry,
        )

    zero = jnp.zeros((size, HD), F32)
    dk_sum, dv_sum = lax.fori_loop(block, highest, visit, (zero, zero))
    q_width = heads * HD
    done = pl.ds(pl.multiple_of(first_key, size), size)
    cos = cos_ref[...]
    sin = sin_ref[...]
    dq = jnp.transpose(dq_acc[:, done]) * HD**-0.5
    dq = dq * jnp.tile(cos, (1, q_width // 128)) - swap_halves(dq) * jnp.tile(sin, (1, q_width // 128))
    send_ref[0, :, :q_width] = dq.astype(BF)
    dkv = jnp.concatenate([dk_sum * (1.0 / LOG2E), dv_sum], axis=1)
    lane = lax.broadcasted_iota(jnp.int32, dkv.shape, 1)
    send_ref[0, :, q_width:] = jnp.where(lane < HD, dkv * cos - swap_halves(dkv) * sin, dkv).astype(BF)


def attend_back(zeros, qkv, d_out, lse, cos, sin, start, stop, out=None, before=None):
    length, width = qkv.shape
    q_width = width - 2 * HD
    heads = q_width // HD
    size = BLOCK
    blocks = length // size
    whole = lambda *shape: pl.BlockSpec(shape, lambda j, z: (0,) * len(shape))
    if before is None:
        operands = (out,)
        specs = [whole(length, q_width)]
        aliases = {}
    else:
        send, d_query, delta = before
        operands = (delta, d_query, send)
        specs = [whole(blocks, heads, size), whole(q_width, length), pl.BlockSpec(memory_space=pl.ANY)]
        aliases = {9: 0}
    return pl.pallas_call(
        functools.partial(attend_back_kernel, heads=heads, start=start),
        grid_spec=pltpu.PrefetchScalarGridSpec(
            num_scalar_prefetch=1,
            grid=(stop - start,),
            in_specs=[
                whole(length, q_width),
                pl.BlockSpec((size, 2 * HD), lambda j, z: (j + start, q_width // (2 * HD))),
                whole(length, q_width),
                whole(blocks, heads, size),
                pl.BlockSpec((size, 128), lambda j, z: (j + start, 0)),
                pl.BlockSpec((size, 128), lambda j, z: (j + start, 0)),
            ]
            + specs,
            out_specs=[
                pl.BlockSpec((1, size, width), lambda j, z: (j + start, 0, 0)),
                whole(q_width, length),
                whole(blocks, heads, size),
            ],
            scratch_shapes=[
                pltpu.VMEM((heads, length, HD), BF),
                pltpu.VMEM((heads, length, HD), BF),
            ],
        ),
        out_shape=[
            jax.ShapeDtypeStruct((blocks, size, width), BF),
            jax.ShapeDtypeStruct((q_width, length), F32),
            jax.ShapeDtypeStruct((blocks, heads, size), F32),
        ],
        input_output_aliases=aliases,
        compiler_params=pltpu.CompilerParams(vmem_limit_bytes=58 * 2**20),
        cost_estimate=SHORT,
        name="attend_back",
    )(zeros, qkv, qkv, d_out, lse, cos, sin, *operands)


def turn_tables(positions):
    cosine, sine = rope_tables(positions, HD)
    return jnp.concatenate([cosine] * 4, axis=1), jnp.concatenate([-sine, sine, -sine, sine], axis=1)


def fast_body(tokens, segment_ids, selected, cotangent, w_qkv, w_out, w_gate_up, w_down, g_attn, g_mlp):
    _, rows, width = tokens.shape
    devices = 2 * CHIPS
    me = lax.axis_index("sp")
    core = me & 1
    planes = lax.axis_size("dp")
    share = width // devices
    kv_width = KV * HD
    first_mask, second_mask = rel_masks(core)
    other = me ^ 1
    chip = me // 2
    place_list = [me, me ^ first_mask, me ^ second_mask, me ^ 6]
    place_list += [other, other ^ second_mask, other ^ first_mask, other ^ 6]
    places = jnp.stack(place_list)
    hidden_chip = 2 * w_down.shape[0]
    quarter = share // planes
    plane = lax.axis_index("dp")
    length = devices * rows
    blocks = length // BLOCK

    count = jnp.sum((segment_ids == 0).astype(F32))
    vectors = jnp.stack([g_attn.astype(F32), g_mlp.astype(F32)] + [jnp.full((share,), count)] * 6)
    paired = [w_qkv[:, :width]]
    for head in range(KV):
        paired.append(w_qkv[:, width + head * HD : width + (head + 1) * HD])
        paired.append(w_qkv[:, width + kv_width + head * HD : width + kv_width + (head + 1) * HD])
    qkv_own = jnp.concatenate(paired, axis=1)
    gu_rows = lax.dynamic_slice_in_dim(w_gate_up, plane * quarter, quarter, 0)
    gu_send = []
    for place in range(CHIPS):
        for begin in (place * hidden_chip, (CHIPS + place) * hidden_chip):
            gu_send.append(gu_rows[:, begin : begin + hidden_chip])
    gu_send = jnp.stack([jnp.concatenate(gu_send[2 * c : 2 * c + 2], axis=1) for c in range(CHIPS)])
    vectors = gather_vectors(vectors, me)
    vectors, qkv_own, gu_send = fence(vectors, qkv_own, gu_send)
    qkv_first = send_first(qkv_own)
    attn_gain = vectors[0:1]
    mlp_gain = vectors[1:2]
    zeros = jnp.sum(vectors[2].reshape(devices, share)[:, 0]).astype(jnp.int32)
    zeros_one = zeros.reshape(1)
    local_pos = me * rows + jnp.arange(rows, dtype=jnp.int32) - segment_ids.reshape(rows) * zeros
    cos, sin = turn_tables(local_pos)
    dy = (cotangent * selected[:, :, None].astype(BF)).reshape(rows, width)
    qkv_own, qkv_first, cos, sin = fence(qkv_own, qkv_first, cos, sin)
    qkv_second = send_second(qkv_own)
    qkv_theirs = [send_sibling(qkv_own), send_sibling(qkv_first)]
    all_places = jnp.arange(length, dtype=jnp.int32)
    cos_all, sin_all = turn_tables(all_places - jnp.where(all_places >= zeros, zeros, 0))
    qkv_first, qkv_second, cos_all, sin_all, *qkv_theirs = fence(qkv_first, qkv_second, cos_all, sin_all, *qkv_theirs)
    qkv_far = send_second(qkv_first)
    qkv_theirs.append(send_sibling(qkv_second))
    qkv_far, dy, *qkv_theirs = fence(qkv_far, dy, *qkv_theirs)
    qkv_theirs.append(send_sibling(qkv_far))
    qkv_parts = [qkv_own, qkv_first, qkv_second, qkv_far] + qkv_theirs
    x_bf = tokens.reshape(rows, width)
    x_bf, w_out, gu_send, *qkv_parts = fence(x_bf, w_out, gu_send, *qkv_parts)
    out_first = send_first(w_out)
    gu_part = lax.all_to_all(gu_send, "sp", 0, 0, axis_index_groups=SAME_CORE, tiled=True)
    qkv_send, normed, inv_one = project(places, x_bf, attn_gain, cos, sin, qkv_parts)
    gu_mine = lax.all_gather(after(gu_part, qkv_send), "dp", axis=0, tiled=False)
    gu_mine = lax.all_gather(after(gu_part, qkv_send), "dp", axis=0, tiled=False)
    down_theirs = send_sibling(w_down)
    w_dn = jnp.where(
        core == 0, jnp.concatenate([w_down, down_theirs], axis=0), jnp.concatenate([down_theirs, w_down], axis=0)
    )
    qkv_heads = lax.all_to_all(qkv_send, "sp", 0, 0, tiled=True).reshape(length, qkv_send.shape[2])

    cuts = (0, (5 * blocks) // 8, (7 * blocks) // 8, blocks)
    qkv_heads, w_dn, out_first = fence(qkv_heads, w_dn, out_first)
    out_second = send_second(after(w_out, qkv_heads))
    dy_first = send_first(after(dy, qkv_heads))
    fwd = attend(zeros_one, qkv_heads, cuts[0], cuts[1])
    qkv_heads, out_second, dy_first, out_first, dy, *fwd = fence(qkv_heads, out_second, dy_first, out_first, dy, *fwd)
    out_far = send_second(out_first)
    dy_second = send_second(dy)
    fwd = attend(zeros_one, qkv_heads, cuts[1], cuts[2], fwd)
    qkv_heads, out_far, dy_second, dy_first, *fwd = fence(qkv_heads, out_far, dy_second, dy_first, *fwd)
    dy_far = send_second(dy_first)
    gu_theirs = send_sibling(after(gu_mine, fwd[2]))
    out_heads, out_send, lse = attend(zeros_one, qkv_heads, cuts[2], cuts[3], fwd)
    out_parts = [w_out, out_first, out_second, out_far]
    out_parts = out_parts + [send_sibling(part) for part in out_parts]
    out_send, gu_mine, gu_theirs = fence(out_send, gu_mine, gu_theirs)
    attn_tok = lax.all_to_all(out_send, "sp", 0, 0, tiled=True)
    w_gu = join(core, gu_mine, gu_theirs)
    attn_tok, w_gu, dy_far, *out_parts = fence(attn_tok, w_gu, dy_far, *out_parts)
    residual, inv_two, inner = out_proj(places, attn_tok, x_bf, mlp_gain, out_parts)

    b_first = send_first(inner)
    own = ffn(inner, dy, w_gu, w_dn)
    inner, b_first, *own = fence(inner, b_first, *own)
    b_second = send_second(inner)
    first = ffn(b_first, dy_first, w_gu, w_dn)
    b_first, b_second, *first = fence(b_first, b_second, *first)
    b_far = send_second(b_first)
    second = ffn(b_second, dy_second, w_gu, w_dn)
    b_far, db_first, *second = fence(b_far, first[3], *second)
    db_got_first = send_first(db_first)
    far = ffn(b_far, dy_far, w_gu, w_dn)
    db_got_first, db_far, *hid_rows = fence(db_got_first, far[3], own[0], first[0], second[0], far[0])

    b_rows = [inner, b_first, b_second, b_far]
    db_got_far = send_first(db_far)
    gu_keep, gu_give = grad_gu(
        core,
        b_rows,
        [own[1], first[1], second[1], far[1]],
        [own[2], first[2], second[2], far[2]],
        share,
        planes,
    )
    db_got_far, gu_keep, gu_give, *hid_rows = fence(db_got_far, gu_keep, gu_give, *hid_rows)
    db_pass = (second[3].astype(F32) + db_got_far.astype(F32)).astype(BF)
    db_pass, gu_give, *hid_rows = fence(db_pass, gu_give, *hid_rows)
    db_passed = send_second(db_pass)
    gu_got = send_sibling(gu_give)
    dn_keep, dn_give = grad_dn(core, hid_rows, [dy, dy_first, dy_second, dy_far])
    gu_got, dn_keep, dn_give = fence(gu_got, dn_keep, dn_give)
    gu_sum = (gu_keep.astype(F32) + gu_got.astype(F32)).astype(BF)
    gu_sum, db_passed, dn_give = fence(gu_sum, db_passed, dn_give)
    gu_z = lax.psum_scatter(
        gu_sum.reshape(planes * CHIPS * quarter, 2 * hidden_chip), "dp", scatter_dimension=0, tiled=True
    )
    gu_z = gu_z.reshape(CHIPS, quarter, 2 * hidden_chip)
    dn_got = send_sibling(dn_give)
    d_resid, d_branch, d_send = resid_back(
        places, own[3], db_got_first, db_passed, residual, inv_two, mlp_gain, dy, out_parts
    )
    d_send, d_branch, dn_got = fence(d_send, d_branch, dn_got)
    d_heads = lax.all_to_all(d_send, "sp", 0, 0, tiled=True).reshape(length, share)
    wo_keep, wo_give = grad_wo(core, attn_tok, d_branch)
    dn_sum = (dn_keep.astype(F32) + dn_got.astype(F32)).astype(BF)
    d_heads, wo_keep, wo_give, normed, dn_sum = fence(d_heads, wo_keep, wo_give, normed, dn_sum)

    def back_call(heads, start, stop, **kwargs):
        return attend_back(zeros_one, qkv_heads, heads, lse, cos_all, sin_all, start, stop, **kwargs)

    turns = (0, blocks // 4, (3 * blocks) // 8, blocks)
    wo_got = send_sibling(wo_give)
    a_first = send_first(normed)
    a_second = send_second(normed)
    a_theirs = [send_sibling(normed)]
    bwd = back_call(d_heads, turns[0], turns[1], out=out_heads)
    d_heads, a_first, a_second, wo_got, gu_z, dn_sum, *moves = fence(
        d_heads, a_first, a_second, wo_got, gu_z, dn_sum, *a_theirs, *bwd
    )
    a_theirs, bwd = moves[:1], moves[1:]

    def wo_part(place):
        return pick(wo_keep, place).astype(F32) + pick(wo_got, place).astype(F32)

    dn_z = lax.psum_scatter(dn_sum, "dp", scatter_dimension=0, tiled=True)
    gu_z = lax.all_to_all(gu_z, "sp", 0, 0, axis_index_groups=SAME_CORE, tiled=True)
    a_theirs += [send_sibling(a_first), send_sibling(a_second)]
    bwd = back_call(d_heads, turns[1], turns[2], before=bwd)
    d_heads, gu_z, a_first, *moves = fence(d_heads, gu_z, a_first, *a_theirs, *bwd)
    a_theirs, bwd = moves[:3], moves[3:]

    wo_first = wo_part(chip ^ (first_mask // 2)).astype(BF)
    wo_far = wo_part(chip ^ 3).astype(BF)
    d_heads, gu_z, a_first, wo_first, wo_far = fence(d_heads, gu_z, a_first, wo_first, wo_far)
    gu_all = lax.all_gather(gu_z, "dp", axis=0, tiled=False)
    a_far = send_second(a_first)
    wo_far = send_first(wo_far)
    wo_first = send_first(wo_first)
    bwd = back_call(d_heads, turns[2], turns[3], before=bwd)
    wo_pass = (wo_part(chip ^ (second_mask // 2)) + wo_far.astype(F32)).astype(BF)
    dp_heads, wo_first, wo_pass, a_far, dn_z = fence(bwd[0], wo_first, wo_pass, a_far, dn_z)

    wo_passed = send_second(wo_pass)
    a_theirs.append(send_sibling(a_far))
    back = lax.all_to_all(dp_heads, "sp", 0, 0, tiled=True)
    grad_wq = grad_qkv(places, [normed, a_first, a_second, a_far] + list(a_theirs), dp_heads, planes)
    wo_passed, grad_wq = fence(wo_passed, grad_wq)
    wo_rows = (wo_part(chip) + wo_first.astype(F32) + wo_passed.astype(F32)).astype(BF)
    split = grad_wq.shape[2]
    last_parts = [jnp.concatenate([grad_wq, wo_rows.reshape(planes, quarter, width)], axis=2)]
    y_far, y_first = far[4], first[4]
    moves = None
    for step in range(1, planes):
        moves = line_scatter_sends(last_parts, moves, step, 0)
        y_far, y_first, *moves = fence(y_far, y_first, *moves)
        moves = line_scatter_move(moves, step)
        if step == 1:
            dn_all = lax.all_gather(dn_z, "dp", axis=0, tiled=False)
            back, *moves = fence(back, *moves)
        elif step == 2:
            y_got_far = send_first(y_far)
            y_got_far, gu_all, *moves = fence(y_got_far, gu_all, *moves)
        moves = fence(*moves)
    last_z = line_scatter_end(last_parts, moves, 0)
    wq_z = last_z[:, :split].reshape(quarter, devices, split // devices).transpose(1, 0, 2)
    wq_z, wo_z, gu_all = fence(wq_z, last_z[:, split:], gu_all)
    wq_z = lax.all_to_all(wq_z, "sp", 0, 0, tiled=True)
    grad_tokens = in_back(places, back, x_bf, inv_one, attn_gain, d_resid, qkv_parts).reshape(tokens.shape)
    y_pass = (second[4].astype(F32) + y_got_far.astype(F32)).astype(BF)
    last_z = jnp.concatenate([wq_z.transpose(1, 0, 2).reshape(quarter, split), wo_z], axis=1)
    last_z, grad_tokens, y_pass, y_first = fence(last_z, grad_tokens, y_pass, y_first)
    y_got_first = send_first(y_first)
    y_passed = send_second(y_pass)
    last_steps = [(last_z, last_z)]
    outs = []
    for step in range(1, planes):
        if step == planes - 1:
            y_got_first, y_passed, *moves = fence(y_got_first, y_passed, *last_steps[-1])
            last_steps[-1] = tuple(moves)
        last_steps.append(line_gather_move(last_steps[-1], step))
        if step == 1:
            outs += spread(gu_all, w_gate_up, g_mlp.astype(F32).reshape(share, 1))
        elif step == 2:
            outs.append(dn_all.astype(F32).reshape(w_down.shape))
        if step == planes - 1:
            y_sum = own[4].astype(F32) + y_got_first.astype(F32) + y_passed.astype(F32)
            outs.append((residual + y_sum).astype(BF).reshape(tokens.shape))
        moves = fence(*last_steps[-1], *outs)
        last_steps[-1], outs = tuple(moves[:2]), list(moves[2:])
    grad_w_gate_up, grad_g_mlp, grad_w_down, output = outs
    grad_w_qkv, grad_g_attn, grad_w_out = spread_last(last_steps, w_qkv, g_attn.astype(F32).reshape(share, 1), width)
    return (
        output,
        grad_tokens,
        grad_w_qkv,
        grad_w_out,
        grad_w_gate_up,
        grad_w_down,
        grad_g_attn.reshape(share),
        grad_g_mlp.reshape(share),
    )


def solution(mesh):
    in_specs = (
        P("dp", "sp", None),
        P("dp", "sp"),
        P("dp", "sp"),
        P("dp", "sp", None),
        P("sp", None),
        P("sp", None),
        P("sp", None),
        P("sp", None),
        P("sp"),
        P("sp"),
    )
    out_specs = (
        P("dp", "sp", None),
        P("dp", "sp", None),
        P("sp", None),
        P("sp", None),
        P("sp", None),
        P("sp", None),
        P("sp"),
        P("sp"),
    )
    body = fast_body if dict(mesh.shape) == {"dp": 4, "sp": 2 * CHIPS} else general_body
    return jax.shard_map(body, mesh=mesh, in_specs=in_specs, out_specs=out_specs, check_vma=False)
```
